32 devices in a mesh: wide: 16 (over z, x, core), req: 2 (over y).
Axes of the slice: x: 2, y: 2, z: 4, core: 2. Of those that a mesh axis runs over, the one named last changes fastest.
Arguments:
- x_in: bfloat16 [512, 8192], P('req', 'wide'), may hold values from -6 to 6
- w_xz: bfloat16 [8192, 2, 16384], P('req', None, 'wide'), may hold values from -0.0625 to 0.0625
- w_dt: bfloat16 [8192, 256], P('req', 'wide'), may hold values from -0.0625 to 0.0625
- w_bc: bfloat16 [8192, 4096], P('req', 'wide'), may hold values from -0.0625 to 0.0625
- dt_bias: float32 [256], P('wide'), may hold values from -7 to -3
- a_log: float32 [256], P('wide'), may hold values from 0 to 2.77
- d_skip: float32 [256], P('wide'), may hold values from 0.5 to 1.5
- conv_x_w: float32 [4, 16384], P(None, 'wide'), may hold values from -3 to 3
- conv_x_b: float32 [16384], P('wide'), may hold values from -3 to 3
- conv_bc_w: float32 [4, 4096], P(None, 'wide'), may hold values from -3 to 3
- conv_bc_b: float32 [4096], P('wide'), may hold values from -3 to 3
- norm_gain: float32 [16384], P('wide'), may hold values from 0.5 to 1.5
- stretch_start: int32 [2, 2], P('req'), may hold values from 0 to 255, as said below
- prefix_len: int32 [4], P('req'), may hold values from 0 to 32768, as said below
- state_slot: int32 [4], replicated, may hold values from 0 to 15, as said below
- ssm_pool: float32 [16, 256, 64, 256], P('req', 'wide'), may hold values from -6 to 6
- conv_x_pool: bfloat16 [16, 3, 16384], P('req', None, 'wide'), may hold values from -6 to 6
- conv_bc_pool: bfloat16 [16, 3, 4096], P('req', None, 'wide'), may hold values from -6 to 6
Outputs:
- y_out: bfloat16 [512, 16384], P('req', 'wide')
- new_state: float32 [4, 256, 64, 256], P('req', 'wide')
The draws below stay inside these ranges and needn't reach their ends.
Inputs may be any that keep to these rules, and one draw needn't show every extreme that they name: `stretch_start`: each row is 0 first and rises strictly; the 2 requests of an index of req cover its 256 tokens in order. `prefix_len`: zero means no cached state; in every draw some request has zero and one has 32768. `state_slot`: distinct slots; slot s is owned by index s // 8 of req; owners hold very uneven numbers of the requested slots.
All inputs are finite; a program needn't handle non-finite values.
Results may differ from the reference program's by a relative error of at most 0.014.
Values may be sent and summed in bfloat16 or wider, within the bound.
No kernel may reach another device: no remote copies, remote signals or barrier semaphores. Data moves between devices by JAX's collectives and lax.ppermute only.
A program may use at most 192 MiB of HBM per device.

```python
import jax
import jax.numpy as jnp
from jax import lax

D = 8192
HEADS = 256
HEAD_DIM = 64
STATE = 256
GROUPS = 8
CONV = 4
TOK_G = 256
REQ_G = 2
SLOTS_DEV = 8
PREFIX_MOST = 32768
TOKENS = 512
REQS = 4
STATE_SLOT_TOTAL = 16
N_REQ = 2


def draw_stretch_start(key, part):
    row_keys = jax.random.split(key, N_REQ)

    def one_row(row_key):
        split_positions = jax.random.permutation(row_key, TOK_G - 1)[:REQ_G - 1] + 1
        return jnp.concatenate([jnp.zeros((1,), jnp.int32), jnp.sort(split_positions).astype(jnp.int32)])
    rows = jax.vmap(one_row)(row_keys).astype(jnp.int32)
    first_key = jax.random.fold_in(key, 7)
    first_picks = jax.random.permutation(first_key, TOK_G - 2)[:REQ_G - 2] + 1
    first_row = jnp.concatenate([jnp.zeros((1,), jnp.int32), jnp.sort(first_picks).astype(jnp.int32), jnp.full((1,), TOK_G - 1, jnp.int32)])
    rows = rows.at[0].set(first_row)
    return rows.astype(jnp.int32)


def draw_prefix_len(key, part):
    initial_random_key, second_key = jax.random.split(key)
    values = jax.random.randint(initial_random_key, (REQS,), -(PREFIX_MOST // 4), PREFIX_MOST + 1)
    values = jnp.maximum(values, 0)
    selected_entries = jax.random.permutation(second_key, REQS)
    values = values.at[selected_entries[0]].set(0)
    if REQS > 1:
        values = values.at[selected_entries[1]].set(PREFIX_MOST)
    return values.astype(jnp.int32)


def draw_state_slot(key, part):
    initial_random_key, second_key, third_key = jax.random.split(key, 3)
    holder_preference = jax.random.randint(initial_random_key, (N_REQ,), 0, 4)
    random_jitter = jax.random.randint(second_key, (STATE_SLOT_TOTAL,), 0, 4096)
    holder_numbers = jnp.arange(STATE_SLOT_TOTAL, dtype=jnp.int32) // SLOTS_DEV
    combined_scores = (holder_preference[holder_numbers] * 4096 + random_jitter) * STATE_SLOT_TOTAL + jnp.arange(STATE_SLOT_TOTAL, dtype=jnp.int32)
    combined_scores = combined_scores.at[STATE_SLOT_TOTAL - 1].set(jnp.max(combined_scores) + 1)
    top_values, chosen = lax.top_k(combined_scores, REQS)
    shuffle = jax.random.permutation(third_key, REQS)
    return chosen[shuffle].astype(jnp.int32)


def block_levels(stream_key, shape, cuts, least, largest):
    loudness, own = 1.0, jax.random.fold_in(stream_key, 6)
    for dim, blocks in cuts:
        heights = jnp.exp(jax.random.uniform(jax.random.fold_in(own, dim), (blocks,), jnp.float32, least / len(cuts), largest / len(cuts)))
        loudness = loudness * jnp.repeat(heights, shape[dim] // blocks).reshape([-1 if axis == dim else 1 for axis in range(len(shape))])
    return loudness


def scatter_about(rng, shape, spread, bound, cuts=(), kind=jnp.bfloat16):
    array = spread * jax.random.normal(rng, shape, jnp.float32)
    if cuts:
        array = array * block_levels(rng, shape, cuts, -0.22, 0.18)
    return jnp.clip(array, -bound, bound).astype(kind)


def setup_inputs(seed: int = 0) -> dict:
    key_list = jax.random.split(jax.random.key(seed), 19)
    x_in = scatter_about(key_list[0], (TOKENS, D), 1.0, 6.0, ((0, 2), (1, 16)))
    w_xz = scatter_about(key_list[1], (D, 2, HEADS * HEAD_DIM), D ** -0.5, 0.0625, ((0, 2), (2, 16)))
    w_dt = scatter_about(key_list[2], (D, HEADS), D ** -0.5, 0.0625, ((0, 2), (1, 16)))
    w_bc = scatter_about(key_list[3], (D, 2 * GROUPS * STATE), D ** -0.5, 0.0625, ((0, 2), (1, 16)))
    dt_bias = jnp.clip(-7.0 + 4.0 * jax.random.uniform(key_list[4], (HEADS,), jnp.float32) ** block_levels(key_list[4], (HEADS,), ((0, 16),), -0.2, 0.2), -7.0, -3.0)
    a_log = jnp.clip(2.77 * jax.random.uniform(key_list[5], (HEADS,), jnp.float32) ** block_levels(key_list[5], (HEADS,), ((0, 16),), -0.2, 0.2), 0.0, 2.77)
    d_skip = jnp.clip(0.5 + 1.0 * jax.random.uniform(key_list[6], (HEADS,), jnp.float32) ** block_levels(key_list[6], (HEADS,), ((0, 16),), -0.2, 0.2), 0.5, 1.5)
    conv_x_w = scatter_about(key_list[7], (CONV, HEADS * HEAD_DIM), 0.5, 3.0, ((1, 16),), jnp.float32)
    conv_x_b = scatter_about(key_list[8], (HEADS * HEAD_DIM,), 0.5, 3.0, ((0, 16),), jnp.float32)
    conv_bc_w = scatter_about(key_list[9], (CONV, 2 * GROUPS * STATE), 0.5, 3.0, ((1, 16),), jnp.float32)
    conv_bc_b = scatter_about(key_list[10], (2 * GROUPS * STATE,), 0.5, 3.0, ((0, 16),), jnp.float32)
    norm_gain = jnp.clip(1.0 + 0.1 * jax.random.normal(key_list[11], (HEADS * HEAD_DIM,), jnp.float32), 0.5, 1.5)
    stretch_start = draw_stretch_start(jax.random.fold_in(key_list[18], 71), 0)
    prefix_len = draw_prefix_len(jax.random.fold_in(key_list[18], 71), 0)
    state_slot = draw_state_slot(jax.random.fold_in(key_list[18], 71), 0)
    ssm_pool = scatter_about(key_list[15], (STATE_SLOT_TOTAL, HEADS, HEAD_DIM, STATE), 1.0, 6.0, ((0, 2), (1, 16)), jnp.float32)
    conv_x_pool = scatter_about(key_list[16], (STATE_SLOT_TOTAL, CONV - 1, HEADS * HEAD_DIM), 1.0, 6.0, ((0, 2), (2, 16)))
    conv_bc_pool = scatter_about(key_list[17], (STATE_SLOT_TOTAL, CONV - 1, 2 * GROUPS * STATE), 1.0, 6.0, ((0, 2), (2, 16)))
    return {"x_in": x_in, "w_xz": w_xz, "w_dt": w_dt, "w_bc": w_bc, "dt_bias": dt_bias, "a_log": a_log, "d_skip": d_skip, "conv_x_w": conv_x_w, "conv_x_b": conv_x_b, "conv_bc_w": conv_bc_w, "conv_bc_b": conv_bc_b, "norm_gain": norm_gain, "stretch_start": stretch_start, "prefix_len": prefix_len, "state_slot": state_slot, "ssm_pool": ssm_pool, "conv_x_pool": conv_x_pool, "conv_bc_pool": conv_bc_pool}


NORM_EPS = 1e-05

def segments(starts, count_tok):
    position = jnp.arange(count_tok, dtype=jnp.int32)
    seg_ids = lax.optimization_barrier(jnp.sum((position[:, None] >= starts[None, :]).astype(jnp.int32), 1)) - 1
    member = seg_ids[:, None] == jnp.arange(starts.shape[0], dtype=jnp.int32)[None, :]
    offset = position - lax.optimization_barrier(jnp.sum(jnp.where(member, starts[None, :], 0), 1))
    same_req = seg_ids[:, None] == seg_ids[None, :]
    causal = position[:, None] >= position[None, :]
    return (member.astype(jnp.float32), offset, (same_req & causal).astype(jnp.float32))

def causal_conv(inputs, cache, kernel, bias, member, offset):
    kernel_len = kernel.shape[0]
    count_tok, channels = inputs.shape
    count_req = cache.shape[0]
    history = jnp.dot(member, cache.reshape(count_req, (kernel_len - 1) * channels), precision=lax.Precision.HIGHEST)
    history = history.reshape(count_tok, kernel_len - 1, channels)
    values = inputs.astype(jnp.float32)
    total = bias[None, :] + kernel[kernel_len - 1][None, :] * values
    for lag_step in range(1, kernel_len):
        shifted = jnp.concatenate([jnp.zeros((lag_step, channels), jnp.float32), values[:count_tok - lag_step]], 0)
        earlier = jnp.zeros((count_tok, channels), jnp.float32)
        for slot_place in range(kernel_len - 1):
            hit_place = offset - lag_step + kernel_len - 1 == slot_place
            earlier = earlier + jnp.where(hit_place[:, None], history[:, slot_place], 0.0)
        chosen = jnp.where((offset >= lag_step)[:, None], shifted, earlier)
        total = total + kernel[kernel_len - 1 - lag_step][None, :] * chosen
    return jax.nn.silu(total).astype(jnp.bfloat16)

def mixer(inputs, dt_raw, b_maps, c_maps, start_state, member, mask, dt_bias, a_log, d_skip):
    count_tok, heads_here, head_width = inputs.shape
    groups_here = b_maps.shape[1]
    per_group = heads_here // groups_here
    count_req = start_state.shape[0]
    state_width = b_maps.shape[2]
    high = lax.Precision.HIGHEST
    step_size = jax.nn.softplus(dt_raw.astype(jnp.float32) + dt_bias[None, :])
    decay_rate = step_size * (-jnp.exp(a_log))[None, :]
    cumulative = jnp.dot(mask, decay_rate, precision=high)
    scores = jnp.einsum('tgn,sgn->gts', c_maps.astype(jnp.float32), b_maps.astype(jnp.float32), precision=high)
    spread_gap = jnp.minimum(cumulative.T[:, :, None] - cumulative.T[:, None, :], 0.0)
    decay = jnp.exp(spread_gap) * mask[None] * step_size.T[:, None, :]
    weights = decay.reshape(groups_here, per_group, count_tok, count_tok) * scores[:, None]
    weights = weights.astype(jnp.bfloat16).reshape(heads_here, count_tok, count_tok)
    values = inputs.astype(jnp.float32)
    intra = jnp.einsum('hts,shp->thp', weights.astype(jnp.float32), values, precision=high)
    grouped_state = start_state.reshape(count_req, groups_here, per_group, head_width, state_width)
    from_state = jnp.einsum('tgn,jgkpn->jtgkp', c_maps.astype(jnp.float32), grouped_state, precision=high)
    from_state = jnp.einsum('tj,jtgkp->tgkp', member, from_state, precision=high).reshape(count_tok, heads_here, head_width)
    from_state = from_state * jnp.exp(cumulative)[:, :, None]
    result = intra + from_state + d_skip[None, :, None] * values
    ends = jnp.dot(member.T, decay_rate, precision=high)
    to_end = jnp.exp(jnp.dot(member, ends, precision=high) - cumulative)
    carried = (to_end * step_size)[:, :, None] * values
    split_req = (member.T[:, :, None, None] * carried[None]).astype(jnp.bfloat16)
    split_req = split_req.reshape(count_req, count_tok, groups_here, per_group, head_width)
    fresh = jnp.einsum('jtgkp,tgn->jgkpn', split_req.astype(jnp.float32), b_maps.astype(jnp.float32), precision=high)
    fresh = fresh.reshape(count_req, heads_here, head_width, state_width)
    final_state = jnp.exp(ends)[:, :, None, None] * start_state + fresh
    return (result, final_state)

def reference(x_in, w_xz, w_dt, w_bc, dt_bias, a_log, d_skip, conv_x_w, conv_x_b, conv_bc_w, conv_bc_b, norm_gain, stretch_start, prefix_len, state_slot, ssm_pool, conv_x_pool, conv_bc_pool):
    channels = HEADS * HEAD_DIM
    flat_xz = w_xz.reshape(D, 2 * channels)
    grouped_x = x_in.reshape(N_REQ, TOK_G, D)
    slot_rows = state_slot.reshape(N_REQ, REQ_G)
    prefix_rows = prefix_len.reshape(N_REQ, REQ_G)

    def one_group(items):
        features, starts, prefix_here, slot_here = items
        proj_xz = jnp.dot(features, flat_xz, preferred_element_type=jnp.float32).astype(jnp.bfloat16)
        proj_xz = proj_xz.reshape(TOK_G, 2, channels)
        dt_raw = jnp.dot(features, w_dt, preferred_element_type=jnp.float32).astype(jnp.bfloat16)
        bc_raw = jnp.dot(features, w_bc, preferred_element_type=jnp.float32).astype(jnp.bfloat16)
        member, offset, mask = segments(starts, TOK_G)
        has_cache = (prefix_here > 0).astype(jnp.float32)
        start_state = ssm_pool[slot_here] * has_cache[:, None, None, None]
        cache_x = conv_x_pool[slot_here].astype(jnp.float32) * has_cache[:, None, None]
        cache_bc = conv_bc_pool[slot_here].astype(jnp.float32) * has_cache[:, None, None]
        x_conv = causal_conv(proj_xz[:, 1], cache_x, conv_x_w, conv_x_b, member, offset)
        bc_conv = causal_conv(bc_raw, cache_bc, conv_bc_w, conv_bc_b, member, offset)
        bc_conv = bc_conv.reshape(TOK_G, GROUPS, 2, STATE)
        result, final_state = mixer(x_conv.reshape(TOK_G, HEADS, HEAD_DIM), dt_raw, bc_conv[:, :, 0], bc_conv[:, :, 1], start_state, member, mask, dt_bias, a_log, d_skip)
        gated = result.reshape(TOK_G, channels) * jax.nn.silu(proj_xz[:, 0].astype(jnp.float32))
        by_group = gated.reshape(TOK_G, GROUPS, channels // GROUPS)
        mean_sq = lax.optimization_barrier(jnp.mean(by_group * by_group, -1, keepdims=True))
        normed = (by_group * lax.rsqrt(mean_sq + NORM_EPS)).reshape(TOK_G, channels) * norm_gain[None, :]
        return (normed.astype(jnp.bfloat16), final_state)
    outputs, states = lax.map(one_group, (grouped_x, stretch_start, prefix_rows, slot_rows))
    return (outputs.reshape(TOKENS, channels), states.reshape(REQS, HEADS, HEAD_DIM, STATE))
```

```python
import jax
import jax.numpy as jnp
from jax import lax
from jax.sharding import PartitionSpec as P

GROUPS = 8
NORM_EPS = 1e-05
F32 = jnp.float32
BF16 = jnp.bfloat16


def partner_2(block, axis, bit):
    count = lax.axis_size(axis)
    route = []
    for low in range(count):
        high = low | 1 << bit
        if high != low and high < count:
            route += [(low, high), (high, low)]
    return lax.ppermute(block, axis, route)


def shift_req(block, step):
    count = lax.axis_size("req")
    return lax.ppermute(block, "req", [(i, (i + step) % count) for i in range(count)])


def segments(starts, count_tok):
    position = jnp.arange(count_tok, dtype=jnp.int32)
    seg_ids = jnp.sum((position[:, None] >= starts[None, :]).astype(jnp.int32), 1) - 1
    member = seg_ids[:, None] == jnp.arange(starts.shape[0], dtype=jnp.int32)[None, :]
    offset = position - jnp.sum(jnp.where(member, starts[None, :], 0), 1)
    same_req = seg_ids[:, None] == seg_ids[None, :]
    causal = position[:, None] >= position[None, :]
    return (member.astype(F32), offset, (same_req & causal).astype(F32))


def causal_conv(inputs, cache, kernel, bias, member, offset):
    kernel_len = kernel.shape[0]
    count_tok, channels = inputs.shape
    count_req = cache.shape[0]
    history = jnp.dot(
        member.astype(BF16),
        cache.astype(BF16).reshape(count_req, (kernel_len - 1) * channels),
        preferred_element_type=F32,
    )
    history = history.reshape(count_tok, kernel_len - 1, channels)
    values = inputs.astype(F32)
    total = bias[None, :] + kernel[kernel_len - 1][None, :] * values
    for lag_step in range(1, kernel_len):
        shifted = jnp.concatenate(
            [jnp.zeros((lag_step, channels), F32), values[: count_tok - lag_step]], 0
        )
        earlier = jnp.zeros((count_tok, channels), F32)
        for slot_place in range(kernel_len - 1):
            hit_place = offset - lag_step + kernel_len - 1 == slot_place
            earlier = earlier + jnp.where(hit_place[:, None], history[:, slot_place], 0.0)
        chosen = jnp.where((offset >= lag_step)[:, None], shifted, earlier)
        total = total + kernel[kernel_len - 1 - lag_step][None, :] * chosen
    return jax.nn.silu(total).astype(BF16)


def mixer(inputs, dt_raw, b_maps, c_maps, start_state, member, mask, dt_bias, a_log, d_skip):
    high = lax.Precision.HIGHEST
    step_size = jax.nn.softplus(dt_raw.astype(F32) + dt_bias[None, :])
    decay_rate = step_size * (-jnp.exp(a_log))[None, :]
    cumulative = jnp.dot(mask, decay_rate, precision=high)
    scores = jnp.dot(c_maps, b_maps.T, preferred_element_type=F32)
    spread_gap = jnp.minimum(cumulative.T[:, :, None] - cumulative.T[:, None, :], 0.0)
    decay = jnp.exp(spread_gap) * mask[None] * step_size.T[:, None, :]
    weights = (decay * scores[None]).astype(BF16)
    intra = jnp.einsum("hts,shp->thp", weights, inputs, preferred_element_type=F32)
    values = inputs.astype(F32)
    from_state = jnp.einsum(
        "tn,jhpn->jthp", c_maps, start_state.astype(BF16), preferred_element_type=F32
    )
    from_state = jnp.sum(member.T[:, :, None, None] * from_state, 0)
    from_state = from_state * jnp.exp(cumulative)[:, :, None]
    result = intra + from_state + d_skip[None, :, None] * values
    ends = jnp.dot(member.T, decay_rate, precision=high)
    to_end = jnp.exp(jnp.dot(member, ends, precision=high) - cumulative)
    carried = (to_end * step_size)[:, :, None] * values
    split_req = (member.T[:, :, None, None] * carried[None]).astype(BF16)
    fresh = jnp.einsum("jthp,tn->jhpn", split_req, b_maps, preferred_element_type=F32)
    final_state = jnp.exp(ends)[:, :, None, None] * start_state + fresh
    return (result, final_state)


def spread_plan():
    far, across = [], []
    for z in range(4):
        for rest in range(4):
            for r in range(2):
                place = (z * 4 + rest) * 2 + r
                if z // 2 == r:
                    other = (z + 2) % 4
                    far.append((place, (other * 4 + rest) * 2 + r))
                if z // 2 != r:
                    across.append((place, place ^ 1))
    return far, across


def spread(block, far):
    wide_index = lax.axis_index("wide")
    axes = ("wide", "req")
    moved = lax.ppermute(block, axes, far)
    block = jnp.where(wide_index // 8 == lax.axis_index("req"), block, moved)
    tokens, width = block.shape
    for bit in (2, 1, 0):
        other = partner_2(block, "wide", bit)
        upper = (wide_index >> bit) % 2 == 1
        if bit:
            block = jnp.where(
                upper, jnp.concatenate([other, block], 1), jnp.concatenate([block, other], 1)
            )
    mine, other = (half.reshape(tokens, 2, 2, width) for half in (block, other))
    pair = jnp.stack([jnp.where(upper, other, mine), jnp.where(upper, mine, other)], 1)
    return pair.transpose(0, 3, 2, 1, 4).reshape(tokens, 8 * width)


def features_of(x_in):
    req_count = lax.axis_size("req")
    wide_count = lax.axis_size("wide")
    me = lax.axis_index("req")
    if req_count == 2 and wide_count == 16:
        far, across = spread_plan()
        crossed = lax.ppermute(x_in, ("wide", "req"), across)
        return [spread(x_in, far), spread(crossed, far)]
    own = lax.all_gather(x_in, "wide", axis=1, tiled=True)
    parts = own.reshape(own.shape[0], req_count, own.shape[1] // req_count).transpose(1, 0, 2)
    got = lax.all_to_all(parts, "req", split_axis=0, concat_axis=0, tiled=True)
    return [
        lax.dynamic_index_in_dim(got, (me + step) % req_count, 0, False)
        for step in range(req_count)
    ]


def on_device(
    x_in,
    w_xz,
    w_dt,
    w_bc,
    dt_bias,
    a_log,
    d_skip,
    conv_x_w,
    conv_x_b,
    conv_bc_w,
    conv_bc_b,
    norm_gain,
    stretch_start,
    prefix_len,
    state_slot,
    ssm_pool,
    conv_x_pool,
    conv_bc_pool,
):
    count_tok = x_in.shape[0]
    local_width = w_xz.shape[2]
    local_heads = w_dt.shape[1]
    state_part = w_bc.shape[1]
    me = lax.axis_index("req")
    req_count = lax.axis_size("req")
    slot_count = ssm_pool.shape[0]
    group_reqs = prefix_len.shape[0]

    conv_pool = jnp.concatenate([conv_x_pool, conv_bc_pool], 2)

    def of_request(pool, request):
        slot = jnp.clip(state_slot[request] - me * slot_count, 0, slot_count - 1)
        return lax.dynamic_index_in_dim(pool, slot, 0, False)

    got_state = [[] for _ in range(group_reqs)]
    got_conv = [[] for _ in range(group_reqs)]
    for step in range(1, req_count):
        to = (me + step) % req_count
        for j in range(group_reqs):
            got_conv[j].append(shift_req(of_request(conv_pool, to * group_reqs + j), step))
    for step in range(1, req_count):
        to = (me + step) % req_count
        for j in range(group_reqs):
            block = of_request(ssm_pool, to * group_reqs + j).astype(BF16)
            got_state[j].append(shift_req(block, step))
    start_state, cache = [], []
    for j in range(group_reqs):
        request = me * group_reqs + j
        came_from = (me - state_slot[request] // slot_count) % req_count
        state = of_request(ssm_pool, request)
        conv = of_request(conv_pool, request)
        for step in range(1, req_count):
            state = jnp.where(came_from == step, got_state[j][step - 1].astype(F32), state)
            conv = jnp.where(came_from == step, got_conv[j][step - 1], conv)
        live = prefix_len[j] > 0
        start_state.append(jnp.where(live, state, 0.0))
        cache.append(jnp.where(live, conv, 0))
    start_state = jnp.stack(start_state)
    cache = jnp.stack(cache)

    w_pair = lax.optimization_barrier(jnp.transpose(w_xz, (1, 0, 2)))
    w_map = jnp.concatenate([w_bc, w_dt], 1)
    features = features_of(x_in)
    sums = {}
    for name, weight in (("map", w_map), ("xr", w_pair[1]), ("z", w_pair[0])):
        total = None
        for step in range(1, req_count):
            part = jnp.dot(features[step], weight, preferred_element_type=F32).astype(BF16)
            came = shift_req(part, step).astype(F32)
            total = came if total is None else total + came
        sums[name] = total
    for name, weight in (("map", w_map), ("xr", w_pair[1]), ("z", w_pair[0])):
        own = jnp.dot(features[0], weight, preferred_element_type=F32)
        sums[name] = (own if sums[name] is None else own + sums[name]).astype(BF16)

    bc_raw = sums["map"][:, :state_part]
    dt_raw = sums["map"][:, state_part:]
    member, offset, mask = segments(stretch_start[0], count_tok)
    bc_conv = causal_conv(bc_raw, cache[:, :, local_width:], conv_bc_w, conv_bc_b, member, offset)
    x_conv = causal_conv(sums["xr"], cache[:, :, :local_width], conv_x_w, conv_x_b, member, offset)
    wide_index = lax.axis_index("wide")
    group_span = lax.axis_size("wide") // GROUPS
    bit_total = group_span.bit_length() - 1
    joined = bc_conv
    for bit_index in range(bit_total):
        partner = partner_2(joined, "wide", bit_index)
        upper_half = wide_index // (1 << bit_index) % 2 == 1
        joined = jnp.where(
            upper_half, jnp.concatenate([partner, joined], 1), jnp.concatenate([joined, partner], 1)
        )
    state_width = joined.shape[1] // 2
    b_maps = joined[:, :state_width]
    c_maps = joined[:, state_width:]
    head_width = local_width // local_heads
    result, final_state = mixer(
        x_conv.reshape(count_tok, local_heads, head_width),
        dt_raw,
        b_maps,
        c_maps,
        start_state,
        member,
        mask,
        dt_bias,
        a_log,
        d_skip,
    )
    gated = result.reshape(count_tok, local_width) * jax.nn.silu(sums["z"].astype(F32))
    square_sum = jnp.sum(gated * gated, 1)
    for bit_index in range(bit_total):
        square_sum = square_sum + partner_2(square_sum, "wide", bit_index)
    mean_sq = square_sum / (local_width * group_span)
    normed = gated * lax.rsqrt(mean_sq + NORM_EPS)[:, None] * norm_gain[None, :]
    return (normed.astype(BF16), final_state)


def solution(mesh):
    in_specs = (
        P("req", "wide"),
        P("req", None, "wide"),
        P("req", "wide"),
        P("req", "wide"),
        P("wide"),
        P("wide"),
        P("wide"),
        P(None, "wide"),
        P("wide"),
        P(None, "wide"),
        P("wide"),
        P("wide"),
        P("req", None),
        P("req"),
        P(),
        P("req", "wide", None, None),
        P("req", None, "wide"),
        P("req", None, "wide"),
    )
    out_specs = (P("req", "wide"), P("req", "wide", None, None))
    return jax.shard_map(
        on_device, mesh=mesh, in_specs=in_specs, out_specs=out_specs, check_vma=False
    )
```

```python
import functools

import jax
import jax.numpy as jnp
from jax import lax
from jax.experimental import pallas as pl
from jax.experimental.pallas import tpu as pltpu
from jax.sharding import PartitionSpec as P

GROUPS = 8
NORM_EPS = 1e-05
F32 = jnp.float32
BF16 = jnp.bfloat16
HIGH = lax.Precision.HIGHEST
VMEM_BYTES = 48 * 1024 * 1024
HEADS_STEP = 4
COLUMNS = 256


def cost(flops, bytes_accessed):
    return pl.CostEstimate(flops=int(flops), bytes_accessed=int(bytes_accessed), transcendentals=0)


def params():
    return pltpu.CompilerParams(vmem_limit_bytes=VMEM_BYTES)


def partner_2(block, axis, bit):
    count = lax.axis_size(axis)
    route = []
    for low in range(count):
        high = low | 1 << bit
        if high != low and high < count:
            route += [(low, high), (high, low)]
    return lax.ppermute(block, axis, route)


def shift_req(block, step):
    count = lax.axis_size("req")
    return lax.ppermute(block, "req", [(i, (i + step) % count) for i in range(count)])


def spread_routes():
    far, across, diagonal = [], [], []
    for z in range(4):
        for rest in range(4):
            for r in range(2):
                place = (z * 4 + rest) * 2 + r
                other = (((z + 2) % 4) * 4 + rest) * 2 + r
                if z // 2 == r:
                    far.append((place, other))
                else:
                    across.append((place, place ^ 1))
                    diagonal.append((place, other ^ 1))
    return far, across, diagonal


def quad(block):
    along_z = partner_2(block, "wide", 2)
    along_x = partner_2(block, "wide", 1)
    both = partner_2(along_z, "wide", 1)
    four = jnp.stack([block, along_x, along_z, both])
    return [four, partner_2(four, "wide", 0)]


def features_of(x_in):
    req_count = lax.axis_size("req")
    wide_count = lax.axis_size("wide")
    me = lax.axis_index("req")
    if req_count == 2 and wide_count == 16:
        wide_index = lax.axis_index("wide")
        axes = ("wide", "req")
        far, across, diagonal = spread_routes()
        across = lax.ppermute(x_in, axes, across)
        diagonal = lax.ppermute(x_in, axes, diagonal)
        far = lax.ppermute(x_in, axes, far)
        near = wide_index // 8 == me
        theirs = quad(jnp.where(near, across, diagonal))
        own = quad(jnp.where(near, x_in, far))
        rows = (wide_index % 8) ^ jnp.array([0, 2, 4, 6, 1, 3, 5, 7], jnp.int32)
        return [own, theirs], rows
    own = lax.all_gather(x_in, "wide", axis=1, tiled=True)
    parts = own.reshape(own.shape[0], req_count, own.shape[1] // req_count).transpose(1, 0, 2)
    got = lax.all_to_all(parts, "req", split_axis=0, concat_axis=0, tiled=True)
    blocks = [
        [lax.dynamic_index_in_dim(got, (me + step) % req_count, 0, True)]
        for step in range(req_count)
    ]
    return blocks, jnp.zeros((1,), jnp.int32)


def project_kernel(block_total, weight_total, rows_ref, *refs):
    blocks = refs[:block_total]
    weights = refs[block_total : block_total + weight_total]
    out_ref = refs[block_total + weight_total]
    held = refs[block_total + weight_total + 1 : block_total + 2 * weight_total + 1]
    sems = refs[-1]
    copies = []
    for place in range(weight_total):
        copy = pltpu.make_async_copy(weights[place], held[place], sems.at[place])
        copy.start()
        copies.append(copy)
    column = 0
    for place in range(weight_total):
        copies[place].wait()
        total = None
        index = 0
        for block in blocks:
            for part in range(block.shape[0]):
                depth = block.shape[2]
                start = pl.multiple_of(rows_ref[index] * depth, depth)
                term = jnp.dot(
                    block[part],
                    held[place][pl.ds(start, depth), :],
                    preferred_element_type=F32,
                )
                total = term if total is None else total + term
                index += 1
        width = held[place].shape[1]
        out_ref[:, column : column + width] = total.astype(out_ref.dtype)
        column += width


def project(blocks, rows, weights, kind):
    tokens = blocks[0].shape[1]
    width = sum(weight.shape[1] for weight in weights)
    depth = weights[0].shape[0]
    any_space = pl.BlockSpec(memory_space=pl.ANY)
    return pl.pallas_call(
        functools.partial(project_kernel, len(blocks), len(weights)),
        out_shape=jax.ShapeDtypeStruct((tokens, width), kind),
        in_specs=[pl.BlockSpec(memory_space=pltpu.SMEM)]
        + [pl.BlockSpec(memory_space=pltpu.VMEM)] * len(blocks)
        + [any_space] * len(weights),
        out_specs=pl.BlockSpec(memory_space=pltpu.VMEM),
        scratch_shapes=[pltpu.VMEM(weight.shape, BF16) for weight in weights]
        + [pltpu.SemaphoreType.DMA((len(weights),))],
        compiler_params=params(),
        cost_estimate=cost(2 * tokens * width * depth, 2 * depth * (width + tokens)),
    )(rows, *blocks, *weights)


def token_places(starts, count_tok, shape, axis):
    position = lax.broadcasted_iota(jnp.int32, shape, axis)
    seg = jnp.full(shape, -1, jnp.int32)
    first = jnp.zeros(shape, jnp.int32)
    for start in starts:
        seg = seg + (position >= start).astype(jnp.int32)
        first = jnp.where(position >= start, start, first)
    return position, seg, first


def conv_silu(values, cache_ref, kernel_ref, bias_ref, seg, offset):
    kernel_len = kernel_ref.shape[0]
    taps = [kernel_ref[k : k + 1, :] for k in range(kernel_len)]
    total = bias_ref[...] + taps[kernel_len - 1] * values
    for lag in range(1, kernel_len):
        earlier = pltpu.roll(values, lag, 0)
        total = total + taps[kernel_len - 1 - lag] * jnp.where(offset >= lag, earlier, 0.0)
    cached = jnp.zeros_like(values)
    for request in range(cache_ref.shape[0]):
        for place in range(kernel_len - 1):
            history = jnp.zeros_like(bias_ref[...])
            for lag in range(place + 1, kernel_len):
                at = kernel_len - 1 + place - lag
                history = history + taps[kernel_len - 1 - lag] * cache_ref[request, at : at + 1, :]
            cached = jnp.where((seg == request) & (offset == place), history, cached)
    total = total + cached
    return total * jax.nn.sigmoid(total)


def prep_kernel(
    count_req, got_total, starts_ref, own_ref, *refs
):
    got = refs[:got_total]
    cache_ref, kernel_ref, bias_ref, dt_bias_ref, a_log_ref = refs[got_total : got_total + 5]
    bc_ref, cum_ref, step_ref, coef_ref, decay_ref = refs[got_total + 5 :]
    tokens = own_ref.shape[0]
    channels = bias_ref.shape[1]
    heads = dt_bias_ref.shape[1]
    starts = [starts_ref[0, j] for j in range(count_req)]
    total = own_ref[...]
    for ref in got:
        total = total + ref[...].astype(F32)
    total = total.astype(BF16).astype(F32)
    position, seg, first = token_places(starts, tokens, (tokens, channels), 0)
    bc = conv_silu(total[:, :channels], cache_ref, kernel_ref, bias_ref, seg, position - first)
    bc_ref[...] = bc.astype(BF16)
    raw = total[:, channels : channels + heads] + dt_bias_ref[...]
    step = jnp.maximum(raw, 0.0) + jnp.log1p(jnp.exp(-jnp.abs(raw)))
    rate = step * (-jnp.exp(a_log_ref[...]))
    position, seg, first = token_places(starts, tokens, (tokens, tokens), 0)
    other, seg_other, first_other = token_places(starts, tokens, (tokens, tokens), 1)
    same = seg == seg_other
    mask = jnp.where(same & (position >= other), 1.0, 0.0)
    after = jnp.where(same & (position < other), 1.0, 0.0)
    cum = jnp.dot(mask, rate, precision=HIGH, preferred_element_type=F32)
    left = jnp.dot(after, rate, precision=HIGH, preferred_element_type=F32)
    cum_ref[...] = cum
    step_ref[...] = step
    coef_ref[...] = jnp.exp(left) * step
    at, seg_at, _ = token_places(starts, tokens, (8, tokens), 1)
    row = lax.broadcasted_iota(jnp.int32, (8, tokens), 0)
    ends = jnp.dot(
        jnp.where(seg_at == row, 1.0, 0.0), rate, precision=HIGH, preferred_element_type=F32
    )
    decay_ref[...] = jnp.exp(ends)


def prep(starts, own, got, cache, kernel, bias, dt_bias, a_log):
    tokens = own.shape[0]
    channels = bias.shape[0]
    heads = dt_bias.shape[0]
    count_req = cache.shape[0]
    vmem = pl.BlockSpec(memory_space=pltpu.VMEM)
    small = jax.ShapeDtypeStruct((tokens, heads), F32)
    return pl.pallas_call(
        functools.partial(prep_kernel, count_req, len(got)),
        out_shape=[
            jax.ShapeDtypeStruct((tokens, channels), BF16),
            small,
            small,
            small,
            jax.ShapeDtypeStruct((8, heads), F32),
        ],
        in_specs=[pl.BlockSpec(memory_space=pltpu.SMEM)] + [vmem] * (6 + len(got)),
        out_specs=[vmem] * 5,
        compiler_params=params(),
        cost_estimate=cost(4e8, 1e6),
    )(starts, own, *got, cache, kernel, bias[None], dt_bias[None], a_log[None])


def pack_kernel(slots_ref, pool_ref, conv_ref, out_ref):
    heads, width, state = pool_ref.shape[1:]
    out_ref[0, : heads * width, :] = pool_ref[0].reshape(heads * width, state).astype(BF16)
    out_ref[0, heads * width :, :] = conv_ref[0]


def pack(pool, conv_rows, slots):
    _, heads, width, state = pool.shape
    count_req, rows, _ = conv_rows.shape
    return pl.pallas_call(
        pack_kernel,
        out_shape=jax.ShapeDtypeStruct((count_req, heads * width + rows, state), BF16),
        grid_spec=pltpu.PrefetchScalarGridSpec(
            num_scalar_prefetch=1,
            grid=(count_req,),
            in_specs=[
                pl.BlockSpec((1, heads, width, state), lambda j, slots: (slots[j], 0, 0, 0)),
                pl.BlockSpec((1, rows, state), lambda j, slots: (j, 0, 0)),
            ],
            out_specs=pl.BlockSpec((1, heads * width + rows, state), lambda j, slots: (j, 0, 0)),
        ),
        compiler_params=params(),
        cost_estimate=cost(0, 6 * count_req * heads * width * state),
    )(slots, pool, conv_rows)


def mixer_kernel(count_req, got_total, slots_ref, flags_ref, starts_ref, *refs):
    own_ref = refs[0]
    got = refs[1 : 1 + got_total]
    rest = refs[1 + got_total :]
    cache_ref, kernel_ref, bias_ref, b_ref, c_ref = rest[:5]
    cum_ref, cum_t_ref, step_t_ref, coef_ref, decay_ref, skip_ref = rest[5:11]
    pools = rest[11 : 11 + count_req]
    states = rest[11 + count_req : 11 + count_req + got_total]
    out_ref, state_ref, scores_ref, c_part_ref, b_part_ref = rest[11 + count_req + got_total :]
    tokens, channels = own_ref.shape
    heads, width, state = pools[0].shape[1:]
    starts = [starts_ref[j] for j in range(count_req)]

    @pl.when(pl.program_id(0) == 0)
    def _():
        position, seg, _ = token_places(starts, tokens, (tokens, tokens), 0)
        other, seg_other, _ = token_places(starts, tokens, (tokens, tokens), 1)
        scores = lax.dot_general(
            c_ref[...], b_ref[...], (((1,), (1,)), ((), ())), preferred_element_type=F32
        )
        scores_ref[...] = jnp.where((seg == seg_other) & (position >= other), scores, 0.0)
        _, seg, _ = token_places(starts, tokens, (tokens, state), 0)
        b_maps = b_ref[...].astype(F32)
        c_maps = c_ref[...].astype(F32)
        for j in range(count_req):
            place = slice(j * state, (j + 1) * state)
            b_part_ref[:, place] = jnp.where(seg == j, b_maps, 0.0).astype(BF16)
            c_part_ref[:, place] = jnp.where(seg == j, c_maps, 0.0).astype(BF16)

    total = own_ref[...]
    for ref in got:
        total = total + ref[...].astype(F32)
    total = total.astype(BF16).astype(F32)
    position, seg, first = token_places(starts, tokens, (tokens, channels), 0)
    values = conv_silu(total, cache_ref, kernel_ref, bias_ref, seg, position - first)
    inputs = values.astype(BF16)
    values = inputs.astype(F32)

    lane_head = lax.broadcasted_iota(jnp.int32, (tokens, channels), 1) // width
    scores = scores_ref[...]
    cum = cum_ref[0]
    cum_t = cum_t_ref[0]
    step_t = step_t_ref[0]
    coef = coef_ref[0]
    grown = jnp.exp(cum)
    grown_wide = jnp.zeros((tokens, channels), F32)
    coef_wide = jnp.zeros((tokens, channels), F32)
    result = jnp.zeros((tokens, channels), F32)
    for h in range(heads):
        gap = jnp.minimum(cum[:, h : h + 1] - cum_t[h : h + 1, :], 0.0)
        weights = (jnp.exp(gap) * scores * step_t[h : h + 1, :]).astype(BF16)
        mine = lane_head == h
        result = result + jnp.dot(
            weights, jnp.where(mine, values, 0.0).astype(BF16), preferred_element_type=F32
        )
        grown_wide = jnp.where(mine, grown[:, h : h + 1], grown_wide)
        coef_wide = jnp.where(mine, coef[:, h : h + 1], coef_wide)

    from_state = jnp.zeros((tokens, channels), F32)
    carried = (coef_wide * values).astype(BF16)
    fresh = lax.dot_general(
        carried, b_part_ref[...], (((0,), (0,)), ((), ())), preferred_element_type=F32
    )
    for j in range(count_req):
        place = slice(j * state, (j + 1) * state)
        start = pools[j][0].reshape(channels, state) * flags_ref[j, 0].astype(F32)
        for step in range(got_total):
            start = start + states[step][j].astype(F32) * flags_ref[j, step + 1].astype(F32)
        from_state = from_state + lax.dot_general(
            c_part_ref[:, place],
            start.astype(BF16),
            (((1,), (1,)), ((), ())),
            preferred_element_type=F32,
        )
        first_head = pl.program_id(0) * heads
        for h in range(heads):
            rows = slice(h * width, (h + 1) * width)
            state_ref[j, h] = decay_ref[j, first_head + h] * start[rows] + fresh[rows, place]
    out_ref[...] = result + grown_wide * from_state + skip_ref[...] * values


def mixer(
    slots, flags, starts, own, got, cache, kernel, bias, b_maps, c_maps, cum, step, coef, decay,
    skip, pool, states
):
    tokens, channels = own.shape
    _, heads, width, state = pool.shape
    count_req = cache.shape[0]
    kernel_len = kernel.shape[0]
    part = min(HEADS_STEP, heads)
    steps = heads // part
    wide = part * width
    columns = lambda i, *_: (0, i)
    whole = lambda i, *_: (0, 0)

    def by_step(array):
        return array.reshape(tokens, steps, part).transpose(1, 0, 2)

    def by_step_t(array):
        return array.T.reshape(steps, part, tokens)

    in_specs = (
        [pl.BlockSpec((tokens, wide), columns)] * (1 + len(got))
        + [
            pl.BlockSpec((count_req, kernel_len - 1, wide), lambda i, *_: (0, 0, i)),
            pl.BlockSpec((kernel_len, wide), columns),
            pl.BlockSpec((1, wide), columns),
            pl.BlockSpec((tokens, state), whole),
            pl.BlockSpec((tokens, state), whole),
            pl.BlockSpec((1, tokens, part), lambda i, *_: (i, 0, 0)),
            pl.BlockSpec((1, part, tokens), lambda i, *_: (i, 0, 0)),
            pl.BlockSpec((1, part, tokens), lambda i, *_: (i, 0, 0)),
            pl.BlockSpec((1, tokens, part), lambda i, *_: (i, 0, 0)),
            pl.BlockSpec(memory_space=pltpu.SMEM),
            pl.BlockSpec((1, wide), columns),
        ]
        + [
            pl.BlockSpec(
                (1, part, width, state),
                functools.partial(lambda j, i, slots, *_: (slots[j], i, 0, 0), j),
            )
            for j in range(count_req)
        ]
        + [pl.BlockSpec((count_req, wide, state), lambda i, *_: (0, i, 0))] * len(states)
    )
    return pl.pallas_call(
        functools.partial(mixer_kernel, count_req, len(got)),
        out_shape=[
            jax.ShapeDtypeStruct((tokens, channels), F32),
            jax.ShapeDtypeStruct((count_req, heads, width, state), F32),
        ],
        grid_spec=pltpu.PrefetchScalarGridSpec(
            num_scalar_prefetch=3,
            grid=(steps,),
            in_specs=in_specs,
            out_specs=[
                pl.BlockSpec((tokens, wide), columns),
                pl.BlockSpec((count_req, part, width, state), lambda i, *_: (0, i, 0, 0)),
            ],
            scratch_shapes=[
                pltpu.VMEM((tokens, tokens), F32),
                pltpu.VMEM((tokens, count_req * state), BF16),
                pltpu.VMEM((tokens, count_req * state), BF16),
            ],
        ),
        compiler_params=params(),
        cost_estimate=cost(5e9, 8e6),
    )(
        slots, flags, starts, own, *got, cache, kernel, bias[None], b_maps, c_maps,
        by_step(cum), by_step_t(cum), by_step_t(step), by_step(coef), decay,
        jnp.repeat(skip, width)[None], *([pool] * count_req), *states
    )


def on_device(
    x_in,
    w_xz,
    w_dt,
    w_bc,
    dt_bias,
    a_log,
    d_skip,
    conv_x_w,
    conv_x_b,
    conv_bc_w,
    conv_bc_b,
    norm_gain,
    stretch_start,
    prefix_len,
    state_slot,
    ssm_pool,
    conv_x_pool,
    conv_bc_pool,
):
    local_width = w_xz.shape[2]
    state_part = w_bc.shape[1]
    me = lax.axis_index("req")
    req_count = lax.axis_size("req")
    slot_count, heads, head_width, state = ssm_pool.shape
    group_reqs = prefix_len.shape[0]
    lags = conv_x_pool.shape[1]
    conv_width = local_width + state_part

    features, rows = features_of(x_in)

    def slots_of(index):
        asked = lax.dynamic_slice_in_dim(state_slot, index * group_reqs, group_reqs)
        return jnp.clip(asked - me * slot_count, 0, slot_count - 1)

    def conv_of(slots):
        hit = slots[:, None] == jnp.arange(slot_count)[None, :]
        parts = [
            jnp.sum(jnp.where(hit[:, :, None, None], pool[None], 0), 1)
            for pool in (conv_x_pool, conv_bc_pool)
        ]
        return jnp.concatenate(parts, 2)

    conv_size = lags * conv_width
    conv_rows = -(-conv_size // (16 * state)) * 16
    got_states = []
    for step in range(1, req_count):
        slots = slots_of((me + step) % req_count)
        flat = conv_of(slots).reshape(group_reqs, conv_size)
        flat = jnp.pad(flat, ((0, 0), (0, conv_rows * state - conv_size)))
        packed = pack(ssm_pool, flat.reshape(group_reqs, conv_rows, state), slots)
        got_states.append(shift_req(packed, step))

    own_slots = slots_of(me)
    asked = lax.dynamic_slice_in_dim(state_slot, me * group_reqs, group_reqs)
    came_from = (me - asked // slot_count) % req_count
    live = prefix_len > 0
    flags = (live[:, None] & (came_from[:, None] == jnp.arange(req_count)[None, :])).astype(
        jnp.int32
    )
    cache = conv_of(own_slots)
    for step in range(1, req_count):
        got = got_states[step - 1][:, heads * head_width :].reshape(group_reqs, -1)
        got = got[:, :conv_size].reshape(cache.shape)
        cache = jnp.where((came_from == step)[:, None, None], got, cache)
    cache = jnp.where(live[:, None, None], cache, 0).astype(F32)

    pieces = []
    for first in range(0, local_width, COLUMNS):
        piece = jnp.transpose(w_xz[:, :, first : first + COLUMNS], (1, 0, 2))
        pieces.append(lax.optimization_barrier(piece))
    weights = {
        "map": [w_bc, w_dt],
        "xr": [piece[1] for piece in pieces],
        "z": [piece[0] for piece in pieces],
    }
    came = {name: [] for name in weights}
    for step in range(1, req_count):
        for name in weights:
            part = project(features[step], rows, weights[name], BF16)
            came[name].append(shift_req(part, step))
    own = {name: project(features[0], rows, weights[name], F32) for name in weights}

    bc_conv, cum, step, coef, decay = prep(
        stretch_start, own["map"], came["map"], cache[:, :, local_width:], conv_bc_w, conv_bc_b,
        dt_bias, a_log
    )
    wide_index = lax.axis_index("wide")
    group_span = lax.axis_size("wide") // GROUPS
    bit_total = group_span.bit_length() - 1
    joined = bc_conv
    for bit_index in range(bit_total):
        partner = partner_2(joined, "wide", bit_index)
        upper_half = wide_index // (1 << bit_index) % 2 == 1
        joined = jnp.where(
            upper_half, jnp.concatenate([partner, joined], 1), jnp.concatenate([joined, partner], 1)
        )
    state_width = joined.shape[1] // 2
    result, final_state = mixer(
        own_slots, flags, stretch_start[0], own["xr"], came["xr"], cache[:, :, :local_width],
        conv_x_w, conv_x_b, joined[:, :state_width], joined[:, state_width:], cum, step, coef,
        decay, d_skip, ssm_pool, got_states
    )
    gate = own["z"]
    for got in came["z"]:
        gate = gate + got.astype(F32)
    gated = result * jax.nn.silu(gate.astype(BF16).astype(F32))
    square_sum = jnp.sum(gated * gated, 1)
    for bit_index in range(bit_total):
        square_sum = square_sum + partner_2(square_sum, "wide", bit_index)
    mean_sq = square_sum / (local_width * group_span)
    normed = gated * lax.rsqrt(mean_sq + NORM_EPS)[:, None] * norm_gain[None, :]
    return (normed.astype(BF16), final_state)


def solution(mesh):
    in_specs = (
        P("req", "wide"),
        P("req", None, "wide"),
        P("req", "wide"),
        P("req", "wide"),
        P("wide"),
        P("wide"),
        P("wide"),
        P(None, "wide"),
        P("wide"),
        P(None, "wide"),
        P("wide"),
        P("wide"),
        P("req", None),
        P("req"),
        P(),
        P("req", "wide", None, None),
        P("req", None, "wide"),
        P("req", None, "wide"),
    )
    out_specs = (P("req", "wide"), P("req", "wide", None, None))
    return jax.shard_map(
        on_device, mesh=mesh, in_specs=in_specs, out_specs=out_specs, check_vma=False
    )
```

```python
import functools

import jax
import jax.numpy as jnp
from jax import lax
from jax.experimental import pallas as pl
from jax.experimental.pallas import tpu as pltpu
from jax.sharding import PartitionSpec as P

GROUPS = 8
NORM_EPS = 1e-05
F32 = jnp.float32
BF16 = jnp.bfloat16
HIGH = lax.Precision.HIGHEST
VMEM_BYTES = 16 * 1024 * 1024
HEADS_STEP = 4


def cost(flops, bytes_accessed):
    return pl.CostEstimate(flops=int(flops), bytes_accessed=int(bytes_accessed), transcendentals=0)


def params():
    return pltpu.CompilerParams(vmem_limit_bytes=VMEM_BYTES)


def partner_2(block, axis, bit):
    count = lax.axis_size(axis)
    route = []
    for low in range(count):
        high = low | 1 << bit
        if high != low and high < count:
            route += [(low, high), (high, low)]
    return lax.ppermute(block, axis, route)


def shift_req(block, step):
    count = lax.axis_size("req")
    return lax.ppermute(block, "req", [(i, (i + step) % count) for i in range(count)])


def spread_routes():
    far, across, diagonal = [], [], []
    for z in range(4):
        for rest in range(4):
            for r in range(2):
                place = (z * 4 + rest) * 2 + r
                other = (((z + 2) % 4) * 4 + rest) * 2 + r
                if z // 2 == r:
                    far.append((place, other))
                else:
                    across.append((place, place ^ 1))
                    diagonal.append((place, other ^ 1))
    return far, across, diagonal


def quad(block, along_x_last):
    wide_index = lax.axis_index("wide")
    upper_z, upper_x, upper = ((wide_index >> bit) % 2 == 1 for bit in (2, 1, 0))
    along_z = partner_2(block, "wide", 2)
    along_x = partner_2(block, "wide", 1)
    if along_x_last:
        both = partner_2(along_z, "wide", 1)
    else:
        both = partner_2(along_x, "wide", 2)

    def ordered(flag, mine, other):
        return [jnp.where(flag, other, mine), jnp.where(flag, mine, other)]

    here = ordered(upper_x, block, along_x)
    there = ordered(upper_x, along_z, both)
    rows = [ordered(upper_z, here[x], there[x]) for x in range(2)]
    mine = jnp.concatenate([rows[x][z] for z in range(2) for x in range(2)], 1)
    other = partner_2(mine, "wide", 0)
    tokens, width = block.shape
    pair = ordered(upper, mine, other)
    pair = jnp.stack([half.reshape(tokens, 4, width) for half in pair], 2)
    return pair.reshape(tokens, 8 * width)


def features_of(x_in):
    req_count = lax.axis_size("req")
    wide_count = lax.axis_size("wide")
    me = lax.axis_index("req")
    if req_count == 2 and wide_count == 16:
        axes = ("wide", "req")
        far, across, diagonal = spread_routes()
        across = lax.ppermute(x_in, axes, across)
        diagonal = lax.ppermute(x_in, axes, diagonal)
        far = lax.ppermute(x_in, axes, far)
        near = lax.axis_index("wide") // 8 == me
        theirs = jnp.where(near, across, diagonal)
        return [quad(jnp.where(near, x_in, far), False), quad(theirs, True)], theirs
    own = lax.all_gather(x_in, "wide", axis=1, tiled=True)
    parts = own.reshape(own.shape[0], req_count, own.shape[1] // req_count).transpose(1, 0, 2)
    got = lax.all_to_all(parts, "req", split_axis=0, concat_axis=0, tiled=True)
    blocks = [
        lax.dynamic_index_in_dim(got, (me + step) % req_count, 0, False)
        for step in range(req_count)
    ]
    return blocks, x_in


def token_places(starts, count_tok, shape, axis):
    position = lax.broadcasted_iota(jnp.int32, shape, axis)
    seg = jnp.full(shape, -1, jnp.int32)
    first = jnp.zeros(shape, jnp.int32)
    for start in starts:
        seg = seg + (position >= start).astype(jnp.int32)
        first = jnp.where(position >= start, start, first)
    return position, seg, first


def conv_silu(values, cache_ref, kernel_ref, bias_ref, seg, offset):
    kernel_len = kernel_ref.shape[0]
    taps = [kernel_ref[k : k + 1, :] for k in range(kernel_len)]
    total = bias_ref[...] + taps[kernel_len - 1] * values
    for lag in range(1, kernel_len):
        earlier = pltpu.roll(values, lag, 0)
        total = total + taps[kernel_len - 1 - lag] * jnp.where(offset >= lag, earlier, 0.0)
    cached = jnp.zeros_like(values)
    for request in range(cache_ref.shape[0]):
        for place in range(kernel_len - 1):
            history = jnp.zeros_like(bias_ref[...])
            for lag in range(place + 1, kernel_len):
                at = kernel_len - 1 + place - lag
                history = history + taps[kernel_len - 1 - lag] * cache_ref[request, at : at + 1, :]
            cached = jnp.where((seg == request) & (offset == place), history, cached)
    total = total + cached
    return total * jax.nn.sigmoid(total)


def prep_kernel(
    count_req, got_total, starts_ref, own_ref, *refs
):
    got = refs[:got_total]
    cache_ref, kernel_ref, bias_ref, dt_bias_ref, a_log_ref = refs[got_total : got_total + 5]
    bc_ref, cum_ref, cum_t_ref, step_t_ref, coef_ref, decay_ref = refs[got_total + 5 :]
    tokens = own_ref.shape[0]
    channels = bias_ref.shape[1]
    heads = dt_bias_ref.shape[1]
    starts = [starts_ref[0, j] for j in range(count_req)]
    total = own_ref[...]
    for ref in got:
        total = total + ref[...].astype(F32)
    total = total.astype(BF16).astype(F32)
    position, seg, first = token_places(starts, tokens, (tokens, channels), 0)
    bc = conv_silu(total[:, :channels], cache_ref, kernel_ref, bias_ref, seg, position - first)
    bc_ref[...] = bc.astype(BF16)
    raw = total[:, channels : channels + heads] + dt_bias_ref[...]
    step = jnp.maximum(raw, 0.0) + jnp.log1p(jnp.exp(-jnp.abs(raw)))
    rate = step * (-jnp.exp(a_log_ref[...]))
    position, seg, first = token_places(starts, tokens, (tokens, tokens), 0)
    other, seg_other, first_other = token_places(starts, tokens, (tokens, tokens), 1)
    same = seg == seg_other
    mask = jnp.where(same & (position >= other), 1.0, 0.0)
    after = jnp.where(same & (position < other), 1.0, 0.0)
    cum = jnp.dot(mask, rate, precision=HIGH, preferred_element_type=F32)
    left = jnp.dot(after, rate, precision=HIGH, preferred_element_type=F32)
    cum_t = lax.dot_general(
        rate, mask, (((0,), (1,)), ((), ())), precision=HIGH, preferred_element_type=F32
    )
    step_t = step.T
    coef = jnp.exp(left) * step
    part = cum_ref.shape[2]
    for i in range(cum_ref.shape[0]):
        place = slice(i * part, (i + 1) * part)
        cum_ref[i] = cum[:, place]
        cum_t_ref[i] = cum_t[place, :]
        step_t_ref[i] = step_t[place, :]
        coef_ref[i] = coef[:, place]
    at, seg_at, _ = token_places(starts, tokens, (8, tokens), 1)
    row = lax.broadcasted_iota(jnp.int32, (8, tokens), 0)
    ends = jnp.dot(
        jnp.where(seg_at == row, 1.0, 0.0), rate, precision=HIGH, preferred_element_type=F32
    )
    decay_ref[...] = jnp.exp(ends)


def prep(starts, own, got, cache, kernel, bias, dt_bias, a_log):
    tokens = own.shape[0]
    channels = bias.shape[0]
    heads = dt_bias.shape[0]
    count_req = cache.shape[0]
    vmem = pl.BlockSpec(memory_space=pltpu.VMEM)
    part = min(HEADS_STEP, heads)
    tall = jax.ShapeDtypeStruct((heads // part, tokens, part), F32)
    flat = jax.ShapeDtypeStruct((heads // part, part, tokens), F32)
    return pl.pallas_call(
        functools.partial(prep_kernel, count_req, len(got)),
        out_shape=[
            jax.ShapeDtypeStruct((tokens, channels), BF16),
            tall,
            flat,
            flat,
            tall,
            jax.ShapeDtypeStruct((8, heads), F32),
        ],
        in_specs=[pl.BlockSpec(memory_space=pltpu.SMEM)] + [vmem] * (6 + len(got)),
        out_specs=[vmem] * 6,
        compiler_params=params(),
        cost_estimate=cost(4e8, 1e6),
    )(starts, own, *got, cache, kernel, bias[None], dt_bias[None], a_log[None])


def pack_kernel(slots_ref, pool_ref, conv_ref, out_ref):
    heads, width, state = pool_ref.shape[1:]
    out_ref[0, : heads * width, :] = pool_ref[0].reshape(heads * width, state).astype(BF16)
    out_ref[0, heads * width :, :] = conv_ref[0]


def pack(pool, conv_rows, slots):
    _, heads, width, state = pool.shape
    count_req, rows, _ = conv_rows.shape
    return pl.pallas_call(
        pack_kernel,
        out_shape=jax.ShapeDtypeStruct((count_req, heads * width + rows, state), BF16),
        grid_spec=pltpu.PrefetchScalarGridSpec(
            num_scalar_prefetch=1,
            grid=(count_req,),
            in_specs=[
                pl.BlockSpec((1, heads, width, state), lambda j, slots: (slots[j], 0, 0, 0)),
                pl.BlockSpec((1, rows, state), lambda j, slots: (j, 0, 0)),
            ],
            out_specs=pl.BlockSpec((1, heads * width + rows, state), lambda j, slots: (j, 0, 0)),
        ),
        compiler_params=params(),
        cost_estimate=cost(0, 6 * count_req * heads * width * state),
    )(slots, pool, conv_rows)


def mixer_kernel(count_req, got_total, slots_ref, flags_ref, starts_ref, *refs):
    own_ref = refs[0]
    got = refs[1 : 1 + got_total]
    rest = refs[1 + got_total :]
    cache_ref, kernel_ref, bias_ref, b_ref, c_ref = rest[:5]
    cum_ref, cum_t_ref, step_t_ref, coef_ref, decay_ref, skip_ref = rest[5:11]
    pools = rest[11 : 11 + count_req]
    states = rest[11 + count_req : 11 + count_req + got_total]
    out_ref, state_ref, scores_ref, c_part_ref, b_part_ref = rest[11 + count_req + got_total :]
    tokens, channels = own_ref.shape
    heads, width, state = pools[0].shape[1:]
    starts = [starts_ref[j] for j in range(count_req)]

    @pl.when(pl.program_id(0) == 0)
    def _():
        position, seg, _ = token_places(starts, tokens, (tokens, tokens), 0)
        other, seg_other, _ = token_places(starts, tokens, (tokens, tokens), 1)
        scores = lax.dot_general(
            c_ref[...], b_ref[...], (((1,), (1,)), ((), ())), preferred_element_type=F32
        )
        scores_ref[...] = jnp.where((seg == seg_other) & (position >= other), scores, 0.0)
        _, seg, _ = token_places(starts, tokens, (tokens, state), 0)
        b_maps = b_ref[...].astype(F32)
        c_maps = c_ref[...].astype(F32)
        for j in range(count_req):
            place = slice(j * state, (j + 1) * state)
            b_part_ref[:, place] = jnp.where(seg == j, b_maps, 0.0).astype(BF16)
            c_part_ref[:, place] = jnp.where(seg == j, c_maps, 0.0).astype(BF16)

    total = own_ref[...]
    for ref in got:
        total = total + ref[...].astype(F32)
    total = total.astype(BF16).astype(F32)
    position, seg, first = token_places(starts, tokens, (tokens, channels), 0)
    values = conv_silu(total, cache_ref, kernel_ref, bias_ref, seg, position - first)
    inputs = values.astype(BF16)
    values = inputs.astype(F32)

    lane_head = lax.broadcasted_iota(jnp.int32, (tokens, channels), 1) // width
    scores = scores_ref[...]
    cum = cum_ref[0]
    cum_t = cum_t_ref[0]
    step_t = step_t_ref[0]
    coef = coef_ref[0]
    grown = jnp.exp(cum)
    grown_wide = jnp.zeros((tokens, channels), F32)
    coef_wide = jnp.zeros((tokens, channels), F32)
    result = jnp.zeros((tokens, channels), F32)
    for h in range(heads):
        gap = jnp.minimum(cum[:, h : h + 1] - cum_t[h : h + 1, :], 0.0)
        weights = (jnp.exp(gap) * scores * step_t[h : h + 1, :]).astype(BF16)
        mine = lane_head == h
        result = result + jnp.dot(
            weights, jnp.where(mine, values, 0.0).astype(BF16), preferred_element_type=F32
        )
        grown_wide = jnp.where(mine, grown[:, h : h + 1], grown_wide)
        coef_wide = jnp.where(mine, coef[:, h : h + 1], coef_wide)

    from_state = jnp.zeros((tokens, channels), F32)
    carried = (coef_wide * values).astype(BF16)
    fresh = lax.dot_general(
        carried, b_part_ref[...], (((0,), (0,)), ((), ())), preferred_element_type=F32
    )
    for j in range(count_req):
        place = slice(j * state, (j + 1) * state)
        start = pools[j][0].reshape(channels, state) * flags_ref[j, 0].astype(F32)
        for step in range(got_total):
            start = start + states[step][j].astype(F32) * flags_ref[j, step + 1].astype(F32)
        from_state = from_state + lax.dot_general(
            c_part_ref[:, place],
            start.astype(BF16),
            (((1,), (1,)), ((), ())),
            preferred_element_type=F32,
        )
        first_head = pl.program_id(0) * heads
        for h in range(heads):
            rows = slice(h * width, (h + 1) * width)
            state_ref[j, h] = decay_ref[j, first_head + h] * start[rows] + fresh[rows, place]
    out_ref[...] = result + grown_wide * from_state + skip_ref[...] * values


def mixer(
    slots, flags, starts, own, got, cache, kernel, bias, b_maps, c_maps, cum, cum_t, step_t, coef,
    decay, skip, pool, states
):
    tokens, channels = own.shape
    _, heads, width, state = pool.shape
    count_req = cache.shape[0]
    kernel_len = kernel.shape[0]
    part = min(HEADS_STEP, heads)
    steps = heads // part
    wide = part * width
    columns = lambda i, *_: (0, i)
    whole = lambda i, *_: (0, 0)

    in_specs = (
        [pl.BlockSpec((tokens, wide), columns)] * (1 + len(got))
        + [
            pl.BlockSpec((count_req, kernel_len - 1, wide), lambda i, *_: (0, 0, i)),
            pl.BlockSpec((kernel_len, wide), columns),
            pl.BlockSpec((1, wide), columns),
            pl.BlockSpec((tokens, state), whole),
            pl.BlockSpec((tokens, state), whole),
            pl.BlockSpec((1, tokens, part), lambda i, *_: (i, 0, 0)),
            pl.BlockSpec((1, part, tokens), lambda i, *_: (i, 0, 0)),
            pl.BlockSpec((1, part, tokens), lambda i, *_: (i, 0, 0)),
            pl.BlockSpec((1, tokens, part), lambda i, *_: (i, 0, 0)),
            pl.BlockSpec(memory_space=pltpu.SMEM),
            pl.BlockSpec((1, wide), columns),
        ]
        + [
            pl.BlockSpec(
                (1, part, width, state),
                functools.partial(lambda j, i, slots, *_: (slots[j], i, 0, 0), j),
            )
            for j in range(count_req)
        ]
        + [pl.BlockSpec((count_req, wide, state), lambda i, *_: (0, i, 0))] * len(states)
    )
    return pl.pallas_call(
        functools.partial(mixer_kernel, count_req, len(got)),
        out_shape=[
            jax.ShapeDtypeStruct((tokens, channels), F32),
            jax.ShapeDtypeStruct((count_req, heads, width, state), F32),
        ],
        grid_spec=pltpu.PrefetchScalarGridSpec(
            num_scalar_prefetch=3,
            grid=(steps,),
            in_specs=in_specs,
            out_specs=[
                pl.BlockSpec((tokens, wide), columns),
                pl.BlockSpec((count_req, part, width, state), lambda i, *_: (0, i, 0, 0)),
            ],
            scratch_shapes=[
                pltpu.VMEM((tokens, tokens), F32),
                pltpu.VMEM((tokens, count_req * state), BF16),
                pltpu.VMEM((tokens, count_req * state), BF16),
            ],
        ),
        compiler_params=params(),
        cost_estimate=cost(5e9, 8e6),
    )(
        slots, flags, starts, own, *got, cache, kernel, bias[None], b_maps, c_maps,
        cum, cum_t, step_t, coef, decay,
        jnp.repeat(skip, width)[None], *([pool] * count_req), *states
    )


def on_device(
    x_in,
    w_xz,
    w_dt,
    w_bc,
    dt_bias,
    a_log,
    d_skip,
    conv_x_w,
    conv_x_b,
    conv_bc_w,
    conv_bc_b,
    norm_gain,
    stretch_start,
    prefix_len,
    state_slot,
    ssm_pool,
    conv_x_pool,
    conv_bc_pool,
):
    local_width = w_xz.shape[2]
    state_part = w_bc.shape[1]
    me = lax.axis_index("req")
    req_count = lax.axis_size("req")
    slot_count, heads, head_width, state = ssm_pool.shape
    group_reqs = prefix_len.shape[0]
    lags = conv_x_pool.shape[1]
    conv_width = local_width + state_part

    features, arrived = features_of(x_in)

    def slots_of(index):
        asked = lax.dynamic_slice_in_dim(state_slot, index * group_reqs, group_reqs)
        return jnp.clip(asked - me * slot_count, 0, slot_count - 1)

    def conv_of(slots):
        hit = slots[:, None] == jnp.arange(slot_count)[None, :]
        parts = [
            jnp.sum(jnp.where(hit[:, :, None, None], pool[None], 0), 1)
            for pool in (conv_x_pool, conv_bc_pool)
        ]
        return jnp.concatenate(parts, 2)

    conv_size = lags * conv_width
    conv_rows = -(-conv_size // (16 * state)) * 16
    got_states = []
    for step in range(1, req_count):
        slots = slots_of((me + step) % req_count)
        flat = conv_of(slots).reshape(group_reqs, conv_size)
        flat = jnp.pad(flat, ((0, 0), (0, conv_rows * state - conv_size)))
        packed = pack(ssm_pool, flat.reshape(group_reqs, conv_rows, state), slots)
        got_states.append(shift_req(packed, step))

    own_slots = slots_of(me)
    asked = lax.dynamic_slice_in_dim(state_slot, me * group_reqs, group_reqs)
    came_from = (me - asked // slot_count) % req_count
    live = prefix_len > 0
    flags = (live[:, None] & (came_from[:, None] == jnp.arange(req_count)[None, :])).astype(
        jnp.int32
    )
    cache = conv_of(own_slots)
    for step in range(1, req_count):
        got = got_states[step - 1][:, heads * head_width :].reshape(group_reqs, -1)
        got = got[:, :conv_size].reshape(cache.shape)
        cache = jnp.where((came_from == step)[:, None, None], got, cache)
    cache = jnp.where(live[:, None, None], cache, 0).astype(F32)

    half = w_xz.shape[0] // 2
    first = lax.optimization_barrier(jnp.transpose(w_xz[:half], (1, 0, 2)))
    last, _ = lax.optimization_barrier((w_xz[half:], arrived))
    last = lax.optimization_barrier(jnp.transpose(last, (1, 0, 2)))
    w_map = jnp.concatenate([w_bc, w_dt], 1)
    weights = {
        "map": (w_map[:half], w_map[half:]),
        "xr": (first[1], last[1]),
        "z": (first[0], last[0]),
    }

    def project(block, name):
        return jnp.dot(
            block[:, :half], weights[name][0], preferred_element_type=F32
        ) + jnp.dot(block[:, half:], weights[name][1], preferred_element_type=F32)

    came = {name: [] for name in weights}
    order = features[0]
    for step in range(1, req_count):
        block = features[step]
        for name in weights:
            part, block = lax.optimization_barrier((project(block, name).astype(BF16), block))
            came[name].append(shift_req(part, step))
            order, _ = lax.optimization_barrier((order, part))
    own = {}
    for name in weights:
        own[name], order = lax.optimization_barrier((project(order, name), order))

    bc_conv, cum, cum_t, step_t, coef, decay = prep(
        stretch_start, own["map"], came["map"], cache[:, :, local_width:], conv_bc_w, conv_bc_b,
        dt_bias, a_log
    )
    wide_index = lax.axis_index("wide")
    group_span = lax.axis_size("wide") // GROUPS
    bit_total = group_span.bit_length() - 1
    joined = bc_conv
    for bit_index in range(bit_total):
        partner = partner_2(joined, "wide", bit_index)
        upper_half = wide_index // (1 << bit_index) % 2 == 1
        joined = jnp.where(
            upper_half, jnp.concatenate([partner, joined], 1), jnp.concatenate([joined, partner], 1)
        )
    state_width = joined.shape[1] // 2
    result, final_state = mixer(
        own_slots, flags, stretch_start[0], own["xr"], came["xr"], cache[:, :, :local_width],
        conv_x_w, conv_x_b, joined[:, :state_width], joined[:, state_width:], cum, cum_t,
        step_t, coef, decay, d_skip, ssm_pool, got_states
    )
    gate = own["z"]
    for got in came["z"]:
        gate = gate + got.astype(F32)
    gated = result * jax.nn.silu(gate.astype(BF16).astype(F32))
    square_sum = jnp.sum(gated * gated, 1)
    for bit_index in range(bit_total):
        square_sum = square_sum + partner_2(square_sum, "wide", bit_index)
    mean_sq = square_sum / (local_width * group_span)
    normed = gated * lax.rsqrt(mean_sq + NORM_EPS)[:, None] * norm_gain[None, :]
    return (normed.astype(BF16), final_state)


def solution(mesh):
    in_specs = (
        P("req", "wide"),
        P("req", None, "wide"),
        P("req", "wide"),
        P("req", "wide"),
        P("wide"),
        P("wide"),
        P("wide"),
        P(None, "wide"),
        P("wide"),
        P(None, "wide"),
        P("wide"),
        P("wide"),
        P("req", None),
        P("req"),
        P(),
        P("req", "wide", None, None),
        P("req", None, "wide"),
        P("req", None, "wide"),
    )
    out_specs = (P("req", "wide"), P("req", "wide", None, None))
    return jax.shard_map(
        on_device, mesh=mesh, in_specs=in_specs, out_specs=out_specs, check_vma=False
    )
```

```python
import functools

import jax
import jax.numpy as jnp
from jax import lax
from jax.experimental import pallas as pl
from jax.experimental.pallas import tpu as pltpu
from jax.sharding import PartitionSpec as P

GROUPS = 8
NORM_EPS = 1e-05
F32 = jnp.float32
BF16 = jnp.bfloat16
HIGH = lax.Precision.HIGHEST
VMEM_BYTES = 16 * 1024 * 1024
HEADS_STEP = 4


def cost(flops, bytes_accessed):
    return pl.CostEstimate(flops=int(flops), bytes_accessed=int(bytes_accessed), transcendentals=0)


def params(limit=VMEM_BYTES):
    return pltpu.CompilerParams(vmem_limit_bytes=limit)


def partner_2(block, axis, bit):
    count = lax.axis_size(axis)
    route = []
    for low in range(count):
        high = low | 1 << bit
        if high != low and high < count:
            route += [(low, high), (high, low)]
    return lax.ppermute(block, axis, route)


def shift_req(block, step):
    count = lax.axis_size("req")
    return lax.ppermute(block, "req", [(i, (i + step) % count) for i in range(count)])


def spread_routes():
    far, across, diagonal = [], [], []
    for z in range(4):
        for rest in range(4):
            for r in range(2):
                place = (z * 4 + rest) * 2 + r
                other = (((z + 2) % 4) * 4 + rest) * 2 + r
                if z // 2 == r:
                    far.append((place, other))
                else:
                    across.append((place, place ^ 1))
                    diagonal.append((place, other ^ 1))
    return far, across, diagonal


def arrange_kernel(places_ref, *refs):
    out_ref = refs[-1]
    index = 0
    for ref in refs[:-1]:
        for part in range(ref.shape[0]):
            width = ref.shape[2]
            place = pl.multiple_of(places_ref[index] * width, width)
            out_ref[:, pl.ds(place, width)] = ref[part]
            index += 1


def arrange(stacks, places):
    tokens, width = stacks[0].shape[1:]
    total = sum(stack.shape[0] for stack in stacks) * width
    return pl.pallas_call(
        arrange_kernel,
        out_shape=jax.ShapeDtypeStruct((tokens, total), stacks[0].dtype),
        in_specs=[pl.BlockSpec(memory_space=pltpu.SMEM)]
        + [pl.BlockSpec(memory_space=pltpu.VMEM)] * len(stacks),
        out_specs=pl.BlockSpec(memory_space=pltpu.VMEM),
        compiler_params=params(),
        cost_estimate=cost(0, 4 * tokens * total),
    )(places, *stacks)


def quad(block, along_x_last):
    along_z = partner_2(block, "wide", 2)
    along_x = partner_2(block, "wide", 1)
    if along_x_last:
        both = partner_2(along_z, "wide", 1)
    else:
        both = partner_2(along_x, "wide", 2)
    four = jnp.stack([block, along_x, along_z, both])
    other = partner_2(four, "wide", 0)
    apart = jnp.array([0, 2, 4, 6, 1, 3, 5, 7], jnp.int32)
    return arrange([four, other], (lax.axis_index("wide") % 8) ^ apart)


def features_of(x_in):
    req_count = lax.axis_size("req")
    wide_count = lax.axis_size("wide")
    me = lax.axis_index("req")
    if req_count == 2 and wide_count == 16:
        axes = ("wide", "req")
        far, across, diagonal = spread_routes()
        across = lax.ppermute(x_in, axes, across)
        diagonal = lax.ppermute(x_in, axes, diagonal)
        far = lax.ppermute(x_in, axes, far)
        near = lax.axis_index("wide") // 8 == me
        theirs = jnp.where(near, across, diagonal)
        return [quad(jnp.where(near, x_in, far), False), quad(theirs, True)]
    own = lax.all_gather(x_in, "wide", axis=1, tiled=True)
    parts = own.reshape(own.shape[0], req_count, own.shape[1] // req_count).transpose(1, 0, 2)
    got = lax.all_to_all(parts, "req", split_axis=0, concat_axis=0, tiled=True)
    blocks = [
        lax.dynamic_index_in_dim(got, (me + step) % req_count, 0, False)
        for step in range(req_count)
    ]
    return blocks


def token_places(starts, count_tok, shape, axis):
    position = lax.broadcasted_iota(jnp.int32, shape, axis)
    seg = jnp.full(shape, -1, jnp.int32)
    first = jnp.zeros(shape, jnp.int32)
    for start in starts:
        seg = seg + (position >= start).astype(jnp.int32)
        first = jnp.where(position >= start, start, first)
    return position, seg, first


def conv_silu(values, cache_ref, kernel_ref, bias_ref, seg, offset):
    kernel_len = kernel_ref.shape[0]
    taps = [kernel_ref[k : k + 1, :] for k in range(kernel_len)]
    total = bias_ref[...] + taps[kernel_len - 1] * values
    for lag in range(1, kernel_len):
        earlier = pltpu.roll(values, lag, 0)
        total = total + taps[kernel_len - 1 - lag] * jnp.where(offset >= lag, earlier, 0.0)
    cached = jnp.zeros_like(values)
    for request in range(cache_ref.shape[0]):
        for place in range(kernel_len - 1):
            history = jnp.zeros_like(bias_ref[...])
            for lag in range(place + 1, kernel_len):
                at = kernel_len - 1 + place - lag
                history = history + taps[kernel_len - 1 - lag] * cache_ref[request, at : at + 1, :]
            cached = jnp.where((seg == request) & (offset == place), history, cached)
    total = total + cached
    return total * jax.nn.sigmoid(total)


def prep_kernel(
    count_req, got_total, starts_ref, own_ref, *refs
):
    got = refs[:got_total]
    cache_ref, kernel_ref, bias_ref, dt_bias_ref, a_log_ref = refs[got_total : got_total + 5]
    bc_ref, cum_ref, cum_t_ref, step_t_ref, coef_ref, decay_ref = refs[got_total + 5 :]
    tokens = own_ref.shape[0]
    channels = bias_ref.shape[1]
    heads = dt_bias_ref.shape[1]
    starts = [starts_ref[0, j] for j in range(count_req)]
    total = own_ref[...]
    for ref in got:
        total = total + ref[...].astype(F32)
    total = total.astype(BF16).astype(F32)
    position, seg, first = token_places(starts, tokens, (tokens, channels), 0)
    bc = conv_silu(total[:, :channels], cache_ref, kernel_ref, bias_ref, seg, position - first)
    bc_ref[...] = bc.astype(BF16)
    raw = total[:, channels : channels + heads] + dt_bias_ref[...]
    step = jnp.maximum(raw, 0.0) + jnp.log1p(jnp.exp(-jnp.abs(raw)))
    rate = step * (-jnp.exp(a_log_ref[...]))
    position, seg, first = token_places(starts, tokens, (tokens, tokens), 0)
    other, seg_other, first_other = token_places(starts, tokens, (tokens, tokens), 1)
    same = seg == seg_other
    mask = jnp.where(same & (position >= other), 1.0, 0.0)
    after = jnp.where(same & (position < other), 1.0, 0.0)
    cum = jnp.dot(mask, rate, precision=HIGH, preferred_element_type=F32)
    left = jnp.dot(after, rate, precision=HIGH, preferred_element_type=F32)
    cum_t = lax.dot_general(
        rate, mask, (((0,), (1,)), ((), ())), precision=HIGH, preferred_element_type=F32
    )
    step_t = step.T
    coef = jnp.exp(left) * step
    part = cum_ref.shape[2]
    for i in range(cum_ref.shape[0]):
        place = slice(i * part, (i + 1) * part)
        cum_ref[i] = cum[:, place]
        cum_t_ref[i] = cum_t[place, :]
        step_t_ref[i] = step_t[place, :]
        coef_ref[i] = coef[:, place]
    at, seg_at, _ = token_places(starts, tokens, (8, tokens), 1)
    row = lax.broadcasted_iota(jnp.int32, (8, tokens), 0)
    ends = jnp.dot(
        jnp.where(seg_at == row, 1.0, 0.0), rate, precision=HIGH, preferred_element_type=F32
    )
    decay_ref[...] = jnp.exp(ends)


def prep(starts, own, got, cache, kernel, bias, dt_bias, a_log):
    tokens = own.shape[0]
    channels = bias.shape[0]
    heads = dt_bias.shape[0]
    count_req = cache.shape[0]
    vmem = pl.BlockSpec(memory_space=pltpu.VMEM)
    part = min(HEADS_STEP, heads)
    tall = jax.ShapeDtypeStruct((heads // part, tokens, part), F32)
    flat = jax.ShapeDtypeStruct((heads // part, part, tokens), F32)
    return pl.pallas_call(
        functools.partial(prep_kernel, count_req, len(got)),
        out_shape=[
            jax.ShapeDtypeStruct((tokens, channels), BF16),
            tall,
            flat,
            flat,
            tall,
            jax.ShapeDtypeStruct((8, heads), F32),
        ],
        in_specs=[pl.BlockSpec(memory_space=pltpu.SMEM)] + [vmem] * (6 + len(got)),
        out_specs=[vmem] * 6,
        compiler_params=params(),
        cost_estimate=cost(4e8, 1e6),
    )(starts, own, *got, cache, kernel, bias[None], dt_bias[None], a_log[None])


def pack_kernel(slots_ref, pool_ref, conv_ref, out_ref):
    heads, width, state = pool_ref.shape[1:]
    out_ref[0, : heads * width, :] = pool_ref[0].reshape(heads * width, state).astype(BF16)
    out_ref[0, heads * width :, :] = conv_ref[0]


def pack(pool, conv_rows, slots):
    _, heads, width, state = pool.shape
    count_req, rows, _ = conv_rows.shape
    return pl.pallas_call(
        pack_kernel,
        out_shape=jax.ShapeDtypeStruct((count_req, heads * width + rows, state), BF16),
        grid_spec=pltpu.PrefetchScalarGridSpec(
            num_scalar_prefetch=1,
            grid=(count_req,),
            in_specs=[
                pl.BlockSpec((1, heads, width, state), lambda j, slots: (slots[j], 0, 0, 0)),
                pl.BlockSpec((1, rows, state), lambda j, slots: (j, 0, 0)),
            ],
            out_specs=pl.BlockSpec((1, heads * width + rows, state), lambda j, slots: (j, 0, 0)),
        ),
        compiler_params=params(3 * VMEM_BYTES),
        cost_estimate=cost(0, 6 * count_req * heads * width * state),
    )(slots, pool, conv_rows)


def mixer_kernel(count_req, got_total, slots_ref, flags_ref, starts_ref, *refs):
    own_ref = refs[0]
    got = refs[1 : 1 + got_total]
    rest = refs[1 + got_total :]
    cache_ref, kernel_ref, bias_ref, b_ref, c_ref = rest[:5]
    cum_ref, cum_t_ref, step_t_ref, coef_ref, decay_ref, skip_ref = rest[5:11]
    pools = rest[11 : 11 + count_req]
    states = rest[11 + count_req : 11 + count_req + got_total]
    out_ref, state_ref, scores_ref, c_part_ref, b_part_ref = rest[11 + count_req + got_total :]
    tokens, channels = own_ref.shape
    heads, width, state = pools[0].shape[1:]
    starts = [starts_ref[j] for j in range(count_req)]

    @pl.when(pl.program_id(0) == 0)
    def _():
        position, seg, _ = token_places(starts, tokens, (tokens, tokens), 0)
        other, seg_other, _ = token_places(starts, tokens, (tokens, tokens), 1)
        scores = lax.dot_general(
            c_ref[...], b_ref[...], (((1,), (1,)), ((), ())), preferred_element_type=F32
        )
        scores_ref[...] = jnp.where((seg == seg_other) & (position >= other), scores, 0.0)
        _, seg, _ = token_places(starts, tokens, (tokens, state), 0)
        b_maps = b_ref[...].astype(F32)
        c_maps = c_ref[...].astype(F32)
        for j in range(count_req):
            place = slice(j * state, (j + 1) * state)
            b_part_ref[:, place] = jnp.where(seg == j, b_maps, 0.0).astype(BF16)
            c_part_ref[:, place] = jnp.where(seg == j, c_maps, 0.0).astype(BF16)

    total = own_ref[...]
    for ref in got:
        total = total + ref[...].astype(F32)
    total = total.astype(BF16).astype(F32)
    position, seg, first = token_places(starts, tokens, (tokens, channels), 0)
    values = conv_silu(total, cache_ref, kernel_ref, bias_ref, seg, position - first)
    inputs = values.astype(BF16)
    values = inputs.astype(F32)

    lane_head = lax.broadcasted_iota(jnp.int32, (tokens, channels), 1) // width
    scores = scores_ref[...]
    cum = cum_ref[0]
    cum_t = cum_t_ref[0]
    step_t = step_t_ref[0]
    coef = coef_ref[0]
    grown = jnp.exp(cum)
    grown_wide = jnp.zeros((tokens, channels), F32)
    coef_wide = jnp.zeros((tokens, channels), F32)
    result = jnp.zeros((tokens, channels), F32)
    for h in range(heads):
        gap = jnp.minimum(cum[:, h : h + 1] - cum_t[h : h + 1, :], 0.0)
        weights = (jnp.exp(gap) * scores * step_t[h : h + 1, :]).astype(BF16)
        mine = lane_head == h
        result = result + jnp.dot(
            weights, jnp.where(mine, values, 0.0).astype(BF16), preferred_element_type=F32
        )
        grown_wide = jnp.where(mine, grown[:, h : h + 1], grown_wide)
        coef_wide = jnp.where(mine, coef[:, h : h + 1], coef_wide)

    from_state = jnp.zeros((tokens, channels), F32)
    carried = (coef_wide * values).astype(BF16)
    fresh = lax.dot_general(
        carried, b_part_ref[...], (((0,), (0,)), ((), ())), preferred_element_type=F32
    )
    for j in range(count_req):
        place = slice(j * state, (j + 1) * state)
        start = pools[j][0].reshape(channels, state) * flags_ref[j, 0].astype(F32)
        for step in range(got_total):
            start = start + states[step][j].astype(F32) * flags_ref[j, step + 1].astype(F32)
        from_state = from_state + lax.dot_general(
            c_part_ref[:, place],
            start.astype(BF16),
            (((1,), (1,)), ((), ())),
            preferred_element_type=F32,
        )
        first_head = pl.program_id(0) * heads
        for h in range(heads):
            rows = slice(h * width, (h + 1) * width)
            state_ref[j, h] = decay_ref[j, first_head + h] * start[rows] + fresh[rows, place]
    out_ref[...] = result + grown_wide * from_state + skip_ref[...] * values


def mixer(
    slots, flags, starts, own, got, cache, kernel, bias, b_maps, c_maps, cum, cum_t, step_t, coef,
    decay, skip, pool, states
):
    tokens, channels = own.shape
    _, heads, width, state = pool.shape
    count_req = cache.shape[0]
    kernel_len = kernel.shape[0]
    part = min(HEADS_STEP, heads)
    steps = heads // part
    wide = part * width
    columns = lambda i, *_: (0, i)
    whole = lambda i, *_: (0, 0)

    in_specs = (
        [pl.BlockSpec((tokens, wide), columns)] * (1 + len(got))
        + [
            pl.BlockSpec((count_req, kernel_len - 1, wide), lambda i, *_: (0, 0, i)),
            pl.BlockSpec((kernel_len, wide), columns),
            pl.BlockSpec((1, wide), columns),
            pl.BlockSpec((tokens, state), whole),
            pl.BlockSpec((tokens, state), whole),
            pl.BlockSpec((1, tokens, part), lambda i, *_: (i, 0, 0)),
            pl.BlockSpec((1, part, tokens), lambda i, *_: (i, 0, 0)),
            pl.BlockSpec((1, part, tokens), lambda i, *_: (i, 0, 0)),
            pl.BlockSpec((1, tokens, part), lambda i, *_: (i, 0, 0)),
            pl.BlockSpec(memory_space=pltpu.SMEM),
            pl.BlockSpec((1, wide), columns),
        ]
        + [
            pl.BlockSpec(
                (1, part, width, state),
                functools.partial(lambda j, i, slots, *_: (slots[j], i, 0, 0), j),
            )
            for j in range(count_req)
        ]
        + [pl.BlockSpec((count_req, wide, state), lambda i, *_: (0, i, 0))] * len(states)
    )
    return pl.pallas_call(
        functools.partial(mixer_kernel, count_req, len(got)),
        out_shape=[
            jax.ShapeDtypeStruct((tokens, channels), F32),
            jax.ShapeDtypeStruct((count_req, heads, width, state), F32),
        ],
        grid_spec=pltpu.PrefetchScalarGridSpec(
            num_scalar_prefetch=3,
            grid=(steps,),
            in_specs=in_specs,
            out_specs=[
                pl.BlockSpec((tokens, wide), columns),
                pl.BlockSpec((count_req, part, width, state), lambda i, *_: (0, i, 0, 0)),
            ],
            scratch_shapes=[
                pltpu.VMEM((tokens, tokens), F32),
                pltpu.VMEM((tokens, count_req * state), BF16),
                pltpu.VMEM((tokens, count_req * state), BF16),
            ],
        ),
        compiler_params=params(),
        cost_estimate=cost(5e9, 8e6),
    )(
        slots, flags, starts, own, *got, cache, kernel, bias[None], b_maps, c_maps,
        cum, cum_t, step_t, coef, decay,
        jnp.repeat(skip, width)[None], *([pool] * count_req), *states
    )


def on_device(
    x_in,
    w_xz,
    w_dt,
    w_bc,
    dt_bias,
    a_log,
    d_skip,
    conv_x_w,
    conv_x_b,
    conv_bc_w,
    conv_bc_b,
    norm_gain,
    stretch_start,
    prefix_len,
    state_slot,
    ssm_pool,
    conv_x_pool,
    conv_bc_pool,
):
    local_width = w_xz.shape[2]
    state_part = w_bc.shape[1]
    me = lax.axis_index("req")
    req_count = lax.axis_size("req")
    slot_count, heads, head_width, state = ssm_pool.shape
    group_reqs = prefix_len.shape[0]
    lags = conv_x_pool.shape[1]
    conv_width = local_width + state_part

    features = features_of(x_in)

    def slots_of(index):
        asked = lax.dynamic_slice_in_dim(state_slot, index * group_reqs, group_reqs)
        return jnp.clip(asked - me * slot_count, 0, slot_count - 1)

    def conv_of(slots):
        hit = slots[:, None] == jnp.arange(slot_count)[None, :]
        parts = [
            jnp.sum(jnp.where(hit[:, :, None, None], pool[None], 0), 1)
            for pool in (conv_x_pool, conv_bc_pool)
        ]
        return jnp.concatenate(parts, 2)

    conv_size = lags * conv_width
    conv_rows = -(-conv_size // (16 * state)) * 16
    got_states = []
    for step in range(1, req_count):
        slots = slots_of((me + step) % req_count)
        flat = conv_of(slots).reshape(group_reqs, conv_size)
        flat = jnp.pad(flat, ((0, 0), (0, conv_rows * state - conv_size)))
        packed = pack(ssm_pool, flat.reshape(group_reqs, conv_rows, state), slots)
        got_states.append(shift_req(packed, step))

    own_slots = slots_of(me)
    asked = lax.dynamic_slice_in_dim(state_slot, me * group_reqs, group_reqs)
    came_from = (me - asked // slot_count) % req_count
    live = prefix_len > 0
    flags = (live[:, None] & (came_from[:, None] == jnp.arange(req_count)[None, :])).astype(
        jnp.int32
    )
    cache = conv_of(own_slots)
    for step in range(1, req_count):
        got = got_states[step - 1][:, heads * head_width :].reshape(group_reqs, -1)
        got = got[:, :conv_size].reshape(cache.shape)
        cache = jnp.where((came_from == step)[:, None, None], got, cache)
    cache = jnp.where(live[:, None, None], cache, 0).astype(F32)

    w_map = jnp.concatenate([w_bc, w_dt], 1)

    def project(block, kind):
        low = jnp.dot(block, w_map, preferred_element_type=F32).astype(kind)
        low, block = lax.optimization_barrier((low, block))
        high = jnp.einsum("td,dkc->ktc", block, w_xz, preferred_element_type=F32)
        return {"map": low, "xr": high[1].astype(kind), "z": high[0].astype(kind)}

    came = {"map": [], "xr": [], "z": []}
    order = features[0]
    for step in range(1, req_count):
        part = project(features[step], BF16)
        for name in came:
            came[name].append(shift_req(part[name], step))
        order, _ = lax.optimization_barrier((order, part))
    own = lax.optimization_barrier(project(order, F32))

    bc_conv, cum, cum_t, step_t, coef, decay = prep(
        stretch_start, own["map"], came["map"], cache[:, :, local_width:], conv_bc_w, conv_bc_b,
        dt_bias, a_log
    )
    wide_index = lax.axis_index("wide")
    group_span = lax.axis_size("wide") // GROUPS
    bit_total = group_span.bit_length() - 1
    joined = bc_conv
    for bit_index in range(bit_total):
        partner = partner_2(joined, "wide", bit_index)
        upper_half = wide_index // (1 << bit_index) % 2 == 1
        joined = jnp.where(
            upper_half, jnp.concatenate([partner, joined], 1), jnp.concatenate([joined, partner], 1)
        )
    state_width = joined.shape[1] // 2
    result, final_state = mixer(
        own_slots, flags, stretch_start[0], own["xr"], came["xr"], cache[:, :, :local_width],
        conv_x_w, conv_x_b, joined[:, :state_width], joined[:, state_width:], cum, cum_t,
        step_t, coef, decay, d_skip, ssm_pool, got_states
    )
    gate = own["z"]
    for got in came["z"]:
        gate = gate + got.astype(F32)
    gated = result * jax.nn.silu(gate.astype(BF16).astype(F32))
    square_sum = jnp.sum(gated * gated, 1)
    for bit_index in range(bit_total):
        square_sum = square_sum + partner_2(square_sum, "wide", bit_index)
    mean_sq = square_sum / (local_width * group_span)
    normed = gated * lax.rsqrt(mean_sq + NORM_EPS)[:, None] * norm_gain[None, :]
    return (normed.astype(BF16), final_state)


def solution(mesh):
    in_specs = (
        P("req", "wide"),
        P("req", None, "wide"),
        P("req", "wide"),
        P("req", "wide"),
        P("wide"),
        P("wide"),
        P("wide"),
        P(None, "wide"),
        P("wide"),
        P(None, "wide"),
        P("wide"),
        P("wide"),
        P("req", None),
        P("req"),
        P(),
        P("req", "wide", None, None),
        P("req", None, "wide"),
        P("req", None, "wide"),
    )
    out_specs = (P("req", "wide"), P("req", "wide", None, None))
    return jax.shard_map(
        on_device, mesh=mesh, in_specs=in_specs, out_specs=out_specs, check_vma=False
    )
```

```python
import functools

import jax
import jax.numpy as jnp
from jax import lax
from jax.experimental import pallas as pl
from jax.experimental.layout import Layout, with_layout_constraint
from jax.experimental.pallas import tpu as pltpu
from jax.sharding import PartitionSpec as P

GROUPS = 8
NORM_EPS = 1e-05
F32 = jnp.float32
BF16 = jnp.bfloat16
HIGH = lax.Precision.HIGHEST
VMEM_BYTES = 16 * 1024 * 1024
HEADS_STEP = 4


def cost(flops, bytes_accessed):
    return pl.CostEstimate(flops=int(flops), bytes_accessed=int(bytes_accessed), transcendentals=0)


def params(limit=VMEM_BYTES):
    return pltpu.CompilerParams(vmem_limit_bytes=limit)


def partner_2(block, axis, bit):
    count = lax.axis_size(axis)
    route = []
    for low in range(count):
        high = low | 1 << bit
        if high != low and high < count:
            route += [(low, high), (high, low)]
    return lax.ppermute(block, axis, route)


def shift_req(block, step):
    count = lax.axis_size("req")
    return lax.ppermute(block, "req", [(i, (i + step) % count) for i in range(count)])


def spread_routes():
    first, second = [], []
    for z in range(4):
        for rest in range(4):
            for r in range(2):
                place = (z * 4 + rest) * 2 + r
                other = (((z + 2) % 4) * 4 + rest) * 2 + r
                if z // 2 == r:
                    first.append((place, other))
                else:
                    first.append((place, place ^ 1))
                    second.append((place, other ^ 1))
    return first, second


def arrange_kernel(places_ref, *refs):
    out_ref = refs[-1]
    index = 0
    for ref in refs[:-1]:
        for part in range(ref.shape[0]):
            width = ref.shape[2]
            place = pl.multiple_of(places_ref[index] * width, width)
            out_ref[:, pl.ds(place, width)] = ref[part]
            index += 1


def arrange(stacks, places):
    tokens, width = stacks[0].shape[1:]
    total = sum(stack.shape[0] for stack in stacks) * width
    return pl.pallas_call(
        arrange_kernel,
        out_shape=jax.ShapeDtypeStruct((tokens, total), stacks[0].dtype),
        in_specs=[pl.BlockSpec(memory_space=pltpu.SMEM)]
        + [pl.BlockSpec(memory_space=pltpu.VMEM)] * len(stacks),
        out_specs=pl.BlockSpec(memory_space=pltpu.VMEM),
        compiler_params=params(),
        cost_estimate=cost(1e6, 1e4),
    )(places, *stacks)


def after(value, *others):
    return lax.optimization_barrier((value, others))[0]


def near_blocks(x_in):
    axes = ("wide", "req")
    first, second = spread_routes()
    first = lax.ppermute(x_in, axes, first)
    second = lax.ppermute(x_in, axes, second)
    near = lax.axis_index("wide") // 8 == lax.axis_index("req")
    return jnp.where(near, x_in, first), jnp.where(near, first, second)


def quad_arrange(four, other):
    apart = jnp.array([0, 2, 4, 6, 1, 3, 5, 7], jnp.int32)
    return arrange([four, other], (lax.axis_index("wide") % 8) ^ apart)


def features_in_general(x_in):
    req_count = lax.axis_size("req")
    me = lax.axis_index("req")
    own = lax.all_gather(x_in, "wide", axis=1, tiled=True)
    parts = own.reshape(own.shape[0], req_count, own.shape[1] // req_count).transpose(1, 0, 2)
    got = lax.all_to_all(parts, "req", split_axis=0, concat_axis=0, tiled=True)
    return [
        lax.dynamic_index_in_dim(got, (me + step) % req_count, 0, False)
        for step in range(req_count)
    ]


def grab_kernel(first, w_ref, _, out_ref, sem):
    copy = pltpu.make_async_copy(w_ref.at[pl.ds(first, out_ref.shape[0])], out_ref, sem)
    copy.start()
    copy.wait()


def relayout(w_xz, chunk, chunks, behind):
    rows = w_xz.shape[0] // chunks
    in_hbm = pl.BlockSpec(memory_space=pltpu.HBM)
    held = pl.pallas_call(
        functools.partial(grab_kernel, chunk * rows),
        out_shape=jax.ShapeDtypeStruct((rows,) + w_xz.shape[1:], w_xz.dtype),
        in_specs=[in_hbm, pl.BlockSpec(memory_space=pl.ANY)],
        out_specs=pl.BlockSpec(memory_space=pltpu.VMEM),
        scratch_shapes=[pltpu.SemaphoreType.DMA],
        compiler_params=params(),
        cost_estimate=cost(0, 4 * rows * w_xz.shape[1] * w_xz.shape[2]),
    )(w_xz, behind)
    rows_last = with_layout_constraint(jnp.transpose(held, (1, 0, 2)), Layout((0, 1, 2)))
    return lax.optimization_barrier(rows_last)


def token_places(starts, count_tok, shape, axis):
    position = lax.broadcasted_iota(jnp.int32, shape, axis)
    seg = jnp.full(shape, -1, jnp.int32)
    first = jnp.zeros(shape, jnp.int32)
    for start in starts:
        seg = seg + (position >= start).astype(jnp.int32)
        first = jnp.where(position >= start, start, first)
    return position, seg, first


def conv_silu(values, cache_ref, kernel_ref, bias_ref, seg, offset):
    kernel_len = kernel_ref.shape[0]
    taps = [kernel_ref[k : k + 1, :] for k in range(kernel_len)]
    total = bias_ref[...] + taps[kernel_len - 1] * values
    for lag in range(1, kernel_len):
        earlier = pltpu.roll(values, lag, 0)
        total = total + taps[kernel_len - 1 - lag] * jnp.where(offset >= lag, earlier, 0.0)
    cached = jnp.zeros_like(values)
    for request in range(cache_ref.shape[0]):
        for place in range(kernel_len - 1):
            history = jnp.zeros_like(bias_ref[...])
            for lag in range(place + 1, kernel_len):
                at = kernel_len - 1 + place - lag
                history = history + taps[kernel_len - 1 - lag] * cache_ref[request, at : at + 1, :]
            cached = jnp.where((seg == request) & (offset == place), history, cached)
    total = total + cached
    return total * jax.nn.sigmoid(total)


def prep_kernel(
    count_req, got_total, starts_ref, own_ref, *refs
):
    got = refs[:got_total]
    cache_ref, kernel_ref, bias_ref, dt_bias_ref, a_log_ref = refs[got_total : got_total + 5]
    bc_ref, cum_ref, cum_t_ref, step_t_ref, coef_ref, decay_ref = refs[got_total + 5 :]
    tokens = own_ref.shape[0]
    channels = bias_ref.shape[1]
    heads = dt_bias_ref.shape[1]
    starts = [starts_ref[0, j] for j in range(count_req)]
    total = own_ref[...]
    for ref in got:
        total = total + ref[...].astype(F32)
    total = total.astype(BF16).astype(F32)
    position, seg, first = token_places(starts, tokens, (tokens, channels), 0)
    bc = conv_silu(total[:, :channels], cache_ref, kernel_ref, bias_ref, seg, position - first)
    bc_ref[...] = bc.astype(BF16)
    raw = total[:, channels : channels + heads] + dt_bias_ref[...]
    step = jnp.maximum(raw, 0.0) + jnp.log1p(jnp.exp(-jnp.abs(raw)))
    rate = step * (-jnp.exp(a_log_ref[...]))
    position, seg, first = token_places(starts, tokens, (tokens, tokens), 0)
    other, seg_other, first_other = token_places(starts, tokens, (tokens, tokens), 1)
    same = seg == seg_other
    mask = jnp.where(same & (position >= other), 1.0, 0.0)
    after = jnp.where(same & (position < other), 1.0, 0.0)
    cum = jnp.dot(mask, rate, precision=HIGH, preferred_element_type=F32)
    left = jnp.dot(after, rate, precision=HIGH, preferred_element_type=F32)
    cum_t = lax.dot_general(
        rate, mask, (((0,), (1,)), ((), ())), precision=HIGH, preferred_element_type=F32
    )
    step_t = step.T
    coef = jnp.exp(left) * step
    part = cum_ref.shape[2]
    for i in range(cum_ref.shape[0]):
        place = slice(i * part, (i + 1) * part)
        cum_ref[i] = cum[:, place]
        cum_t_ref[i] = cum_t[place, :]
        step_t_ref[i] = step_t[place, :]
        coef_ref[i] = coef[:, place]
    at, seg_at, _ = token_places(starts, tokens, (8, tokens), 1)
    row = lax.broadcasted_iota(jnp.int32, (8, tokens), 0)
    ends = jnp.dot(
        jnp.where(seg_at == row, 1.0, 0.0), rate, precision=HIGH, preferred_element_type=F32
    )
    decay_ref[...] = jnp.exp(ends)


def prep(starts, own, got, cache, kernel, bias, dt_bias, a_log):
    tokens = own.shape[0]
    channels = bias.shape[0]
    heads = dt_bias.shape[0]
    count_req = cache.shape[0]
    vmem = pl.BlockSpec(memory_space=pltpu.VMEM)
    part = min(HEADS_STEP, heads)
    tall = jax.ShapeDtypeStruct((heads // part, tokens, part), F32)
    flat = jax.ShapeDtypeStruct((heads // part, part, tokens), F32)
    return pl.pallas_call(
        functools.partial(prep_kernel, count_req, len(got)),
        out_shape=[
            jax.ShapeDtypeStruct((tokens, channels), BF16),
            tall,
            flat,
            flat,
            tall,
            jax.ShapeDtypeStruct((8, heads), F32),
        ],
        in_specs=[pl.BlockSpec(memory_space=pltpu.SMEM)] + [vmem] * (6 + len(got)),
        out_specs=[vmem] * 6,
        compiler_params=params(),
        cost_estimate=cost(1e6, 1e4),
    )(starts, own, *got, cache, kernel, bias[None], dt_bias[None], a_log[None])


def pack_kernel(slots_ref, own_slots_ref, pool_ref, own_pool_ref, conv_ref, out_ref, own_ref):
    heads, width, state = pool_ref.shape[1:]
    out_ref[0, : heads * width, :] = pool_ref[0].reshape(heads * width, state).astype(BF16)
    out_ref[0, heads * width :, :] = conv_ref[0]
    own_ref[...] = own_pool_ref[...]


def pack(pool, conv_rows, slots, own_slots):
    _, heads, width, state = pool.shape
    count_req, rows, _ = conv_rows.shape
    block = (1, heads, width, state)
    return pl.pallas_call(
        pack_kernel,
        out_shape=[
            jax.ShapeDtypeStruct((count_req, heads * width + rows, state), BF16),
            jax.ShapeDtypeStruct((count_req, heads, width, state), F32),
        ],
        grid_spec=pltpu.PrefetchScalarGridSpec(
            num_scalar_prefetch=2,
            grid=(count_req,),
            in_specs=[
                pl.BlockSpec(block, lambda j, slots, own: (slots[j], 0, 0, 0)),
                pl.BlockSpec(block, lambda j, slots, own: (own[j], 0, 0, 0)),
                pl.BlockSpec((1, rows, state), lambda j, *_: (j, 0, 0)),
            ],
            out_specs=[
                pl.BlockSpec((1, heads * width + rows, state), lambda j, *_: (j, 0, 0)),
                pl.BlockSpec(block, lambda j, *_: (j, 0, 0, 0)),
            ],
        ),
        compiler_params=params(3 * VMEM_BYTES),
        cost_estimate=cost(0, 14 * count_req * heads * width * state),
    )(slots, own_slots, pool, pool, conv_rows)


def mixer_kernel(count_req, got_total, flags_ref, starts_ref, *refs):
    own_ref = refs[0]
    got = refs[1 : 1 + got_total]
    rest = refs[1 + got_total :]
    cache_ref, kernel_ref, bias_ref, b_ref, c_ref = rest[:5]
    cum_ref, cum_t_ref, step_t_ref, coef_ref, decay_ref, skip_ref = rest[5:11]
    held_ref = rest[11]
    states = rest[12 : 12 + got_total]
    out_ref, state_ref, scores_ref, c_part_ref, b_part_ref = rest[12 + got_total :]
    tokens, channels = own_ref.shape
    heads, width, state = held_ref.shape[1:]
    starts = [starts_ref[j] for j in range(count_req)]

    @pl.when(pl.program_id(0) == 0)
    def _():
        position, seg, _ = token_places(starts, tokens, (tokens, tokens), 0)
        other, seg_other, _ = token_places(starts, tokens, (tokens, tokens), 1)
        scores = lax.dot_general(
            c_ref[...], b_ref[...], (((1,), (1,)), ((), ())), preferred_element_type=F32
        )
        scores_ref[...] = jnp.where((seg == seg_other) & (position >= other), scores, 0.0)
        _, seg, _ = token_places(starts, tokens, (tokens, state), 0)
        b_maps = b_ref[...].astype(F32)
        c_maps = c_ref[...].astype(F32)
        for j in range(count_req):
            place = slice(j * state, (j + 1) * state)
            b_part_ref[:, place] = jnp.where(seg == j, b_maps, 0.0).astype(BF16)
            c_part_ref[:, place] = jnp.where(seg == j, c_maps, 0.0).astype(BF16)

    total = own_ref[...]
    for ref in got:
        total = total + ref[...].astype(F32)
    total = total.astype(BF16).astype(F32)
    position, seg, first = token_places(starts, tokens, (tokens, channels), 0)
    values = conv_silu(total, cache_ref, kernel_ref, bias_ref, seg, position - first)
    inputs = values.astype(BF16)
    values = inputs.astype(F32)

    lane_head = lax.broadcasted_iota(jnp.int32, (tokens, channels), 1) // width
    scores = scores_ref[...]
    cum = cum_ref[0]
    cum_t = cum_t_ref[0]
    step_t = step_t_ref[0]
    coef = coef_ref[0]
    grown = jnp.exp(cum)
    grown_wide = jnp.zeros((tokens, channels), F32)
    coef_wide = jnp.zeros((tokens, channels), F32)
    result = jnp.zeros((tokens, channels), F32)
    for h in range(heads):
        gap = jnp.minimum(cum[:, h : h + 1] - cum_t[h : h + 1, :], 0.0)
        weights = (jnp.exp(gap) * scores * step_t[h : h + 1, :]).astype(BF16)
        mine = lane_head == h
        result = result + jnp.dot(
            weights, jnp.where(mine, values, 0.0).astype(BF16), preferred_element_type=F32
        )
        grown_wide = jnp.where(mine, grown[:, h : h + 1], grown_wide)
        coef_wide = jnp.where(mine, coef[:, h : h + 1], coef_wide)

    from_state = jnp.zeros((tokens, channels), F32)
    carried = (coef_wide * values).astype(BF16)
    fresh = lax.dot_general(
        carried, b_part_ref[...], (((0,), (0,)), ((), ())), preferred_element_type=F32
    )
    for j in range(count_req):
        place = slice(j * state, (j + 1) * state)
        start = held_ref[j].reshape(channels, state) * flags_ref[j, 0].astype(F32)
        for step in range(got_total):
            start = start + states[step][j].astype(F32) * flags_ref[j, step + 1].astype(F32)
        from_state = from_state + lax.dot_general(
            c_part_ref[:, place],
            start.astype(BF16),
            (((1,), (1,)), ((), ())),
            preferred_element_type=F32,
        )
        first_head = pl.program_id(0) * heads
        for h in range(heads):
            rows = slice(h * width, (h + 1) * width)
            state_ref[j, h] = decay_ref[j, first_head + h] * start[rows] + fresh[rows, place]
    out_ref[...] = result + grown_wide * from_state + skip_ref[...] * values


def mixer(
    flags, starts, own, got, cache, kernel, bias, b_maps, c_maps, cum, cum_t, step_t, coef,
    decay, skip, held, states
):
    tokens, channels = own.shape
    count_req, heads, width, state = held.shape
    kernel_len = kernel.shape[0]
    part = min(HEADS_STEP, heads)
    steps = heads // part
    wide = part * width
    columns = lambda i, *_: (0, i)
    whole = lambda i, *_: (0, 0)

    in_specs = (
        [pl.BlockSpec((tokens, wide), columns)] * (1 + len(got))
        + [
            pl.BlockSpec((count_req, kernel_len - 1, wide), lambda i, *_: (0, 0, i)),
            pl.BlockSpec((kernel_len, wide), columns),
            pl.BlockSpec((1, wide), columns),
            pl.BlockSpec((tokens, state), whole),
            pl.BlockSpec((tokens, state), whole),
            pl.BlockSpec((1, tokens, part), lambda i, *_: (i, 0, 0)),
            pl.BlockSpec((1, part, tokens), lambda i, *_: (i, 0, 0)),
            pl.BlockSpec((1, part, tokens), lambda i, *_: (i, 0, 0)),
            pl.BlockSpec((1, tokens, part), lambda i, *_: (i, 0, 0)),
            pl.BlockSpec(memory_space=pltpu.SMEM),
            pl.BlockSpec((1, wide), columns),
        ]
        + [pl.BlockSpec((count_req, part, width, state), lambda i, *_: (0, i, 0, 0))]
        + [pl.BlockSpec((count_req, wide, state), lambda i, *_: (0, i, 0))] * len(states)
    )
    return pl.pallas_call(
        functools.partial(mixer_kernel, count_req, len(got)),
        out_shape=[
            jax.ShapeDtypeStruct((tokens, channels), F32),
            jax.ShapeDtypeStruct((count_req, heads, width, state), F32),
        ],
        grid_spec=pltpu.PrefetchScalarGridSpec(
            num_scalar_prefetch=2,
            grid=(steps,),
            in_specs=in_specs,
            out_specs=[
                pl.BlockSpec((tokens, wide), columns),
                pl.BlockSpec((count_req, part, width, state), lambda i, *_: (0, i, 0, 0)),
            ],
            scratch_shapes=[
                pltpu.VMEM((tokens, tokens), F32),
                pltpu.VMEM((tokens, count_req * state), BF16),
                pltpu.VMEM((tokens, count_req * state), BF16),
            ],
        ),
        compiler_params=params(),
        cost_estimate=cost(1e6, 1e4),
    )(
        flags, starts, own, *got, cache, kernel, bias[None], b_maps, c_maps,
        cum, cum_t, step_t, coef, decay,
        jnp.repeat(skip, width)[None], held, *states
    )


def on_device(
    x_in,
    w_xz,
    w_dt,
    w_bc,
    dt_bias,
    a_log,
    d_skip,
    conv_x_w,
    conv_x_b,
    conv_bc_w,
    conv_bc_b,
    norm_gain,
    stretch_start,
    prefix_len,
    state_slot,
    ssm_pool,
    conv_x_pool,
    conv_bc_pool,
):
    local_width = w_xz.shape[2]
    state_part = w_bc.shape[1]
    me = lax.axis_index("req")
    req_count = lax.axis_size("req")
    slot_count, heads, head_width, state = ssm_pool.shape
    group_reqs = prefix_len.shape[0]
    lags = conv_x_pool.shape[1]
    conv_width = local_width + state_part

    count_wide = lax.axis_size("wide")
    if req_count == 2 and count_wide == 16:
        own_block, their_block = near_blocks(x_in)

    def slots_of(index):
        asked = lax.dynamic_slice_in_dim(state_slot, index * group_reqs, group_reqs)
        return jnp.clip(asked - me * slot_count, 0, slot_count - 1)

    def conv_of(slots):
        hit = slots[:, None] == jnp.arange(slot_count)[None, :]
        parts = [
            jnp.sum(jnp.where(hit[:, :, None, None], pool[None], 0), 1)
            for pool in (conv_x_pool, conv_bc_pool)
        ]
        return jnp.concatenate(parts, 2)

    conv_size = lags * conv_width
    conv_rows = -(-conv_size // (16 * state)) * 16
    own_slots = slots_of(me)
    got_states = []
    for step in range(1, req_count):
        slots = slots_of((me + step) % req_count)
        flat = conv_of(slots).reshape(group_reqs, conv_size)
        flat = jnp.pad(flat, ((0, 0), (0, conv_rows * state - conv_size)))
        packed, held = pack(
            ssm_pool, flat.reshape(group_reqs, conv_rows, state), slots, own_slots
        )
        got_states.append(shift_req(packed, step))

    asked = lax.dynamic_slice_in_dim(state_slot, me * group_reqs, group_reqs)
    came_from = (me - asked // slot_count) % req_count
    live = prefix_len > 0
    flags = (live[:, None] & (came_from[:, None] == jnp.arange(req_count)[None, :])).astype(
        jnp.int32
    )
    cache = conv_of(own_slots)
    for step in range(1, req_count):
        got = got_states[step - 1][:, heads * head_width :].reshape(group_reqs, -1)
        got = got[:, :conv_size].reshape(cache.shape)
        cache = jnp.where((came_from == step)[:, None, None], got, cache)
    cache = jnp.where(live[:, None, None], cache, 0).astype(F32)

    chunks = 4
    if req_count == 2 and count_wide == 16:
        weights = [relayout(w_xz, k, chunks, packed) for k in range(2)]
        block = after(their_block, *weights)
        along_z = partner_2(block, "wide", 2)
        along_x = partner_2(block, "wide", 1)
        weights.append(relayout(w_xz, 2, chunks, block))
        own_block = after(own_block, weights[2])
        both = partner_2(after(along_z, weights[2]), "wide", 1)
        own_z = partner_2(own_block, "wide", 2)
        weights.append(relayout(w_xz, 3, chunks, own_block))
        four = jnp.stack([block, along_x, along_z, after(both, weights[3])])
        other = partner_2(four, "wide", 0)
        own_x = partner_2(after(own_block, four), "wide", 1)
        own_both = partner_2(after(own_z, four), "wide", 1)
        theirs = quad_arrange(four, other)
        own_four = jnp.stack([own_block, own_x, own_z, own_both])
        own_other = partner_2(own_four, "wide", 0)
        features = [(own_four, own_other), theirs]
    else:
        weights = [relayout(w_xz, k, chunks, packed) for k in range(chunks)]
        features = features_in_general(x_in)
    w_map = jnp.concatenate([w_bc, w_dt], 1)
    depth = w_xz.shape[0] // chunks

    def project(block, name):
        if name == "map":
            return jnp.dot(block, w_map, preferred_element_type=F32)
        total = None
        for k in range(chunks):
            term = jnp.dot(
                block[:, k * depth : (k + 1) * depth],
                weights[k][1 if name == "xr" else 0],
                preferred_element_type=F32,
            )
            total = term if total is None else total + term
        return total

    came = {"map": [], "xr": [], "z": []}
    done = []
    for step in range(1, req_count):
        block = features[step]
        for name in came:
            part, block = lax.optimization_barrier((project(block, name).astype(BF16), block))
            came[name].append(shift_req(part, step))
            done.append(part)
    block = after(features[0], *done)
    if req_count == 2 and count_wide == 16:
        block = quad_arrange(*block)
    own = {}
    for name in came:
        own[name], block = lax.optimization_barrier((project(block, name), block))

    bc_conv, cum, cum_t, step_t, coef, decay = prep(
        stretch_start, own["map"], came["map"], cache[:, :, local_width:], conv_bc_w, conv_bc_b,
        dt_bias, a_log
    )
    wide_index = lax.axis_index("wide")
    group_span = lax.axis_size("wide") // GROUPS
    bit_total = group_span.bit_length() - 1
    joined = bc_conv
    for bit_index in range(bit_total):
        partner = partner_2(joined, "wide", bit_index)
        upper_half = wide_index // (1 << bit_index) % 2 == 1
        joined = jnp.where(
            upper_half, jnp.concatenate([partner, joined], 1), jnp.concatenate([joined, partner], 1)
        )
    state_width = joined.shape[1] // 2
    result, final_state = mixer(
        flags, stretch_start[0], own["xr"], came["xr"], cache[:, :, :local_width],
        conv_x_w, conv_x_b, joined[:, :state_width], joined[:, state_width:], cum, cum_t,
        step_t, coef, decay, d_skip, held, got_states
    )
    gate = own["z"]
    for got in came["z"]:
        gate = gate + got.astype(F32)
    gated = result * jax.nn.silu(gate.astype(BF16).astype(F32))
    square_sum = jnp.sum(gated * gated, 1)
    for bit_index in range(bit_total):
        square_sum = square_sum + partner_2(square_sum, "wide", bit_index)
    mean_sq = square_sum / (local_width * group_span)
    normed = gated * lax.rsqrt(mean_sq + NORM_EPS)[:, None] * norm_gain[None, :]
    return (normed.astype(BF16), final_state)


def solution(mesh):
    in_specs = (
        P("req", "wide"),
        P("req", None, "wide"),
        P("req", "wide"),
        P("req", "wide"),
        P("wide"),
        P("wide"),
        P("wide"),
        P(None, "wide"),
        P("wide"),
        P(None, "wide"),
        P("wide"),
        P("wide"),
        P("req", None),
        P("req"),
        P(),
        P("req", "wide", None, None),
        P("req", None, "wide"),
        P("req", None, "wide"),
    )
    out_specs = (P("req", "wide"), P("req", "wide", None, None))
    return jax.shard_map(
        on_device, mesh=mesh, in_specs=in_specs, out_specs=out_specs, check_vma=False
    )
```

```python
import functools

import jax
import jax.numpy as jnp
from jax import lax
from jax.experimental import pallas as pl
from jax.experimental.layout import Layout, with_layout_constraint
from jax.experimental.pallas import tpu as pltpu
from jax.sharding import PartitionSpec as P

GROUPS = 8
NORM_EPS = 1e-05
F32 = jnp.float32
BF16 = jnp.bfloat16
HIGH = lax.Precision.HIGHEST
VMEM_BYTES = 16 * 1024 * 1024
HEADS_STEP = 4


def cost(flops, bytes_accessed):
    return pl.CostEstimate(flops=int(flops), bytes_accessed=int(bytes_accessed), transcendentals=0)


def params(limit=VMEM_BYTES):
    return pltpu.CompilerParams(vmem_limit_bytes=limit)


def partner_2(block, axis, bit):
    count = lax.axis_size(axis)
    route = []
    for low in range(count):
        high = low | 1 << bit
        if high != low and high < count:
            route += [(low, high), (high, low)]
    return lax.ppermute(block, axis, route)


def shift_req(block, step):
    count = lax.axis_size("req")
    return lax.ppermute(block, "req", [(i, (i + step) % count) for i in range(count)])


def spread_routes():
    first, second = [], []
    for z in range(4):
        for rest in range(4):
            for r in range(2):
                place = (z * 4 + rest) * 2 + r
                other = (((z + 2) % 4) * 4 + rest) * 2 + r
                if z // 2 == r:
                    first.append((place, other))
                else:
                    first.append((place, place ^ 1))
                    second.append((place, other ^ 1))
    return first, second


def arrange_kernel(places_ref, *refs):
    out_ref = refs[-1]
    index = 0
    for ref in refs[:-1]:
        for part in range(ref.shape[0]):
            width = ref.shape[2]
            place = pl.multiple_of(places_ref[index] * width, width)
            out_ref[:, pl.ds(place, width)] = ref[part]
            index += 1


def arrange(stacks, places):
    tokens, width = stacks[0].shape[1:]
    total = sum(stack.shape[0] for stack in stacks) * width
    return pl.pallas_call(
        arrange_kernel,
        out_shape=jax.ShapeDtypeStruct((tokens, total), stacks[0].dtype),
        in_specs=[pl.BlockSpec(memory_space=pltpu.SMEM)]
        + [pl.BlockSpec(memory_space=pltpu.VMEM)] * len(stacks),
        out_specs=pl.BlockSpec(memory_space=pltpu.VMEM),
        compiler_params=params(),
        cost_estimate=cost(1e6, 1e4),
    )(places, *stacks)


def after(value, *others):
    return lax.optimization_barrier((value, others))[0]


def near_blocks(x_in):
    axes = ("wide", "req")
    first, second = spread_routes()
    first = lax.ppermute(x_in, axes, first)
    second = lax.ppermute(x_in, axes, second)
    near = lax.axis_index("wide") // 8 == lax.axis_index("req")
    return jnp.where(near, x_in, first), jnp.where(near, first, second)


def quad_arrange(four, other):
    apart = jnp.array([0, 4, 2, 6, 1, 5, 3, 7], jnp.int32)
    return arrange([four, other], (lax.axis_index("wide") % 8) ^ apart)


def features_in_general(x_in):
    req_count = lax.axis_size("req")
    me = lax.axis_index("req")
    own = lax.all_gather(x_in, "wide", axis=1, tiled=True)
    parts = own.reshape(own.shape[0], req_count, own.shape[1] // req_count).transpose(1, 0, 2)
    got = lax.all_to_all(parts, "req", split_axis=0, concat_axis=0, tiled=True)
    return [
        lax.dynamic_index_in_dim(got, (me + step) % req_count, 0, False)
        for step in range(req_count)
    ]


def pinned(array):
    return lax.optimization_barrier(
        with_layout_constraint(array, Layout(tuple(range(array.ndim))))
    )


def token_places(starts, count_tok, shape, axis):
    position = lax.broadcasted_iota(jnp.int32, shape, axis)
    seg = jnp.full(shape, -1, jnp.int32)
    first = jnp.zeros(shape, jnp.int32)
    for start in starts:
        seg = seg + (position >= start).astype(jnp.int32)
        first = jnp.where(position >= start, start, first)
    return position, seg, first


def conv_silu(values, cache_ref, kernel_ref, bias_ref, seg, offset):
    kernel_len = kernel_ref.shape[0]
    taps = [kernel_ref[k : k + 1, :] for k in range(kernel_len)]
    total = bias_ref[...] + taps[kernel_len - 1] * values
    for lag in range(1, kernel_len):
        earlier = pltpu.roll(values, lag, 0)
        total = total + taps[kernel_len - 1 - lag] * jnp.where(offset >= lag, earlier, 0.0)
    cached = jnp.zeros_like(values)
    for request in range(cache_ref.shape[0]):
        for place in range(kernel_len - 1):
            history = jnp.zeros_like(bias_ref[...])
            for lag in range(place + 1, kernel_len):
                at = kernel_len - 1 + place - lag
                history = history + taps[kernel_len - 1 - lag] * cache_ref[request, at : at + 1, :]
            cached = jnp.where((seg == request) & (offset == place), history, cached)
    total = total + cached
    return total * jax.nn.sigmoid(total)


def prep_kernel(
    count_req, got_total, starts_ref, own_ref, *refs
):
    got = refs[:got_total]
    cache_ref, kernel_ref, bias_ref, dt_bias_ref, a_log_ref = refs[got_total : got_total + 5]
    bc_ref, cum_ref, cum_t_ref, step_t_ref, coef_ref, decay_ref = refs[got_total + 5 :]
    tokens = own_ref.shape[0]
    channels = bias_ref.shape[1]
    heads = dt_bias_ref.shape[1]
    starts = [starts_ref[0, j] for j in range(count_req)]
    total = own_ref[...]
    for ref in got:
        total = total + ref[...].astype(F32)
    total = total.astype(BF16).astype(F32)
    position, seg, first = token_places(starts, tokens, (tokens, channels), 0)
    bc = conv_silu(total[:, :channels], cache_ref, kernel_ref, bias_ref, seg, position - first)
    bc_ref[...] = bc.astype(BF16)
    raw = total[:, channels : channels + heads] + dt_bias_ref[...]
    step = jnp.maximum(raw, 0.0) + jnp.log1p(jnp.exp(-jnp.abs(raw)))
    rate = step * (-jnp.exp(a_log_ref[...]))
    position, seg, first = token_places(starts, tokens, (tokens, tokens), 0)
    other, seg_other, first_other = token_places(starts, tokens, (tokens, tokens), 1)
    same = seg == seg_other
    mask = jnp.where(same & (position >= other), 1.0, 0.0)
    after = jnp.where(same & (position < other), 1.0, 0.0)
    cum = jnp.dot(mask, rate, precision=HIGH, preferred_element_type=F32)
    left = jnp.dot(after, rate, precision=HIGH, preferred_element_type=F32)
    cum_t = lax.dot_general(
        rate, mask, (((0,), (1,)), ((), ())), precision=HIGH, preferred_element_type=F32
    )
    step_t = step.T
    coef = jnp.exp(left) * step
    part = cum_ref.shape[2]
    for i in range(cum_ref.shape[0]):
        place = slice(i * part, (i + 1) * part)
        cum_ref[i] = cum[:, place]
        cum_t_ref[i] = cum_t[place, :]
        step_t_ref[i] = step_t[place, :]
        coef_ref[i] = coef[:, place]
    at, seg_at, _ = token_places(starts, tokens, (8, tokens), 1)
    row = lax.broadcasted_iota(jnp.int32, (8, tokens), 0)
    ends = jnp.dot(
        jnp.where(seg_at == row, 1.0, 0.0), rate, precision=HIGH, preferred_element_type=F32
    )
    decay_ref[...] = jnp.exp(ends)


def prep(starts, own, got, cache, kernel, bias, dt_bias, a_log):
    tokens = own.shape[0]
    channels = bias.shape[0]
    heads = dt_bias.shape[0]
    count_req = cache.shape[0]
    vmem = pl.BlockSpec(memory_space=pltpu.VMEM)
    part = min(HEADS_STEP, heads)
    tall = jax.ShapeDtypeStruct((heads // part, tokens, part), F32)
    flat = jax.ShapeDtypeStruct((heads // part, part, tokens), F32)
    return pl.pallas_call(
        functools.partial(prep_kernel, count_req, len(got)),
        out_shape=[
            jax.ShapeDtypeStruct((tokens, channels), BF16),
            tall,
            flat,
            flat,
            tall,
            jax.ShapeDtypeStruct((8, heads), F32),
        ],
        in_specs=[pl.BlockSpec(memory_space=pltpu.SMEM)] + [vmem] * (6 + len(got)),
        out_specs=[vmem] * 6,
        compiler_params=params(),
        cost_estimate=cost(1e6, 1e4),
    )(starts, own, *got, cache, kernel, bias[None], dt_bias[None], a_log[None])


def pack_kernel(slots_ref, own_slots_ref, pool_ref, own_pool_ref, conv_ref, out_ref, own_ref):
    heads, width, state = pool_ref.shape[1:]
    out_ref[0, : heads * width, :] = pool_ref[0].reshape(heads * width, state).astype(BF16)
    out_ref[0, heads * width :, :] = conv_ref[0]
    own_ref[...] = own_pool_ref[...]


def pack(pool, conv_rows, slots, own_slots):
    _, heads, width, state = pool.shape
    count_req, rows, _ = conv_rows.shape
    block = (1, heads, width, state)
    return pl.pallas_call(
        pack_kernel,
        out_shape=[
            jax.ShapeDtypeStruct((count_req, heads * width + rows, state), BF16),
            jax.ShapeDtypeStruct((count_req, heads, width, state), F32),
        ],
        grid_spec=pltpu.PrefetchScalarGridSpec(
            num_scalar_prefetch=2,
            grid=(count_req,),
            in_specs=[
                pl.BlockSpec(block, lambda j, slots, own: (slots[j], 0, 0, 0)),
                pl.BlockSpec(block, lambda j, slots, own: (own[j], 0, 0, 0)),
                pl.BlockSpec((1, rows, state), lambda j, *_: (j, 0, 0)),
            ],
            out_specs=[
                pl.BlockSpec((1, heads * width + rows, state), lambda j, *_: (j, 0, 0)),
                pl.BlockSpec(block, lambda j, *_: (j, 0, 0, 0)),
            ],
        ),
        compiler_params=params(3 * VMEM_BYTES),
        cost_estimate=cost(0, 14 * count_req * heads * width * state),
    )(slots, own_slots, pool, pool, conv_rows)


def mixer_kernel(count_req, got_total, flags_ref, starts_ref, *refs):
    own_ref = refs[0]
    got = refs[1 : 1 + got_total]
    rest = refs[1 + got_total :]
    cache_ref, kernel_ref, bias_ref, b_ref, c_ref = rest[:5]
    cum_ref, cum_t_ref, step_t_ref, coef_ref, decay_ref, skip_ref = rest[5:11]
    held_ref = rest[11]
    states = rest[12 : 12 + got_total]
    out_ref, state_ref, scores_ref, c_part_ref, b_part_ref = rest[12 + got_total :]
    tokens, channels = own_ref.shape
    heads, width, state = held_ref.shape[1:]
    starts = [starts_ref[j] for j in range(count_req)]

    @pl.when(pl.program_id(0) == 0)
    def _():
        position, seg, _ = token_places(starts, tokens, (tokens, tokens), 0)
        other, seg_other, _ = token_places(starts, tokens, (tokens, tokens), 1)
        scores = lax.dot_general(
            c_ref[...], b_ref[...], (((1,), (1,)), ((), ())), preferred_element_type=F32
        )
        scores_ref[...] = jnp.where((seg == seg_other) & (position >= other), scores, 0.0)
        _, seg, _ = token_places(starts, tokens, (tokens, state), 0)
        b_maps = b_ref[...].astype(F32)
        c_maps = c_ref[...].astype(F32)
        for j in range(count_req):
            place = slice(j * state, (j + 1) * state)
            b_part_ref[:, place] = jnp.where(seg == j, b_maps, 0.0).astype(BF16)
            c_part_ref[:, place] = jnp.where(seg == j, c_maps, 0.0).astype(BF16)

    total = own_ref[...]
    for ref in got:
        total = total + ref[...].astype(F32)
    total = total.astype(BF16).astype(F32)
    position, seg, first = token_places(starts, tokens, (tokens, channels), 0)
    values = conv_silu(total, cache_ref, kernel_ref, bias_ref, seg, position - first)
    inputs = values.astype(BF16)
    values = inputs.astype(F32)

    lane_head = lax.broadcasted_iota(jnp.int32, (tokens, channels), 1) // width
    scores = scores_ref[...]
    cum = cum_ref[0]
    cum_t = cum_t_ref[0]
    step_t = step_t_ref[0]
    coef = coef_ref[0]
    grown = jnp.exp(cum)
    grown_wide = jnp.zeros((tokens, channels), F32)
    coef_wide = jnp.zeros((tokens, channels), F32)
    result = jnp.zeros((tokens, channels), F32)
    for h in range(heads):
        gap = jnp.minimum(cum[:, h : h + 1] - cum_t[h : h + 1, :], 0.0)
        weights = (jnp.exp(gap) * scores * step_t[h : h + 1, :]).astype(BF16)
        mine = lane_head == h
        result = result + jnp.dot(
            weights, jnp.where(mine, values, 0.0).astype(BF16), preferred_element_type=F32
        )
        grown_wide = jnp.where(mine, grown[:, h : h + 1], grown_wide)
        coef_wide = jnp.where(mine, coef[:, h : h + 1], coef_wide)

    from_state = jnp.zeros((tokens, channels), F32)
    carried = (coef_wide * values).astype(BF16)
    fresh = lax.dot_general(
        carried, b_part_ref[...], (((0,), (0,)), ((), ())), preferred_element_type=F32
    )
    for j in range(count_req):
        place = slice(j * state, (j + 1) * state)
        start = held_ref[j].reshape(channels, state) * flags_ref[j, 0].astype(F32)
        for step in range(got_total):
            start = start + states[step][j].astype(F32) * flags_ref[j, step + 1].astype(F32)
        from_state = from_state + lax.dot_general(
            c_part_ref[:, place],
            start.astype(BF16),
            (((1,), (1,)), ((), ())),
            preferred_element_type=F32,
        )
        first_head = pl.program_id(0) * heads
        for h in range(heads):
            rows = slice(h * width, (h + 1) * width)
            state_ref[j, h] = decay_ref[j, first_head + h] * start[rows] + fresh[rows, place]
    out_ref[...] = result + grown_wide * from_state + skip_ref[...] * values


def mixer(
    flags, starts, own, got, cache, kernel, bias, b_maps, c_maps, cum, cum_t, step_t, coef,
    decay, skip, held, states
):
    tokens, channels = own.shape
    count_req, heads, width, state = held.shape
    kernel_len = kernel.shape[0]
    part = min(HEADS_STEP, heads)
    steps = heads // part
    wide = part * width
    columns = lambda i, *_: (0, i)
    whole = lambda i, *_: (0, 0)

    in_specs = (
        [pl.BlockSpec((tokens, wide), columns)] * (1 + len(got))
        + [
            pl.BlockSpec((count_req, kernel_len - 1, wide), lambda i, *_: (0, 0, i)),
            pl.BlockSpec((kernel_len, wide), columns),
            pl.BlockSpec((1, wide), columns),
            pl.BlockSpec((tokens, state), whole),
            pl.BlockSpec((tokens, state), whole),
            pl.BlockSpec((1, tokens, part), lambda i, *_: (i, 0, 0)),
            pl.BlockSpec((1, part, tokens), lambda i, *_: (i, 0, 0)),
            pl.BlockSpec((1, part, tokens), lambda i, *_: (i, 0, 0)),
            pl.BlockSpec((1, tokens, part), lambda i, *_: (i, 0, 0)),
            pl.BlockSpec(memory_space=pltpu.SMEM),
            pl.BlockSpec((1, wide), columns),
        ]
        + [pl.BlockSpec((count_req, part, width, state), lambda i, *_: (0, i, 0, 0))]
        + [pl.BlockSpec((count_req, wide, state), lambda i, *_: (0, i, 0))] * len(states)
    )
    return pl.pallas_call(
        functools.partial(mixer_kernel, count_req, len(got)),
        out_shape=[
            jax.ShapeDtypeStruct((tokens, channels), F32),
            jax.ShapeDtypeStruct((count_req, heads, width, state), F32),
        ],
        grid_spec=pltpu.PrefetchScalarGridSpec(
            num_scalar_prefetch=2,
            grid=(steps,),
            in_specs=in_specs,
            out_specs=[
                pl.BlockSpec((tokens, wide), columns),
                pl.BlockSpec((count_req, part, width, state), lambda i, *_: (0, i, 0, 0)),
            ],
            scratch_shapes=[
                pltpu.VMEM((tokens, tokens), F32),
                pltpu.VMEM((tokens, count_req * state), BF16),
                pltpu.VMEM((tokens, count_req * state), BF16),
            ],
        ),
        compiler_params=params(),
        cost_estimate=cost(1e6, 1e4),
    )(
        flags, starts, own, *got, cache, kernel, bias[None], b_maps, c_maps,
        cum, cum_t, step_t, coef, decay,
        jnp.repeat(skip, width)[None], held, *states
    )


def on_device(
    x_in,
    w_xz,
    w_dt,
    w_bc,
    dt_bias,
    a_log,
    d_skip,
    conv_x_w,
    conv_x_b,
    conv_bc_w,
    conv_bc_b,
    norm_gain,
    stretch_start,
    prefix_len,
    state_slot,
    ssm_pool,
    conv_x_pool,
    conv_bc_pool,
):
    local_width = w_xz.shape[2]
    state_part = w_bc.shape[1]
    me = lax.axis_index("req")
    req_count = lax.axis_size("req")
    slot_count, heads, head_width, state = ssm_pool.shape
    group_reqs = prefix_len.shape[0]
    lags = conv_x_pool.shape[1]
    conv_width = local_width + state_part

    direct = req_count == 2 and lax.axis_size("wide") == 16
    w_pair = jnp.transpose(w_xz, (1, 0, 2))
    w_step = w_dt
    if direct:
        own_block, block = near_blocks(x_in)
        w_pair = pinned(w_pair)
        block = after(block, w_pair)
        along_z = partner_2(block, "wide", 2)
        along_x = partner_2(block, "wide", 1)
        w_step = pinned(after(w_dt, block))

    def slots_of(index):
        asked = lax.dynamic_slice_in_dim(state_slot, index * group_reqs, group_reqs)
        return jnp.clip(asked - me * slot_count, 0, slot_count - 1)

    def conv_of(slots):
        hit = slots[:, None] == jnp.arange(slot_count)[None, :]
        parts = [
            jnp.sum(jnp.where(hit[:, :, None, None], pool[None], 0), 1)
            for pool in (conv_x_pool, conv_bc_pool)
        ]
        return jnp.concatenate(parts, 2)

    conv_size = lags * conv_width
    conv_rows = -(-conv_size // (16 * state)) * 16
    own_slots = slots_of(me)
    got_states = []
    for step in range(1, req_count):
        slots = slots_of((me + step) % req_count)
        flat = conv_of(slots).reshape(group_reqs, conv_size)
        if direct:
            flat = after(flat, block)
        flat = jnp.pad(flat, ((0, 0), (0, conv_rows * state - conv_size)))
        packed, held = pack(
            ssm_pool, flat.reshape(group_reqs, conv_rows, state), slots, own_slots
        )
        got_states.append(shift_req(packed, step))

    asked = lax.dynamic_slice_in_dim(state_slot, me * group_reqs, group_reqs)
    came_from = (me - asked // slot_count) % req_count
    live = prefix_len > 0
    flags = (live[:, None] & (came_from[:, None] == jnp.arange(req_count)[None, :])).astype(
        jnp.int32
    )
    cache = conv_of(own_slots)
    for step in range(1, req_count):
        got = got_states[step - 1][:, heads * head_width :].reshape(group_reqs, -1)
        got = got[:, :conv_size].reshape(cache.shape)
        cache = jnp.where((came_from == step)[:, None, None], got, cache)
    cache = jnp.where(live[:, None, None], cache, 0).astype(F32)

    if direct:
        both = partner_2(after(along_z, packed, w_step), "wide", 1)
        own_block = after(own_block, packed)
        own_z = partner_2(own_block, "wide", 2)
        four = jnp.stack([block, along_z, along_x, both])
        other = partner_2(four, "wide", 0)
        own_pair = after(jnp.stack([own_block, own_z]), four)
        own_four = jnp.concatenate([own_pair, partner_2(own_pair, "wide", 1)], 0)
        own_other = partner_2(own_four, "wide", 0)
        features = [(own_four, own_other), quad_arrange(four, other)]
    else:
        features = features_in_general(x_in)
    weights = {
        "map": jnp.concatenate([w_bc, w_step], 1),
        "xr": w_pair[1],
        "z": w_pair[0],
    }

    def project(block, name):
        return jnp.dot(block, weights[name], preferred_element_type=F32)

    came = {"map": [], "xr": [], "z": []}
    done = []
    for step in range(1, req_count):
        block = features[step]
        for name in came:
            if name == "z":
                block = after(block, came["map"][-1])
            part, block = lax.optimization_barrier((project(block, name).astype(BF16), block))
            came[name].append(shift_req(part, step))
            done.append(part)
    block = after(features[0], *done)
    if direct:
        block = quad_arrange(*block)
    own = {}
    for name in came:
        own[name], block = lax.optimization_barrier((project(block, name), block))

    bc_conv, cum, cum_t, step_t, coef, decay = prep(
        stretch_start, own["map"], came["map"], cache[:, :, local_width:], conv_bc_w, conv_bc_b,
        dt_bias, a_log
    )
    wide_index = lax.axis_index("wide")
    group_span = lax.axis_size("wide") // GROUPS
    bit_total = group_span.bit_length() - 1
    joined = bc_conv
    for bit_index in range(bit_total):
        partner = partner_2(joined, "wide", bit_index)
        upper_half = wide_index // (1 << bit_index) % 2 == 1
        joined = jnp.where(
            upper_half, jnp.concatenate([partner, joined], 1), jnp.concatenate([joined, partner], 1)
        )
    state_width = joined.shape[1] // 2
    result, final_state = mixer(
        flags, stretch_start[0], own["xr"], came["xr"], cache[:, :, :local_width],
        conv_x_w, conv_x_b, joined[:, :state_width], joined[:, state_width:], cum, cum_t,
        step_t, coef, decay, d_skip, held, got_states
    )
    gate = own["z"]
    for got in came["z"]:
        gate = gate + got.astype(F32)
    gated = result * jax.nn.silu(gate.astype(BF16).astype(F32))
    square_sum = jnp.sum(gated * gated, 1)
    for bit_index in range(bit_total):
        square_sum = square_sum + partner_2(square_sum, "wide", bit_index)
    mean_sq = square_sum / (local_width * group_span)
    normed = gated * lax.rsqrt(mean_sq + NORM_EPS)[:, None] * norm_gain[None, :]
    return (normed.astype(BF16), final_state)


def solution(mesh):
    in_specs = (
        P("req", "wide"),
        P("req", None, "wide"),
        P("req", "wide"),
        P("req", "wide"),
        P("wide"),
        P("wide"),
        P("wide"),
        P(None, "wide"),
        P("wide"),
        P(None, "wide"),
        P("wide"),
        P("wide"),
        P("req", None),
        P("req"),
        P(),
        P("req", "wide", None, None),
        P("req", None, "wide"),
        P("req", None, "wide"),
    )
    out_specs = (P("req", "wide"), P("req", "wide", None, None))
    return jax.shard_map(
        on_device, mesh=mesh, in_specs=in_specs, out_specs=out_specs, check_vma=False
    )
```

```python
import functools

import jax
import jax.numpy as jnp
from jax import lax
from jax.experimental import pallas as pl
from jax.experimental.layout import Layout, with_layout_constraint
from jax.experimental.pallas import tpu as pltpu
from jax.sharding import PartitionSpec as P

GROUPS = 8
NORM_EPS = 1e-05
F32 = jnp.float32
BF16 = jnp.bfloat16
HIGH = lax.Precision.HIGHEST
VMEM_BYTES = 16 * 1024 * 1024
HEADS_STEP = 4


def cost(flops, bytes_accessed):
    return pl.CostEstimate(flops=int(flops), bytes_accessed=int(bytes_accessed), transcendentals=0)


def params(limit=VMEM_BYTES):
    return pltpu.CompilerParams(vmem_limit_bytes=limit)


def partner_2(block, axis, bit):
    count = lax.axis_size(axis)
    route = []
    for low in range(count):
        high = low | 1 << bit
        if high != low and high < count:
            route += [(low, high), (high, low)]
    return lax.ppermute(block, axis, route)


def shift_req(block, step):
    count = lax.axis_size("req")
    return lax.ppermute(block, "req", [(i, (i + step) % count) for i in range(count)])


def spread_routes():
    first, second = [], []
    for z in range(4):
        for rest in range(4):
            for r in range(2):
                place = (z * 4 + rest) * 2 + r
                other = (((z + 2) % 4) * 4 + rest) * 2 + r
                if z // 2 == r:
                    first.append((place, other))
                else:
                    first.append((place, place ^ 1))
                    second.append((place, other ^ 1))
    return first, second


def arrange_kernel(places_ref, *refs):
    out_ref = refs[-1]
    index = 0
    for ref in refs[:-1]:
        for part in range(ref.shape[0]):
            width = ref.shape[2]
            place = pl.multiple_of(places_ref[index] * width, width)
            out_ref[:, pl.ds(place, width)] = ref[part]
            index += 1


def arrange(stacks, places):
    tokens, width = stacks[0].shape[1:]
    total = sum(stack.shape[0] for stack in stacks) * width
    return pl.pallas_call(
        arrange_kernel,
        out_shape=jax.ShapeDtypeStruct((tokens, total), stacks[0].dtype),
        in_specs=[pl.BlockSpec(memory_space=pltpu.SMEM)]
        + [pl.BlockSpec(memory_space=pltpu.VMEM)] * len(stacks),
        out_specs=pl.BlockSpec(memory_space=pltpu.VMEM),
        compiler_params=params(),
        cost_estimate=cost(1e6, 1e4),
    )(places, *stacks)


def after(value, *others):
    return lax.optimization_barrier((value, others))[0]


def near_blocks(x_in):
    axes = ("wide", "req")
    first, second = spread_routes()
    first = lax.ppermute(x_in, axes, first)
    second = lax.ppermute(x_in, axes, second)
    near = lax.axis_index("wide") // 8 == lax.axis_index("req")
    return jnp.where(near, x_in, first), jnp.where(near, first, second)


def quad_arrange(four, other):
    apart = jnp.array([0, 4, 2, 6, 1, 5, 3, 7], jnp.int32)
    return arrange([four, other], (lax.axis_index("wide") % 8) ^ apart)


def features_in_general(x_in):
    req_count = lax.axis_size("req")
    me = lax.axis_index("req")
    own = lax.all_gather(x_in, "wide", axis=1, tiled=True)
    parts = own.reshape(own.shape[0], req_count, own.shape[1] // req_count).transpose(1, 0, 2)
    got = lax.all_to_all(parts, "req", split_axis=0, concat_axis=0, tiled=True)
    return [
        lax.dynamic_index_in_dim(got, (me + step) % req_count, 0, False)
        for step in range(req_count)
    ]


def pinned(array):
    return lax.optimization_barrier(
        with_layout_constraint(array, Layout(tuple(range(array.ndim))))
    )


def token_places(starts, count_tok, shape, axis):
    position = lax.broadcasted_iota(jnp.int32, shape, axis)
    seg = jnp.full(shape, -1, jnp.int32)
    first = jnp.zeros(shape, jnp.int32)
    for start in starts:
        seg = seg + (position >= start).astype(jnp.int32)
        first = jnp.where(position >= start, start, first)
    return position, seg, first


def conv_silu(values, cache_ref, kernel_ref, bias_ref, seg, offset):
    kernel_len = kernel_ref.shape[0]
    taps = [kernel_ref[k : k + 1, :] for k in range(kernel_len)]
    total = bias_ref[...] + taps[kernel_len - 1] * values
    for lag in range(1, kernel_len):
        earlier = pltpu.roll(values, lag, 0)
        total = total + taps[kernel_len - 1 - lag] * jnp.where(offset >= lag, earlier, 0.0)
    cached = jnp.zeros_like(values)
    for request in range(cache_ref.shape[0]):
        for place in range(kernel_len - 1):
            history = jnp.zeros_like(bias_ref[...])
            for lag in range(place + 1, kernel_len):
                at = kernel_len - 1 + place - lag
                history = history + taps[kernel_len - 1 - lag] * cache_ref[request, at : at + 1, :]
            cached = jnp.where((seg == request) & (offset == place), history, cached)
    total = total + cached
    return total * jax.nn.sigmoid(total)


def prep_kernel(
    count_req, got_total, starts_ref, own_ref, *refs
):
    got = refs[:got_total]
    cache_ref, kernel_ref, bias_ref, dt_bias_ref, a_log_ref = refs[got_total : got_total + 5]
    bc_ref, cum_ref, cum_t_ref, step_t_ref, coef_ref, decay_ref = refs[got_total + 5 :]
    tokens = own_ref.shape[0]
    channels = bias_ref.shape[1]
    heads = dt_bias_ref.shape[1]
    starts = [starts_ref[0, j] for j in range(count_req)]
    total = own_ref[...]
    for ref in got:
        total = total + ref[...].astype(F32)
    total = total.astype(BF16).astype(F32)
    position, seg, first = token_places(starts, tokens, (tokens, channels), 0)
    bc = conv_silu(total[:, :channels], cache_ref, kernel_ref, bias_ref, seg, position - first)
    bc_ref[...] = bc.astype(BF16)
    raw = total[:, channels : channels + heads] + dt_bias_ref[...]
    step = jnp.maximum(raw, 0.0) + jnp.log1p(jnp.exp(-jnp.abs(raw)))
    rate = step * (-jnp.exp(a_log_ref[...]))
    position, seg, first = token_places(starts, tokens, (tokens, tokens), 0)
    other, seg_other, first_other = token_places(starts, tokens, (tokens, tokens), 1)
    same = seg == seg_other
    mask = jnp.where(same & (position >= other), 1.0, 0.0)
    after = jnp.where(same & (position < other), 1.0, 0.0)
    cum = jnp.dot(mask, rate, precision=HIGH, preferred_element_type=F32)
    left = jnp.dot(after, rate, precision=HIGH, preferred_element_type=F32)
    cum_t = lax.dot_general(
        rate, mask, (((0,), (1,)), ((), ())), precision=HIGH, preferred_element_type=F32
    )
    step_t = step.T
    coef = jnp.exp(left) * step
    part = cum_ref.shape[2]
    for i in range(cum_ref.shape[0]):
        place = slice(i * part, (i + 1) * part)
        cum_ref[i] = cum[:, place]
        cum_t_ref[i] = cum_t[place, :]
        step_t_ref[i] = step_t[place, :]
        coef_ref[i] = coef[:, place]
    at, seg_at, _ = token_places(starts, tokens, (8, tokens), 1)
    row = lax.broadcasted_iota(jnp.int32, (8, tokens), 0)
    ends = jnp.dot(
        jnp.where(seg_at == row, 1.0, 0.0), rate, precision=HIGH, preferred_element_type=F32
    )
    decay_ref[...] = jnp.exp(ends)


def prep(starts, own, got, cache, kernel, bias, dt_bias, a_log):
    tokens = own.shape[0]
    channels = bias.shape[0]
    heads = dt_bias.shape[0]
    count_req = cache.shape[0]
    vmem = pl.BlockSpec(memory_space=pltpu.VMEM)
    part = min(HEADS_STEP, heads)
    tall = jax.ShapeDtypeStruct((heads // part, tokens, part), F32)
    flat = jax.ShapeDtypeStruct((heads // part, part, tokens), F32)
    return pl.pallas_call(
        functools.partial(prep_kernel, count_req, len(got)),
        out_shape=[
            jax.ShapeDtypeStruct((tokens, channels), BF16),
            tall,
            flat,
            flat,
            tall,
            jax.ShapeDtypeStruct((8, heads), F32),
        ],
        in_specs=[pl.BlockSpec(memory_space=pltpu.SMEM)] + [vmem] * (6 + len(got)),
        out_specs=[vmem] * 6,
        compiler_params=params(),
        cost_estimate=cost(1e6, 1e4),
    )(starts, own, *got, cache, kernel, bias[None], dt_bias[None], a_log[None])


def pack_kernel(slots_ref, own_slots_ref, pool_ref, own_pool_ref, conv_ref, out_ref, own_ref):
    heads, width, state = pool_ref.shape[1:]
    out_ref[0, : heads * width, :] = pool_ref[0].reshape(heads * width, state).astype(BF16)
    out_ref[0, heads * width :, :] = conv_ref[0]
    own_ref[...] = own_pool_ref[...]


def pack(pool, conv_rows, slots, own_slots):
    _, heads, width, state = pool.shape
    count_req, rows, _ = conv_rows.shape
    block = (1, heads, width, state)
    return pl.pallas_call(
        pack_kernel,
        out_shape=[
            jax.ShapeDtypeStruct((count_req, heads * width + rows, state), BF16),
            jax.ShapeDtypeStruct((count_req, heads, width, state), F32),
        ],
        grid_spec=pltpu.PrefetchScalarGridSpec(
            num_scalar_prefetch=2,
            grid=(count_req,),
            in_specs=[
                pl.BlockSpec(block, lambda j, slots, own: (slots[j], 0, 0, 0)),
                pl.BlockSpec(block, lambda j, slots, own: (own[j], 0, 0, 0)),
                pl.BlockSpec((1, rows, state), lambda j, *_: (j, 0, 0)),
            ],
            out_specs=[
                pl.BlockSpec((1, heads * width + rows, state), lambda j, *_: (j, 0, 0)),
                pl.BlockSpec(block, lambda j, *_: (j, 0, 0, 0)),
            ],
        ),
        compiler_params=params(3 * VMEM_BYTES),
        cost_estimate=cost(0, 14 * count_req * heads * width * state),
    )(slots, own_slots, pool, pool, conv_rows)


def mixer_kernel(count_req, got_total, flags_ref, starts_ref, *refs):
    own_ref = refs[0]
    got = refs[1 : 1 + got_total]
    rest = refs[1 + got_total :]
    cache_ref, kernel_ref, bias_ref, b_ref, c_ref = rest[:5]
    cum_ref, cum_t_ref, step_t_ref, coef_ref, decay_ref, skip_ref = rest[5:11]
    held_ref = rest[11]
    states = rest[12 : 12 + got_total]
    out_ref, state_ref, scores_ref, c_part_ref, b_part_ref = rest[12 + got_total :]
    tokens, channels = own_ref.shape
    heads, width, state = held_ref.shape[1:]
    starts = [starts_ref[j] for j in range(count_req)]

    @pl.when(pl.program_id(0) == 0)
    def _():
        position, seg, _ = token_places(starts, tokens, (tokens, tokens), 0)
        other, seg_other, _ = token_places(starts, tokens, (tokens, tokens), 1)
        scores = lax.dot_general(
            c_ref[...], b_ref[...], (((1,), (1,)), ((), ())), preferred_element_type=F32
        )
        scores_ref[...] = jnp.where((seg == seg_other) & (position >= other), scores, 0.0)
        _, seg, _ = token_places(starts, tokens, (tokens, state), 0)
        b_maps = b_ref[...].astype(F32)
        c_maps = c_ref[...].astype(F32)
        for j in range(count_req):
            place = slice(j * state, (j + 1) * state)
            b_part_ref[:, place] = jnp.where(seg == j, b_maps, 0.0).astype(BF16)
            c_part_ref[:, place] = jnp.where(seg == j, c_maps, 0.0).astype(BF16)

    total = own_ref[...]
    for ref in got:
        total = total + ref[...].astype(F32)
    total = total.astype(BF16).astype(F32)
    position, seg, first = token_places(starts, tokens, (tokens, channels), 0)
    values = conv_silu(total, cache_ref, kernel_ref, bias_ref, seg, position - first)
    inputs = values.astype(BF16)
    values = inputs.astype(F32)

    lane_head = lax.broadcasted_iota(jnp.int32, (tokens, channels), 1) // width
    scores = scores_ref[...]
    cum = cum_ref[0]
    cum_t = cum_t_ref[0]
    step_t = step_t_ref[0]
    coef = coef_ref[0]
    grown = jnp.exp(cum)
    grown_wide = jnp.zeros((tokens, channels), F32)
    coef_wide = jnp.zeros((tokens, channels), F32)
    result = jnp.zeros((tokens, channels), F32)
    for h in range(heads):
        gap = jnp.minimum(cum[:, h : h + 1] - cum_t[h : h + 1, :], 0.0)
        weights = (jnp.exp(gap) * scores * step_t[h : h + 1, :]).astype(BF16)
        mine = lane_head == h
        result = result + jnp.dot(
            weights, jnp.where(mine, values, 0.0).astype(BF16), preferred_element_type=F32
        )
        grown_wide = jnp.where(mine, grown[:, h : h + 1], grown_wide)
        coef_wide = jnp.where(mine, coef[:, h : h + 1], coef_wide)

    from_state = jnp.zeros((tokens, channels), F32)
    carried = (coef_wide * values).astype(BF16)
    fresh = lax.dot_general(
        carried, b_part_ref[...], (((0,), (0,)), ((), ())), preferred_element_type=F32
    )
    for j in range(count_req):
        place = slice(j * state, (j + 1) * state)
        start = held_ref[j].reshape(channels, state) * flags_ref[j, 0].astype(F32)
        for step in range(got_total):
            start = start + states[step][j].astype(F32) * flags_ref[j, step + 1].astype(F32)
        from_state = from_state + lax.dot_general(
            c_part_ref[:, place],
            start.astype(BF16),
            (((1,), (1,)), ((), ())),
            preferred_element_type=F32,
        )
        first_head = pl.program_id(0) * heads
        for h in range(heads):
            rows = slice(h * width, (h + 1) * width)
            state_ref[j, h] = decay_ref[j, first_head + h] * start[rows] + fresh[rows, place]
    out_ref[...] = result + grown_wide * from_state + skip_ref[...] * values


def mixer(
    flags, starts, own, got, cache, kernel, bias, b_maps, c_maps, cum, cum_t, step_t, coef,
    decay, skip, held, states
):
    tokens, channels = own.shape
    count_req, heads, width, state = held.shape
    kernel_len = kernel.shape[0]
    part = min(HEADS_STEP, heads)
    steps = heads // part
    wide = part * width
    columns = lambda i, *_: (0, i)
    whole = lambda i, *_: (0, 0)

    in_specs = (
        [pl.BlockSpec((tokens, wide), columns)] * (1 + len(got))
        + [
            pl.BlockSpec((count_req, kernel_len - 1, wide), lambda i, *_: (0, 0, i)),
            pl.BlockSpec((kernel_len, wide), columns),
            pl.BlockSpec((1, wide), columns),
            pl.BlockSpec((tokens, state), whole),
            pl.BlockSpec((tokens, state), whole),
            pl.BlockSpec((1, tokens, part), lambda i, *_: (i, 0, 0)),
            pl.BlockSpec((1, part, tokens), lambda i, *_: (i, 0, 0)),
            pl.BlockSpec((1, part, tokens), lambda i, *_: (i, 0, 0)),
            pl.BlockSpec((1, tokens, part), lambda i, *_: (i, 0, 0)),
            pl.BlockSpec(memory_space=pltpu.SMEM),
            pl.BlockSpec((1, wide), columns),
        ]
        + [pl.BlockSpec((count_req, part, width, state), lambda i, *_: (0, i, 0, 0))]
        + [pl.BlockSpec((count_req, wide, state), lambda i, *_: (0, i, 0))] * len(states)
    )
    return pl.pallas_call(
        functools.partial(mixer_kernel, count_req, len(got)),
        out_shape=[
            jax.ShapeDtypeStruct((tokens, channels), F32),
            jax.ShapeDtypeStruct((count_req, heads, width, state), F32),
        ],
        grid_spec=pltpu.PrefetchScalarGridSpec(
            num_scalar_prefetch=2,
            grid=(steps,),
            in_specs=in_specs,
            out_specs=[
                pl.BlockSpec((tokens, wide), columns),
                pl.BlockSpec((count_req, part, width, state), lambda i, *_: (0, i, 0, 0)),
            ],
            scratch_shapes=[
                pltpu.VMEM((tokens, tokens), F32),
                pltpu.VMEM((tokens, count_req * state), BF16),
                pltpu.VMEM((tokens, count_req * state), BF16),
            ],
        ),
        compiler_params=params(),
        cost_estimate=cost(1e6, 1e4),
    )(
        flags, starts, own, *got, cache, kernel, bias[None], b_maps, c_maps,
        cum, cum_t, step_t, coef, decay,
        jnp.repeat(skip, width)[None], held, *states
    )


def on_device(
    x_in,
    w_xz,
    w_dt,
    w_bc,
    dt_bias,
    a_log,
    d_skip,
    conv_x_w,
    conv_x_b,
    conv_bc_w,
    conv_bc_b,
    norm_gain,
    stretch_start,
    prefix_len,
    state_slot,
    ssm_pool,
    conv_x_pool,
    conv_bc_pool,
):
    local_width = w_xz.shape[2]
    state_part = w_bc.shape[1]
    me = lax.axis_index("req")
    req_count = lax.axis_size("req")
    slot_count, heads, head_width, state = ssm_pool.shape
    group_reqs = prefix_len.shape[0]
    lags = conv_x_pool.shape[1]
    conv_width = local_width + state_part

    direct = req_count == 2 and lax.axis_size("wide") == 16
    w_pair = jnp.transpose(w_xz, (1, 0, 2))
    w_step = w_dt
    if direct:
        own_block, block = near_blocks(x_in)
        w_pair = pinned(w_pair)
        block = after(block, w_pair)
        along_z = partner_2(block, "wide", 2)
        along_x = partner_2(block, "wide", 1)
        w_step = pinned(after(w_dt, block))

    def slots_of(index):
        asked = lax.dynamic_slice_in_dim(state_slot, index * group_reqs, group_reqs)
        return jnp.clip(asked - me * slot_count, 0, slot_count - 1)

    def conv_of(slots):
        hit = slots[:, None] == jnp.arange(slot_count)[None, :]
        parts = [
            jnp.sum(jnp.where(hit[:, :, None, None], pool[None], 0), 1)
            for pool in (conv_x_pool, conv_bc_pool)
        ]
        return jnp.concatenate(parts, 2)

    conv_size = lags * conv_width
    conv_rows = -(-conv_size // (16 * state)) * 16
    own_slots = slots_of(me)
    got_states = []
    for step in range(1, req_count):
        slots = slots_of((me + step) % req_count)
        flat = conv_of(slots).reshape(group_reqs, conv_size)
        if direct:
            flat = after(flat, block)
        flat = jnp.pad(flat, ((0, 0), (0, conv_rows * state - conv_size)))
        packed, held = pack(
            ssm_pool, flat.reshape(group_reqs, conv_rows, state), slots, own_slots
        )
        got_states.append(shift_req(packed, step))

    asked = lax.dynamic_slice_in_dim(state_slot, me * group_reqs, group_reqs)
    came_from = (me - asked // slot_count) % req_count
    live = prefix_len > 0
    flags = (live[:, None] & (came_from[:, None] == jnp.arange(req_count)[None, :])).astype(
        jnp.int32
    )
    if direct:
        both = partner_2(after(along_z, packed, w_step), "wide", 1)
        own_block = after(own_block, packed)
        own_z = partner_2(own_block, "wide", 2)
        four = jnp.stack([block, along_z, along_x, both])
        other = partner_2(four, "wide", 0)
        own_pair = after(jnp.stack([own_block, own_z]), four)
        own_got = partner_2(own_pair, "wide", 1)
        features = [own_got, quad_arrange(four, other)]
    else:
        features = features_in_general(x_in)
    weights = {
        "map": jnp.concatenate([w_bc, w_step], 1),
        "xr": w_pair[1],
        "z": w_pair[0],
    }

    def project(block, name):
        return jnp.dot(block, weights[name], preferred_element_type=F32)

    came = {"map": [], "xr": [], "z": []}
    done, parts = [], {}
    for step in range(1, req_count):
        block = features[step]
        for name in came:
            if name == "z":
                block = after(block, came["map"][-1], got_states[step - 1])
            part, block = lax.optimization_barrier((project(block, name).astype(BF16), block))
            came[name].append(shift_req(part, step))
            parts[name] = part
            done.append(part)
    block = features[0]
    if direct:
        own_four = jnp.concatenate([own_pair, after(block, parts["xr"])], 0)
        own_other = partner_2(own_four, "wide", 0)
        block = quad_arrange(own_four, after(own_other, *done))
    else:
        block = after(block, *done)
    own = {}
    for name in came:
        own[name], block = lax.optimization_barrier((project(block, name), block))

    cache = conv_of(own_slots)
    for step in range(1, req_count):
        got = after(got_states[step - 1], parts["xr"])[:, heads * head_width :].reshape(group_reqs, -1)
        got = got[:, :conv_size].reshape(cache.shape)
        cache = jnp.where((came_from == step)[:, None, None], got, cache)
    cache = jnp.where(live[:, None, None], cache, 0).astype(F32)

    bc_conv, cum, cum_t, step_t, coef, decay = prep(
        stretch_start, own["map"], came["map"], cache[:, :, local_width:], conv_bc_w, conv_bc_b,
        dt_bias, a_log
    )
    wide_index = lax.axis_index("wide")
    group_span = lax.axis_size("wide") // GROUPS
    bit_total = group_span.bit_length() - 1
    joined = bc_conv
    for bit_index in range(bit_total):
        partner = partner_2(joined, "wide", bit_index)
        upper_half = wide_index // (1 << bit_index) % 2 == 1
        joined = jnp.where(
            upper_half, jnp.concatenate([partner, joined], 1), jnp.concatenate([joined, partner], 1)
        )
    state_width = joined.shape[1] // 2
    came_xr = [after(got, own["xr"], bc_conv) for got in came["xr"]]
    result, final_state = mixer(
        flags, stretch_start[0], own["xr"], came_xr, cache[:, :, :local_width],
        conv_x_w, conv_x_b, joined[:, :state_width], joined[:, state_width:], cum, cum_t,
        step_t, coef, decay, d_skip, held, got_states
    )
    gate = own["z"]
    for got in came["z"]:
        gate = gate + got.astype(F32)
    gated = result * jax.nn.silu(gate.astype(BF16).astype(F32))
    square_sum = jnp.sum(gated * gated, 1)
    for bit_index in range(bit_total):
        square_sum = square_sum + partner_2(square_sum, "wide", bit_index)
    mean_sq = square_sum / (local_width * group_span)
    normed = gated * lax.rsqrt(mean_sq + NORM_EPS)[:, None] * norm_gain[None, :]
    return (normed.astype(BF16), final_state)


def solution(mesh):
    in_specs = (
        P("req", "wide"),
        P("req", None, "wide"),
        P("req", "wide"),
        P("req", "wide"),
        P("wide"),
        P("wide"),
        P("wide"),
        P(None, "wide"),
        P("wide"),
        P(None, "wide"),
        P("wide"),
        P("wide"),
        P("req", None),
        P("req"),
        P(),
        P("req", "wide", None, None),
        P("req", None, "wide"),
        P("req", None, "wide"),
    )
    out_specs = (P("req", "wide"), P("req", "wide", None, None))
    return jax.shard_map(
        on_device, mesh=mesh, in_specs=in_specs, out_specs=out_specs, check_vma=False
    )
```

```python
import functools

import jax
import jax.numpy as jnp
from jax import lax
from jax.experimental import pallas as pl
from jax.experimental.layout import Layout, with_layout_constraint
from jax.experimental.pallas import tpu as pltpu
from jax.sharding import PartitionSpec as P

GROUPS = 8
NORM_EPS = 1e-05
F32 = jnp.float32
BF16 = jnp.bfloat16
HIGH = lax.Precision.HIGHEST
VMEM_BYTES = 16 * 1024 * 1024
HEADS_STEP = 4


def cost(flops, bytes_accessed):
    return pl.CostEstimate(flops=int(flops), bytes_accessed=int(bytes_accessed), transcendentals=0)


def params(limit=VMEM_BYTES):
    return pltpu.CompilerParams(vmem_limit_bytes=limit)


def partner_2(block, axis, bit):
    count = lax.axis_size(axis)
    route = []
    for low in range(count):
        high = low | 1 << bit
        if high != low and high < count:
            route += [(low, high), (high, low)]
    return lax.ppermute(block, axis, route)


def shift_req(block, step):
    count = lax.axis_size("req")
    return lax.ppermute(block, "req", [(i, (i + step) % count) for i in range(count)])


def spread_routes():
    first, second = [], []
    for z in range(4):
        for rest in range(4):
            for r in range(2):
                place = (z * 4 + rest) * 2 + r
                other = (((z + 2) % 4) * 4 + rest) * 2 + r
                if z // 2 == r:
                    first.append((place, other))
                else:
                    first.append((place, place ^ 1))
                    second.append((place, other ^ 1))
    return first, second


def arrange_kernel(places_ref, *refs):
    out_ref = refs[-1]
    index = 0
    for ref in refs[:-1]:
        for part in range(ref.shape[0]):
            width = ref.shape[2]
            place = pl.multiple_of(places_ref[index] * width, width)
            out_ref[:, pl.ds(place, width)] = ref[part]
            index += 1


def arrange(stacks, places):
    tokens, width = stacks[0].shape[1:]
    total = sum(stack.shape[0] for stack in stacks) * width
    return pl.pallas_call(
        arrange_kernel,
        out_shape=jax.ShapeDtypeStruct((tokens, total), stacks[0].dtype),
        in_specs=[pl.BlockSpec(memory_space=pltpu.SMEM)]
        + [pl.BlockSpec(memory_space=pltpu.VMEM)] * len(stacks),
        out_specs=pl.BlockSpec(memory_space=pltpu.VMEM),
        compiler_params=params(),
        cost_estimate=cost(1e6, 1e4),
    )(places, *stacks)


def after(value, *others):
    return lax.optimization_barrier((value, others))[0]


def near_blocks(x_in):
    axes = ("wide", "req")
    first, second = spread_routes()
    first = lax.ppermute(x_in, axes, first)
    second = lax.ppermute(x_in, axes, second)
    near = lax.axis_index("wide") // 8 == lax.axis_index("req")
    return jnp.where(near, x_in, first), jnp.where(near, first, second)


def quad_arrange(four, other):
    apart = jnp.array([0, 4, 2, 6, 1, 5, 3, 7], jnp.int32)
    return arrange([four, other], (lax.axis_index("wide") % 8) ^ apart)


def features_in_general(x_in):
    req_count = lax.axis_size("req")
    me = lax.axis_index("req")
    own = lax.all_gather(x_in, "wide", axis=1, tiled=True)
    parts = own.reshape(own.shape[0], req_count, own.shape[1] // req_count).transpose(1, 0, 2)
    got = lax.all_to_all(parts, "req", split_axis=0, concat_axis=0, tiled=True)
    return [
        lax.dynamic_index_in_dim(got, (me + step) % req_count, 0, False)
        for step in range(req_count)
    ]


def pinned(array):
    return lax.optimization_barrier(
        with_layout_constraint(array, Layout(tuple(range(array.ndim))))
    )


def token_places(starts, count_tok, shape, axis):
    position = lax.broadcasted_iota(jnp.int32, shape, axis)
    seg = jnp.full(shape, -1, jnp.int32)
    first = jnp.zeros(shape, jnp.int32)
    for start in starts:
        seg = seg + (position >= start).astype(jnp.int32)
        first = jnp.where(position >= start, start, first)
    return position, seg, first


def conv_silu(values, cache_ref, kernel_ref, bias_ref, seg, offset):
    kernel_len = kernel_ref.shape[0]
    taps = [kernel_ref[k : k + 1, :] for k in range(kernel_len)]
    total = bias_ref[...] + taps[kernel_len - 1] * values
    for lag in range(1, kernel_len):
        earlier = pltpu.roll(values, lag, 0)
        total = total + taps[kernel_len - 1 - lag] * jnp.where(offset >= lag, earlier, 0.0)
    cached = jnp.zeros_like(values)
    for request in range(cache_ref.shape[0]):
        for place in range(kernel_len - 1):
            history = jnp.zeros_like(bias_ref[...])
            for lag in range(place + 1, kernel_len):
                at = kernel_len - 1 + place - lag
                history = history + taps[kernel_len - 1 - lag] * cache_ref[request, at : at + 1, :]
            cached = jnp.where((seg == request) & (offset == place), history, cached)
    total = total + cached
    return total * jax.nn.sigmoid(total)


def prep_kernel(
    count_req, got_total, starts_ref, own_ref, *refs
):
    got = refs[:got_total]
    cache_ref, kernel_ref, bias_ref, dt_bias_ref, a_log_ref = refs[got_total : got_total + 5]
    bc_ref, cum_ref, cum_t_ref, step_t_ref, coef_ref, decay_ref = refs[got_total + 5 :]
    tokens = own_ref.shape[0]
    channels = bias_ref.shape[1]
    heads = dt_bias_ref.shape[1]
    starts = [starts_ref[0, j] for j in range(count_req)]
    total = own_ref[...]
    for ref in got:
        total = total + ref[...].astype(F32)
    total = total.astype(BF16).astype(F32)
    position, seg, first = token_places(starts, tokens, (tokens, channels), 0)
    bc = conv_silu(total[:, :channels], cache_ref, kernel_ref, bias_ref, seg, position - first)
    bc_ref[...] = bc.astype(BF16)
    raw = total[:, channels : channels + heads] + dt_bias_ref[...]
    step = jnp.maximum(raw, 0.0) + jnp.log1p(jnp.exp(-jnp.abs(raw)))
    rate = step * (-jnp.exp(a_log_ref[...]))
    position, seg, first = token_places(starts, tokens, (tokens, tokens), 0)
    other, seg_other, first_other = token_places(starts, tokens, (tokens, tokens), 1)
    same = seg == seg_other
    mask = jnp.where(same & (position >= other), 1.0, 0.0)
    after = jnp.where(same & (position < other), 1.0, 0.0)
    cum = jnp.dot(mask, rate, precision=HIGH, preferred_element_type=F32)
    left = jnp.dot(after, rate, precision=HIGH, preferred_element_type=F32)
    cum_t = lax.dot_general(
        rate, mask, (((0,), (1,)), ((), ())), precision=HIGH, preferred_element_type=F32
    )
    step_t = step.T
    coef = jnp.exp(left) * step
    part = cum_ref.shape[2]
    for i in range(cum_ref.shape[0]):
        place = slice(i * part, (i + 1) * part)
        cum_ref[i] = cum[:, place]
        cum_t_ref[i] = cum_t[place, :]
        step_t_ref[i] = step_t[place, :]
        coef_ref[i] = coef[:, place]
    at, seg_at, _ = token_places(starts, tokens, (8, tokens), 1)
    row = lax.broadcasted_iota(jnp.int32, (8, tokens), 0)
    ends = jnp.dot(
        jnp.where(seg_at == row, 1.0, 0.0), rate, precision=HIGH, preferred_element_type=F32
    )
    decay_ref[...] = jnp.exp(ends)


def prep(starts, own, got, cache, kernel, bias, dt_bias, a_log):
    tokens = own.shape[0]
    channels = bias.shape[0]
    heads = dt_bias.shape[0]
    count_req = cache.shape[0]
    vmem = pl.BlockSpec(memory_space=pltpu.VMEM)
    part = min(HEADS_STEP, heads)
    tall = jax.ShapeDtypeStruct((heads // part, tokens, part), F32)
    flat = jax.ShapeDtypeStruct((heads // part, part, tokens), F32)
    return pl.pallas_call(
        functools.partial(prep_kernel, count_req, len(got)),
        out_shape=[
            jax.ShapeDtypeStruct((tokens, channels), BF16),
            tall,
            flat,
            flat,
            tall,
            jax.ShapeDtypeStruct((8, heads), F32),
        ],
        in_specs=[pl.BlockSpec(memory_space=pltpu.SMEM)] + [vmem] * (6 + len(got)),
        out_specs=[vmem] * 6,
        compiler_params=params(),
        cost_estimate=cost(1e6, 1e4),
    )(starts, own, *got, cache, kernel, bias[None], dt_bias[None], a_log[None])


def pack_kernel(slots_ref, own_slots_ref, pool_ref, own_pool_ref, conv_ref, out_ref, own_ref):
    heads, width, state = pool_ref.shape[1:]
    out_ref[0, : heads * width, :] = pool_ref[0].reshape(heads * width, state).astype(BF16)
    out_ref[0, heads * width :, :] = conv_ref[0]
    own_ref[...] = own_pool_ref[...]


def pack(pool, conv_rows, slots, own_slots):
    _, heads, width, state = pool.shape
    count_req, rows, _ = conv_rows.shape
    block = (1, heads, width, state)
    return pl.pallas_call(
        pack_kernel,
        out_shape=[
            jax.ShapeDtypeStruct((count_req, heads * width + rows, state), BF16),
            jax.ShapeDtypeStruct((count_req, heads, width, state), F32),
        ],
        grid_spec=pltpu.PrefetchScalarGridSpec(
            num_scalar_prefetch=2,
            grid=(count_req,),
            in_specs=[
                pl.BlockSpec(block, lambda j, slots, own: (slots[j], 0, 0, 0)),
                pl.BlockSpec(block, lambda j, slots, own: (own[j], 0, 0, 0)),
                pl.BlockSpec((1, rows, state), lambda j, *_: (j, 0, 0)),
            ],
            out_specs=[
                pl.BlockSpec((1, heads * width + rows, state), lambda j, *_: (j, 0, 0)),
                pl.BlockSpec(block, lambda j, *_: (j, 0, 0, 0)),
            ],
        ),
        compiler_params=params(12 * 1024 * 1024),
        cost_estimate=cost(0, 14 * count_req * heads * width * state),
    )(slots, own_slots, pool, pool, conv_rows)


def mixer_kernel(count_req, got_total, flags_ref, starts_ref, *refs):
    own_ref = refs[0]
    got = refs[1 : 1 + got_total]
    rest = refs[1 + got_total :]
    cache_ref, kernel_ref, bias_ref, b_ref, c_ref = rest[:5]
    cum_ref, cum_t_ref, step_t_ref, coef_ref, decay_ref, skip_ref = rest[5:11]
    held_ref = rest[11]
    states = rest[12 : 12 + got_total]
    out_ref, state_ref, scores_ref, c_part_ref, b_part_ref = rest[12 + got_total :]
    tokens, channels = own_ref.shape
    heads, width, state = held_ref.shape[1:]
    starts = [starts_ref[j] for j in range(count_req)]

    @pl.when(pl.program_id(0) == 0)
    def _():
        position, seg, _ = token_places(starts, tokens, (tokens, tokens), 0)
        other, seg_other, _ = token_places(starts, tokens, (tokens, tokens), 1)
        scores = lax.dot_general(
            c_ref[...], b_ref[...], (((1,), (1,)), ((), ())), preferred_element_type=F32
        )
        scores_ref[...] = jnp.where((seg == seg_other) & (position >= other), scores, 0.0)
        _, seg, _ = token_places(starts, tokens, (tokens, state), 0)
        b_maps = b_ref[...].astype(F32)
        c_maps = c_ref[...].astype(F32)
        for j in range(count_req):
            place = slice(j * state, (j + 1) * state)
            b_part_ref[:, place] = jnp.where(seg == j, b_maps, 0.0).astype(BF16)
            c_part_ref[:, place] = jnp.where(seg == j, c_maps, 0.0).astype(BF16)

    total = own_ref[...]
    for ref in got:
        total = total + ref[...].astype(F32)
    total = total.astype(BF16).astype(F32)
    position, seg, first = token_places(starts, tokens, (tokens, channels), 0)
    values = conv_silu(total, cache_ref, kernel_ref, bias_ref, seg, position - first)
    inputs = values.astype(BF16)
    values = inputs.astype(F32)

    lane_head = lax.broadcasted_iota(jnp.int32, (tokens, channels), 1) // width
    scores = scores_ref[...]
    cum = cum_ref[0]
    cum_t = cum_t_ref[0]
    step_t = step_t_ref[0]
    coef = coef_ref[0]
    grown = jnp.exp(cum)
    grown_wide = jnp.zeros((tokens, channels), F32)
    coef_wide = jnp.zeros((tokens, channels), F32)
    result = jnp.zeros((tokens, channels), F32)
    for h in range(heads):
        gap = jnp.minimum(cum[:, h : h + 1] - cum_t[h : h + 1, :], 0.0)
        weights = (jnp.exp(gap) * scores * step_t[h : h + 1, :]).astype(BF16)
        mine = lane_head == h
        result = result + jnp.dot(
            weights, jnp.where(mine, values, 0.0).astype(BF16), preferred_element_type=F32
        )
        grown_wide = jnp.where(mine, grown[:, h : h + 1], grown_wide)
        coef_wide = jnp.where(mine, coef[:, h : h + 1], coef_wide)

    from_state = jnp.zeros((tokens, channels), F32)
    carried = (coef_wide * values).astype(BF16)
    fresh = lax.dot_general(
        carried, b_part_ref[...], (((0,), (0,)), ((), ())), preferred_element_type=F32
    )
    for j in range(count_req):
        place = slice(j * state, (j + 1) * state)
        start = held_ref[j].reshape(channels, state) * flags_ref[j, 0].astype(F32)
        for step in range(got_total):
            start = start + states[step][j].astype(F32) * flags_ref[j, step + 1].astype(F32)
        from_state = from_state + lax.dot_general(
            c_part_ref[:, place],
            start.astype(BF16),
            (((1,), (1,)), ((), ())),
            preferred_element_type=F32,
        )
        first_head = pl.program_id(0) * heads
        for h in range(heads):
            rows = slice(h * width, (h + 1) * width)
            state_ref[j, h] = decay_ref[j, first_head + h] * start[rows] + fresh[rows, place]
    out_ref[...] = result + grown_wide * from_state + skip_ref[...] * values


def mixer(
    flags, starts, own, got, cache, kernel, bias, b_maps, c_maps, cum, cum_t, step_t, coef,
    decay, skip, held, states
):
    tokens, channels = own.shape
    count_req, heads, width, state = held.shape
    kernel_len = kernel.shape[0]
    part = min(HEADS_STEP, heads)
    steps = heads // part
    wide = part * width
    columns = lambda i, *_: (0, i)
    whole = lambda i, *_: (0, 0)

    in_specs = (
        [pl.BlockSpec((tokens, wide), columns)] * (1 + len(got))
        + [
            pl.BlockSpec((count_req, kernel_len - 1, wide), lambda i, *_: (0, 0, i)),
            pl.BlockSpec((kernel_len, wide), columns),
            pl.BlockSpec((1, wide), columns),
            pl.BlockSpec((tokens, state), whole),
            pl.BlockSpec((tokens, state), whole),
            pl.BlockSpec((1, tokens, part), lambda i, *_: (i, 0, 0)),
            pl.BlockSpec((1, part, tokens), lambda i, *_: (i, 0, 0)),
            pl.BlockSpec((1, part, tokens), lambda i, *_: (i, 0, 0)),
            pl.BlockSpec((1, tokens, part), lambda i, *_: (i, 0, 0)),
            pl.BlockSpec(memory_space=pltpu.SMEM),
            pl.BlockSpec((1, wide), columns),
        ]
        + [pl.BlockSpec((count_req, part, width, state), lambda i, *_: (0, i, 0, 0))]
        + [pl.BlockSpec((count_req, wide, state), lambda i, *_: (0, i, 0))] * len(states)
    )
    return pl.pallas_call(
        functools.partial(mixer_kernel, count_req, len(got)),
        out_shape=[
            jax.ShapeDtypeStruct((tokens, channels), F32),
            jax.ShapeDtypeStruct((count_req, heads, width, state), F32),
        ],
        grid_spec=pltpu.PrefetchScalarGridSpec(
            num_scalar_prefetch=2,
            grid=(steps,),
            in_specs=in_specs,
            out_specs=[
                pl.BlockSpec((tokens, wide), columns),
                pl.BlockSpec((count_req, part, width, state), lambda i, *_: (0, i, 0, 0)),
            ],
            scratch_shapes=[
                pltpu.VMEM((tokens, tokens), F32),
                pltpu.VMEM((tokens, count_req * state), BF16),
                pltpu.VMEM((tokens, count_req * state), BF16),
            ],
        ),
        compiler_params=params(),
        cost_estimate=cost(1e6, 1e4),
    )(
        flags, starts, own, *got, cache, kernel, bias[None], b_maps, c_maps,
        cum, cum_t, step_t, coef, decay,
        jnp.repeat(skip, width)[None], held, *states
    )


def on_device(
    x_in,
    w_xz,
    w_dt,
    w_bc,
    dt_bias,
    a_log,
    d_skip,
    conv_x_w,
    conv_x_b,
    conv_bc_w,
    conv_bc_b,
    norm_gain,
    stretch_start,
    prefix_len,
    state_slot,
    ssm_pool,
    conv_x_pool,
    conv_bc_pool,
):
    local_width = w_xz.shape[2]
    state_part = w_bc.shape[1]
    me = lax.axis_index("req")
    req_count = lax.axis_size("req")
    slot_count, heads, head_width, state = ssm_pool.shape
    group_reqs = prefix_len.shape[0]
    lags = conv_x_pool.shape[1]
    conv_width = local_width + state_part

    direct = req_count == 2 and lax.axis_size("wide") == 16
    w_pair = jnp.transpose(w_xz, (1, 0, 2))
    w_step = w_dt
    if direct:
        own_block, block = near_blocks(x_in)
        w_pair = pinned(w_pair)
        block = after(block, w_pair)
        along_z = partner_2(block, "wide", 2)
        along_x = partner_2(block, "wide", 1)
        w_step = pinned(after(w_dt, block))

    def slots_of(index):
        asked = lax.dynamic_slice_in_dim(state_slot, index * group_reqs, group_reqs)
        return jnp.clip(asked - me * slot_count, 0, slot_count - 1)

    def conv_of(slots):
        hit = slots[:, None] == jnp.arange(slot_count)[None, :]
        parts = [
            jnp.sum(jnp.where(hit[:, :, None, None], pool[None], 0), 1)
            for pool in (conv_x_pool, conv_bc_pool)
        ]
        return jnp.concatenate(parts, 2)

    conv_size = lags * conv_width
    conv_rows = -(-conv_size // (16 * state)) * 16
    own_slots = slots_of(me)
    got_states = []
    for step in range(1, req_count):
        slots = slots_of((me + step) % req_count)
        flat = conv_of(slots).reshape(group_reqs, conv_size)
        if direct:
            flat = after(flat, block)
        flat = jnp.pad(flat, ((0, 0), (0, conv_rows * state - conv_size)))
        packed, held = pack(
            ssm_pool, flat.reshape(group_reqs, conv_rows, state), slots, own_slots
        )
        got_states.append(shift_req(packed, step))

    asked = lax.dynamic_slice_in_dim(state_slot, me * group_reqs, group_reqs)
    came_from = (me - asked // slot_count) % req_count
    live = prefix_len > 0
    flags = (live[:, None] & (came_from[:, None] == jnp.arange(req_count)[None, :])).astype(
        jnp.int32
    )
    if direct:
        both = partner_2(after(along_z, packed, w_step), "wide", 1)
        own_block = after(own_block, packed)
        own_z = partner_2(own_block, "wide", 2)
        four = after(jnp.stack([block, along_z, along_x, both]), own_z)
        other = partner_2(four, "wide", 0)
        own_pair = after(jnp.stack([own_block, own_z]), four)
        own_got = partner_2(own_pair, "wide", 1)
        features = [own_got, quad_arrange(four, other)]
    else:
        features = features_in_general(x_in)
    weights = {
        "map": jnp.concatenate([w_bc, w_step], 1),
        "xr": w_pair[1],
        "z": w_pair[0],
    }

    def project(block, name):
        return jnp.dot(block, weights[name], preferred_element_type=F32)

    came = {"xr": [], "map": [], "z": []}
    done, parts = [], {}
    for step in range(1, req_count):
        block = features[step]
        for name in came:
            part, block = lax.optimization_barrier((project(block, name).astype(BF16), block))
            came[name].append(shift_req(part, step))
            parts[name] = part
            done.append(part)
    block = features[0]
    if direct:
        own_four = jnp.concatenate([own_pair, after(block, parts["xr"])], 0)
        own_other = partner_2(own_four, "wide", 0)
        block = quad_arrange(own_four, after(own_other, *done, *came["map"]))
    else:
        block = after(block, *done)
    own = {}
    for name in ("map", "xr", "z"):
        own[name], block = lax.optimization_barrier((project(block, name), block))

    cache = conv_of(own_slots)
    for step in range(1, req_count):
        got = after(got_states[step - 1], parts["xr"])[:, heads * head_width :].reshape(group_reqs, -1)
        got = got[:, :conv_size].reshape(cache.shape)
        cache = jnp.where((came_from == step)[:, None, None], got, cache)
    cache = jnp.where(live[:, None, None], cache, 0).astype(F32)

    bc_conv, cum, cum_t, step_t, coef, decay = prep(
        stretch_start, own["map"], came["map"], cache[:, :, local_width:], conv_bc_w, conv_bc_b,
        dt_bias, a_log
    )
    wide_index = lax.axis_index("wide")
    group_span = lax.axis_size("wide") // GROUPS
    bit_total = group_span.bit_length() - 1
    joined = bc_conv
    for bit_index in range(bit_total):
        partner = partner_2(joined, "wide", bit_index)
        upper_half = wide_index // (1 << bit_index) % 2 == 1
        joined = jnp.where(
            upper_half, jnp.concatenate([partner, joined], 1), jnp.concatenate([joined, partner], 1)
        )
    state_width = joined.shape[1] // 2
    came_xr = [after(got, own["xr"], bc_conv) for got in came["xr"]]
    result, final_state = mixer(
        flags, stretch_start[0], own["xr"], came_xr, cache[:, :, :local_width],
        conv_x_w, conv_x_b, joined[:, :state_width], joined[:, state_width:], cum, cum_t,
        step_t, coef, decay, d_skip, held, got_states
    )
    gate = own["z"]
    for got in came["z"]:
        gate = gate + got.astype(F32)
    gated = result * jax.nn.silu(gate.astype(BF16).astype(F32))
    square_sum = jnp.sum(gated * gated, 1)
    for bit_index in range(bit_total):
        square_sum = square_sum + partner_2(square_sum, "wide", bit_index)
    mean_sq = square_sum / (local_width * group_span)
    normed = gated * lax.rsqrt(mean_sq + NORM_EPS)[:, None] * norm_gain[None, :]
    return (normed.astype(BF16), final_state)


def solution(mesh):
    in_specs = (
        P("req", "wide"),
        P("req", None, "wide"),
        P("req", "wide"),
        P("req", "wide"),
        P("wide"),
        P("wide"),
        P("wide"),
        P(None, "wide"),
        P("wide"),
        P(None, "wide"),
        P("wide"),
        P("wide"),
        P("req", None),
        P("req"),
        P(),
        P("req", "wide", None, None),
        P("req", None, "wide"),
        P("req", None, "wide"),
    )
    out_specs = (P("req", "wide"), P("req", "wide", None, None))
    return jax.shard_map(
        on_device, mesh=mesh, in_specs=in_specs, out_specs=out_specs, check_vma=False
    )
```

```python
import functools

import jax
import jax.numpy as jnp
from jax import lax
from jax.experimental import pallas as pl
from jax.experimental.layout import Layout, with_layout_constraint
from jax.experimental.pallas import tpu as pltpu
from jax.sharding import PartitionSpec as P

GROUPS = 8
NORM_EPS = 1e-05
F32 = jnp.float32
BF16 = jnp.bfloat16
HIGH = lax.Precision.HIGHEST
VMEM_BYTES = 16 * 1024 * 1024
HEADS_STEP = 4
COLUMNS = 256


def cost(flops, bytes_accessed):
    return pl.CostEstimate(flops=int(flops), bytes_accessed=int(bytes_accessed), transcendentals=0)


def params(limit=VMEM_BYTES):
    return pltpu.CompilerParams(vmem_limit_bytes=limit)


def partner_2(block, axis, bit):
    count = lax.axis_size(axis)
    route = []
    for low in range(count):
        high = low | 1 << bit
        if high != low and high < count:
            route += [(low, high), (high, low)]
    return lax.ppermute(block, axis, route)


def shift_req(block, step):
    count = lax.axis_size("req")
    return lax.ppermute(block, "req", [(i, (i + step) % count) for i in range(count)])


def spread_routes():
    first, second = [], []
    for z in range(4):
        for rest in range(4):
            for r in range(2):
                place = (z * 4 + rest) * 2 + r
                other = (((z + 2) % 4) * 4 + rest) * 2 + r
                if z // 2 == r:
                    first.append((place, other))
                else:
                    first.append((place, place ^ 1))
                    second.append((place, other ^ 1))
    return first, second


def arrange_kernel(places_ref, *refs):
    out_ref = refs[-1]
    index = 0
    for ref in refs[:-1]:
        for part in range(ref.shape[0]):
            width = ref.shape[2]
            place = pl.multiple_of(places_ref[index] * width, width)
            out_ref[:, pl.ds(place, width)] = ref[part]
            index += 1


def arrange(stacks, places):
    tokens, width = stacks[0].shape[1:]
    total = sum(stack.shape[0] for stack in stacks) * width
    return pl.pallas_call(
        arrange_kernel,
        out_shape=jax.ShapeDtypeStruct((tokens, total), stacks[0].dtype),
        in_specs=[pl.BlockSpec(memory_space=pltpu.SMEM)]
        + [pl.BlockSpec(memory_space=pltpu.VMEM)] * len(stacks),
        out_specs=pl.BlockSpec(memory_space=pltpu.VMEM),
        compiler_params=params(),
        cost_estimate=cost(1e6, 1e4),
    )(places, *stacks)


def after(value, *others):
    return lax.optimization_barrier((value, others))[0]


def near_blocks(x_in):
    axes = ("wide", "req")
    first, second = spread_routes()
    first = lax.ppermute(x_in, axes, first)
    second = lax.ppermute(x_in, axes, second)
    near = lax.axis_index("wide") // 8 == lax.axis_index("req")
    return jnp.where(near, x_in, first), jnp.where(near, first, second)


def quad_arrange(four, other):
    apart = jnp.array([0, 4, 2, 6, 1, 5, 3, 7], jnp.int32)
    return arrange([four, other], (lax.axis_index("wide") % 8) ^ apart)


def features_in_general(x_in):
    req_count = lax.axis_size("req")
    me = lax.axis_index("req")
    own = lax.all_gather(x_in, "wide", axis=1, tiled=True)
    parts = own.reshape(own.shape[0], req_count, own.shape[1] // req_count).transpose(1, 0, 2)
    got = lax.all_to_all(parts, "req", split_axis=0, concat_axis=0, tiled=True)
    return [
        lax.dynamic_index_in_dim(got, (me + step) % req_count, 0, False)
        for step in range(req_count)
    ]


def pinned(array):
    return lax.optimization_barrier(
        with_layout_constraint(array, Layout(tuple(range(array.ndim))))
    )


def product_kernel(x_ref, w_ref, out_ref):
    total = jnp.dot(x_ref[...], w_ref[0], preferred_element_type=F32)
    out_ref[...] = total.astype(out_ref.dtype)


def product(block, w_pair, which, kind):
    tokens, depth = block.shape
    width = w_pair.shape[2]
    tile = min(COLUMNS, width)
    return pl.pallas_call(
        product_kernel,
        out_shape=jax.ShapeDtypeStruct((tokens, width), kind),
        grid=(width // tile,),
        in_specs=[
            pl.BlockSpec((tokens, depth), lambda n: (0, 0)),
            pl.BlockSpec((1, depth, tile), lambda n: (which, 0, n)),
        ],
        out_specs=pl.BlockSpec((tokens, tile), lambda n: (0, n)),
        compiler_params=params(3 * VMEM_BYTES),
        cost_estimate=cost(2 * tokens * depth * width, 2 * depth * width),
    )(block, w_pair)


def token_places(starts, count_tok, shape, axis):
    position = lax.broadcasted_iota(jnp.int32, shape, axis)
    seg = jnp.full(shape, -1, jnp.int32)
    first = jnp.zeros(shape, jnp.int32)
    for start in starts:
        seg = seg + (position >= start).astype(jnp.int32)
        first = jnp.where(position >= start, start, first)
    return position, seg, first


def conv_silu(values, cache_ref, kernel_ref, bias_ref, seg, offset):
    kernel_len = kernel_ref.shape[0]
    taps = [kernel_ref[k : k + 1, :] for k in range(kernel_len)]
    total = bias_ref[...] + taps[kernel_len - 1] * values
    for lag in range(1, kernel_len):
        earlier = pltpu.roll(values, lag, 0)
        total = total + taps[kernel_len - 1 - lag] * jnp.where(offset >= lag, earlier, 0.0)
    cached = jnp.zeros_like(values)
    for request in range(cache_ref.shape[0]):
        for place in range(kernel_len - 1):
            history = jnp.zeros_like(bias_ref[...])
            for lag in range(place + 1, kernel_len):
                at = kernel_len - 1 + place - lag
                history = history + taps[kernel_len - 1 - lag] * cache_ref[request, at : at + 1, :]
            cached = jnp.where((seg == request) & (offset == place), history, cached)
    total = total + cached
    return total * jax.nn.sigmoid(total)


def prep_kernel(
    count_req, got_total, starts_ref, own_ref, *refs
):
    got = refs[:got_total]
    cache_ref, kernel_ref, bias_ref, dt_bias_ref, a_log_ref = refs[got_total : got_total + 5]
    bc_ref, cum_ref, cum_t_ref, step_t_ref, coef_ref, decay_ref = refs[got_total + 5 :]
    tokens = own_ref.shape[0]
    channels = bias_ref.shape[1]
    heads = dt_bias_ref.shape[1]
    starts = [starts_ref[0, j] for j in range(count_req)]
    total = own_ref[...]
    for ref in got:
        total = total + ref[...].astype(F32)
    total = total.astype(BF16).astype(F32)
    position, seg, first = token_places(starts, tokens, (tokens, channels), 0)
    bc = conv_silu(total[:, :channels], cache_ref, kernel_ref, bias_ref, seg, position - first)
    bc_ref[...] = bc.astype(BF16)
    raw = total[:, channels : channels + heads] + dt_bias_ref[...]
    step = jnp.maximum(raw, 0.0) + jnp.log1p(jnp.exp(-jnp.abs(raw)))
    rate = step * (-jnp.exp(a_log_ref[...]))
    position, seg, first = token_places(starts, tokens, (tokens, tokens), 0)
    other, seg_other, first_other = token_places(starts, tokens, (tokens, tokens), 1)
    same = seg == seg_other
    mask = jnp.where(same & (position >= other), 1.0, 0.0)
    after = jnp.where(same & (position < other), 1.0, 0.0)
    cum = jnp.dot(mask, rate, precision=HIGH, preferred_element_type=F32)
    left = jnp.dot(after, rate, precision=HIGH, preferred_element_type=F32)
    cum_t = lax.dot_general(
        rate, mask, (((0,), (1,)), ((), ())), precision=HIGH, preferred_element_type=F32
    )
    step_t = step.T
    coef = jnp.exp(left) * step
    part = cum_ref.shape[2]
    for i in range(cum_ref.shape[0]):
        place = slice(i * part, (i + 1) * part)
        cum_ref[i] = cum[:, place]
        cum_t_ref[i] = cum_t[place, :]
        step_t_ref[i] = step_t[place, :]
        coef_ref[i] = coef[:, place]
    at, seg_at, _ = token_places(starts, tokens, (8, tokens), 1)
    row = lax.broadcasted_iota(jnp.int32, (8, tokens), 0)
    ends = jnp.dot(
        jnp.where(seg_at == row, 1.0, 0.0), rate, precision=HIGH, preferred_element_type=F32
    )
    decay_ref[...] = jnp.exp(ends)


def prep(starts, own, got, cache, kernel, bias, dt_bias, a_log):
    tokens = own.shape[0]
    channels = bias.shape[0]
    heads = dt_bias.shape[0]
    count_req = cache.shape[0]
    vmem = pl.BlockSpec(memory_space=pltpu.VMEM)
    part = min(HEADS_STEP, heads)
    tall = jax.ShapeDtypeStruct((heads // part, tokens, part), F32)
    flat = jax.ShapeDtypeStruct((heads // part, part, tokens), F32)
    return pl.pallas_call(
        functools.partial(prep_kernel, count_req, len(got)),
        out_shape=[
            jax.ShapeDtypeStruct((tokens, channels), BF16),
            tall,
            flat,
            flat,
            tall,
            jax.ShapeDtypeStruct((8, heads), F32),
        ],
        in_specs=[pl.BlockSpec(memory_space=pltpu.SMEM)] + [vmem] * (6 + len(got)),
        out_specs=[vmem] * 6,
        compiler_params=params(),
        cost_estimate=cost(1e6, 1e4),
    )(starts, own, *got, cache, kernel, bias[None], dt_bias[None], a_log[None])


def pack_kernel(slots_ref, own_slots_ref, pool_ref, own_pool_ref, conv_ref, out_ref, own_ref):
    heads, width, state = pool_ref.shape[1:]
    out_ref[0, : heads * width, :] = pool_ref[0].reshape(heads * width, state).astype(BF16)
    out_ref[0, heads * width :, :] = conv_ref[0]
    own_ref[...] = own_pool_ref[...]


def pack(pool, conv_rows, slots, own_slots):
    _, heads, width, state = pool.shape
    count_req, rows, _ = conv_rows.shape
    block = (1, heads, width, state)
    return pl.pallas_call(
        pack_kernel,
        out_shape=[
            jax.ShapeDtypeStruct((count_req, heads * width + rows, state), BF16),
            jax.ShapeDtypeStruct((count_req, heads, width, state), F32),
        ],
        grid_spec=pltpu.PrefetchScalarGridSpec(
            num_scalar_prefetch=2,
            grid=(count_req,),
            in_specs=[
                pl.BlockSpec(block, lambda j, slots, own: (slots[j], 0, 0, 0)),
                pl.BlockSpec(block, lambda j, slots, own: (own[j], 0, 0, 0)),
                pl.BlockSpec((1, rows, state), lambda j, *_: (j, 0, 0)),
            ],
            out_specs=[
                pl.BlockSpec((1, heads * width + rows, state), lambda j, *_: (j, 0, 0)),
                pl.BlockSpec(block, lambda j, *_: (j, 0, 0, 0)),
            ],
        ),
        compiler_params=params(3 * VMEM_BYTES),
        cost_estimate=cost(0, 14 * count_req * heads * width * state),
    )(slots, own_slots, pool, pool, conv_rows)


def mixer_kernel(count_req, got_total, flags_ref, starts_ref, *refs):
    own_ref = refs[0]
    got = refs[1 : 1 + got_total]
    rest = refs[1 + got_total :]
    cache_ref, kernel_ref, bias_ref, b_ref, c_ref = rest[:5]
    cum_ref, cum_t_ref, step_t_ref, coef_ref, decay_ref, skip_ref = rest[5:11]
    held_ref = rest[11]
    states = rest[12 : 12 + got_total]
    out_ref, state_ref, scores_ref, c_part_ref, b_part_ref = rest[12 + got_total :]
    tokens, channels = own_ref.shape
    heads, width, state = held_ref.shape[1:]
    starts = [starts_ref[j] for j in range(count_req)]

    @pl.when(pl.program_id(0) == 0)
    def _():
        position, seg, _ = token_places(starts, tokens, (tokens, tokens), 0)
        other, seg_other, _ = token_places(starts, tokens, (tokens, tokens), 1)
        scores = lax.dot_general(
            c_ref[...], b_ref[...], (((1,), (1,)), ((), ())), preferred_element_type=F32
        )
        scores_ref[...] = jnp.where((seg == seg_other) & (position >= other), scores, 0.0)
        _, seg, _ = token_places(starts, tokens, (tokens, state), 0)
        b_maps = b_ref[...].astype(F32)
        c_maps = c_ref[...].astype(F32)
        for j in range(count_req):
            place = slice(j * state, (j + 1) * state)
            b_part_ref[:, place] = jnp.where(seg == j, b_maps, 0.0).astype(BF16)
            c_part_ref[:, place] = jnp.where(seg == j, c_maps, 0.0).astype(BF16)

    total = own_ref[...]
    for ref in got:
        total = total + ref[...].astype(F32)
    total = total.astype(BF16).astype(F32)
    position, seg, first = token_places(starts, tokens, (tokens, channels), 0)
    values = conv_silu(total, cache_ref, kernel_ref, bias_ref, seg, position - first)
    inputs = values.astype(BF16)
    values = inputs.astype(F32)

    lane_head = lax.broadcasted_iota(jnp.int32, (tokens, channels), 1) // width
    scores = scores_ref[...]
    cum = cum_ref[0]
    cum_t = cum_t_ref[0]
    step_t = step_t_ref[0]
    coef = coef_ref[0]
    grown = jnp.exp(cum)
    grown_wide = jnp.zeros((tokens, channels), F32)
    coef_wide = jnp.zeros((tokens, channels), F32)
    result = jnp.zeros((tokens, channels), F32)
    for h in range(heads):
        gap = jnp.minimum(cum[:, h : h + 1] - cum_t[h : h + 1, :], 0.0)
        weights = (jnp.exp(gap) * scores * step_t[h : h + 1, :]).astype(BF16)
        mine = lane_head == h
        result = result + jnp.dot(
            weights, jnp.where(mine, values, 0.0).astype(BF16), preferred_element_type=F32
        )
        grown_wide = jnp.where(mine, grown[:, h : h + 1], grown_wide)
        coef_wide = jnp.where(mine, coef[:, h : h + 1], coef_wide)

    from_state = jnp.zeros((tokens, channels), F32)
    carried = (coef_wide * values).astype(BF16)
    fresh = lax.dot_general(
        carried, b_part_ref[...], (((0,), (0,)), ((), ())), preferred_element_type=F32
    )
    for j in range(count_req):
        place = slice(j * state, (j + 1) * state)
        start = held_ref[j].reshape(channels, state) * flags_ref[j, 0].astype(F32)
        for step in range(got_total):
            start = start + states[step][j].astype(F32) * flags_ref[j, step + 1].astype(F32)
        from_state = from_state + lax.dot_general(
            c_part_ref[:, place],
            start.astype(BF16),
            (((1,), (1,)), ((), ())),
            preferred_element_type=F32,
        )
        first_head = pl.program_id(0) * heads
        for h in range(heads):
            rows = slice(h * width, (h + 1) * width)
            state_ref[j, h] = decay_ref[j, first_head + h] * start[rows] + fresh[rows, place]
    out_ref[...] = result + grown_wide * from_state + skip_ref[...] * values


def mixer(
    flags, starts, own, got, cache, kernel, bias, b_maps, c_maps, cum, cum_t, step_t, coef,
    decay, skip, held, states
):
    tokens, channels = own.shape
    count_req, heads, width, state = held.shape
    kernel_len = kernel.shape[0]
    part = min(HEADS_STEP, heads)
    steps = heads // part
    wide = part * width
    columns = lambda i, *_: (0, i)
    whole = lambda i, *_: (0, 0)

    in_specs = (
        [pl.BlockSpec((tokens, wide), columns)] * (1 + len(got))
        + [
            pl.BlockSpec((count_req, kernel_len - 1, wide), lambda i, *_: (0, 0, i)),
            pl.BlockSpec((kernel_len, wide), columns),
            pl.BlockSpec((1, wide), columns),
            pl.BlockSpec((tokens, state), whole),
            pl.BlockSpec((tokens, state), whole),
            pl.BlockSpec((1, tokens, part), lambda i, *_: (i, 0, 0)),
            pl.BlockSpec((1, part, tokens), lambda i, *_: (i, 0, 0)),
            pl.BlockSpec((1, part, tokens), lambda i, *_: (i, 0, 0)),
            pl.BlockSpec((1, tokens, part), lambda i, *_: (i, 0, 0)),
            pl.BlockSpec(memory_space=pltpu.SMEM),
            pl.BlockSpec((1, wide), columns),
        ]
        + [pl.BlockSpec((count_req, part, width, state), lambda i, *_: (0, i, 0, 0))]
        + [pl.BlockSpec((count_req, wide, state), lambda i, *_: (0, i, 0))] * len(states)
    )
    return pl.pallas_call(
        functools.partial(mixer_kernel, count_req, len(got)),
        out_shape=[
            jax.ShapeDtypeStruct((tokens, channels), F32),
            jax.ShapeDtypeStruct((count_req, heads, width, state), F32),
        ],
        grid_spec=pltpu.PrefetchScalarGridSpec(
            num_scalar_prefetch=2,
            grid=(steps,),
            in_specs=in_specs,
            out_specs=[
                pl.BlockSpec((tokens, wide), columns),
                pl.BlockSpec((count_req, part, width, state), lambda i, *_: (0, i, 0, 0)),
            ],
            scratch_shapes=[
                pltpu.VMEM((tokens, tokens), F32),
                pltpu.VMEM((tokens, count_req * state), BF16),
                pltpu.VMEM((tokens, count_req * state), BF16),
            ],
        ),
        compiler_params=params(),
        cost_estimate=cost(1e6, 1e4),
    )(
        flags, starts, own, *got, cache, kernel, bias[None], b_maps, c_maps,
        cum, cum_t, step_t, coef, decay,
        jnp.repeat(skip, width)[None], held, *states
    )


def on_device(
    x_in,
    w_xz,
    w_dt,
    w_bc,
    dt_bias,
    a_log,
    d_skip,
    conv_x_w,
    conv_x_b,
    conv_bc_w,
    conv_bc_b,
    norm_gain,
    stretch_start,
    prefix_len,
    state_slot,
    ssm_pool,
    conv_x_pool,
    conv_bc_pool,
):
    local_width = w_xz.shape[2]
    state_part = w_bc.shape[1]
    me = lax.axis_index("req")
    req_count = lax.axis_size("req")
    slot_count, heads, head_width, state = ssm_pool.shape
    group_reqs = prefix_len.shape[0]
    lags = conv_x_pool.shape[1]
    conv_width = local_width + state_part

    direct = req_count == 2 and lax.axis_size("wide") == 16
    w_pair = jnp.transpose(w_xz, (1, 0, 2))
    w_step = w_dt
    if direct:
        own_block, block = near_blocks(x_in)
        w_pair = pinned(w_pair)
        block = after(block, w_pair)
        along_z = partner_2(block, "wide", 2)
        along_x = partner_2(block, "wide", 1)
        w_step = pinned(after(w_dt, block))

    def slots_of(index):
        asked = lax.dynamic_slice_in_dim(state_slot, index * group_reqs, group_reqs)
        return jnp.clip(asked - me * slot_count, 0, slot_count - 1)

    def conv_of(slots):
        hit = slots[:, None] == jnp.arange(slot_count)[None, :]
        parts = [
            jnp.sum(jnp.where(hit[:, :, None, None], pool[None], 0), 1)
            for pool in (conv_x_pool, conv_bc_pool)
        ]
        return jnp.concatenate(parts, 2)

    conv_size = lags * conv_width
    conv_rows = -(-conv_size // (16 * state)) * 16
    own_slots = slots_of(me)
    got_states = []
    for step in range(1, req_count):
        slots = slots_of((me + step) % req_count)
        flat = conv_of(slots).reshape(group_reqs, conv_size)
        if direct:
            flat = after(flat, block)
        flat = jnp.pad(flat, ((0, 0), (0, conv_rows * state - conv_size)))
        packed, held = pack(
            ssm_pool, flat.reshape(group_reqs, conv_rows, state), slots, own_slots
        )
        got_states.append(shift_req(packed, step))

    asked = lax.dynamic_slice_in_dim(state_slot, me * group_reqs, group_reqs)
    came_from = (me - asked // slot_count) % req_count
    live = prefix_len > 0
    flags = (live[:, None] & (came_from[:, None] == jnp.arange(req_count)[None, :])).astype(
        jnp.int32
    )
    if direct:
        both = partner_2(after(along_z, packed, w_step), "wide", 1)
        own_block = after(own_block, packed)
        own_z = partner_2(own_block, "wide", 2)
        four = after(jnp.stack([block, along_z, along_x, both]), own_z)
        other = partner_2(four, "wide", 0)
        own_pair = after(jnp.stack([own_block, own_z]), four)
        own_got = partner_2(own_pair, "wide", 1)
        features = [own_got, quad_arrange(four, other)]
    else:
        features = features_in_general(x_in)
    w_map = jnp.concatenate([w_bc, w_step], 1)

    def project(block, name, kind):
        if name == "map":
            return jnp.dot(block, w_map, preferred_element_type=F32).astype(kind)
        return product(block, w_pair, 1 if name == "xr" else 0, kind)

    came = {"xr": [], "map": [], "z": []}
    done, parts = [], {}
    for step in range(1, req_count):
        block = features[step]
        for name in came:
            if name == "map":
                block = after(block, got_states[step - 1])
            part, block = lax.optimization_barrier((project(block, name, BF16), block))
            came[name].append(shift_req(part, step))
            parts[name] = part
            done.append(part)
    block = features[0]
    if direct:
        own_four = jnp.concatenate([own_pair, after(block, parts["xr"])], 0)
        own_other = partner_2(own_four, "wide", 0)
        block = quad_arrange(own_four, after(own_other, *done, *came["map"]))
    else:
        block = after(block, *done)
    own = {}
    for name in ("map", "xr", "z"):
        own[name], block = lax.optimization_barrier((project(block, name, F32), block))

    cache = conv_of(own_slots)
    for step in range(1, req_count):
        got = after(got_states[step - 1], parts["xr"])[:, heads * head_width :].reshape(group_reqs, -1)
        got = got[:, :conv_size].reshape(cache.shape)
        cache = jnp.where((came_from == step)[:, None, None], got, cache)
    cache = jnp.where(live[:, None, None], cache, 0).astype(F32)

    bc_conv, cum, cum_t, step_t, coef, decay = prep(
        stretch_start, own["map"], came["map"], cache[:, :, local_width:], conv_bc_w, conv_bc_b,
        dt_bias, a_log
    )
    wide_index = lax.axis_index("wide")
    group_span = lax.axis_size("wide") // GROUPS
    bit_total = group_span.bit_length() - 1
    joined = bc_conv
    for bit_index in range(bit_total):
        partner = partner_2(joined, "wide", bit_index)
        upper_half = wide_index // (1 << bit_index) % 2 == 1
        joined = jnp.where(
            upper_half, jnp.concatenate([partner, joined], 1), jnp.concatenate([joined, partner], 1)
        )
    state_width = joined.shape[1] // 2
    came_xr = [after(got, own["xr"], bc_conv) for got in came["xr"]]
    result, final_state = mixer(
        flags, stretch_start[0], own["xr"], came_xr, cache[:, :, :local_width],
        conv_x_w, conv_x_b, joined[:, :state_width], joined[:, state_width:], cum, cum_t,
        step_t, coef, decay, d_skip, held, got_states
    )
    gate = own["z"]
    for got in came["z"]:
        gate = gate + got.astype(F32)
    gated = result * jax.nn.silu(gate.astype(BF16).astype(F32))
    square_sum = jnp.sum(gated * gated, 1)
    for bit_index in range(bit_total):
        square_sum = square_sum + partner_2(square_sum, "wide", bit_index)
    mean_sq = square_sum / (local_width * group_span)
    normed = gated * lax.rsqrt(mean_sq + NORM_EPS)[:, None] * norm_gain[None, :]
    return (normed.astype(BF16), final_state)


def solution(mesh):
    in_specs = (
        P("req", "wide"),
        P("req", None, "wide"),
        P("req", "wide"),
        P("req", "wide"),
        P("wide"),
        P("wide"),
        P("wide"),
        P(None, "wide"),
        P("wide"),
        P(None, "wide"),
        P("wide"),
        P("wide"),
        P("req", None),
        P("req"),
        P(),
        P("req", "wide", None, None),
        P("req", None, "wide"),
        P("req", None, "wide"),
    )
    out_specs = (P("req", "wide"), P("req", "wide", None, None))
    return jax.shard_map(
        on_device, mesh=mesh, in_specs=in_specs, out_specs=out_specs, check_vma=False
    )
```

```python
import functools

import jax
import jax.numpy as jnp
from jax import lax
from jax.experimental import pallas as pl
from jax.experimental.layout import Layout, with_layout_constraint
from jax.experimental.pallas import tpu as pltpu
from jax.sharding import PartitionSpec as P

GROUPS = 8
NORM_EPS = 1e-05
F32 = jnp.float32
BF16 = jnp.bfloat16
HIGH = lax.Precision.HIGHEST
VMEM_BYTES = 16 * 1024 * 1024
LARGE_BYTES = 40 * 1024 * 1024
HEADS_STEP = 4


def cost(flops, bytes_accessed):
    return pl.CostEstimate(flops=int(flops), bytes_accessed=int(bytes_accessed), transcendentals=0)


def params(limit=VMEM_BYTES):
    return pltpu.CompilerParams(vmem_limit_bytes=limit)


def partner_2(block, axis, bit):
    count = lax.axis_size(axis)
    route = []
    for low in range(count):
        high = low | 1 << bit
        if high != low and high < count:
            route += [(low, high), (high, low)]
    return lax.ppermute(block, axis, route)


def shift_req(block, step):
    count = lax.axis_size("req")
    return lax.ppermute(block, "req", [(i, (i + step) % count) for i in range(count)])


def spread_routes():
    first, second = [], []
    for z in range(4):
        for rest in range(4):
            for r in range(2):
                place = (z * 4 + rest) * 2 + r
                other = (((z + 2) % 4) * 4 + rest) * 2 + r
                if z // 2 == r:
                    first.append((place, other))
                else:
                    first.append((place, place ^ 1))
                    second.append((place, other ^ 1))
    return first, second


def arrange_kernel(places_ref, *refs):
    out_ref = refs[-1]
    index = 0
    for ref in refs[:-1]:
        for part in range(ref.shape[0]):
            width = ref.shape[2]
            place = pl.multiple_of(places_ref[index] * width, width)
            out_ref[:, pl.ds(place, width)] = ref[part]
            index += 1


def arrange(stacks, places):
    tokens, width = stacks[0].shape[1:]
    total = sum(stack.shape[0] for stack in stacks) * width
    return pl.pallas_call(
        arrange_kernel,
        out_shape=jax.ShapeDtypeStruct((tokens, total), stacks[0].dtype),
        in_specs=[pl.BlockSpec(memory_space=pltpu.SMEM)]
        + [pl.BlockSpec(memory_space=pltpu.VMEM)] * len(stacks),
        out_specs=pl.BlockSpec(memory_space=pltpu.VMEM),
        compiler_params=params(),
        cost_estimate=cost(1e6, 1e4),
    )(places, *stacks)


def after(value, *others):
    return lax.optimization_barrier((value, others))[0]


def near_blocks(x_in):
    axes = ("wide", "req")
    first, second = spread_routes()
    first = lax.ppermute(x_in, axes, first)
    second = lax.ppermute(x_in, axes, second)
    near = lax.axis_index("wide") // 8 == lax.axis_index("req")
    return jnp.where(near, x_in, first), jnp.where(near, first, second)


def quad_arrange(stacks, apart):
    places = (lax.axis_index("wide") % 8) ^ jnp.array(apart, jnp.int32)
    return arrange(stacks, places)


def features_in_general(x_in):
    req_count = lax.axis_size("req")
    me = lax.axis_index("req")
    own = lax.all_gather(x_in, "wide", axis=1, tiled=True)
    parts = own.reshape(own.shape[0], req_count, own.shape[1] // req_count).transpose(1, 0, 2)
    got = lax.all_to_all(parts, "req", split_axis=0, concat_axis=0, tiled=True)
    return [
        lax.dynamic_index_in_dim(got, (me + step) % req_count, 0, False)
        for step in range(req_count)
    ]


def pinned(array):
    return lax.optimization_barrier(
        with_layout_constraint(array, Layout(tuple(range(array.ndim))))
    )


def stage_kernel(which, w_ref, _, out_ref, sem):
    copy = pltpu.make_async_copy(w_ref.at[which], out_ref, sem)
    copy.start()
    copy.wait()


def stage(w_pair, which, behind):
    return pl.pallas_call(
        functools.partial(stage_kernel, which),
        out_shape=jax.ShapeDtypeStruct(w_pair.shape[1:], w_pair.dtype),
        in_specs=[pl.BlockSpec(memory_space=pl.ANY)] * 2,
        out_specs=pl.BlockSpec(memory_space=pltpu.VMEM),
        scratch_shapes=[pltpu.SemaphoreType.DMA],
        compiler_params=params(LARGE_BYTES),
        cost_estimate=cost(0, 2 * w_pair.shape[1] * w_pair.shape[2]),
    )(w_pair, behind)


def token_places(starts, count_tok, shape, axis):
    position = lax.broadcasted_iota(jnp.int32, shape, axis)
    seg = jnp.full(shape, -1, jnp.int32)
    first = jnp.zeros(shape, jnp.int32)
    for start in starts:
        seg = seg + (position >= start).astype(jnp.int32)
        first = jnp.where(position >= start, start, first)
    return position, seg, first


def conv_silu(values, cache_ref, kernel_ref, bias_ref, seg, offset):
    kernel_len = kernel_ref.shape[0]
    taps = [kernel_ref[k : k + 1, :] for k in range(kernel_len)]
    total = bias_ref[...] + taps[kernel_len - 1] * values
    for lag in range(1, kernel_len):
        earlier = pltpu.roll(values, lag, 0)
        total = total + taps[kernel_len - 1 - lag] * jnp.where(offset >= lag, earlier, 0.0)
    cached = jnp.zeros_like(values)
    for request in range(cache_ref.shape[0]):
        for place in range(kernel_len - 1):
            history = jnp.zeros_like(bias_ref[...])
            for lag in range(place + 1, kernel_len):
                at = kernel_len - 1 + place - lag
                history = history + taps[kernel_len - 1 - lag] * cache_ref[request, at : at + 1, :]
            cached = jnp.where((seg == request) & (offset == place), history, cached)
    total = total + cached
    return total * jax.nn.sigmoid(total)


def prep_kernel(
    count_req, got_total, starts_ref, own_ref, *refs
):
    got = refs[:got_total]
    cache_ref, kernel_ref, bias_ref, dt_bias_ref, a_log_ref = refs[got_total : got_total + 5]
    bc_ref, cum_ref, cum_t_ref, step_t_ref, coef_ref, decay_ref = refs[got_total + 5 :]
    tokens = own_ref.shape[0]
    channels = bias_ref.shape[1]
    heads = dt_bias_ref.shape[1]
    starts = [starts_ref[0, j] for j in range(count_req)]
    total = own_ref[...]
    for ref in got:
        total = total + ref[...].astype(F32)
    total = total.astype(BF16).astype(F32)
    position, seg, first = token_places(starts, tokens, (tokens, channels), 0)
    bc = conv_silu(total[:, :channels], cache_ref, kernel_ref, bias_ref, seg, position - first)
    bc_ref[...] = bc.astype(BF16)
    raw = total[:, channels : channels + heads] + dt_bias_ref[...]
    step = jnp.maximum(raw, 0.0) + jnp.log1p(jnp.exp(-jnp.abs(raw)))
    rate = step * (-jnp.exp(a_log_ref[...]))
    position, seg, first = token_places(starts, tokens, (tokens, tokens), 0)
    other, seg_other, first_other = token_places(starts, tokens, (tokens, tokens), 1)
    same = seg == seg_other
    mask = jnp.where(same & (position >= other), 1.0, 0.0)
    after = jnp.where(same & (position < other), 1.0, 0.0)
    cum = jnp.dot(mask, rate, precision=HIGH, preferred_element_type=F32)
    left = jnp.dot(after, rate, precision=HIGH, preferred_element_type=F32)
    cum_t = lax.dot_general(
        rate, mask, (((0,), (1,)), ((), ())), precision=HIGH, preferred_element_type=F32
    )
    step_t = step.T
    coef = jnp.exp(left) * step
    part = cum_ref.shape[2]
    for i in range(cum_ref.shape[0]):
        place = slice(i * part, (i + 1) * part)
        cum_ref[i] = cum[:, place]
        cum_t_ref[i] = cum_t[place, :]
        step_t_ref[i] = step_t[place, :]
        coef_ref[i] = coef[:, place]
    at, seg_at, _ = token_places(starts, tokens, (8, tokens), 1)
    row = lax.broadcasted_iota(jnp.int32, (8, tokens), 0)
    ends = jnp.dot(
        jnp.where(seg_at == row, 1.0, 0.0), rate, precision=HIGH, preferred_element_type=F32
    )
    decay_ref[...] = jnp.exp(ends)


def prep(starts, own, got, cache, kernel, bias, dt_bias, a_log):
    tokens = own.shape[0]
    channels = bias.shape[0]
    heads = dt_bias.shape[0]
    count_req = cache.shape[0]
    vmem = pl.BlockSpec(memory_space=pltpu.VMEM)
    part = min(HEADS_STEP, heads)
    tall = jax.ShapeDtypeStruct((heads // part, tokens, part), F32)
    flat = jax.ShapeDtypeStruct((heads // part, part, tokens), F32)
    return pl.pallas_call(
        functools.partial(prep_kernel, count_req, len(got)),
        out_shape=[
            jax.ShapeDtypeStruct((tokens, channels), BF16),
            tall,
            flat,
            flat,
            tall,
            jax.ShapeDtypeStruct((8, heads), F32),
        ],
        in_specs=[pl.BlockSpec(memory_space=pltpu.SMEM)] + [vmem] * (6 + len(got)),
        out_specs=[vmem] * 6,
        compiler_params=params(),
        cost_estimate=cost(1e6, 1e4),
    )(starts, own, *got, cache, kernel, bias[None], dt_bias[None], a_log[None])


def pack_kernel(slots_ref, pool_ref, out_ref):
    out_ref[...] = pool_ref[...].reshape(out_ref.shape).astype(out_ref.dtype)


def pack(pool, slots, shape, kind):
    count_req = slots.shape[0]
    block = (1,) + pool.shape[1:]
    return pl.pallas_call(
        pack_kernel,
        out_shape=jax.ShapeDtypeStruct((count_req,) + shape, kind),
        grid_spec=pltpu.PrefetchScalarGridSpec(
            num_scalar_prefetch=1,
            grid=(count_req,),
            in_specs=[pl.BlockSpec(block, lambda j, slots: (slots[j], 0, 0, 0))],
            out_specs=pl.BlockSpec((1,) + shape, lambda j, slots: (j,) + (0,) * len(shape)),
        ),
        compiler_params=params(3 * VMEM_BYTES),
        cost_estimate=cost(0, 6 * pool[0].size * count_req),
    )(slots, pool)


def mixer_kernel(count_req, got_total, flags_ref, starts_ref, *refs):
    own_ref = refs[0]
    got = refs[1 : 1 + got_total]
    rest = refs[1 + got_total :]
    cache_ref, kernel_ref, bias_ref, b_ref, c_ref = rest[:5]
    cum_ref, cum_t_ref, step_t_ref, coef_ref, decay_ref, skip_ref = rest[5:11]
    held_ref = rest[11]
    states = rest[12 : 12 + got_total]
    out_ref, state_ref, scores_ref, c_part_ref, b_part_ref = rest[12 + got_total :]
    tokens, channels = own_ref.shape
    heads, width, state = held_ref.shape[1:]
    starts = [starts_ref[j] for j in range(count_req)]

    @pl.when(pl.program_id(0) == 0)
    def _():
        position, seg, _ = token_places(starts, tokens, (tokens, tokens), 0)
        other, seg_other, _ = token_places(starts, tokens, (tokens, tokens), 1)
        scores = lax.dot_general(
            c_ref[...], b_ref[...], (((1,), (1,)), ((), ())), preferred_element_type=F32
        )
        scores_ref[...] = jnp.where((seg == seg_other) & (position >= other), scores, 0.0)
        _, seg, _ = token_places(starts, tokens, (tokens, state), 0)
        b_maps = b_ref[...].astype(F32)
        c_maps = c_ref[...].astype(F32)
        for j in range(count_req):
            place = slice(j * state, (j + 1) * state)
            b_part_ref[:, place] = jnp.where(seg == j, b_maps, 0.0).astype(BF16)
            c_part_ref[:, place] = jnp.where(seg == j, c_maps, 0.0).astype(BF16)

    total = own_ref[...]
    for ref in got:
        total = total + ref[...].astype(F32)
    total = total.astype(BF16).astype(F32)
    position, seg, first = token_places(starts, tokens, (tokens, channels), 0)
    values = conv_silu(total, cache_ref, kernel_ref, bias_ref, seg, position - first)
    inputs = values.astype(BF16)
    values = inputs.astype(F32)

    lane_head = lax.broadcasted_iota(jnp.int32, (tokens, channels), 1) // width
    scores = scores_ref[...]
    cum = cum_ref[0]
    cum_t = cum_t_ref[0]
    step_t = step_t_ref[0]
    coef = coef_ref[0]
    grown = jnp.exp(cum)
    grown_wide = jnp.zeros((tokens, channels), F32)
    coef_wide = jnp.zeros((tokens, channels), F32)
    result = jnp.zeros((tokens, channels), F32)
    for h in range(heads):
        gap = jnp.minimum(cum[:, h : h + 1] - cum_t[h : h + 1, :], 0.0)
        weights = (jnp.exp(gap) * scores * step_t[h : h + 1, :]).astype(BF16)
        mine = lane_head == h
        result = result + jnp.dot(
            weights, jnp.where(mine, values, 0.0).astype(BF16), preferred_element_type=F32
        )
        grown_wide = jnp.where(mine, grown[:, h : h + 1], grown_wide)
        coef_wide = jnp.where(mine, coef[:, h : h + 1], coef_wide)

    from_state = jnp.zeros((tokens, channels), F32)
    carried = (coef_wide * values).astype(BF16)
    fresh = lax.dot_general(
        carried, b_part_ref[...], (((0,), (0,)), ((), ())), preferred_element_type=F32
    )
    for j in range(count_req):
        place = slice(j * state, (j + 1) * state)
        start = held_ref[j].reshape(channels, state) * flags_ref[j, 0].astype(F32)
        for step in range(got_total):
            start = start + states[step][j].astype(F32) * flags_ref[j, step + 1].astype(F32)
        from_state = from_state + lax.dot_general(
            c_part_ref[:, place],
            start.astype(BF16),
            (((1,), (1,)), ((), ())),
            preferred_element_type=F32,
        )
        first_head = pl.program_id(0) * heads
        for h in range(heads):
            rows = slice(h * width, (h + 1) * width)
            state_ref[j, h] = decay_ref[j, first_head + h] * start[rows] + fresh[rows, place]
    out_ref[...] = result + grown_wide * from_state + skip_ref[...] * values


def mixer(
    flags, starts, own, got, cache, kernel, bias, b_maps, c_maps, cum, cum_t, step_t, coef,
    decay, skip, held, states
):
    tokens, channels = own.shape
    count_req, heads, width, state = held.shape
    kernel_len = kernel.shape[0]
    part = min(HEADS_STEP, heads)
    steps = heads // part
    wide = part * width
    columns = lambda i, *_: (0, i)
    whole = lambda i, *_: (0, 0)

    in_specs = (
        [pl.BlockSpec((tokens, wide), columns)] * (1 + len(got))
        + [
            pl.BlockSpec((count_req, kernel_len - 1, wide), lambda i, *_: (0, 0, i)),
            pl.BlockSpec((kernel_len, wide), columns),
            pl.BlockSpec((1, wide), columns),
            pl.BlockSpec((tokens, state), whole),
            pl.BlockSpec((tokens, state), whole),
            pl.BlockSpec((1, tokens, part), lambda i, *_: (i, 0, 0)),
            pl.BlockSpec((1, part, tokens), lambda i, *_: (i, 0, 0)),
            pl.BlockSpec((1, part, tokens), lambda i, *_: (i, 0, 0)),
            pl.BlockSpec((1, tokens, part), lambda i, *_: (i, 0, 0)),
            pl.BlockSpec(memory_space=pltpu.SMEM),
            pl.BlockSpec((1, wide), columns),
        ]
        + [pl.BlockSpec((count_req, part, width, state), lambda i, *_: (0, i, 0, 0))]
        + [pl.BlockSpec((count_req, wide, state), lambda i, *_: (0, i, 0))] * len(states)
    )
    return pl.pallas_call(
        functools.partial(mixer_kernel, count_req, len(got)),
        out_shape=[
            jax.ShapeDtypeStruct((tokens, channels), F32),
            jax.ShapeDtypeStruct((count_req, heads, width, state), F32),
        ],
        grid_spec=pltpu.PrefetchScalarGridSpec(
            num_scalar_prefetch=2,
            grid=(steps,),
            in_specs=in_specs,
            out_specs=[
                pl.BlockSpec((tokens, wide), columns),
                pl.BlockSpec((count_req, part, width, state), lambda i, *_: (0, i, 0, 0)),
            ],
            scratch_shapes=[
                pltpu.VMEM((tokens, tokens), F32),
                pltpu.VMEM((tokens, count_req * state), BF16),
                pltpu.VMEM((tokens, count_req * state), BF16),
            ],
        ),
        compiler_params=params(),
        cost_estimate=cost(1e6, 1e4),
    )(
        flags, starts, own, *got, cache, kernel, bias[None], b_maps, c_maps,
        cum, cum_t, step_t, coef, decay,
        jnp.repeat(skip, width)[None], held, *states
    )


def on_device(
    x_in,
    w_xz,
    w_dt,
    w_bc,
    dt_bias,
    a_log,
    d_skip,
    conv_x_w,
    conv_x_b,
    conv_bc_w,
    conv_bc_b,
    norm_gain,
    stretch_start,
    prefix_len,
    state_slot,
    ssm_pool,
    conv_x_pool,
    conv_bc_pool,
):
    local_width = w_xz.shape[2]
    state_part = w_bc.shape[1]
    me = lax.axis_index("req")
    req_count = lax.axis_size("req")
    slot_count, heads, head_width, state = ssm_pool.shape
    group_reqs = prefix_len.shape[0]
    lags = conv_x_pool.shape[1]
    conv_width = local_width + state_part

    direct = req_count == 2 and lax.axis_size("wide") == 16
    if direct:
        own_block, block = near_blocks(x_in)

    def slots_of(index):
        asked = lax.dynamic_slice_in_dim(state_slot, index * group_reqs, group_reqs)
        return jnp.clip(asked - me * slot_count, 0, slot_count - 1)

    def conv_of(slots):
        hit = slots[:, None] == jnp.arange(slot_count)[None, :]
        parts = [
            jnp.sum(jnp.where(hit[:, :, None, None], pool[None], 0), 1)
            for pool in (conv_x_pool, conv_bc_pool)
        ]
        return jnp.concatenate(parts, 2)

    got_states = []
    for step in range(1, req_count):
        slots = slots_of((me + step) % req_count)
        packed = pack(ssm_pool, slots, (heads * head_width, state), BF16)
        got_states.append(shift_req(packed, step))
    own_slots = slots_of(me)
    asked = lax.dynamic_slice_in_dim(state_slot, me * group_reqs, group_reqs)
    came_from = (me - asked // slot_count) % req_count
    live = prefix_len > 0
    flags = (live[:, None] & (came_from[:, None] == jnp.arange(req_count)[None, :])).astype(
        jnp.int32
    )

    w_pair = jnp.transpose(w_xz, (1, 0, 2))
    w_step = w_dt
    if direct:
        w_pair = pinned(w_pair)
        block = after(block, w_pair)
        along_z = partner_2(block, "wide", 2)
        along_x = partner_2(block, "wide", 1)
        w_step = pinned(after(w_dt, block))
        own_slots = after(own_slots, block)
    held = pack(ssm_pool, own_slots, (heads, head_width, state), F32)
    got_conv = []
    for step in range(1, req_count):
        slots = slots_of((me + step) % req_count)
        if direct:
            slots = after(slots, block)
        got_conv.append(shift_req(conv_of(slots), step))

    if direct:
        near_three = after(jnp.stack([block, along_z, along_x]), held, w_step)
        both = partner_2(after(along_z, held, w_step, *got_states, *got_conv), "wide", 1)
        core_three = partner_2(near_three, "wide", 0)
        own_block = after(own_block, held)
        own_z = partner_2(own_block, "wide", 2)
        w_xr = stage(w_pair, 1, near_three)
        w_z = stage(w_pair, 0, near_three)
        both = after(both[None], own_z, w_xr, w_z)
        core_both = partner_2(both, "wide", 0)
        own_pair = after(jnp.stack([own_block, own_z]), both)
        own_got = partner_2(own_pair, "wide", 1)
        theirs = quad_arrange(
            [near_three, both, core_three, core_both], [0, 4, 2, 6, 1, 5, 3, 7]
        )
        features = [own_got, theirs]
    else:
        features = features_in_general(x_in)
        w_z, w_xr = w_pair[0], w_pair[1]
    w_map = jnp.concatenate([w_bc, w_step], 1)

    weights = {"xr": w_xr, "map": w_map, "z": w_z}

    def project(block, name, kind):
        return jnp.dot(block, weights[name], preferred_element_type=F32).astype(kind)

    came = {"xr": [], "map": [], "z": []}
    done, parts = [], {}
    for step in range(1, req_count):
        block = features[step]
        for name in came:
            part, block = lax.optimization_barrier((project(block, name, BF16), block))
            parts[name] = part
            part = shift_req(part, step)
            came[name].append(part)
            done.append(part)
    block = features[0]
    if direct:
        own_four = jnp.concatenate([own_pair, after(block, parts["xr"])], 0)
        own_core = after(partner_2(own_four, "wide", 0), *done, *came["map"])
        block = quad_arrange([own_four, own_core], [0, 4, 2, 6, 1, 5, 3, 7])
    else:
        block = after(block, *done)
    own = {}
    for name in ("map", "xr", "z"):
        own[name], block = lax.optimization_barrier((project(block, name, F32), block))

    cache = conv_of(own_slots)
    for step in range(1, req_count):
        cache = jnp.where((came_from == step)[:, None, None], got_conv[step - 1], cache)
    cache = jnp.where(live[:, None, None], cache, 0).astype(F32)

    bc_conv, cum, cum_t, step_t, coef, decay = prep(
        stretch_start, own["map"], came["map"], cache[:, :, local_width:], conv_bc_w, conv_bc_b,
        dt_bias, a_log
    )
    wide_index = lax.axis_index("wide")
    group_span = lax.axis_size("wide") // GROUPS
    bit_total = group_span.bit_length() - 1
    joined = bc_conv
    for bit_index in range(bit_total):
        partner = partner_2(joined, "wide", bit_index)
        upper_half = wide_index // (1 << bit_index) % 2 == 1
        joined = jnp.where(
            upper_half, jnp.concatenate([partner, joined], 1), jnp.concatenate([joined, partner], 1)
        )
    state_width = joined.shape[1] // 2
    came_xr = [after(got, own["xr"], bc_conv) for got in came["xr"]]
    result, final_state = mixer(
        flags, stretch_start[0], own["xr"], came_xr, cache[:, :, :local_width],
        conv_x_w, conv_x_b, joined[:, :state_width], joined[:, state_width:], cum, cum_t,
        step_t, coef, decay, d_skip, held, got_states
    )
    gate = own["z"]
    for got in came["z"]:
        gate = gate + got.astype(F32)
    gated = result * jax.nn.silu(gate.astype(BF16).astype(F32))
    square_sum = jnp.sum(gated * gated, 1)
    for bit_index in range(bit_total):
        square_sum = square_sum + partner_2(square_sum, "wide", bit_index)
    mean_sq = square_sum / (local_width * group_span)
    normed = gated * lax.rsqrt(mean_sq + NORM_EPS)[:, None] * norm_gain[None, :]
    return (normed.astype(BF16), final_state)


def solution(mesh):
    in_specs = (
        P("req", "wide"),
        P("req", None, "wide"),
        P("req", "wide"),
        P("req", "wide"),
        P("wide"),
        P("wide"),
        P("wide"),
        P(None, "wide"),
        P("wide"),
        P(None, "wide"),
        P("wide"),
        P("wide"),
        P("req", None),
        P("req"),
        P(),
        P("req", "wide", None, None),
        P("req", None, "wide"),
        P("req", None, "wide"),
    )
    out_specs = (P("req", "wide"), P("req", "wide", None, None))
    return jax.shard_map(
        on_device, mesh=mesh, in_specs=in_specs, out_specs=out_specs, check_vma=False
    )
```

```python
import functools

import jax
import jax.numpy as jnp
from jax import lax
from jax.experimental import pallas as pl
from jax.experimental.layout import Layout, with_layout_constraint
from jax.experimental.pallas import tpu as pltpu
from jax.sharding import PartitionSpec as P

GROUPS = 8
NORM_EPS = 1e-05
F32 = jnp.float32
BF16 = jnp.bfloat16
HIGH = lax.Precision.HIGHEST
VMEM_BYTES = 16 * 1024 * 1024
HEADS_STEP = 4


def cost(flops, bytes_accessed):
    return pl.CostEstimate(flops=int(flops), bytes_accessed=int(bytes_accessed), transcendentals=0)


def params(limit=VMEM_BYTES):
    return pltpu.CompilerParams(vmem_limit_bytes=limit)


def partner_2(block, axis, bit):
    count = lax.axis_size(axis)
    route = []
    for low in range(count):
        high = low | 1 << bit
        if high != low and high < count:
            route += [(low, high), (high, low)]
    return lax.ppermute(block, axis, route)


def shift_req(block, step):
    count = lax.axis_size("req")
    return lax.ppermute(block, "req", [(i, (i + step) % count) for i in range(count)])


def spread_routes():
    first, second = [], []
    for z in range(4):
        for rest in range(4):
            for r in range(2):
                place = (z * 4 + rest) * 2 + r
                other = (((z + 2) % 4) * 4 + rest) * 2 + r
                if z // 2 == r:
                    first.append((place, other))
                else:
                    first.append((place, place ^ 1))
                    second.append((place, other ^ 1))
    return first, second


def arrange_kernel(places_ref, *refs):
    out_ref = refs[-1]
    index = 0
    for ref in refs[:-1]:
        for part in range(ref.shape[0]):
            width = ref.shape[2]
            place = pl.multiple_of(places_ref[index] * width, width)
            out_ref[:, pl.ds(place, width)] = ref[part]
            index += 1


def arrange(stacks, places):
    tokens, width = stacks[0].shape[1:]
    total = sum(stack.shape[0] for stack in stacks) * width
    return pl.pallas_call(
        arrange_kernel,
        out_shape=jax.ShapeDtypeStruct((tokens, total), stacks[0].dtype),
        in_specs=[pl.BlockSpec(memory_space=pltpu.SMEM)]
        + [pl.BlockSpec(memory_space=pltpu.VMEM)] * len(stacks),
        out_specs=pl.BlockSpec(memory_space=pltpu.VMEM),
        compiler_params=params(),
        cost_estimate=cost(1e6, 1e4),
    )(places, *stacks)


def after(value, *others):
    return lax.optimization_barrier((value, others))[0]


def near_blocks(x_in):
    axes = ("wide", "req")
    first, second = spread_routes()
    first = lax.ppermute(x_in, axes, first)
    second = lax.ppermute(x_in, axes, second)
    near = lax.axis_index("wide") // 8 == lax.axis_index("req")
    return jnp.where(near, x_in, first), jnp.where(near, first, second)


def quad_arrange(stacks, apart):
    places = (lax.axis_index("wide") % 8) ^ jnp.array(apart, jnp.int32)
    return arrange(stacks, places)


def features_in_general(x_in):
    req_count = lax.axis_size("req")
    me = lax.axis_index("req")
    own = lax.all_gather(x_in, "wide", axis=1, tiled=True)
    parts = own.reshape(own.shape[0], req_count, own.shape[1] // req_count).transpose(1, 0, 2)
    got = lax.all_to_all(parts, "req", split_axis=0, concat_axis=0, tiled=True)
    return [
        lax.dynamic_index_in_dim(got, (me + step) % req_count, 0, False)
        for step in range(req_count)
    ]


def pinned(array):
    return lax.optimization_barrier(
        with_layout_constraint(array, Layout(tuple(range(array.ndim))))
    )


def token_places(starts, count_tok, shape, axis):
    position = lax.broadcasted_iota(jnp.int32, shape, axis)
    seg = jnp.full(shape, -1, jnp.int32)
    first = jnp.zeros(shape, jnp.int32)
    for start in starts:
        seg = seg + (position >= start).astype(jnp.int32)
        first = jnp.where(position >= start, start, first)
    return position, seg, first


def conv_silu(values, cache_ref, kernel_ref, bias_ref, seg, offset):
    kernel_len = kernel_ref.shape[0]
    taps = [kernel_ref[k : k + 1, :] for k in range(kernel_len)]
    total = bias_ref[...] + taps[kernel_len - 1] * values
    for lag in range(1, kernel_len):
        earlier = pltpu.roll(values, lag, 0)
        total = total + taps[kernel_len - 1 - lag] * jnp.where(offset >= lag, earlier, 0.0)
    cached = jnp.zeros_like(values)
    for request in range(cache_ref.shape[0]):
        for place in range(kernel_len - 1):
            history = jnp.zeros_like(bias_ref[...])
            for lag in range(place + 1, kernel_len):
                at = kernel_len - 1 + place - lag
                history = history + taps[kernel_len - 1 - lag] * cache_ref[request, at : at + 1, :]
            cached = jnp.where((seg == request) & (offset == place), history, cached)
    total = total + cached
    return total * jax.nn.sigmoid(total)


def prep_kernel(
    count_req, got_total, starts_ref, own_ref, *refs
):
    got = refs[:got_total]
    cache_ref, kernel_ref, bias_ref, dt_bias_ref, a_log_ref = refs[got_total : got_total + 5]
    bc_ref, cum_ref, cum_t_ref, step_t_ref, coef_ref, decay_ref = refs[got_total + 5 :]
    tokens = own_ref.shape[0]
    channels = bias_ref.shape[1]
    heads = dt_bias_ref.shape[1]
    starts = [starts_ref[0, j] for j in range(count_req)]
    total = own_ref[...]
    for ref in got:
        total = total + ref[...].astype(F32)
    total = total.astype(BF16).astype(F32)
    position, seg, first = token_places(starts, tokens, (tokens, channels), 0)
    bc = conv_silu(total[:, :channels], cache_ref, kernel_ref, bias_ref, seg, position - first)
    bc_ref[...] = bc.astype(BF16)
    raw = total[:, channels : channels + heads] + dt_bias_ref[...]
    step = jnp.maximum(raw, 0.0) + jnp.log1p(jnp.exp(-jnp.abs(raw)))
    rate = step * (-jnp.exp(a_log_ref[...]))
    position, seg, first = token_places(starts, tokens, (tokens, tokens), 0)
    other, seg_other, first_other = token_places(starts, tokens, (tokens, tokens), 1)
    same = seg == seg_other
    mask = jnp.where(same & (position >= other), 1.0, 0.0)
    after = jnp.where(same & (position < other), 1.0, 0.0)
    cum = jnp.dot(mask, rate, precision=HIGH, preferred_element_type=F32)
    left = jnp.dot(after, rate, precision=HIGH, preferred_element_type=F32)
    cum_t = lax.dot_general(
        rate, mask, (((0,), (1,)), ((), ())), precision=HIGH, preferred_element_type=F32
    )
    step_t = step.T
    coef = jnp.exp(left) * step
    part = cum_ref.shape[2]
    for i in range(cum_ref.shape[0]):
        place = slice(i * part, (i + 1) * part)
        cum_ref[i] = cum[:, place]
        cum_t_ref[i] = cum_t[place, :]
        step_t_ref[i] = step_t[place, :]
        coef_ref[i] = coef[:, place]
    at, seg_at, _ = token_places(starts, tokens, (8, tokens), 1)
    row = lax.broadcasted_iota(jnp.int32, (8, tokens), 0)
    ends = jnp.dot(
        jnp.where(seg_at == row, 1.0, 0.0), rate, precision=HIGH, preferred_element_type=F32
    )
    decay_ref[...] = jnp.exp(ends)


def prep(starts, own, got, cache, kernel, bias, dt_bias, a_log):
    tokens = own.shape[0]
    channels = bias.shape[0]
    heads = dt_bias.shape[0]
    count_req = cache.shape[0]
    vmem = pl.BlockSpec(memory_space=pltpu.VMEM)
    part = min(HEADS_STEP, heads)
    tall = jax.ShapeDtypeStruct((heads // part, tokens, part), F32)
    flat = jax.ShapeDtypeStruct((heads // part, part, tokens), F32)
    return pl.pallas_call(
        functools.partial(prep_kernel, count_req, len(got)),
        out_shape=[
            jax.ShapeDtypeStruct((tokens, channels), BF16),
            tall,
            flat,
            flat,
            tall,
            jax.ShapeDtypeStruct((8, heads), F32),
        ],
        in_specs=[pl.BlockSpec(memory_space=pltpu.SMEM)] + [vmem] * (6 + len(got)),
        out_specs=[vmem] * 6,
        compiler_params=params(),
        cost_estimate=cost(1e6, 1e4),
    )(starts, own, *got, cache, kernel, bias[None], dt_bias[None], a_log[None])


def pack_kernel(slots_ref, pool_ref, out_ref):
    out_ref[...] = pool_ref[...].reshape(out_ref.shape).astype(out_ref.dtype)


def pack(pool, slots, shape, kind):
    count_req = slots.shape[0]
    block = (1,) + pool.shape[1:]
    return pl.pallas_call(
        pack_kernel,
        out_shape=jax.ShapeDtypeStruct((count_req,) + shape, kind),
        grid_spec=pltpu.PrefetchScalarGridSpec(
            num_scalar_prefetch=1,
            grid=(count_req,),
            in_specs=[pl.BlockSpec(block, lambda j, slots: (slots[j], 0, 0, 0))],
            out_specs=pl.BlockSpec((1,) + shape, lambda j, slots: (j,) + (0,) * len(shape)),
        ),
        compiler_params=params(3 * VMEM_BYTES),
        cost_estimate=cost(0, 6 * pool[0].size * count_req),
    )(slots, pool)


def mixer_kernel(count_req, got_total, flags_ref, starts_ref, *refs):
    own_ref = refs[0]
    got = refs[1 : 1 + got_total]
    rest = refs[1 + got_total :]
    cache_ref, kernel_ref, bias_ref, b_ref, c_ref = rest[:5]
    cum_ref, cum_t_ref, step_t_ref, coef_ref, decay_ref, skip_ref = rest[5:11]
    held_ref = rest[11]
    states = rest[12 : 12 + got_total]
    out_ref, state_ref, scores_ref, c_part_ref, b_part_ref = rest[12 + got_total :]
    tokens, channels = own_ref.shape
    heads, width, state = held_ref.shape[1:]
    starts = [starts_ref[j] for j in range(count_req)]

    @pl.when(pl.program_id(0) == 0)
    def _():
        position, seg, _ = token_places(starts, tokens, (tokens, tokens), 0)
        other, seg_other, _ = token_places(starts, tokens, (tokens, tokens), 1)
        scores = lax.dot_general(
            c_ref[...], b_ref[...], (((1,), (1,)), ((), ())), preferred_element_type=F32
        )
        scores_ref[...] = jnp.where((seg == seg_other) & (position >= other), scores, 0.0)
        _, seg, _ = token_places(starts, tokens, (tokens, state), 0)
        b_maps = b_ref[...].astype(F32)
        c_maps = c_ref[...].astype(F32)
        for j in range(count_req):
            place = slice(j * state, (j + 1) * state)
            b_part_ref[:, place] = jnp.where(seg == j, b_maps, 0.0).astype(BF16)
            c_part_ref[:, place] = jnp.where(seg == j, c_maps, 0.0).astype(BF16)

    total = own_ref[...]
    for ref in got:
        total = total + ref[...].astype(F32)
    total = total.astype(BF16).astype(F32)
    position, seg, first = token_places(starts, tokens, (tokens, channels), 0)
    values = conv_silu(total, cache_ref, kernel_ref, bias_ref, seg, position - first)
    inputs = values.astype(BF16)
    values = inputs.astype(F32)

    lane_head = lax.broadcasted_iota(jnp.int32, (tokens, channels), 1) // width
    scores = scores_ref[...]
    cum = cum_ref[0]
    cum_t = cum_t_ref[0]
    step_t = step_t_ref[0]
    coef = coef_ref[0]
    grown = jnp.exp(cum)
    grown_wide = jnp.zeros((tokens, channels), F32)
    coef_wide = jnp.zeros((tokens, channels), F32)
    result = jnp.zeros((tokens, channels), F32)
    for h in range(heads):
        gap = jnp.minimum(cum[:, h : h + 1] - cum_t[h : h + 1, :], 0.0)
        weights = (jnp.exp(gap) * scores * step_t[h : h + 1, :]).astype(BF16)
        mine = lane_head == h
        result = result + jnp.dot(
            weights, jnp.where(mine, values, 0.0).astype(BF16), preferred_element_type=F32
        )
        grown_wide = jnp.where(mine, grown[:, h : h + 1], grown_wide)
        coef_wide = jnp.where(mine, coef[:, h : h + 1], coef_wide)

    from_state = jnp.zeros((tokens, channels), F32)
    carried = (coef_wide * values).astype(BF16)
    fresh = lax.dot_general(
        carried, b_part_ref[...], (((0,), (0,)), ((), ())), preferred_element_type=F32
    )
    for j in range(count_req):
        place = slice(j * state, (j + 1) * state)
        start = held_ref[j].reshape(channels, state) * flags_ref[j, 0].astype(F32)
        for step in range(got_total):
            start = start + states[step][j].astype(F32) * flags_ref[j, step + 1].astype(F32)
        from_state = from_state + lax.dot_general(
            c_part_ref[:, place],
            start.astype(BF16),
            (((1,), (1,)), ((), ())),
            preferred_element_type=F32,
        )
        first_head = pl.program_id(0) * heads
        for h in range(heads):
            rows = slice(h * width, (h + 1) * width)
            state_ref[j, h] = decay_ref[j, first_head + h] * start[rows] + fresh[rows, place]
    out_ref[...] = result + grown_wide * from_state + skip_ref[...] * values


def mixer(
    flags, starts, own, got, cache, kernel, bias, b_maps, c_maps, cum, cum_t, step_t, coef,
    decay, skip, held, states
):
    tokens, channels = own.shape
    count_req, heads, width, state = held.shape
    kernel_len = kernel.shape[0]
    part = min(HEADS_STEP, heads)
    steps = heads // part
    wide = part * width
    columns = lambda i, *_: (0, i)
    whole = lambda i, *_: (0, 0)

    in_specs = (
        [pl.BlockSpec((tokens, wide), columns)] * (1 + len(got))
        + [
            pl.BlockSpec((count_req, kernel_len - 1, wide), lambda i, *_: (0, 0, i)),
            pl.BlockSpec((kernel_len, wide), columns),
            pl.BlockSpec((1, wide), columns),
            pl.BlockSpec((tokens, state), whole),
            pl.BlockSpec((tokens, state), whole),
            pl.BlockSpec((1, tokens, part), lambda i, *_: (i, 0, 0)),
            pl.BlockSpec((1, part, tokens), lambda i, *_: (i, 0, 0)),
            pl.BlockSpec((1, part, tokens), lambda i, *_: (i, 0, 0)),
            pl.BlockSpec((1, tokens, part), lambda i, *_: (i, 0, 0)),
            pl.BlockSpec(memory_space=pltpu.SMEM),
            pl.BlockSpec((1, wide), columns),
        ]
        + [pl.BlockSpec((count_req, part, width, state), lambda i, *_: (0, i, 0, 0))]
        + [pl.BlockSpec((count_req, wide, state), lambda i, *_: (0, i, 0))] * len(states)
    )
    return pl.pallas_call(
        functools.partial(mixer_kernel, count_req, len(got)),
        out_shape=[
            jax.ShapeDtypeStruct((tokens, channels), F32),
            jax.ShapeDtypeStruct((count_req, heads, width, state), F32),
        ],
        grid_spec=pltpu.PrefetchScalarGridSpec(
            num_scalar_prefetch=2,
            grid=(steps,),
            in_specs=in_specs,
            out_specs=[
                pl.BlockSpec((tokens, wide), columns),
                pl.BlockSpec((count_req, part, width, state), lambda i, *_: (0, i, 0, 0)),
            ],
            scratch_shapes=[
                pltpu.VMEM((tokens, tokens), F32),
                pltpu.VMEM((tokens, count_req * state), BF16),
                pltpu.VMEM((tokens, count_req * state), BF16),
            ],
        ),
        compiler_params=params(),
        cost_estimate=cost(1e6, 1e4),
    )(
        flags, starts, own, *got, cache, kernel, bias[None], b_maps, c_maps,
        cum, cum_t, step_t, coef, decay,
        jnp.repeat(skip, width)[None], held, *states
    )


def on_device(
    x_in,
    w_xz,
    w_dt,
    w_bc,
    dt_bias,
    a_log,
    d_skip,
    conv_x_w,
    conv_x_b,
    conv_bc_w,
    conv_bc_b,
    norm_gain,
    stretch_start,
    prefix_len,
    state_slot,
    ssm_pool,
    conv_x_pool,
    conv_bc_pool,
):
    local_width = w_xz.shape[2]
    state_part = w_bc.shape[1]
    me = lax.axis_index("req")
    req_count = lax.axis_size("req")
    slot_count, heads, head_width, state = ssm_pool.shape
    group_reqs = prefix_len.shape[0]
    lags = conv_x_pool.shape[1]
    conv_width = local_width + state_part

    direct = req_count == 2 and lax.axis_size("wide") == 16
    if direct:
        own_block, block = near_blocks(x_in)

    def slots_of(index):
        asked = lax.dynamic_slice_in_dim(state_slot, index * group_reqs, group_reqs)
        return jnp.clip(asked - me * slot_count, 0, slot_count - 1)

    def conv_of(slots):
        hit = slots[:, None] == jnp.arange(slot_count)[None, :]
        parts = [
            jnp.sum(jnp.where(hit[:, :, None, None], pool[None], 0), 1)
            for pool in (conv_x_pool, conv_bc_pool)
        ]
        return jnp.concatenate(parts, 2)

    got_states, got_conv = [], []
    for step in range(1, req_count):
        slots = slots_of((me + step) % req_count)
        packed = pack(ssm_pool, slots, (heads * head_width, state), BF16)
        got_states.append(shift_req(packed, step))
        got_conv.append(shift_req(conv_of(slots), step))
    own_slots = slots_of(me)
    asked = lax.dynamic_slice_in_dim(state_slot, me * group_reqs, group_reqs)
    came_from = (me - asked // slot_count) % req_count
    live = prefix_len > 0
    flags = (live[:, None] & (came_from[:, None] == jnp.arange(req_count)[None, :])).astype(
        jnp.int32
    )

    w_step = w_dt
    if direct:
        block = after(block, packed)
        along_z = partner_2(block, "wide", 2)
        along_x = partner_2(block, "wide", 1)
        w_step = pinned(after(w_dt, block))
        own_slots = after(own_slots, block)
    held = pack(ssm_pool, own_slots, (heads, head_width, state), F32)
    if direct:
        near_three = after(jnp.stack([block, along_z, along_x]), held, w_step)
        both = partner_2(after(along_z, held, w_step), "wide", 1)
        core_three = partner_2(near_three, "wide", 0)
        own_block = after(own_block, held)
        own_z = partner_2(own_block, "wide", 2)
        both = after(both[None], own_z)
        core_both = partner_2(both, "wide", 0)
        own_pair = after(jnp.stack([own_block, own_z]), both)
        own_got = partner_2(own_pair, "wide", 1)
        core_both = after(core_both, *got_states, *got_conv)
        theirs = quad_arrange(
            [near_three, both, core_three, core_both], [0, 4, 2, 6, 1, 5, 3, 7]
        )
        features = [own_got, theirs]
    else:
        features = features_in_general(x_in)
    w_map = jnp.concatenate([w_bc, w_step], 1)

    def project(block, kind):
        low = jnp.dot(block, w_map, preferred_element_type=F32).astype(kind)
        low, block = lax.optimization_barrier((low, block))
        high = jnp.einsum("td,dkc->ktc", block, w_xz, preferred_element_type=F32)
        return {"map": low, "xr": high[1].astype(kind), "z": high[0].astype(kind)}

    came = {"map": [], "xr": [], "z": []}
    parts = []
    for step in range(1, req_count):
        part = lax.optimization_barrier(project(features[step], BF16))
        for name in came:
            came[name].append(shift_req(part[name], step))
        parts.append(part)
    block = features[0]
    if direct:
        own_four = jnp.concatenate([own_pair, after(block, *parts)], 0)
        own_core = partner_2(own_four, "wide", 0)
        block = quad_arrange([own_four, own_core], [0, 4, 2, 6, 1, 5, 3, 7])
    else:
        block = after(block, *parts)
    own = lax.optimization_barrier(project(block, F32))

    cache = conv_of(own_slots)
    for step in range(1, req_count):
        cache = jnp.where((came_from == step)[:, None, None], got_conv[step - 1], cache)
    cache = jnp.where(live[:, None, None], cache, 0).astype(F32)

    bc_conv, cum, cum_t, step_t, coef, decay = prep(
        stretch_start, own["map"], came["map"], cache[:, :, local_width:], conv_bc_w, conv_bc_b,
        dt_bias, a_log
    )
    wide_index = lax.axis_index("wide")
    group_span = lax.axis_size("wide") // GROUPS
    bit_total = group_span.bit_length() - 1
    joined = bc_conv
    for bit_index in range(bit_total):
        partner = partner_2(joined, "wide", bit_index)
        upper_half = wide_index // (1 << bit_index) % 2 == 1
        joined = jnp.where(
            upper_half, jnp.concatenate([partner, joined], 1), jnp.concatenate([joined, partner], 1)
        )
    state_width = joined.shape[1] // 2
    came_xr = [after(got, own["xr"], bc_conv) for got in came["xr"]]
    result, final_state = mixer(
        flags, stretch_start[0], own["xr"], came_xr, cache[:, :, :local_width],
        conv_x_w, conv_x_b, joined[:, :state_width], joined[:, state_width:], cum, cum_t,
        step_t, coef, decay, d_skip, held, got_states
    )
    gate = own["z"]
    for got in came["z"]:
        gate = gate + got.astype(F32)
    gated = result * jax.nn.silu(gate.astype(BF16).astype(F32))
    square_sum = jnp.sum(gated * gated, 1)
    for bit_index in range(bit_total):
        square_sum = square_sum + partner_2(square_sum, "wide", bit_index)
    mean_sq = square_sum / (local_width * group_span)
    normed = gated * lax.rsqrt(mean_sq + NORM_EPS)[:, None] * norm_gain[None, :]
    return (normed.astype(BF16), final_state)


def solution(mesh):
    in_specs = (
        P("req", "wide"),
        P("req", None, "wide"),
        P("req", "wide"),
        P("req", "wide"),
        P("wide"),
        P("wide"),
        P("wide"),
        P(None, "wide"),
        P("wide"),
        P(None, "wide"),
        P("wide"),
        P("wide"),
        P("req", None),
        P("req"),
        P(),
        P("req", "wide", None, None),
        P("req", None, "wide"),
        P("req", None, "wide"),
    )
    out_specs = (P("req", "wide"), P("req", "wide", None, None))
    return jax.shard_map(
        on_device, mesh=mesh, in_specs=in_specs, out_specs=out_specs, check_vma=False
    )
```

```python
import functools

import jax
import jax.numpy as jnp
from jax import lax
from jax.experimental import pallas as pl
from jax.experimental.layout import Layout, with_layout_constraint
from jax.experimental.pallas import tpu as pltpu
from jax.sharding import PartitionSpec as P

GROUPS = 8
NORM_EPS = 1e-05
F32 = jnp.float32
BF16 = jnp.bfloat16
HIGH = lax.Precision.HIGHEST
VMEM_BYTES = 16 * 1024 * 1024
HEADS_STEP = 4


def cost(flops, bytes_accessed):
    return pl.CostEstimate(flops=int(flops), bytes_accessed=int(bytes_accessed), transcendentals=0)


def params(limit=VMEM_BYTES):
    return pltpu.CompilerParams(vmem_limit_bytes=limit)


def partner_2(block, axis, bit):
    count = lax.axis_size(axis)
    route = []
    for low in range(count):
        high = low | 1 << bit
        if high != low and high < count:
            route += [(low, high), (high, low)]
    return lax.ppermute(block, axis, route)


def shift_req(block, step):
    count = lax.axis_size("req")
    return lax.ppermute(block, "req", [(i, (i + step) % count) for i in range(count)])


def spread_routes():
    first, second = [], []
    for z in range(4):
        for rest in range(4):
            for r in range(2):
                place = (z * 4 + rest) * 2 + r
                other = (((z + 2) % 4) * 4 + rest) * 2 + r
                if z // 2 == r:
                    first.append((place, other))
                else:
                    first.append((place, place ^ 1))
                    second.append((place, other ^ 1))
    return first, second


def arrange_kernel(places_ref, *refs):
    out_ref = refs[-1]
    index = 0
    for ref in refs[:-1]:
        for part in range(ref.shape[0]):
            width = ref.shape[2]
            place = pl.multiple_of(places_ref[index] * width, width)
            out_ref[:, pl.ds(place, width)] = ref[part]
            index += 1


def arrange(stacks, places):
    tokens, width = stacks[0].shape[1:]
    total = sum(stack.shape[0] for stack in stacks) * width
    return pl.pallas_call(
        arrange_kernel,
        out_shape=jax.ShapeDtypeStruct((tokens, total), stacks[0].dtype),
        in_specs=[pl.BlockSpec(memory_space=pltpu.SMEM)]
        + [pl.BlockSpec(memory_space=pltpu.VMEM)] * len(stacks),
        out_specs=pl.BlockSpec(memory_space=pltpu.VMEM),
        compiler_params=params(),
        cost_estimate=cost(1e6, 1e4),
    )(places, *stacks)


def after(value, *others):
    return lax.optimization_barrier((value, others))[0]


def near_blocks(x_in):
    axes = ("wide", "req")
    first, second = spread_routes()
    first = lax.ppermute(x_in, axes, first)
    second = lax.ppermute(x_in, axes, second)
    near = lax.axis_index("wide") // 8 == lax.axis_index("req")
    return jnp.where(near, x_in, first), jnp.where(near, first, second)


def quad_arrange(stacks, apart):
    places = (lax.axis_index("wide") % 8) ^ jnp.array(apart, jnp.int32)
    return arrange(stacks, places)


def features_in_general(x_in):
    req_count = lax.axis_size("req")
    me = lax.axis_index("req")
    own = lax.all_gather(x_in, "wide", axis=1, tiled=True)
    parts = own.reshape(own.shape[0], req_count, own.shape[1] // req_count).transpose(1, 0, 2)
    got = lax.all_to_all(parts, "req", split_axis=0, concat_axis=0, tiled=True)
    return [
        lax.dynamic_index_in_dim(got, (me + step) % req_count, 0, False)
        for step in range(req_count)
    ]


def pinned(array):
    return lax.optimization_barrier(
        with_layout_constraint(array, Layout(tuple(range(array.ndim))))
    )


def token_places(starts, count_tok, shape, axis):
    position = lax.broadcasted_iota(jnp.int32, shape, axis)
    seg = jnp.full(shape, -1, jnp.int32)
    first = jnp.zeros(shape, jnp.int32)
    for start in starts:
        seg = seg + (position >= start).astype(jnp.int32)
        first = jnp.where(position >= start, start, first)
    return position, seg, first


def conv_silu(values, cache_ref, const_ref, seg, offset):
    kernel_len = cache_ref.shape[1] + 1
    taps = [const_ref[k : k + 1, :] for k in range(kernel_len)]
    bias = const_ref[kernel_len : kernel_len + 1, :]
    total = bias + taps[kernel_len - 1] * values
    for lag in range(1, kernel_len):
        earlier = pltpu.roll(values, lag, 0)
        total = total + taps[kernel_len - 1 - lag] * jnp.where(offset >= lag, earlier, 0.0)
    cached = jnp.zeros_like(values)
    for request in range(cache_ref.shape[0]):
        for place in range(kernel_len - 1):
            history = jnp.zeros_like(bias)
            for lag in range(place + 1, kernel_len):
                at = kernel_len - 1 + place - lag
                history = history + taps[kernel_len - 1 - lag] * cache_ref[request, at : at + 1, :]
            cached = jnp.where((seg == request) & (offset == place), history, cached)
    total = total + cached
    return total * jax.nn.sigmoid(total)


def prep_kernel(count_req, got_total, heads, ints_ref, own_ref, *refs):
    got = refs[:got_total]
    cache_ref, const_ref = refs[got_total : got_total + 2]
    bc_ref, cum_ref, cum_t_ref, step_t_ref, coef_ref, decay_ref = refs[got_total + 2 :]
    tokens = own_ref.shape[0]
    channels = const_ref.shape[1]
    kernel_len = cache_ref.shape[1] + 1
    dt_bias = const_ref[kernel_len + 1 : kernel_len + 2, :heads]
    a_log = const_ref[kernel_len + 2 : kernel_len + 3, :heads]
    starts = [ints_ref[j] for j in range(count_req)]
    total = own_ref[...].astype(F32)
    for ref in got:
        total = total + ref[...].astype(F32)
    total = total.astype(BF16).astype(F32)
    position, seg, first = token_places(starts, tokens, (tokens, channels), 0)
    bc = conv_silu(total[:, :channels], cache_ref, const_ref, seg, position - first)
    bc_ref[...] = bc.astype(BF16)
    raw = total[:, channels : channels + heads] + dt_bias
    step = jnp.maximum(raw, 0.0) + jnp.log1p(jnp.exp(-jnp.abs(raw)))
    rate = step * (-jnp.exp(a_log))
    position, seg, first = token_places(starts, tokens, (tokens, tokens), 0)
    other, seg_other, first_other = token_places(starts, tokens, (tokens, tokens), 1)
    same = seg == seg_other
    mask = jnp.where(same & (position >= other), 1.0, 0.0)
    after = jnp.where(same & (position < other), 1.0, 0.0)
    cum = jnp.dot(mask, rate, precision=HIGH, preferred_element_type=F32)
    left = jnp.dot(after, rate, precision=HIGH, preferred_element_type=F32)
    cum_t = lax.dot_general(
        rate, mask, (((0,), (1,)), ((), ())), precision=HIGH, preferred_element_type=F32
    )
    step_t = step.T
    coef = jnp.exp(left) * step
    part = cum_ref.shape[2]
    for i in range(cum_ref.shape[0]):
        place = slice(i * part, (i + 1) * part)
        cum_ref[i] = cum[:, place]
        cum_t_ref[i] = cum_t[place, :]
        step_t_ref[i] = step_t[place, :]
        coef_ref[i] = coef[:, place]
    at, seg_at, _ = token_places(starts, tokens, (8, tokens), 1)
    row = lax.broadcasted_iota(jnp.int32, (8, tokens), 0)
    ends = jnp.dot(
        jnp.where(seg_at == row, 1.0, 0.0), rate, precision=HIGH, preferred_element_type=F32
    )
    decay_ref[...] = jnp.exp(ends)


def prep(ints, own, got, cache, const, heads):
    tokens = own.shape[0]
    channels = const.shape[1]
    count_req = cache.shape[0]
    vmem = pl.BlockSpec(memory_space=pltpu.VMEM)
    part = min(HEADS_STEP, heads)
    tall = jax.ShapeDtypeStruct((heads // part, tokens, part), F32)
    flat = jax.ShapeDtypeStruct((heads // part, part, tokens), F32)
    return pl.pallas_call(
        functools.partial(prep_kernel, count_req, len(got), heads),
        out_shape=[
            jax.ShapeDtypeStruct((tokens, channels), BF16),
            tall,
            flat,
            flat,
            tall,
            jax.ShapeDtypeStruct((8, heads), F32),
        ],
        in_specs=[pl.BlockSpec(memory_space=pltpu.SMEM)] + [vmem] * (3 + len(got)),
        out_specs=[vmem] * 6,
        compiler_params=params(),
        cost_estimate=cost(1e6, 1e4),
    )(ints, own, *got, cache, const)


def pack_kernel(slots_ref, pool_ref, *refs):
    out_ref = refs[-1]
    if len(refs) == 1:
        out_ref[...] = pool_ref[...]
    else:
        rows = pool_ref.shape[1] * pool_ref.shape[2]
        states = pool_ref[0].reshape(rows, pool_ref.shape[3])
        out_ref[0, :rows, :] = states.astype(out_ref.dtype)
        out_ref[0, rows:, :] = refs[0][0]


def pack(pool, slots, conv_rows=None):
    count_req = slots.shape[0]
    _, heads, width, state = pool.shape
    block = (1, heads, width, state)
    in_specs = [pl.BlockSpec(block, lambda j, slots: (slots[j], 0, 0, 0))]
    if conv_rows is None:
        out_block, kind, more = block, F32, []
    else:
        rows = conv_rows.shape[1]
        out_block, kind, more = (1, heads * width + rows, state), BF16, [conv_rows]
        in_specs.append(pl.BlockSpec((1, rows, state), lambda j, slots: (j, 0, 0)))
    return pl.pallas_call(
        pack_kernel,
        out_shape=jax.ShapeDtypeStruct((count_req,) + out_block[1:], kind),
        grid_spec=pltpu.PrefetchScalarGridSpec(
            num_scalar_prefetch=1,
            grid=(count_req,),
            in_specs=in_specs,
            out_specs=pl.BlockSpec(out_block, lambda j, slots: (j,) + (0,) * (len(out_block) - 1)),
        ),
        compiler_params=params(3 * VMEM_BYTES),
        cost_estimate=cost(0, 6 * pool[0].size * count_req),
    )(slots, pool, *more)


def mixer_kernel(count_req, got_total, ints_ref, *refs):
    own_ref = refs[0]
    got = refs[1 : 1 + got_total]
    rest = refs[1 + got_total :]
    cache_ref, const_ref, b_ref, c_ref = rest[:4]
    cum_ref, cum_t_ref, step_t_ref, coef_ref, decay_ref, held_ref = rest[4:10]
    states = rest[10 : 10 + got_total]
    out_ref, state_ref, scores_ref, c_part_ref, b_part_ref = rest[10 + got_total :]
    kernel_len = cache_ref.shape[1] + 1
    skip = const_ref[kernel_len + 1 : kernel_len + 2, :]

    def flag(request, step):
        place = count_req + request * (got_total + 1) + step
        return ints_ref[place].astype(F32)

    tokens, channels = own_ref.shape
    heads, width, state = held_ref.shape[1:]
    starts = [ints_ref[j] for j in range(count_req)]

    @pl.when(pl.program_id(0) == 0)
    def _():
        position, seg, _ = token_places(starts, tokens, (tokens, tokens), 0)
        other, seg_other, _ = token_places(starts, tokens, (tokens, tokens), 1)
        scores = lax.dot_general(
            c_ref[...], b_ref[...], (((1,), (1,)), ((), ())), preferred_element_type=F32
        )
        scores_ref[...] = jnp.where((seg == seg_other) & (position >= other), scores, 0.0)
        _, seg, _ = token_places(starts, tokens, (tokens, state), 0)
        b_maps = b_ref[...].astype(F32)
        c_maps = c_ref[...].astype(F32)
        for j in range(count_req):
            place = slice(j * state, (j + 1) * state)
            b_part_ref[:, place] = jnp.where(seg == j, b_maps, 0.0).astype(BF16)
            c_part_ref[:, place] = jnp.where(seg == j, c_maps, 0.0).astype(BF16)

    total = own_ref[...].astype(F32)
    for ref in got:
        total = total + ref[...].astype(F32)
    total = total.astype(BF16).astype(F32)
    position, seg, first = token_places(starts, tokens, (tokens, channels), 0)
    values = conv_silu(total, cache_ref, const_ref, seg, position - first)
    inputs = values.astype(BF16)
    values = inputs.astype(F32)

    lane_head = lax.broadcasted_iota(jnp.int32, (tokens, channels), 1) // width
    scores = scores_ref[...]
    cum = cum_ref[0]
    cum_t = cum_t_ref[0]
    step_t = step_t_ref[0]
    coef = coef_ref[0]
    grown = jnp.exp(cum)
    grown_wide = jnp.zeros((tokens, channels), F32)
    coef_wide = jnp.zeros((tokens, channels), F32)
    result = jnp.zeros((tokens, channels), F32)
    for h in range(heads):
        gap = jnp.minimum(cum[:, h : h + 1] - cum_t[h : h + 1, :], 0.0)
        weights = (jnp.exp(gap) * scores * step_t[h : h + 1, :]).astype(BF16)
        mine = lane_head == h
        result = result + jnp.dot(
            weights, jnp.where(mine, values, 0.0).astype(BF16), preferred_element_type=F32
        )
        grown_wide = jnp.where(mine, grown[:, h : h + 1], grown_wide)
        coef_wide = jnp.where(mine, coef[:, h : h + 1], coef_wide)

    from_state = jnp.zeros((tokens, channels), F32)
    carried = (coef_wide * values).astype(BF16)
    fresh = lax.dot_general(
        carried, b_part_ref[...], (((0,), (0,)), ((), ())), preferred_element_type=F32
    )
    for j in range(count_req):
        place = slice(j * state, (j + 1) * state)
        start = held_ref[j].reshape(channels, state) * flag(j, 0)
        for step in range(got_total):
            start = start + states[step][j].astype(F32) * flag(j, step + 1)
        from_state = from_state + lax.dot_general(
            c_part_ref[:, place],
            start.astype(BF16),
            (((1,), (1,)), ((), ())),
            preferred_element_type=F32,
        )
        first_head = pl.program_id(0) * heads
        for h in range(heads):
            rows = slice(h * width, (h + 1) * width)
            state_ref[j, h] = decay_ref[j, first_head + h] * start[rows] + fresh[rows, place]
    out_ref[...] = result + grown_wide * from_state + skip * values


def mixer(
    ints, own, got, cache, const, b_maps, c_maps, cum, cum_t, step_t, coef, decay, held, states
):
    tokens, channels = own.shape
    count_req, heads, width, state = held.shape
    kernel_len = cache.shape[1] + 1
    part = min(HEADS_STEP, heads)
    steps = heads // part
    wide = part * width
    columns = lambda i, *_: (0, i)
    whole = lambda i, *_: (0, 0)

    in_specs = (
        [pl.BlockSpec((tokens, wide), columns)] * (1 + len(got))
        + [
            pl.BlockSpec((count_req, kernel_len - 1, wide), lambda i, *_: (0, 0, i)),
            pl.BlockSpec((const.shape[0], wide), columns),
            pl.BlockSpec((tokens, state), whole),
            pl.BlockSpec((tokens, state), whole),
            pl.BlockSpec((1, tokens, part), lambda i, *_: (i, 0, 0)),
            pl.BlockSpec((1, part, tokens), lambda i, *_: (i, 0, 0)),
            pl.BlockSpec((1, part, tokens), lambda i, *_: (i, 0, 0)),
            pl.BlockSpec((1, tokens, part), lambda i, *_: (i, 0, 0)),
            pl.BlockSpec(memory_space=pltpu.SMEM),
        ]
        + [pl.BlockSpec((count_req, part, width, state), lambda i, *_: (0, i, 0, 0))]
        + [pl.BlockSpec((count_req, wide, state), lambda i, *_: (0, i, 0))] * len(states)
    )
    return pl.pallas_call(
        functools.partial(mixer_kernel, count_req, len(got)),
        out_shape=[
            jax.ShapeDtypeStruct((tokens, channels), F32),
            jax.ShapeDtypeStruct((count_req, heads, width, state), F32),
        ],
        grid_spec=pltpu.PrefetchScalarGridSpec(
            num_scalar_prefetch=1,
            grid=(steps,),
            in_specs=in_specs,
            out_specs=[
                pl.BlockSpec((tokens, wide), columns),
                pl.BlockSpec((count_req, part, width, state), lambda i, *_: (0, i, 0, 0)),
            ],
            scratch_shapes=[
                pltpu.VMEM((tokens, tokens), F32),
                pltpu.VMEM((tokens, count_req * state), BF16),
                pltpu.VMEM((tokens, count_req * state), BF16),
            ],
        ),
        compiler_params=params(),
        cost_estimate=cost(1e6, 1e4),
    )(
        ints, own, *got, cache, const, b_maps, c_maps, cum, cum_t, step_t, coef, decay, held,
        *states
    )


def on_device(
    x_in,
    w_xz,
    w_dt,
    w_bc,
    dt_bias,
    a_log,
    d_skip,
    conv_x_w,
    conv_x_b,
    conv_bc_w,
    conv_bc_b,
    norm_gain,
    stretch_start,
    prefix_len,
    state_slot,
    ssm_pool,
    conv_x_pool,
    conv_bc_pool,
):
    local_width = w_xz.shape[2]
    state_part = w_bc.shape[1]
    me = lax.axis_index("req")
    req_count = lax.axis_size("req")
    slot_count, heads, head_width, state = ssm_pool.shape
    group_reqs = prefix_len.shape[0]
    lags = conv_x_pool.shape[1]
    conv_width = local_width + state_part

    direct = req_count == 2 and lax.axis_size("wide") == 16
    if direct:
        own_block, block = near_blocks(x_in)

    def slots_of(index):
        asked = lax.dynamic_slice_in_dim(state_slot, index * group_reqs, group_reqs)
        return jnp.clip(asked - me * slot_count, 0, slot_count - 1)

    def conv_of(slots):
        hit = slots[:, None] == jnp.arange(slot_count)[None, :]
        parts = [
            jnp.sum(jnp.where(hit[:, :, None, None], pool[None], 0), 1)
            for pool in (conv_x_pool, conv_bc_pool)
        ]
        return parts

    conv_size = lags * conv_width
    conv_rows = -(-conv_size // (16 * state)) * 16
    x_size = lags * local_width

    got_states = []
    for step in range(1, req_count):
        slots = slots_of((me + step) % req_count)
        flat = jnp.concatenate([part.reshape(group_reqs, -1) for part in conv_of(slots)], 1)
        flat = jnp.pad(flat, ((0, 0), (0, conv_rows * state - conv_size)))
        packed = pack(ssm_pool, slots, flat.reshape(group_reqs, conv_rows, state))
        got_states.append(shift_req(packed, step))
    own_slots = slots_of(me)
    asked = lax.dynamic_slice_in_dim(state_slot, me * group_reqs, group_reqs)
    came_from = (me - asked // slot_count) % req_count
    live = prefix_len > 0
    flags = (live[:, None] & (came_from[:, None] == jnp.arange(req_count)[None, :])).astype(
        jnp.int32
    )

    w_step = w_dt
    if direct:
        block = after(block, packed)
        along_z = partner_2(block, "wide", 2)
        along_x = partner_2(block, "wide", 1)
        w_step = pinned(after(w_dt, block))
        own_slots = after(own_slots, block)
    held = pack(ssm_pool, own_slots)

    kernel_len = conv_x_w.shape[0]
    skip = jnp.repeat(d_skip, head_width)
    const_x = jnp.stack(
        [conv_x_w[k] for k in range(kernel_len)]
        + [conv_x_b, skip, norm_gain, jnp.zeros_like(skip)]
    )
    wide_heads = lambda array: jnp.pad(array, (0, state_part - heads))
    const_bc = jnp.stack(
        [conv_bc_w[k] for k in range(kernel_len)]
        + [conv_bc_b, wide_heads(dt_bias), wide_heads(a_log), jnp.zeros_like(conv_bc_b)]
    )
    ints = jnp.concatenate([stretch_start[0], flags.reshape(-1)])
    caches = conv_of(own_slots)
    if direct:
        const_x, const_bc, ints = after((const_x, const_bc, ints), block)
        near_three = after(
            jnp.stack([block, along_z, along_x]), held, w_step, const_x, const_bc, ints, *caches
        )
        both = partner_2(after(along_z, held, w_step), "wide", 1)
        core_three = partner_2(near_three, "wide", 0)
        own_block = after(own_block, held)
        own_z = partner_2(own_block, "wide", 2)
        both = after(both[None], own_z)
        core_both = partner_2(both, "wide", 0)
        own_pair = after(jnp.stack([own_block, own_z]), both)
        own_got = partner_2(own_pair, "wide", 1)
        core_both = after(core_both, *got_states)
        theirs = quad_arrange(
            [near_three, both, core_three, core_both], [0, 4, 2, 6, 1, 5, 3, 7]
        )
        features = [own_got, theirs]
    else:
        features = features_in_general(x_in)
    w_map = jnp.concatenate([w_bc, w_step], 1)

    def project(block, kind):
        low = jnp.dot(block, w_map, preferred_element_type=F32).astype(kind)
        low, block = lax.optimization_barrier((low, block))
        high = jnp.einsum("td,dkc->ktc", block, w_xz, preferred_element_type=F32)
        return {"map": low, "xr": high[1].astype(kind), "z": high[0].astype(kind)}

    came = {"map": [], "xr": [], "z": []}
    parts = []
    for step in range(1, req_count):
        part = lax.optimization_barrier(project(features[step], BF16))
        for name in came:
            came[name].append(shift_req(part[name], step))
        parts.append(part)
    block = features[0]
    if direct:
        own_four = jnp.concatenate([own_pair, after(block, *parts)], 0)
        own_core = partner_2(own_four, "wide", 0)
        block = quad_arrange([own_four, own_core], [0, 4, 2, 6, 1, 5, 3, 7])
    else:
        block = after(block, *parts)
    own = lax.optimization_barrier(project(block, BF16))

    for step in range(1, req_count):
        flat = after(got_states[step - 1], block)[:, heads * head_width :]
        flat = flat.reshape(group_reqs, -1)
        got = [flat[:, :x_size], flat[:, x_size:conv_size]]
        caches = [
            jnp.where((came_from == step)[:, None, None], here.reshape(cache.shape), cache)
            for here, cache in zip(got, caches)
        ]
    caches = [jnp.where(live[:, None, None], cache, 0).astype(F32) for cache in caches]
    bc_conv, cum, cum_t, step_t, coef, decay = prep(
        ints, own["map"], came["map"], caches[1], const_bc, heads
    )
    wide_index = lax.axis_index("wide")
    group_span = lax.axis_size("wide") // GROUPS
    bit_total = group_span.bit_length() - 1
    joined = bc_conv
    for bit_index in range(bit_total):
        partner = partner_2(joined, "wide", bit_index)
        upper_half = wide_index // (1 << bit_index) % 2 == 1
        joined = jnp.where(
            upper_half, jnp.concatenate([partner, joined], 1), jnp.concatenate([joined, partner], 1)
        )
    state_width = joined.shape[1] // 2
    came_xr = [after(got, own["xr"], bc_conv) for got in came["xr"]]
    result, final_state = mixer(
        ints, own["xr"], came_xr, caches[0], const_x, joined[:, :state_width],
        joined[:, state_width:], cum, cum_t, step_t, coef, decay, held, got_states
    )
    gate = own["z"].astype(F32)
    for got in came["z"]:
        gate = gate + got.astype(F32)
    gated = result * jax.nn.silu(gate.astype(BF16).astype(F32))
    square_sum = jnp.sum(gated * gated, 1)
    for bit_index in range(bit_total):
        square_sum = square_sum + partner_2(square_sum, "wide", bit_index)
    mean_sq = square_sum / (local_width * group_span)
    normed = gated * lax.rsqrt(mean_sq + NORM_EPS)[:, None] * const_x[kernel_len + 2][None, :]
    return (normed.astype(BF16), final_state)


def solution(mesh):
    in_specs = (
        P("req", "wide"),
        P("req", None, "wide"),
        P("req", "wide"),
        P("req", "wide"),
        P("wide"),
        P("wide"),
        P("wide"),
        P(None, "wide"),
        P("wide"),
        P(None, "wide"),
        P("wide"),
        P("wide"),
        P("req", None),
        P("req"),
        P(),
        P("req", "wide", None, None),
        P("req", None, "wide"),
        P("req", None, "wide"),
    )
    out_specs = (P("req", "wide"), P("req", "wide", None, None))
    return jax.shard_map(
        on_device, mesh=mesh, in_specs=in_specs, out_specs=out_specs, check_vma=False
    )
```

```python
import functools

import jax
import jax.numpy as jnp
from jax import lax
from jax.experimental import pallas as pl
from jax.experimental.layout import Layout, with_layout_constraint
from jax.experimental.pallas import tpu as pltpu
from jax.sharding import PartitionSpec as P

GROUPS = 8
NORM_EPS = 1e-05
F32 = jnp.float32
BF16 = jnp.bfloat16
HIGH = lax.Precision.HIGHEST
VMEM_BYTES = 16 * 1024 * 1024
HEADS_STEP = 4


def cost(flops, bytes_accessed):
    return pl.CostEstimate(flops=int(flops), bytes_accessed=int(bytes_accessed), transcendentals=0)


def params(limit=VMEM_BYTES):
    return pltpu.CompilerParams(vmem_limit_bytes=limit)


def partner_2(block, axis, bit):
    count = lax.axis_size(axis)
    route = []
    for low in range(count):
        high = low | 1 << bit
        if high != low and high < count:
            route += [(low, high), (high, low)]
    return lax.ppermute(block, axis, route)


def shift_req(block, step):
    count = lax.axis_size("req")
    return lax.ppermute(block, "req", [(i, (i + step) % count) for i in range(count)])


def spread_routes():
    first, second = [], []
    for z in range(4):
        for rest in range(4):
            for r in range(2):
                place = (z * 4 + rest) * 2 + r
                other = (((z + 2) % 4) * 4 + rest) * 2 + r
                if z // 2 == r:
                    first.append((place, other))
                else:
                    first.append((place, place ^ 1))
                    second.append((place, other ^ 1))
    return first, second


def arrange_kernel(places_ref, *refs):
    out_ref = refs[-1]
    index = 0
    for ref in refs[:-1]:
        for part in range(ref.shape[0]):
            width = ref.shape[2]
            place = pl.multiple_of(places_ref[index] * width, width)
            out_ref[:, pl.ds(place, width)] = ref[part]
            index += 1


def arrange(stacks, places):
    tokens, width = stacks[0].shape[1:]
    total = sum(stack.shape[0] for stack in stacks) * width
    return pl.pallas_call(
        arrange_kernel,
        out_shape=jax.ShapeDtypeStruct((tokens, total), stacks[0].dtype),
        in_specs=[pl.BlockSpec(memory_space=pltpu.SMEM)]
        + [pl.BlockSpec(memory_space=pltpu.VMEM)] * len(stacks),
        out_specs=pl.BlockSpec(memory_space=pltpu.VMEM),
        compiler_params=params(),
        cost_estimate=cost(1e6, 1e4),
    )(places, *stacks)


def after(value, *others):
    return lax.optimization_barrier((value, others))[0]


def near_blocks(x_in):
    axes = ("wide", "req")
    first, second = spread_routes()
    first = lax.ppermute(x_in, axes, first)
    second = lax.ppermute(x_in, axes, second)
    near = lax.axis_index("wide") // 8 == lax.axis_index("req")
    return jnp.where(near, x_in, first), jnp.where(near, first, second)


def quad_arrange(stacks, apart):
    places = (lax.axis_index("wide") % 8) ^ jnp.array(apart, jnp.int32)
    return arrange(stacks, places)


def features_in_general(x_in):
    req_count = lax.axis_size("req")
    me = lax.axis_index("req")
    own = lax.all_gather(x_in, "wide", axis=1, tiled=True)
    parts = own.reshape(own.shape[0], req_count, own.shape[1] // req_count).transpose(1, 0, 2)
    got = lax.all_to_all(parts, "req", split_axis=0, concat_axis=0, tiled=True)
    return [
        lax.dynamic_index_in_dim(got, (me + step) % req_count, 0, False)
        for step in range(req_count)
    ]


def pinned(array):
    return lax.optimization_barrier(
        with_layout_constraint(array, Layout(tuple(range(array.ndim))))
    )


def token_places(starts, count_tok, shape, axis):
    position = lax.broadcasted_iota(jnp.int32, shape, axis)
    seg = jnp.full(shape, -1, jnp.int32)
    first = jnp.zeros(shape, jnp.int32)
    for start in starts:
        seg = seg + (position >= start).astype(jnp.int32)
        first = jnp.where(position >= start, start, first)
    return position, seg, first


def conv_silu(values, cache, const_ref, seg, offset):
    kernel_len = cache.shape[1] + 1
    taps = [const_ref[k : k + 1, :] for k in range(kernel_len)]
    bias = const_ref[kernel_len : kernel_len + 1, :]
    total = bias + taps[kernel_len - 1] * values
    for lag in range(1, kernel_len):
        earlier = pltpu.roll(values, lag, 0)
        total = total + taps[kernel_len - 1 - lag] * jnp.where(offset >= lag, earlier, 0.0)
    cached = jnp.zeros_like(values)
    for request in range(cache.shape[0]):
        for place in range(kernel_len - 1):
            history = jnp.zeros_like(bias)
            for lag in range(place + 1, kernel_len):
                at = kernel_len - 1 + place - lag
                history = history + taps[kernel_len - 1 - lag] * cache[request, at : at + 1, :]
            cached = jnp.where((seg == request) & (offset == place), history, cached)
    total = total + cached
    return total * jax.nn.sigmoid(total)


def prep_kernel(count_req, got_total, heads, ints_ref, own_ref, *refs):
    got = refs[:got_total]
    cache_ref, const_ref = refs[got_total : got_total + 2]
    bc_ref, cum_ref, cum_t_ref, step_t_ref, coef_ref, decay_ref = refs[got_total + 2 :]
    tokens = own_ref.shape[0]
    channels = const_ref.shape[1]
    kernel_len = cache_ref.shape[1] + 1
    dt_bias = const_ref[kernel_len + 1 : kernel_len + 2, :heads]
    a_log = const_ref[kernel_len + 2 : kernel_len + 3, :heads]
    starts = [ints_ref[j] for j in range(count_req)]
    total = own_ref[...].astype(F32)
    for ref in got:
        total = total + ref[...].astype(F32)
    total = total.astype(BF16).astype(F32)
    position, seg, first = token_places(starts, tokens, (tokens, channels), 0)
    bc = conv_silu(total[:, :channels], cache_ref[:, :, -channels:], const_ref, seg, position - first)
    bc_ref[...] = bc.astype(BF16)
    raw = total[:, channels : channels + heads] + dt_bias
    step = jnp.maximum(raw, 0.0) + jnp.log1p(jnp.exp(-jnp.abs(raw)))
    rate = step * (-jnp.exp(a_log))
    position, seg, first = token_places(starts, tokens, (tokens, tokens), 0)
    other, seg_other, first_other = token_places(starts, tokens, (tokens, tokens), 1)
    same = seg == seg_other
    mask = jnp.where(same & (position >= other), 1.0, 0.0)
    after = jnp.where(same & (position < other), 1.0, 0.0)
    cum = jnp.dot(mask, rate, precision=HIGH, preferred_element_type=F32)
    left = jnp.dot(after, rate, precision=HIGH, preferred_element_type=F32)
    cum_t = lax.dot_general(
        rate, mask, (((0,), (1,)), ((), ())), precision=HIGH, preferred_element_type=F32
    )
    step_t = step.T
    coef = jnp.exp(left) * step
    part = cum_ref.shape[2]
    for i in range(cum_ref.shape[0]):
        place = slice(i * part, (i + 1) * part)
        cum_ref[i] = cum[:, place]
        cum_t_ref[i] = cum_t[place, :]
        step_t_ref[i] = step_t[place, :]
        coef_ref[i] = coef[:, place]
    at, seg_at, _ = token_places(starts, tokens, (8, tokens), 1)
    row = lax.broadcasted_iota(jnp.int32, (8, tokens), 0)
    ends = jnp.dot(
        jnp.where(seg_at == row, 1.0, 0.0), rate, precision=HIGH, preferred_element_type=F32
    )
    decay_ref[...] = jnp.exp(ends)


def prep(ints, own, got, cache, const, heads):
    tokens = own.shape[0]
    channels = const.shape[1]
    count_req = cache.shape[0]
    vmem = pl.BlockSpec(memory_space=pltpu.VMEM)
    part = min(HEADS_STEP, heads)
    tall = jax.ShapeDtypeStruct((heads // part, tokens, part), F32)
    flat = jax.ShapeDtypeStruct((heads // part, part, tokens), F32)
    return pl.pallas_call(
        functools.partial(prep_kernel, count_req, len(got), heads),
        out_shape=[
            jax.ShapeDtypeStruct((tokens, channels), BF16),
            tall,
            flat,
            flat,
            tall,
            jax.ShapeDtypeStruct((8, heads), F32),
        ],
        in_specs=[pl.BlockSpec(memory_space=pltpu.SMEM)] + [vmem] * (3 + len(got)),
        out_specs=[vmem] * 6,
        compiler_params=params(),
        cost_estimate=cost(1e6, 1e4),
    )(ints, own, *got, cache, const)


def pack_kernel(slots_ref, pool_ref, out_ref):
    out_ref[...] = pool_ref[...].reshape(out_ref.shape).astype(out_ref.dtype)


def pack(pool, slots, shape, kind):
    count_req = slots.shape[0]
    block = (1,) + pool.shape[1:]
    return pl.pallas_call(
        pack_kernel,
        out_shape=jax.ShapeDtypeStruct((count_req,) + shape, kind),
        grid_spec=pltpu.PrefetchScalarGridSpec(
            num_scalar_prefetch=1,
            grid=(count_req,),
            in_specs=[pl.BlockSpec(block, lambda j, slots: (slots[j], 0, 0, 0))],
            out_specs=pl.BlockSpec((1,) + shape, lambda j, slots: (j,) + (0,) * len(shape)),
        ),
        compiler_params=params(3 * VMEM_BYTES),
        cost_estimate=cost(0, 6 * pool[0].size * count_req),
    )(slots, pool)


def mixer_kernel(count_req, got_total, ints_ref, *refs):
    own_ref = refs[0]
    got = refs[1 : 1 + got_total]
    rest = refs[1 + got_total :]
    cache_ref, const_ref, b_ref, c_ref = rest[:4]
    cum_ref, cum_t_ref, step_t_ref, coef_ref, decay_ref, held_ref = rest[4:10]
    states = rest[10 : 10 + got_total]
    out_ref, state_ref, scores_ref, c_part_ref, b_part_ref = rest[10 + got_total :]
    kernel_len = cache_ref.shape[1] + 1
    skip = const_ref[kernel_len + 1 : kernel_len + 2, :]

    def flag(request, step):
        place = count_req + request * (got_total + 1) + step
        return ints_ref[place].astype(F32)

    tokens, channels = own_ref.shape
    heads, width, state = held_ref.shape[1:]
    starts = [ints_ref[j] for j in range(count_req)]

    @pl.when(pl.program_id(0) == 0)
    def _():
        position, seg, _ = token_places(starts, tokens, (tokens, tokens), 0)
        other, seg_other, _ = token_places(starts, tokens, (tokens, tokens), 1)
        scores = lax.dot_general(
            c_ref[...], b_ref[...], (((1,), (1,)), ((), ())), preferred_element_type=F32
        )
        scores_ref[...] = jnp.where((seg == seg_other) & (position >= other), scores, 0.0)
        _, seg, _ = token_places(starts, tokens, (tokens, state), 0)
        b_maps = b_ref[...].astype(F32)
        c_maps = c_ref[...].astype(F32)
        for j in range(count_req):
            place = slice(j * state, (j + 1) * state)
            b_part_ref[:, place] = jnp.where(seg == j, b_maps, 0.0).astype(BF16)
            c_part_ref[:, place] = jnp.where(seg == j, c_maps, 0.0).astype(BF16)

    total = own_ref[...].astype(F32)
    for ref in got:
        total = total + ref[...].astype(F32)
    total = total.astype(BF16).astype(F32)
    position, seg, first = token_places(starts, tokens, (tokens, channels), 0)
    values = conv_silu(total, cache_ref[...], const_ref, seg, position - first)
    inputs = values.astype(BF16)
    values = inputs.astype(F32)

    lane_head = lax.broadcasted_iota(jnp.int32, (tokens, channels), 1) // width
    scores = scores_ref[...]
    cum = cum_ref[0]
    cum_t = cum_t_ref[0]
    step_t = step_t_ref[0]
    coef = coef_ref[0]
    grown = jnp.exp(cum)
    grown_wide = jnp.zeros((tokens, channels), F32)
    coef_wide = jnp.zeros((tokens, channels), F32)
    result = jnp.zeros((tokens, channels), F32)
    for h in range(heads):
        gap = jnp.minimum(cum[:, h : h + 1] - cum_t[h : h + 1, :], 0.0)
        weights = (jnp.exp(gap) * scores * step_t[h : h + 1, :]).astype(BF16)
        mine = lane_head == h
        result = result + jnp.dot(
            weights, jnp.where(mine, values, 0.0).astype(BF16), preferred_element_type=F32
        )
        grown_wide = jnp.where(mine, grown[:, h : h + 1], grown_wide)
        coef_wide = jnp.where(mine, coef[:, h : h + 1], coef_wide)

    from_state = jnp.zeros((tokens, channels), F32)
    carried = (coef_wide * values).astype(BF16)
    fresh = lax.dot_general(
        carried, b_part_ref[...], (((0,), (0,)), ((), ())), preferred_element_type=F32
    )
    for j in range(count_req):
        place = slice(j * state, (j + 1) * state)
        start = held_ref[j].reshape(channels, state) * flag(j, 0)
        for step in range(got_total):
            start = start + states[step][j].astype(F32) * flag(j, step + 1)
        from_state = from_state + lax.dot_general(
            c_part_ref[:, place],
            start.astype(BF16),
            (((1,), (1,)), ((), ())),
            preferred_element_type=F32,
        )
        first_head = pl.program_id(0) * heads
        for h in range(heads):
            rows = slice(h * width, (h + 1) * width)
            state_ref[j, h] = decay_ref[j, first_head + h] * start[rows] + fresh[rows, place]
    out_ref[...] = result + grown_wide * from_state + skip * values


def mixer(
    ints, own, got, cache, const, b_maps, c_maps, cum, cum_t, step_t, coef, decay, held, states
):
    tokens, channels = own.shape
    count_req, heads, width, state = held.shape
    kernel_len = cache.shape[1] + 1
    part = min(HEADS_STEP, heads)
    steps = heads // part
    wide = part * width
    columns = lambda i, *_: (0, i)
    whole = lambda i, *_: (0, 0)

    in_specs = (
        [pl.BlockSpec((tokens, wide), columns)] * (1 + len(got))
        + [
            pl.BlockSpec((count_req, kernel_len - 1, wide), lambda i, *_: (0, 0, i)),
            pl.BlockSpec((const.shape[0], wide), columns),
            pl.BlockSpec((tokens, state), whole),
            pl.BlockSpec((tokens, state), whole),
            pl.BlockSpec((1, tokens, part), lambda i, *_: (i, 0, 0)),
            pl.BlockSpec((1, part, tokens), lambda i, *_: (i, 0, 0)),
            pl.BlockSpec((1, part, tokens), lambda i, *_: (i, 0, 0)),
            pl.BlockSpec((1, tokens, part), lambda i, *_: (i, 0, 0)),
            pl.BlockSpec(memory_space=pltpu.SMEM),
        ]
        + [pl.BlockSpec((count_req, part, width, state), lambda i, *_: (0, i, 0, 0))]
        + [pl.BlockSpec((count_req, wide, state), lambda i, *_: (0, i, 0))] * len(states)
    )
    return pl.pallas_call(
        functools.partial(mixer_kernel, count_req, len(got)),
        out_shape=[
            jax.ShapeDtypeStruct((tokens, channels), F32),
            jax.ShapeDtypeStruct((count_req, heads, width, state), F32),
        ],
        grid_spec=pltpu.PrefetchScalarGridSpec(
            num_scalar_prefetch=1,
            grid=(steps,),
            in_specs=in_specs,
            out_specs=[
                pl.BlockSpec((tokens, wide), columns),
                pl.BlockSpec((count_req, part, width, state), lambda i, *_: (0, i, 0, 0)),
            ],
            scratch_shapes=[
                pltpu.VMEM((tokens, tokens), F32),
                pltpu.VMEM((tokens, count_req * state), BF16),
                pltpu.VMEM((tokens, count_req * state), BF16),
            ],
        ),
        compiler_params=params(),
        cost_estimate=cost(1e6, 1e4),
    )(
        ints, own, *got, cache, const, b_maps, c_maps, cum, cum_t, step_t, coef, decay, held,
        *states
    )


def on_device(
    x_in,
    w_xz,
    w_dt,
    w_bc,
    dt_bias,
    a_log,
    d_skip,
    conv_x_w,
    conv_x_b,
    conv_bc_w,
    conv_bc_b,
    norm_gain,
    stretch_start,
    prefix_len,
    state_slot,
    ssm_pool,
    conv_x_pool,
    conv_bc_pool,
):
    local_width = w_xz.shape[2]
    state_part = w_bc.shape[1]
    me = lax.axis_index("req")
    req_count = lax.axis_size("req")
    slot_count, heads, head_width, state = ssm_pool.shape
    group_reqs = prefix_len.shape[0]
    lags = conv_x_pool.shape[1]
    conv_width = local_width + state_part

    direct = req_count == 2 and lax.axis_size("wide") == 16
    if direct:
        own_block, block = near_blocks(x_in)

    def slots_of(index):
        asked = lax.dynamic_slice_in_dim(state_slot, index * group_reqs, group_reqs)
        return jnp.clip(asked - me * slot_count, 0, slot_count - 1)

    def conv_of(slots):
        hit = slots[:, None] == jnp.arange(slot_count)[None, :]
        parts = [
            jnp.sum(jnp.where(hit[:, :, None, None], pool[None], 0), 1)
            for pool in (conv_x_pool, conv_bc_pool)
        ]
        return jnp.concatenate(parts, 2)

    got_states = []
    for step in range(1, req_count):
        slots = slots_of((me + step) % req_count)
        packed = pack(ssm_pool, slots, (heads * head_width, state), BF16)
        got_states.append(shift_req(packed, step))

    w_step = w_dt
    if direct:
        block = after(block, packed)
        along_z = partner_2(block, "wide", 2)
        along_x = partner_2(block, "wide", 1)
        (
            w_step, state_slot, prefix_len, stretch_start, conv_x_pool, conv_bc_pool, conv_x_w,
            conv_x_b, conv_bc_w, conv_bc_b, d_skip, norm_gain, dt_bias, a_log
        ) = lax.optimization_barrier((
            (
                w_dt, state_slot, prefix_len, stretch_start, conv_x_pool, conv_bc_pool, conv_x_w,
                conv_x_b, conv_bc_w, conv_bc_b, d_skip, norm_gain, dt_bias, a_log
            ),
            block,
        ))[0]
        w_step = pinned(w_step)
    own_slots = slots_of(me)
    asked = lax.dynamic_slice_in_dim(state_slot, me * group_reqs, group_reqs)
    came_from = (me - asked // slot_count) % req_count
    live = prefix_len > 0
    flags = (live[:, None] & (came_from[:, None] == jnp.arange(req_count)[None, :])).astype(
        jnp.int32
    )
    held = pack(ssm_pool, own_slots, (heads, head_width, state), F32)
    cache = conv_of(own_slots)
    for step in range(1, req_count):
        got = shift_req(conv_of(slots_of((me + step) % req_count)), step)
        cache = jnp.where((came_from == step)[:, None, None], got, cache)
    cache = jnp.where(live[:, None, None], cache, 0).astype(F32)

    kernel_len = conv_x_w.shape[0]
    skip = jnp.repeat(d_skip, head_width)
    const_x = jnp.stack(
        [conv_x_w[k] for k in range(kernel_len)]
        + [conv_x_b, skip, norm_gain, jnp.zeros_like(skip)]
    )
    wide_heads = lambda array: jnp.pad(array, (0, state_part - heads))
    const_bc = jnp.stack(
        [conv_bc_w[k] for k in range(kernel_len)]
        + [conv_bc_b, wide_heads(dt_bias), wide_heads(a_log), jnp.zeros_like(conv_bc_b)]
    )
    ints = jnp.concatenate([stretch_start[0], flags.reshape(-1)])
    if direct:
        small = (held, w_step, const_x, const_bc, ints, cache)
        near_three = jnp.stack([block, along_z, along_x])
        both = partner_2(after(along_z, *small), "wide", 1)
        core_three = partner_2(near_three, "wide", 0)
        own_block = after(own_block, held)
        own_z = partner_2(own_block, "wide", 2)
        both = after(both[None], own_z)
        core_both = partner_2(both, "wide", 0)
        own_pair = after(jnp.stack([own_block, own_z]), both)
        own_got = partner_2(own_pair, "wide", 1)
        core_both = after(core_both, *got_states)
        theirs = quad_arrange(
            [near_three, both, core_three, core_both], [0, 4, 2, 6, 1, 5, 3, 7]
        )
        features = [own_got, theirs]
    else:
        features = features_in_general(x_in)
    w_map = jnp.concatenate([w_bc, w_step], 1)

    def project(block, kind):
        low = jnp.dot(block, w_map, preferred_element_type=F32).astype(BF16)
        low, block = lax.optimization_barrier((low, block))
        high = jnp.einsum("td,dkc->ktc", block, w_xz, preferred_element_type=F32)
        return {"map": low, "xr": high[1].astype(kind), "z": high[0].astype(kind)}

    came = {"map": [], "xr": [], "z": []}
    parts = []
    for step in range(1, req_count):
        part = lax.optimization_barrier(project(features[step], BF16))
        for name in came:
            came[name].append(shift_req(part[name], step))
        parts.append(part)
    block = features[0]
    if direct:
        own_four = jnp.concatenate([own_pair, after(block, *parts)], 0)
        own_core = partner_2(own_four, "wide", 0)
        block = quad_arrange([own_four, own_core], [0, 4, 2, 6, 1, 5, 3, 7])
    else:
        block = after(block, *parts)
    own = lax.optimization_barrier(project(block, F32))

    bc_conv, cum, cum_t, step_t, coef, decay = prep(
        ints, own["map"], came["map"], cache, const_bc, heads
    )
    wide_index = lax.axis_index("wide")
    group_span = lax.axis_size("wide") // GROUPS
    bit_total = group_span.bit_length() - 1
    joined = bc_conv
    for bit_index in range(bit_total):
        partner = partner_2(joined, "wide", bit_index)
        upper_half = wide_index // (1 << bit_index) % 2 == 1
        joined = jnp.where(
            upper_half, jnp.concatenate([partner, joined], 1), jnp.concatenate([joined, partner], 1)
        )
    state_width = joined.shape[1] // 2
    came_xr = [after(got, own["xr"], bc_conv) for got in came["xr"]]
    result, final_state = mixer(
        ints, own["xr"], came_xr, cache, const_x, joined[:, :state_width],
        joined[:, state_width:], cum, cum_t, step_t, coef, decay, held, got_states
    )
    gate = own["z"].astype(F32)
    for got in came["z"]:
        gate = gate + got.astype(F32)
    gated = result * jax.nn.silu(gate.astype(BF16).astype(F32))
    square_sum = jnp.sum(gated * gated, 1)
    for bit_index in range(bit_total):
        square_sum = square_sum + partner_2(square_sum, "wide", bit_index)
    mean_sq = square_sum / (local_width * group_span)
    normed = gated * lax.rsqrt(mean_sq + NORM_EPS)[:, None] * const_x[kernel_len + 2][None, :]
    return (normed.astype(BF16), final_state)


def solution(mesh):
    in_specs = (
        P("req", "wide"),
        P("req", None, "wide"),
        P("req", "wide"),
        P("req", "wide"),
        P("wide"),
        P("wide"),
        P("wide"),
        P(None, "wide"),
        P("wide"),
        P(None, "wide"),
        P("wide"),
        P("wide"),
        P("req", None),
        P("req"),
        P(),
        P("req", "wide", None, None),
        P("req", None, "wide"),
        P("req", None, "wide"),
    )
    out_specs = (P("req", "wide"), P("req", "wide", None, None))
    return jax.shard_map(
        on_device, mesh=mesh, in_specs=in_specs, out_specs=out_specs, check_vma=False
    )
```

```python
import functools

import jax
import jax.numpy as jnp
from jax import lax
from jax.experimental import pallas as pl
from jax.experimental.layout import Layout, with_layout_constraint
from jax.experimental.pallas import tpu as pltpu
from jax.sharding import PartitionSpec as P

GROUPS = 8
NORM_EPS = 1e-05
F32 = jnp.float32
BF16 = jnp.bfloat16
HIGH = lax.Precision.HIGHEST
VMEM_BYTES = 16 * 1024 * 1024
HEADS_STEP = 4


def cost(flops, bytes_accessed):
    return pl.CostEstimate(flops=int(flops), bytes_accessed=int(bytes_accessed), transcendentals=0)


def params(limit=VMEM_BYTES):
    return pltpu.CompilerParams(vmem_limit_bytes=limit)


def partner_2(block, axis, bit):
    count = lax.axis_size(axis)
    route = []
    for low in range(count):
        high = low | 1 << bit
        if high != low and high < count:
            route += [(low, high), (high, low)]
    return lax.ppermute(block, axis, route)


def shift_req(block, step):
    count = lax.axis_size("req")
    return lax.ppermute(block, "req", [(i, (i + step) % count) for i in range(count)])


def spread_routes():
    first, second = [], []
    for z in range(4):
        for rest in range(4):
            for r in range(2):
                place = (z * 4 + rest) * 2 + r
                other = (((z + 2) % 4) * 4 + rest) * 2 + r
                if z // 2 == r:
                    first.append((place, other))
                else:
                    first.append((place, place ^ 1))
                    second.append((place, other ^ 1))
    return first, second


def arrange_kernel(places_ref, *refs):
    out_ref = refs[-1]
    index = 0
    for ref in refs[:-1]:
        for part in range(ref.shape[0]):
            width = ref.shape[2]
            place = pl.multiple_of(places_ref[index] * width, width)
            out_ref[:, pl.ds(place, width)] = ref[part]
            index += 1


def arrange(stacks, places):
    tokens, width = stacks[0].shape[1:]
    total = sum(stack.shape[0] for stack in stacks) * width
    return pl.pallas_call(
        arrange_kernel,
        out_shape=jax.ShapeDtypeStruct((tokens, total), stacks[0].dtype),
        in_specs=[pl.BlockSpec(memory_space=pltpu.SMEM)]
        + [pl.BlockSpec(memory_space=pltpu.VMEM)] * len(stacks),
        out_specs=pl.BlockSpec(memory_space=pltpu.VMEM),
        compiler_params=params(),
        cost_estimate=cost(1e6, 1e4),
    )(places, *stacks)


def after(value, *others):
    return lax.optimization_barrier((value, others))[0]


def near_blocks(x_in):
    axes = ("wide", "req")
    first, second = spread_routes()
    first = lax.ppermute(x_in, axes, first)
    second = lax.ppermute(x_in, axes, second)
    near = lax.axis_index("wide") // 8 == lax.axis_index("req")
    return jnp.where(near, x_in, first), jnp.where(near, first, second)


def quad_arrange(stacks, apart):
    places = (lax.axis_index("wide") % 8) ^ jnp.array(apart, jnp.int32)
    return arrange(stacks, places)


def features_in_general(x_in):
    req_count = lax.axis_size("req")
    me = lax.axis_index("req")
    own = lax.all_gather(x_in, "wide", axis=1, tiled=True)
    parts = own.reshape(own.shape[0], req_count, own.shape[1] // req_count).transpose(1, 0, 2)
    got = lax.all_to_all(parts, "req", split_axis=0, concat_axis=0, tiled=True)
    return [
        lax.dynamic_index_in_dim(got, (me + step) % req_count, 0, False)
        for step in range(req_count)
    ]


def pinned(array):
    return lax.optimization_barrier(
        with_layout_constraint(array, Layout(tuple(range(array.ndim))))
    )


def token_places(starts, count_tok, shape, axis):
    position = lax.broadcasted_iota(jnp.int32, shape, axis)
    seg = jnp.full(shape, -1, jnp.int32)
    first = jnp.zeros(shape, jnp.int32)
    for start in starts:
        seg = seg + (position >= start).astype(jnp.int32)
        first = jnp.where(position >= start, start, first)
    return position, seg, first


def cached_rows(ints_ref, refs, count_req, first_flag, places, per_place, at, channels):
    rows = []
    for request in range(count_req):
        total = None
        for step, ref in enumerate(refs):
            flag = ints_ref[first_flag + request * len(refs) + step].astype(F32)
            term = ref[request].astype(F32) * flag
            total = term if total is None else total + term
        index = lax.broadcasted_iota(jnp.int32, total.shape, 0)
        rows.append([
            jnp.sum(jnp.where(index == place * per_place + at, total, 0.0), 0, keepdims=True)[
                :, :channels
            ]
            for place in range(places)
        ])
    return rows


def conv_silu(values, cache, const_ref, seg, offset):
    kernel_len = len(cache[0]) + 1
    taps = [const_ref[k : k + 1, :] for k in range(kernel_len)]
    bias = const_ref[kernel_len : kernel_len + 1, :]
    total = bias + taps[kernel_len - 1] * values
    for lag in range(1, kernel_len):
        earlier = pltpu.roll(values, lag, 0)
        total = total + taps[kernel_len - 1 - lag] * jnp.where(offset >= lag, earlier, 0.0)
    cached = jnp.zeros_like(values)
    for request in range(len(cache)):
        for place in range(kernel_len - 1):
            history = jnp.zeros_like(bias)
            for lag in range(place + 1, kernel_len):
                at = kernel_len - 1 + place - lag
                history = history + taps[kernel_len - 1 - lag] * cache[request][at]
            cached = jnp.where((seg == request) & (offset == place), history, cached)
    total = total + cached
    return total * jax.nn.sigmoid(total)


def prep_kernel(count_req, got_total, heads, per_place, places, ints_ref, own_ref, *refs):
    got = refs[:got_total]
    row_refs = refs[got_total : 2 * got_total + 1]
    const_ref, bc_ref, small_ref, decay_ref = refs[2 * got_total + 1 :]
    tokens = own_ref.shape[0]
    channels = const_ref.shape[1]
    dt_bias = const_ref[places + 2 : places + 3, :heads]
    a_log = const_ref[places + 3 : places + 4, :heads]
    starts = [ints_ref[j] for j in range(count_req)]
    total = own_ref[...].astype(F32)
    for ref in got:
        total = total + ref[...].astype(F32)
    total = total.astype(BF16).astype(F32)
    position, seg, first = token_places(starts, tokens, (tokens, channels), 0)
    cache = cached_rows(
        ints_ref, row_refs, count_req, count_req, places, per_place, per_place - 1, channels
    )
    bc = conv_silu(total[:, :channels], cache, const_ref, seg, position - first)
    bc_ref[...] = bc.astype(BF16)
    raw = total[:, channels : channels + heads] + dt_bias
    step = jnp.maximum(raw, 0.0) + jnp.log1p(jnp.exp(-jnp.abs(raw)))
    rate = step * (-jnp.exp(a_log))
    position, seg, first = token_places(starts, tokens, (tokens, tokens), 0)
    other, seg_other, first_other = token_places(starts, tokens, (tokens, tokens), 1)
    same = seg == seg_other
    mask = jnp.where(same & (position >= other), 1.0, 0.0)
    after = jnp.where(same & (position < other), 1.0, 0.0)
    left = jnp.dot(after, rate, precision=HIGH, preferred_element_type=F32)
    cum_t = lax.dot_general(
        rate, mask, (((0,), (1,)), ((), ())), precision=HIGH, preferred_element_type=F32
    )
    step_t = step.T
    coef_t = (jnp.exp(left) * step).T
    steps = small_ref.shape[0]
    part = heads // steps
    for i in range(steps):
        place = slice(i * part, (i + 1) * part)
        for row, array in enumerate((cum_t, step_t, coef_t)):
            small_ref[i, row * part : (row + 1) * part, :] = array[place, :]
    at, seg_at, _ = token_places(starts, tokens, (8, tokens), 1)
    row = lax.broadcasted_iota(jnp.int32, (8, tokens), 0)
    ends = jnp.dot(
        jnp.where(seg_at == row, 1.0, 0.0), rate, precision=HIGH, preferred_element_type=F32
    )
    decay_ref[...] = jnp.exp(ends)


def prep(ints, own, got, row_arrays, row_total, const, heads, per_place, places):
    tokens = own.shape[0]
    channels = const.shape[1]
    part = min(HEADS_STEP, heads)
    count_req = row_arrays[0].shape[0]
    whole = lambda *shape: pl.BlockSpec(shape, lambda i: (0,) * len(shape))
    shapes = [(tokens, channels), (heads // part, 3 * part, tokens), (8, heads)]
    return pl.pallas_call(
        functools.partial(prep_kernel, count_req, len(got), heads, per_place, places),
        out_shape=[
            jax.ShapeDtypeStruct(shape, kind) for shape, kind in zip(shapes, (BF16, F32, F32))
        ],
        grid=(1,),
        in_specs=[pl.BlockSpec(memory_space=pltpu.SMEM)]
        + [whole(*own.shape)] * (1 + len(got))
        + [rows_spec(array, row_total) for array in row_arrays]
        + [whole(*const.shape)],
        out_specs=[whole(*shape) for shape in shapes],
        compiler_params=params(),
        cost_estimate=cost(1e6, 1e4),
    )(ints, own, *got, *row_arrays, const)


def rows_spec(array, row_total):
    last = array.shape[1] // row_total - 1
    block = (array.shape[0], row_total, array.shape[2])
    return pl.BlockSpec(block, lambda i, *_: (0, last, 0))


def conv_rows(slot, pool_refs, row_total, lanes):
    rows = []
    for place in range(pool_refs[0].shape[0]):
        for ref in pool_refs:
            values = ref[place].astype(F32)
            index = lax.broadcasted_iota(jnp.int32, values.shape, 0)
            line = jnp.sum(jnp.where(index == slot, values, 0.0), 0, keepdims=True)
            for first in range(0, line.shape[1], lanes):
                row = line[:, first : first + lanes]
                if row.shape[1] < lanes:
                    row = jnp.concatenate(
                        [row, jnp.zeros((1, lanes - row.shape[1]), F32)], 1
                    )
                rows.append(row)
    rows += [jnp.zeros((1, lanes), F32)] * (row_total - len(rows))
    return jnp.concatenate(rows, 0)


def pack_kernel(row_total, slots_ref, pool_ref, x_ref, bc_ref, *out_refs):
    rows, lanes = pool_ref.shape[1] * pool_ref.shape[2], pool_ref.shape[3]
    slot = slots_ref[pl.program_id(0)]
    conv = conv_rows(slot, (x_ref, bc_ref), row_total, lanes)
    if len(out_refs) == 1:
        out_ref = out_refs[0]
        out_ref[0, :rows, :] = pool_ref[0].reshape(rows, lanes).astype(out_ref.dtype)
        out_ref[0, rows:, :] = conv.astype(out_ref.dtype)
    else:
        out_refs[0][...] = pool_ref[...]
        out_refs[1][0] = conv


def pack(pool, conv_pools, row_total, slots, to_send):
    count_req = slots.shape[0]
    _, heads, width, state = pool.shape
    block = (1, heads, width, state)
    conv_pools = [jnp.transpose(array, (1, 0, 2)) for array in conv_pools]
    shapes = [((1, heads * width + row_total, state), BF16)]
    if not to_send:
        shapes = [(block, F32), ((1, row_total, state), F32)]
    return pl.pallas_call(
        functools.partial(pack_kernel, row_total),
        out_shape=[
            jax.ShapeDtypeStruct((count_req,) + shape[1:], kind) for shape, kind in shapes
        ],
        grid_spec=pltpu.PrefetchScalarGridSpec(
            num_scalar_prefetch=1,
            grid=(count_req,),
            in_specs=[pl.BlockSpec(block, lambda j, slots: (slots[j], 0, 0, 0))]
            + [pl.BlockSpec(array.shape, lambda j, slots: (0, 0, 0)) for array in conv_pools],
            out_specs=[
                pl.BlockSpec(shape, functools.partial(lambda n, j, _: (j,) + (0,) * n, len(shape) - 1))
                for shape, _ in shapes
            ],
        ),
        compiler_params=params(3 * VMEM_BYTES),
        cost_estimate=cost(0, 6 * pool[0].size * count_req),
    )(slots, pool, *conv_pools)


def mixer_kernel(count_req, got_total, per_place, places, ints_ref, *refs):
    own_ref = refs[0]
    got = refs[1 : 1 + got_total]
    rest = refs[1 + got_total :]
    row_refs = rest[: got_total + 1]
    const_ref, b_ref, c_ref, small_ref, decay_ref, held_ref = rest[got_total + 1 : got_total + 7]
    states = rest[got_total + 7 : 2 * got_total + 7]
    out_ref, state_ref, scores_ref, c_part_ref, b_part_ref = rest[2 * got_total + 7 :]
    skip = const_ref[places + 2 : places + 3, :]

    def flag(request, step):
        place = count_req + request * (got_total + 1) + step
        return ints_ref[place].astype(F32)

    tokens, channels = own_ref.shape
    heads, width, state = held_ref.shape[1:]
    starts = [ints_ref[j] for j in range(count_req)]

    @pl.when(pl.program_id(0) == 0)
    def _():
        position, seg, _ = token_places(starts, tokens, (tokens, tokens), 0)
        other, seg_other, _ = token_places(starts, tokens, (tokens, tokens), 1)
        scores = lax.dot_general(
            c_ref[...], b_ref[...], (((1,), (1,)), ((), ())), preferred_element_type=F32
        )
        scores_ref[...] = jnp.where((seg == seg_other) & (position >= other), scores, 0.0)
        _, seg, _ = token_places(starts, tokens, (tokens, state), 0)
        b_maps = b_ref[...].astype(F32)
        c_maps = c_ref[...].astype(F32)
        for j in range(count_req):
            place = slice(j * state, (j + 1) * state)
            b_part_ref[:, place] = jnp.where(seg == j, b_maps, 0.0).astype(BF16)
            c_part_ref[:, place] = jnp.where(seg == j, c_maps, 0.0).astype(BF16)

    total = own_ref[...].astype(F32)
    for ref in got:
        total = total + ref[...].astype(F32)
    total = total.astype(BF16).astype(F32)
    position, seg, first = token_places(starts, tokens, (tokens, channels), 0)
    cache = cached_rows(
        ints_ref, row_refs, count_req, count_req, places, per_place, pl.program_id(0), channels
    )
    values = conv_silu(total, cache, const_ref, seg, position - first)
    inputs = values.astype(BF16)
    values = inputs.astype(F32)

    lane_head = lax.broadcasted_iota(jnp.int32, (tokens, channels), 1) // width
    scores = scores_ref[...]
    small = small_ref[0]
    tall = small.T
    cum_t, step_t = small[:heads], small[heads : 2 * heads]
    cum, coef = tall[:, :heads], tall[:, 2 * heads :]
    grown = jnp.exp(cum)
    grown_wide = jnp.zeros((tokens, channels), F32)
    coef_wide = jnp.zeros((tokens, channels), F32)
    result = jnp.zeros((tokens, channels), F32)
    for h in range(heads):
        gap = jnp.minimum(cum[:, h : h + 1] - cum_t[h : h + 1, :], 0.0)
        weights = (jnp.exp(gap) * scores * step_t[h : h + 1, :]).astype(BF16)
        mine = lane_head == h
        result = result + jnp.dot(
            weights, jnp.where(mine, values, 0.0).astype(BF16), preferred_element_type=F32
        )
        grown_wide = jnp.where(mine, grown[:, h : h + 1], grown_wide)
        coef_wide = jnp.where(mine, coef[:, h : h + 1], coef_wide)

    from_state = jnp.zeros((tokens, channels), F32)
    carried = (coef_wide * values).astype(BF16)
    fresh = lax.dot_general(
        carried, b_part_ref[...], (((0,), (0,)), ((), ())), preferred_element_type=F32
    )
    for j in range(count_req):
        place = slice(j * state, (j + 1) * state)
        start = held_ref[j].reshape(channels, state) * flag(j, 0)
        for step in range(got_total):
            start = start + states[step][j].astype(F32) * flag(j, step + 1)
        from_state = from_state + lax.dot_general(
            c_part_ref[:, place],
            start.astype(BF16),
            (((1,), (1,)), ((), ())),
            preferred_element_type=F32,
        )
        first_head = pl.program_id(0) * heads
        for h in range(heads):
            rows = slice(h * width, (h + 1) * width)
            state_ref[j, h] = decay_ref[j, first_head + h] * start[rows] + fresh[rows, place]
    out_ref[...] = result + grown_wide * from_state + skip * values


def mixer(
    ints, own, got, row_arrays, row_total, const, b_maps, c_maps, small, decay, held, states,
    per_place, places
):
    tokens, channels = own.shape
    count_req, heads, width, state = held.shape
    part = min(HEADS_STEP, heads)
    steps = heads // part
    wide = part * width
    columns = lambda i, *_: (0, i)
    whole = lambda i, *_: (0, 0)

    in_specs = (
        [pl.BlockSpec((tokens, wide), columns)] * (1 + len(got))
        + [rows_spec(array, row_total) for array in row_arrays]
        + [
            pl.BlockSpec((const.shape[0], wide), columns),
            pl.BlockSpec((tokens, state), whole),
            pl.BlockSpec((tokens, state), whole),
            pl.BlockSpec((1,) + small.shape[1:], lambda i, *_: (i, 0, 0)),
            pl.BlockSpec(memory_space=pltpu.SMEM),
        ]
        + [pl.BlockSpec((count_req, part, width, state), lambda i, *_: (0, i, 0, 0))]
        + [pl.BlockSpec((count_req, wide, state), lambda i, *_: (0, i, 0))] * len(states)
    )
    return pl.pallas_call(
        functools.partial(mixer_kernel, count_req, len(got), per_place, places),
        out_shape=[
            jax.ShapeDtypeStruct((tokens, channels), F32),
            jax.ShapeDtypeStruct((count_req, heads, width, state), F32),
        ],
        grid_spec=pltpu.PrefetchScalarGridSpec(
            num_scalar_prefetch=1,
            grid=(steps,),
            in_specs=in_specs,
            out_specs=[
                pl.BlockSpec((tokens, wide), columns),
                pl.BlockSpec((count_req, part, width, state), lambda i, *_: (0, i, 0, 0)),
            ],
            scratch_shapes=[
                pltpu.VMEM((tokens, tokens), F32),
                pltpu.VMEM((tokens, count_req * state), BF16),
                pltpu.VMEM((tokens, count_req * state), BF16),
            ],
        ),
        compiler_params=params(),
        cost_estimate=cost(1e6, 1e4),
    )(
        ints, own, *got, *row_arrays, const, b_maps, c_maps, small, decay, held, *states
    )


def on_device(
    x_in,
    w_xz,
    w_dt,
    w_bc,
    dt_bias,
    a_log,
    d_skip,
    conv_x_w,
    conv_x_b,
    conv_bc_w,
    conv_bc_b,
    norm_gain,
    stretch_start,
    prefix_len,
    state_slot,
    ssm_pool,
    conv_x_pool,
    conv_bc_pool,
):
    local_width = w_xz.shape[2]
    state_part = w_bc.shape[1]
    me = lax.axis_index("req")
    req_count = lax.axis_size("req")
    slot_count, heads, head_width, state = ssm_pool.shape
    group_reqs = prefix_len.shape[0]
    lags = conv_x_pool.shape[1]

    direct = req_count == 2 and lax.axis_size("wide") == 16
    if direct:
        own_block, block = near_blocks(x_in)

    def slots_of(index):
        asked = lax.dynamic_slice_in_dim(state_slot, index * group_reqs, group_reqs)
        return jnp.clip(asked - me * slot_count, 0, slot_count - 1)

    per_place = -(-local_width // state) - (-state_part // state)
    row_total = -(-lags * per_place // 16) * 16
    conv_pools = (conv_x_pool, conv_bc_pool)
    got_states = []
    for step in range(1, req_count):
        slots = slots_of((me + step) % req_count)
        packed = pack(ssm_pool, conv_pools, row_total, slots, True)[0]
        got_states.append(shift_req(packed, step))

    w_step = w_dt
    if direct:
        block = after(block, packed)
        along_z = partner_2(block, "wide", 2)
        along_x = partner_2(block, "wide", 1)
        (
            w_step, state_slot, prefix_len, stretch_start, conv_x_w,
            conv_x_b, conv_bc_w, conv_bc_b, d_skip, norm_gain, dt_bias, a_log
        ) = lax.optimization_barrier((
            (
                w_dt, state_slot, prefix_len, stretch_start, conv_x_w,
                conv_x_b, conv_bc_w, conv_bc_b, d_skip, norm_gain, dt_bias, a_log
            ),
            block,
        ))[0]
        w_step = pinned(w_step)
    own_slots = slots_of(me)
    asked = lax.dynamic_slice_in_dim(state_slot, me * group_reqs, group_reqs)
    came_from = (me - asked // slot_count) % req_count
    live = prefix_len > 0
    flags = (live[:, None] & (came_from[:, None] == jnp.arange(req_count)[None, :])).astype(
        jnp.int32
    )
    held, own_rows = pack(ssm_pool, conv_pools, row_total, own_slots, False)

    kernel_len = conv_x_w.shape[0]
    skip = jnp.repeat(d_skip, head_width)
    const_x = jnp.stack(
        [conv_x_w[k] for k in range(kernel_len)]
        + [conv_x_b, skip, norm_gain, jnp.zeros_like(skip)]
    )
    wide_heads = lambda array: jnp.pad(array, (0, state_part - heads))
    const_bc = jnp.stack(
        [conv_bc_w[k] for k in range(kernel_len)]
        + [conv_bc_b, wide_heads(dt_bias), wide_heads(a_log), jnp.zeros_like(conv_bc_b)]
    )
    ints = jnp.concatenate([stretch_start[0], flags.reshape(-1)])
    if direct:
        small = (held, w_step, const_x, const_bc, ints)
        near_three = jnp.stack([block, along_z, along_x])
        both = partner_2(after(along_z, *small), "wide", 1)
        core_three = partner_2(near_three, "wide", 0)
        own_block = after(own_block, held)
        own_z = partner_2(own_block, "wide", 2)
        both = after(both[None], own_z)
        core_both = partner_2(both, "wide", 0)
        own_pair = after(jnp.stack([own_block, own_z]), both)
        own_got = partner_2(own_pair, "wide", 1)
        core_both = after(core_both, *got_states)
        theirs = quad_arrange(
            [near_three, both, core_three, core_both], [0, 4, 2, 6, 1, 5, 3, 7]
        )
        features = [own_got, theirs]
    else:
        features = features_in_general(x_in)
    w_map = jnp.concatenate([w_bc, w_step], 1)

    def project(block, kind):
        low = jnp.dot(block, w_map, preferred_element_type=F32).astype(BF16)
        low, block = lax.optimization_barrier((low, block))
        high = jnp.einsum("td,dkc->ktc", block, w_xz, preferred_element_type=F32)
        return {"map": low, "xr": high[1].astype(kind), "z": high[0].astype(kind)}

    came = {"map": [], "xr": [], "z": []}
    parts = []
    for step in range(1, req_count):
        part = lax.optimization_barrier(project(features[step], BF16))
        for name in came:
            came[name].append(shift_req(part[name], step))
        parts.append(part)
    block = features[0]
    if direct:
        own_four = jnp.concatenate([own_pair, after(block, *parts)], 0)
        own_core = partner_2(own_four, "wide", 0)
        block = quad_arrange([own_four, own_core], [0, 4, 2, 6, 1, 5, 3, 7])
    else:
        block = after(block, *parts)
    own = lax.optimization_barrier(project(block, F32))

    row_arrays = [own_rows] + got_states
    bc_conv, small, decay = prep(
        ints, own["map"], came["map"], row_arrays, row_total, const_bc, heads, per_place, lags
    )
    wide_index = lax.axis_index("wide")
    group_span = lax.axis_size("wide") // GROUPS
    bit_total = group_span.bit_length() - 1
    joined = bc_conv
    for bit_index in range(bit_total):
        partner = partner_2(joined, "wide", bit_index)
        upper_half = wide_index // (1 << bit_index) % 2 == 1
        joined = jnp.where(
            upper_half, jnp.concatenate([partner, joined], 1), jnp.concatenate([joined, partner], 1)
        )
    state_width = joined.shape[1] // 2
    came_xr = [after(got, own["xr"], bc_conv) for got in came["xr"]]
    result, final_state = mixer(
        ints, own["xr"], came_xr, row_arrays, row_total, const_x, joined[:, :state_width],
        joined[:, state_width:], small, decay, held, got_states, per_place, lags
    )
    gate = own["z"].astype(F32)
    for got in came["z"]:
        gate = gate + got.astype(F32)
    gated = result * jax.nn.silu(gate.astype(BF16).astype(F32))
    square_sum = jnp.sum(gated * gated, 1)
    for bit_index in range(bit_total):
        square_sum = square_sum + partner_2(square_sum, "wide", bit_index)
    mean_sq = square_sum / (local_width * group_span)
    normed = gated * lax.rsqrt(mean_sq + NORM_EPS)[:, None] * const_x[kernel_len + 2][None, :]
    return (normed.astype(BF16), final_state)


def solution(mesh):
    in_specs = (
        P("req", "wide"),
        P("req", None, "wide"),
        P("req", "wide"),
        P("req", "wide"),
        P("wide"),
        P("wide"),
        P("wide"),
        P(None, "wide"),
        P("wide"),
        P(None, "wide"),
        P("wide"),
        P("wide"),
        P("req", None),
        P("req"),
        P(),
        P("req", "wide", None, None),
        P("req", None, "wide"),
        P("req", None, "wide"),
    )
    out_specs = (P("req", "wide"), P("req", "wide", None, None))
    return jax.shard_map(
        on_device, mesh=mesh, in_specs=in_specs, out_specs=out_specs, check_vma=False
    )
```

```python
import functools

import jax
import jax.numpy as jnp
from jax import lax
from jax.experimental import pallas as pl
from jax.experimental.layout import Layout, with_layout_constraint
from jax.experimental.pallas import tpu as pltpu
from jax.sharding import PartitionSpec as P

GROUPS = 8
NORM_EPS = 1e-05
F32 = jnp.float32
BF16 = jnp.bfloat16
HIGH = lax.Precision.HIGHEST
VMEM_BYTES = 16 * 1024 * 1024
HEADS_STEP = 4


def cost(flops, bytes_accessed):
    return pl.CostEstimate(flops=int(flops), bytes_accessed=int(bytes_accessed), transcendentals=0)


def params(limit=VMEM_BYTES):
    return pltpu.CompilerParams(vmem_limit_bytes=limit)


def partner_2(block, axis, bit):
    count = lax.axis_size(axis)
    route = []
    for low in range(count):
        high = low | 1 << bit
        if high != low and high < count:
            route += [(low, high), (high, low)]
    return lax.ppermute(block, axis, route)


def shift_req(block, step):
    count = lax.axis_size("req")
    return lax.ppermute(block, "req", [(i, (i + step) % count) for i in range(count)])


def spread_routes():
    first, second = [], []
    for z in range(4):
        for rest in range(4):
            for r in range(2):
                place = (z * 4 + rest) * 2 + r
                other = (((z + 2) % 4) * 4 + rest) * 2 + r
                if z // 2 == r:
                    first.append((place, other))
                else:
                    first.append((place, place ^ 1))
                    second.append((place, other ^ 1))
    return first, second


def arrange_kernel(places_ref, *refs):
    out_ref = refs[-1]
    index = 0
    for ref in refs[:-1]:
        for part in range(ref.shape[0]):
            width = ref.shape[2]
            place = pl.multiple_of(places_ref[index] * width, width)
            out_ref[:, pl.ds(place, width)] = ref[part]
            index += 1


def arrange(stacks, places):
    tokens, width = stacks[0].shape[1:]
    total = sum(stack.shape[0] for stack in stacks) * width
    return pl.pallas_call(
        arrange_kernel,
        out_shape=jax.ShapeDtypeStruct((tokens, total), stacks[0].dtype),
        in_specs=[pl.BlockSpec(memory_space=pltpu.SMEM)]
        + [pl.BlockSpec(memory_space=pltpu.VMEM)] * len(stacks),
        out_specs=pl.BlockSpec(memory_space=pltpu.VMEM),
        compiler_params=params(),
        cost_estimate=cost(1e6, 1e4),
    )(places, *stacks)


def after(value, *others):
    return lax.optimization_barrier((value, others))[0]


def near_blocks(x_in):
    axes = ("wide", "req")
    first, second = spread_routes()
    first = lax.ppermute(x_in, axes, first)
    second = lax.ppermute(x_in, axes, second)
    near = lax.axis_index("wide") // 8 == lax.axis_index("req")
    return jnp.where(near, x_in, first), jnp.where(near, first, second)


def quad_arrange(stacks, apart):
    places = (lax.axis_index("wide") % 8) ^ jnp.array(apart, jnp.int32)
    return arrange(stacks, places)


def features_in_general(x_in):
    req_count = lax.axis_size("req")
    me = lax.axis_index("req")
    own = lax.all_gather(x_in, "wide", axis=1, tiled=True)
    parts = own.reshape(own.shape[0], req_count, own.shape[1] // req_count).transpose(1, 0, 2)
    got = lax.all_to_all(parts, "req", split_axis=0, concat_axis=0, tiled=True)
    return [
        lax.dynamic_index_in_dim(got, (me + step) % req_count, 0, False)
        for step in range(req_count)
    ]


def pinned(array):
    return lax.optimization_barrier(
        with_layout_constraint(array, Layout(tuple(range(array.ndim))))
    )


def token_places(starts, count_tok, shape, axis):
    position = lax.broadcasted_iota(jnp.int32, shape, axis)
    seg = jnp.full(shape, -1, jnp.int32)
    first = jnp.zeros(shape, jnp.int32)
    for start in starts:
        seg = seg + (position >= start).astype(jnp.int32)
        first = jnp.where(position >= start, start, first)
    return position, seg, first


def cached_rows(ints_ref, refs, count_req, first_flag, places, per_place, at, channels):
    rows = []
    for request in range(count_req):
        total = None
        for step, ref in enumerate(refs):
            flag = ints_ref[first_flag + request * len(refs) + step].astype(F32)
            term = ref[request].astype(F32) * flag
            total = term if total is None else total + term
        index = lax.broadcasted_iota(jnp.int32, total.shape, 0)
        rows.append([
            jnp.sum(jnp.where(index == place * per_place + at, total, 0.0), 0, keepdims=True)[
                :, :channels
            ]
            for place in range(places)
        ])
    return rows


def conv_silu(values, cache, const_ref, seg, offset):
    kernel_len = len(cache[0]) + 1
    taps = [const_ref[k : k + 1, :] for k in range(kernel_len)]
    bias = const_ref[kernel_len : kernel_len + 1, :]
    total = bias + taps[kernel_len - 1] * values
    for lag in range(1, kernel_len):
        earlier = pltpu.roll(values, lag, 0)
        total = total + taps[kernel_len - 1 - lag] * jnp.where(offset >= lag, earlier, 0.0)
    cached = jnp.zeros_like(values)
    for request in range(len(cache)):
        for place in range(kernel_len - 1):
            history = jnp.zeros_like(bias)
            for lag in range(place + 1, kernel_len):
                at = kernel_len - 1 + place - lag
                history = history + taps[kernel_len - 1 - lag] * cache[request][at]
            cached = jnp.where((seg == request) & (offset == place), history, cached)
    total = total + cached
    return total * jax.nn.sigmoid(total)


def prep_kernel(count_req, got_total, heads, per_place, places, ints_ref, own_ref, *refs):
    got = refs[:got_total]
    row_refs = refs[got_total : 2 * got_total + 1]
    const_ref, bc_ref, small_ref, decay_ref = refs[2 * got_total + 1 :]
    tokens = own_ref.shape[0]
    channels = const_ref.shape[1]
    dt_bias = const_ref[places + 2 : places + 3, :heads]
    a_log = const_ref[places + 3 : places + 4, :heads]
    starts = [ints_ref[j] for j in range(count_req)]
    total = own_ref[...].astype(F32)
    for ref in got:
        total = total + ref[...].astype(F32)
    total = total.astype(BF16).astype(F32)
    position, seg, first = token_places(starts, tokens, (tokens, channels), 0)
    cache = cached_rows(
        ints_ref, row_refs, count_req, count_req, places, per_place, per_place - 1, channels
    )
    bc = conv_silu(total[:, :channels], cache, const_ref, seg, position - first)
    bc_ref[...] = bc.astype(BF16)
    raw = total[:, channels : channels + heads] + dt_bias
    step = jnp.maximum(raw, 0.0) + jnp.log1p(jnp.exp(-jnp.abs(raw)))
    rate = step * (-jnp.exp(a_log))
    position, seg, first = token_places(starts, tokens, (tokens, tokens), 0)
    other, seg_other, first_other = token_places(starts, tokens, (tokens, tokens), 1)
    same = seg == seg_other
    mask = jnp.where(same & (position >= other), 1.0, 0.0)
    after = jnp.where(same & (position < other), 1.0, 0.0)
    left = jnp.dot(after, rate, precision=HIGH, preferred_element_type=F32)
    cum_t = lax.dot_general(
        rate, mask, (((0,), (1,)), ((), ())), precision=HIGH, preferred_element_type=F32
    )
    step_t = step.T
    coef_t = (jnp.exp(left) * step).T
    steps = small_ref.shape[0]
    part = heads // steps
    for i in range(steps):
        place = slice(i * part, (i + 1) * part)
        for row, array in enumerate((cum_t, step_t, coef_t)):
            small_ref[i, row * part : (row + 1) * part, :] = array[place, :]
    at, seg_at, _ = token_places(starts, tokens, (8, tokens), 1)
    row = lax.broadcasted_iota(jnp.int32, (8, tokens), 0)
    ends = jnp.dot(
        jnp.where(seg_at == row, 1.0, 0.0), rate, precision=HIGH, preferred_element_type=F32
    )
    decay_ref[...] = jnp.exp(ends)


def prep(ints, own, got, row_arrays, row_total, const, heads, per_place, places):
    tokens = own.shape[0]
    channels = const.shape[1]
    part = min(HEADS_STEP, heads)
    count_req = row_arrays[0].shape[0]
    whole = lambda *shape: pl.BlockSpec(shape, lambda i: (0,) * len(shape))
    shapes = [(tokens, channels), (heads // part, 3 * part, tokens), (8, heads)]
    return pl.pallas_call(
        functools.partial(prep_kernel, count_req, len(got), heads, per_place, places),
        out_shape=[
            jax.ShapeDtypeStruct(shape, kind) for shape, kind in zip(shapes, (BF16, F32, F32))
        ],
        grid=(1,),
        in_specs=[pl.BlockSpec(memory_space=pltpu.SMEM)]
        + [whole(*own.shape)] * (1 + len(got))
        + [rows_spec(array, row_total) for array in row_arrays]
        + [whole(*const.shape)],
        out_specs=[whole(*shape) for shape in shapes],
        compiler_params=params(),
        cost_estimate=cost(1e6, 1e4),
    )(ints, own, *got, *row_arrays, const)


def rows_spec(array, row_total):
    last = array.shape[1] // row_total - 1
    block = (array.shape[0], row_total, array.shape[2])
    return pl.BlockSpec(block, lambda i, *_: (0, last, 0))


def conv_rows(slot, pool_refs, row_total, lanes):
    rows = []
    for place in range(pool_refs[0].shape[0]):
        for ref in pool_refs:
            values = ref[place].astype(F32)
            index = lax.broadcasted_iota(jnp.int32, values.shape, 0)
            line = jnp.sum(jnp.where(index == slot, values, 0.0), 0, keepdims=True)
            for first in range(0, line.shape[1], lanes):
                row = line[:, first : first + lanes]
                if row.shape[1] < lanes:
                    row = jnp.concatenate(
                        [row, jnp.zeros((1, lanes - row.shape[1]), F32)], 1
                    )
                rows.append(row)
    rows += [jnp.zeros((1, lanes), F32)] * (row_total - len(rows))
    return jnp.concatenate(rows, 0)


def pack_kernel(row_total, slots_ref, pool_ref, x_ref, bc_ref, out_ref):
    rows, lanes = pool_ref.shape[1] * pool_ref.shape[2], pool_ref.shape[3]
    slot = slots_ref[pl.program_id(0)]
    conv = conv_rows(slot, (x_ref, bc_ref), row_total, lanes)
    out_ref[0, :rows, :] = pool_ref[0].reshape(rows, lanes).astype(out_ref.dtype)
    out_ref[0, rows:, :] = conv.astype(out_ref.dtype)


def pack(pool, conv_pools, row_total, slots):
    count_req = slots.shape[0]
    _, heads, width, state = pool.shape
    conv_pools = [jnp.transpose(array, (1, 0, 2)) for array in conv_pools]
    out_block = (1, heads * width + row_total, state)
    return pl.pallas_call(
        functools.partial(pack_kernel, row_total),
        out_shape=jax.ShapeDtypeStruct((count_req,) + out_block[1:], BF16),
        grid_spec=pltpu.PrefetchScalarGridSpec(
            num_scalar_prefetch=1,
            grid=(count_req,),
            in_specs=[
                pl.BlockSpec((1, heads, width, state), lambda j, slots: (slots[j], 0, 0, 0))
            ]
            + [pl.BlockSpec(array.shape, lambda j, slots: (0, 0, 0)) for array in conv_pools],
            out_specs=pl.BlockSpec(out_block, lambda j, slots: (j, 0, 0)),
        ),
        compiler_params=params(3 * VMEM_BYTES),
        cost_estimate=cost(0, 6 * pool[0].size * count_req),
    )(slots, pool, *conv_pools)


def own_rows_kernel(row_total, first_slot, ints_ref, x_ref, bc_ref, out_ref):
    for request in range(out_ref.shape[0]):
        slot = ints_ref[first_slot + request]
        out_ref[request] = conv_rows(slot, (x_ref, bc_ref), row_total, out_ref.shape[2])


def own_rows_of(conv_pools, row_total, ints, count_req, lanes):
    vmem = pl.BlockSpec(memory_space=pltpu.VMEM)
    first_slot = ints.shape[0] - count_req
    return pl.pallas_call(
        functools.partial(own_rows_kernel, row_total, first_slot),
        out_shape=jax.ShapeDtypeStruct((count_req, row_total, lanes), F32),
        in_specs=[pl.BlockSpec(memory_space=pltpu.SMEM), vmem, vmem],
        out_specs=vmem,
        compiler_params=params(),
        cost_estimate=cost(1e6, 1e4),
    )(ints, *[jnp.transpose(array, (1, 0, 2)) for array in conv_pools])


def mixer_kernel(count_req, got_total, per_place, places, ints_ref, *refs):
    own_ref = refs[0]
    got = refs[1 : 1 + got_total]
    rest = refs[1 + got_total :]
    row_refs = rest[: got_total + 1]
    const_ref, b_ref, c_ref, small_ref, decay_ref = rest[got_total + 1 : got_total + 6]
    rest = rest[got_total + 6 :]
    pools, states = rest[:count_req], rest[count_req : count_req + got_total]
    out_ref, state_ref, scores_ref, c_part_ref, b_part_ref = rest[count_req + got_total :]
    skip = const_ref[places + 2 : places + 3, :]

    def flag(request, step):
        place = count_req + request * (got_total + 1) + step
        return ints_ref[place].astype(F32)

    tokens, channels = own_ref.shape
    heads, width, state = pools[0].shape[1:]
    starts = [ints_ref[j] for j in range(count_req)]

    @pl.when(pl.program_id(0) == 0)
    def _():
        position, seg, _ = token_places(starts, tokens, (tokens, tokens), 0)
        other, seg_other, _ = token_places(starts, tokens, (tokens, tokens), 1)
        scores = lax.dot_general(
            c_ref[...], b_ref[...], (((1,), (1,)), ((), ())), preferred_element_type=F32
        )
        scores_ref[...] = jnp.where((seg == seg_other) & (position >= other), scores, 0.0)
        _, seg, _ = token_places(starts, tokens, (tokens, state), 0)
        b_maps = b_ref[...].astype(F32)
        c_maps = c_ref[...].astype(F32)
        for j in range(count_req):
            place = slice(j * state, (j + 1) * state)
            b_part_ref[:, place] = jnp.where(seg == j, b_maps, 0.0).astype(BF16)
            c_part_ref[:, place] = jnp.where(seg == j, c_maps, 0.0).astype(BF16)

    total = own_ref[...].astype(F32)
    for ref in got:
        total = total + ref[...].astype(F32)
    total = total.astype(BF16).astype(F32)
    position, seg, first = token_places(starts, tokens, (tokens, channels), 0)
    cache = cached_rows(
        ints_ref, row_refs, count_req, count_req, places, per_place, pl.program_id(0), channels
    )
    values = conv_silu(total, cache, const_ref, seg, position - first)
    inputs = values.astype(BF16)
    values = inputs.astype(F32)

    lane_head = lax.broadcasted_iota(jnp.int32, (tokens, channels), 1) // width
    scores = scores_ref[...]
    small = small_ref[0]
    tall = small.T
    cum_t, step_t = small[:heads], small[heads : 2 * heads]
    cum, coef = tall[:, :heads], tall[:, 2 * heads :]
    grown = jnp.exp(cum)
    grown_wide = jnp.zeros((tokens, channels), F32)
    coef_wide = jnp.zeros((tokens, channels), F32)
    result = jnp.zeros((tokens, channels), F32)
    for h in range(heads):
        gap = jnp.minimum(cum[:, h : h + 1] - cum_t[h : h + 1, :], 0.0)
        weights = (jnp.exp(gap) * scores * step_t[h : h + 1, :]).astype(BF16)
        mine = lane_head == h
        result = result + jnp.dot(
            weights, jnp.where(mine, values, 0.0).astype(BF16), preferred_element_type=F32
        )
        grown_wide = jnp.where(mine, grown[:, h : h + 1], grown_wide)
        coef_wide = jnp.where(mine, coef[:, h : h + 1], coef_wide)

    from_state = jnp.zeros((tokens, channels), F32)
    carried = (coef_wide * values).astype(BF16)
    fresh = lax.dot_general(
        carried, b_part_ref[...], (((0,), (0,)), ((), ())), preferred_element_type=F32
    )
    for j in range(count_req):
        place = slice(j * state, (j + 1) * state)
        start = pools[j][0].reshape(channels, state) * flag(j, 0)
        for step in range(got_total):
            start = start + states[step][j].astype(F32) * flag(j, step + 1)
        from_state = from_state + lax.dot_general(
            c_part_ref[:, place],
            start.astype(BF16),
            (((1,), (1,)), ((), ())),
            preferred_element_type=F32,
        )
        first_head = pl.program_id(0) * heads
        for h in range(heads):
            rows = slice(h * width, (h + 1) * width)
            state_ref[j, h] = decay_ref[j, first_head + h] * start[rows] + fresh[rows, place]
    out_ref[...] = result + grown_wide * from_state + skip * values


def mixer(
    ints, own, got, row_arrays, row_total, const, b_maps, c_maps, small, decay, pool, states,
    per_place, places
):
    tokens, channels = own.shape
    _, heads, width, state = pool.shape
    count_req = row_arrays[0].shape[0]
    first_slot = ints.shape[0] - count_req
    part = min(HEADS_STEP, heads)
    steps = heads // part
    wide = part * width
    columns = lambda i, *_: (0, i)
    whole = lambda i, *_: (0, 0)

    in_specs = (
        [pl.BlockSpec((tokens, wide), columns)] * (1 + len(got))
        + [rows_spec(array, row_total) for array in row_arrays]
        + [
            pl.BlockSpec((const.shape[0], wide), columns),
            pl.BlockSpec((tokens, state), whole),
            pl.BlockSpec((tokens, state), whole),
            pl.BlockSpec((1,) + small.shape[1:], lambda i, *_: (i, 0, 0)),
            pl.BlockSpec(memory_space=pltpu.SMEM),
        ]
        + [
            pl.BlockSpec(
                (1, part, width, state),
                functools.partial(lambda at, i, ints: (ints[at], i, 0, 0), first_slot + j),
            )
            for j in range(count_req)
        ]
        + [pl.BlockSpec((count_req, wide, state), lambda i, *_: (0, i, 0))] * len(states)
    )
    return pl.pallas_call(
        functools.partial(mixer_kernel, count_req, len(got), per_place, places),
        out_shape=[
            jax.ShapeDtypeStruct((tokens, channels), F32),
            jax.ShapeDtypeStruct((count_req, heads, width, state), F32),
        ],
        grid_spec=pltpu.PrefetchScalarGridSpec(
            num_scalar_prefetch=1,
            grid=(steps,),
            in_specs=in_specs,
            out_specs=[
                pl.BlockSpec((tokens, wide), columns),
                pl.BlockSpec((count_req, part, width, state), lambda i, *_: (0, i, 0, 0)),
            ],
            scratch_shapes=[
                pltpu.VMEM((tokens, tokens), F32),
                pltpu.VMEM((tokens, count_req * state), BF16),
                pltpu.VMEM((tokens, count_req * state), BF16),
            ],
        ),
        compiler_params=params(3 * VMEM_BYTES),
        cost_estimate=cost(1e6, 1e4),
    )(
        ints, own, *got, *row_arrays, const, b_maps, c_maps, small, decay,
        *([pool] * count_req), *states
    )


def on_device(
    x_in,
    w_xz,
    w_dt,
    w_bc,
    dt_bias,
    a_log,
    d_skip,
    conv_x_w,
    conv_x_b,
    conv_bc_w,
    conv_bc_b,
    norm_gain,
    stretch_start,
    prefix_len,
    state_slot,
    ssm_pool,
    conv_x_pool,
    conv_bc_pool,
):
    local_width = w_xz.shape[2]
    state_part = w_bc.shape[1]
    me = lax.axis_index("req")
    req_count = lax.axis_size("req")
    slot_count, heads, head_width, state = ssm_pool.shape
    group_reqs = prefix_len.shape[0]
    lags = conv_x_pool.shape[1]

    direct = req_count == 2 and lax.axis_size("wide") == 16
    if direct:
        own_block, block = near_blocks(x_in)

    def slots_of(index):
        asked = lax.dynamic_slice_in_dim(state_slot, index * group_reqs, group_reqs)
        return jnp.clip(asked - me * slot_count, 0, slot_count - 1)

    per_place = -(-local_width // state) - (-state_part // state)
    row_total = -(-lags * per_place // 16) * 16
    conv_pools = (conv_x_pool, conv_bc_pool)
    got_states = []
    for step in range(1, req_count):
        slots = slots_of((me + step) % req_count)
        packed = pack(ssm_pool, conv_pools, row_total, slots)
        got_states.append(shift_req(packed, step))

    w_step = w_dt
    if direct:
        block = after(block, packed)
        along_z = partner_2(block, "wide", 2)
        along_x = partner_2(block, "wide", 1)
        (
            w_step, state_slot, prefix_len, stretch_start, conv_x_w,
            conv_x_b, conv_bc_w, conv_bc_b, d_skip, norm_gain, dt_bias, a_log
        ) = lax.optimization_barrier((
            (
                w_dt, state_slot, prefix_len, stretch_start, conv_x_w,
                conv_x_b, conv_bc_w, conv_bc_b, d_skip, norm_gain, dt_bias, a_log
            ),
            block,
        ))[0]
        w_step = pinned(w_step)
    own_slots = slots_of(me)
    asked = lax.dynamic_slice_in_dim(state_slot, me * group_reqs, group_reqs)
    came_from = (me - asked // slot_count) % req_count
    live = prefix_len > 0
    flags = (live[:, None] & (came_from[:, None] == jnp.arange(req_count)[None, :])).astype(
        jnp.int32
    )

    kernel_len = conv_x_w.shape[0]
    skip = jnp.repeat(d_skip, head_width)
    const_x = jnp.stack(
        [conv_x_w[k] for k in range(kernel_len)]
        + [conv_x_b, skip, norm_gain, jnp.zeros_like(skip)]
    )
    wide_heads = lambda array: jnp.pad(array, (0, state_part - heads))
    const_bc = jnp.stack(
        [conv_bc_w[k] for k in range(kernel_len)]
        + [conv_bc_b, wide_heads(dt_bias), wide_heads(a_log), jnp.zeros_like(conv_bc_b)]
    )
    ints = jnp.concatenate([stretch_start[0], flags.reshape(-1), own_slots])
    own_rows = own_rows_of(conv_pools, row_total, ints, group_reqs, state)
    if direct:
        both = partner_2(along_z, "wide", 1)
        own_block = after(own_block, along_z)
        own_z = partner_2(own_block, "wide", 2)
        near_three = jnp.stack([block, along_z, along_x])
        core_three = partner_2(near_three, "wide", 0)
        both = after(both[None], own_z, w_step, const_x, const_bc, ints, own_rows)
        core_both = partner_2(both, "wide", 0)
        own_pair = after(jnp.stack([own_block, own_z]), both)
        own_got = partner_2(own_pair, "wide", 1)
        core_both = after(core_both, *got_states)
        theirs = quad_arrange(
            [near_three, both, core_three, core_both], [0, 4, 2, 6, 1, 5, 3, 7]
        )
        features = [own_got, theirs]
    else:
        features = features_in_general(x_in)
    w_map = jnp.concatenate([w_bc, w_step], 1)

    def project(block, kind):
        low = jnp.dot(block, w_map, preferred_element_type=F32).astype(BF16)
        low, block = lax.optimization_barrier((low, block))
        high = jnp.einsum("td,dkc->ktc", block, w_xz, preferred_element_type=F32)
        return {"map": low, "xr": high[1].astype(kind), "z": high[0].astype(kind)}

    came = {"map": [], "xr": [], "z": []}
    parts = []
    for step in range(1, req_count):
        part = lax.optimization_barrier(project(features[step], BF16))
        for name in came:
            came[name].append(shift_req(part[name], step))
        parts.append(part)
    block = features[0]
    if direct:
        own_four = jnp.concatenate([own_pair, after(block, *parts)], 0)
        own_core = partner_2(own_four, "wide", 0)
        block = quad_arrange([own_four, own_core], [0, 4, 2, 6, 1, 5, 3, 7])
    else:
        block = after(block, *parts)
    own = lax.optimization_barrier(project(block, F32))

    row_arrays = [own_rows] + got_states
    bc_conv, small, decay = prep(
        ints, own["map"], came["map"], row_arrays, row_total, const_bc, heads, per_place, lags
    )
    wide_index = lax.axis_index("wide")
    group_span = lax.axis_size("wide") // GROUPS
    bit_total = group_span.bit_length() - 1
    joined = bc_conv
    for bit_index in range(bit_total):
        partner = partner_2(joined, "wide", bit_index)
        upper_half = wide_index // (1 << bit_index) % 2 == 1
        joined = jnp.where(
            upper_half, jnp.concatenate([partner, joined], 1), jnp.concatenate([joined, partner], 1)
        )
    state_width = joined.shape[1] // 2
    came_xr = [after(got, own["xr"], bc_conv) for got in came["xr"]]
    result, final_state = mixer(
        ints, own["xr"], came_xr, row_arrays, row_total, const_x, joined[:, :state_width],
        joined[:, state_width:], small, decay, ssm_pool, got_states,
        per_place, lags
    )
    gate = own["z"].astype(F32)
    for got in came["z"]:
        gate = gate + got.astype(F32)
    gated = result * jax.nn.silu(gate.astype(BF16).astype(F32))
    square_sum = jnp.sum(gated * gated, 1)
    for bit_index in range(bit_total):
        square_sum = square_sum + partner_2(square_sum, "wide", bit_index)
    mean_sq = square_sum / (local_width * group_span)
    normed = gated * lax.rsqrt(mean_sq + NORM_EPS)[:, None] * const_x[kernel_len + 2][None, :]
    return (normed.astype(BF16), final_state)


def solution(mesh):
    in_specs = (
        P("req", "wide"),
        P("req", None, "wide"),
        P("req", "wide"),
        P("req", "wide"),
        P("wide"),
        P("wide"),
        P("wide"),
        P(None, "wide"),
        P("wide"),
        P(None, "wide"),
        P("wide"),
        P("wide"),
        P("req", None),
        P("req"),
        P(),
        P("req", "wide", None, None),
        P("req", None, "wide"),
        P("req", None, "wide"),
    )
    out_specs = (P("req", "wide"), P("req", "wide", None, None))
    return jax.shard_map(
        on_device, mesh=mesh, in_specs=in_specs, out_specs=out_specs, check_vma=False
    )
```

```python
import functools

import jax
import jax.numpy as jnp
from jax import lax
from jax.experimental import pallas as pl
from jax.experimental.layout import Layout, with_layout_constraint
from jax.experimental.pallas import tpu as pltpu
from jax.sharding import PartitionSpec as P

GROUPS = 8
NORM_EPS = 1e-05
F32 = jnp.float32
BF16 = jnp.bfloat16
HIGH = lax.Precision.HIGHEST
VMEM_BYTES = 16 * 1024 * 1024
HEADS_STEP = 4


def cost(flops, bytes_accessed):
    return pl.CostEstimate(flops=int(flops), bytes_accessed=int(bytes_accessed), transcendentals=0)


def params(limit=VMEM_BYTES):
    return pltpu.CompilerParams(vmem_limit_bytes=limit)


def partner_2(block, axis, bit):
    count = lax.axis_size(axis)
    route = []
    for low in range(count):
        high = low | 1 << bit
        if high != low and high < count:
            route += [(low, high), (high, low)]
    return lax.ppermute(block, axis, route)


def shift_req(block, step):
    count = lax.axis_size("req")
    return lax.ppermute(block, "req", [(i, (i + step) % count) for i in range(count)])


def spread_routes():
    far, across, diagonal = [], [], []
    for z in range(4):
        for rest in range(4):
            for r in range(2):
                place = (z * 4 + rest) * 2 + r
                other = (((z + 2) % 4) * 4 + rest) * 2 + r
                if z // 2 == r:
                    far.append((place, other))
                else:
                    across.append((place, place ^ 1))
                    diagonal.append((place, other ^ 1))
    return far, across, diagonal


def arrange_kernel(places_ref, *refs):
    out_ref = refs[-1]
    index = 0
    for ref in refs[:-1]:
        for part in range(ref.shape[0]):
            width = ref.shape[2]
            place = pl.multiple_of(places_ref[index] * width, width)
            out_ref[:, pl.ds(place, width)] = ref[part]
            index += 1


def arrange(stacks, places):
    tokens, width = stacks[0].shape[1:]
    total = sum(stack.shape[0] for stack in stacks) * width
    return pl.pallas_call(
        arrange_kernel,
        out_shape=jax.ShapeDtypeStruct((tokens, total), stacks[0].dtype),
        in_specs=[pl.BlockSpec(memory_space=pltpu.SMEM)]
        + [pl.BlockSpec(memory_space=pltpu.VMEM)] * len(stacks),
        out_specs=pl.BlockSpec(memory_space=pltpu.VMEM),
        compiler_params=params(),
        cost_estimate=cost(1e6, 1e4),
    )(places, *stacks)


def after(value, *others):
    return lax.optimization_barrier((value, others))[0]


def is_near():
    return lax.axis_index("wide") // 8 == lax.axis_index("req")


def first_block(x_in):
    _, across, diagonal = spread_routes()
    diagonal = lax.ppermute(x_in, ("wide", "req"), diagonal)
    across = lax.ppermute(x_in, ("wide", "req"), across)
    return jnp.where(is_near(), across, diagonal)


def first_own_block(x_in):
    far = lax.ppermute(x_in, ("wide", "req"), spread_routes()[0])
    return jnp.where(is_near(), x_in, far)


def quad_arrange(stacks, apart):
    places = (lax.axis_index("wide") % 8) ^ jnp.array(apart, jnp.int32)
    return arrange(stacks, places)


def features_in_general(x_in):
    req_count = lax.axis_size("req")
    me = lax.axis_index("req")
    own = lax.all_gather(x_in, "wide", axis=1, tiled=True)
    parts = own.reshape(own.shape[0], req_count, own.shape[1] // req_count).transpose(1, 0, 2)
    got = lax.all_to_all(parts, "req", split_axis=0, concat_axis=0, tiled=True)
    return [
        lax.dynamic_index_in_dim(got, (me + step) % req_count, 0, False)
        for step in range(req_count)
    ]


def pinned(array):
    return lax.optimization_barrier(
        with_layout_constraint(array, Layout(tuple(range(array.ndim))))
    )


def token_places(starts, count_tok, shape, axis):
    position = lax.broadcasted_iota(jnp.int32, shape, axis)
    seg = jnp.full(shape, -1, jnp.int32)
    first = jnp.zeros(shape, jnp.int32)
    for start in starts:
        seg = seg + (position >= start).astype(jnp.int32)
        first = jnp.where(position >= start, start, first)
    return position, seg, first


def cached_rows(ints_ref, refs, count_req, first_flag, places, per_place, at, channels):
    rows = []
    for request in range(count_req):
        total = None
        for step, ref in enumerate(refs):
            flag = ints_ref[first_flag + request * len(refs) + step].astype(F32)
            term = ref[request].astype(F32) * flag
            total = term if total is None else total + term
        index = lax.broadcasted_iota(jnp.int32, total.shape, 0)
        rows.append([
            jnp.sum(jnp.where(index == place * per_place + at, total, 0.0), 0, keepdims=True)[
                :, :channels
            ]
            for place in range(places)
        ])
    return rows


def conv_silu(values, cache, const_ref, seg, offset):
    kernel_len = len(cache[0]) + 1
    taps = [const_ref[k : k + 1, :] for k in range(kernel_len)]
    bias = const_ref[kernel_len : kernel_len + 1, :]
    total = bias + taps[kernel_len - 1] * values
    for lag in range(1, kernel_len):
        earlier = pltpu.roll(values, lag, 0)
        total = total + taps[kernel_len - 1 - lag] * jnp.where(offset >= lag, earlier, 0.0)
    cached = jnp.zeros_like(values)
    for request in range(len(cache)):
        for place in range(kernel_len - 1):
            history = jnp.zeros_like(bias)
            for lag in range(place + 1, kernel_len):
                at = kernel_len - 1 + place - lag
                history = history + taps[kernel_len - 1 - lag] * cache[request][at]
            cached = jnp.where((seg == request) & (offset == place), history, cached)
    total = total + cached
    return total * jax.nn.sigmoid(total)


def prep_kernel(count_req, got_total, heads, per_place, places, ints_ref, own_ref, *refs):
    got = refs[:got_total]
    row_refs = refs[got_total : 2 * got_total + 1]
    const_ref, bc_ref, small_ref, decay_ref = refs[2 * got_total + 1 :]
    tokens = own_ref.shape[0]
    channels = const_ref.shape[1]
    dt_bias = const_ref[places + 2 : places + 3, :heads]
    a_log = const_ref[places + 3 : places + 4, :heads]
    starts = [ints_ref[j] for j in range(count_req)]
    total = own_ref[...].astype(F32)
    for ref in got:
        total = total + ref[...].astype(F32)
    total = total.astype(BF16).astype(F32)
    position, seg, first = token_places(starts, tokens, (tokens, channels), 0)
    cache = cached_rows(
        ints_ref, row_refs, count_req, count_req, places, per_place, per_place - 1, channels
    )
    bc = conv_silu(total[:, :channels], cache, const_ref, seg, position - first)
    bc_ref[...] = bc.astype(BF16)
    raw = total[:, channels : channels + heads] + dt_bias
    step = jnp.maximum(raw, 0.0) + jnp.log1p(jnp.exp(-jnp.abs(raw)))
    rate = step * (-jnp.exp(a_log))
    position, seg, first = token_places(starts, tokens, (tokens, tokens), 0)
    other, seg_other, first_other = token_places(starts, tokens, (tokens, tokens), 1)
    same = seg == seg_other
    mask = jnp.where(same & (position >= other), 1.0, 0.0)
    after = jnp.where(same & (position < other), 1.0, 0.0)
    left = jnp.dot(after, rate, precision=HIGH, preferred_element_type=F32)
    cum_t = lax.dot_general(
        rate, mask, (((0,), (1,)), ((), ())), precision=HIGH, preferred_element_type=F32
    )
    step_t = step.T
    coef_t = (jnp.exp(left) * step).T
    steps = small_ref.shape[0]
    part = heads // steps
    for i in range(steps):
        place = slice(i * part, (i + 1) * part)
        for row, array in enumerate((cum_t, step_t, coef_t)):
            small_ref[i, row * part : (row + 1) * part, :] = array[place, :]
    at, seg_at, _ = token_places(starts, tokens, (8, tokens), 1)
    row = lax.broadcasted_iota(jnp.int32, (8, tokens), 0)
    ends = jnp.dot(
        jnp.where(seg_at == row, 1.0, 0.0), rate, precision=HIGH, preferred_element_type=F32
    )
    decay_ref[...] = jnp.exp(ends)


def prep(ints, own, got, row_arrays, row_total, const, heads, per_place, places):
    tokens = own.shape[0]
    channels = const.shape[1]
    part = min(HEADS_STEP, heads)
    count_req = row_arrays[0].shape[0]
    whole = lambda *shape: pl.BlockSpec(shape, lambda i: (0,) * len(shape))
    shapes = [(tokens, channels), (heads // part, 3 * part, tokens), (8, heads)]
    return pl.pallas_call(
        functools.partial(prep_kernel, count_req, len(got), heads, per_place, places),
        out_shape=[
            jax.ShapeDtypeStruct(shape, kind) for shape, kind in zip(shapes, (BF16, F32, F32))
        ],
        grid=(1,),
        in_specs=[pl.BlockSpec(memory_space=pltpu.SMEM)]
        + [whole(*own.shape)] * (1 + len(got))
        + [rows_spec(array, row_total) for array in row_arrays]
        + [whole(*const.shape)],
        out_specs=[whole(*shape) for shape in shapes],
        compiler_params=params(),
        cost_estimate=cost(1e6, 1e4),
    )(ints, own, *got, *row_arrays, const)


def rows_spec(array, row_total):
    last = array.shape[1] // row_total - 1
    block = (array.shape[0], row_total, array.shape[2])
    return pl.BlockSpec(block, lambda i, *_: (0, last, 0))


def conv_rows(slot, pool_refs, row_total, lanes):
    rows = []
    for place in range(pool_refs[0].shape[0]):
        for ref in pool_refs:
            values = ref[place].astype(F32)
            index = lax.broadcasted_iota(jnp.int32, values.shape, 0)
            line = jnp.sum(jnp.where(index == slot, values, 0.0), 0, keepdims=True)
            for first in range(0, line.shape[1], lanes):
                row = line[:, first : first + lanes]
                if row.shape[1] < lanes:
                    row = jnp.concatenate(
                        [row, jnp.zeros((1, lanes - row.shape[1]), F32)], 1
                    )
                rows.append(row)
    rows += [jnp.zeros((1, lanes), F32)] * (row_total - len(rows))
    return jnp.concatenate(rows, 0)


def pack_kernel(row_total, slots_ref, pool_ref, x_ref, bc_ref, out_ref):
    rows, lanes = pool_ref.shape[1] * pool_ref.shape[2], pool_ref.shape[3]
    slot = slots_ref[pl.program_id(0)]
    conv = conv_rows(slot, (x_ref, bc_ref), row_total, lanes)
    out_ref[0, :rows, :] = pool_ref[0].reshape(rows, lanes).astype(out_ref.dtype)
    out_ref[0, rows:, :] = conv.astype(out_ref.dtype)


def pack(pool, conv_pools, row_total, slots):
    count_req = slots.shape[0]
    _, heads, width, state = pool.shape
    conv_pools = [jnp.transpose(array, (1, 0, 2)) for array in conv_pools]
    out_block = (1, heads * width + row_total, state)
    return pl.pallas_call(
        functools.partial(pack_kernel, row_total),
        out_shape=jax.ShapeDtypeStruct((count_req,) + out_block[1:], BF16),
        grid_spec=pltpu.PrefetchScalarGridSpec(
            num_scalar_prefetch=1,
            grid=(count_req,),
            in_specs=[
                pl.BlockSpec((1, heads, width, state), lambda j, slots: (slots[j], 0, 0, 0))
            ]
            + [pl.BlockSpec(array.shape, lambda j, slots: (0, 0, 0)) for array in conv_pools],
            out_specs=pl.BlockSpec(out_block, lambda j, slots: (j, 0, 0)),
        ),
        compiler_params=params(3 * VMEM_BYTES),
        cost_estimate=cost(0, 6 * pool[0].size * count_req),
    )(slots, pool, *conv_pools)


def own_rows_kernel(row_total, first_slot, ints_ref, x_ref, bc_ref, out_ref):
    for request in range(out_ref.shape[0]):
        slot = ints_ref[first_slot + request]
        out_ref[request] = conv_rows(slot, (x_ref, bc_ref), row_total, out_ref.shape[2])


def own_rows_of(conv_pools, row_total, ints, count_req, lanes):
    vmem = pl.BlockSpec(memory_space=pltpu.VMEM)
    first_slot = ints.shape[0] - count_req
    return pl.pallas_call(
        functools.partial(own_rows_kernel, row_total, first_slot),
        out_shape=jax.ShapeDtypeStruct((count_req, row_total, lanes), F32),
        in_specs=[pl.BlockSpec(memory_space=pltpu.SMEM), vmem, vmem],
        out_specs=vmem,
        compiler_params=params(),
        cost_estimate=cost(1e6, 1e4),
    )(ints, *[jnp.transpose(array, (1, 0, 2)) for array in conv_pools])


def mixer_kernel(count_req, got_total, per_place, places, ints_ref, *refs):
    own_ref = refs[0]
    got = refs[1 : 1 + got_total]
    rest = refs[1 + got_total :]
    row_refs = rest[: got_total + 1]
    const_ref, b_ref, c_ref, small_ref, decay_ref = rest[got_total + 1 : got_total + 6]
    rest = rest[got_total + 6 :]
    pools, states = rest[:count_req], rest[count_req : count_req + got_total]
    out_ref, state_ref, scores_ref, c_part_ref, b_part_ref = rest[count_req + got_total :]
    skip = const_ref[places + 2 : places + 3, :]

    def flag(request, step):
        place = count_req + request * (got_total + 1) + step
        return ints_ref[place].astype(F32)

    tokens, channels = own_ref.shape
    heads, width, state = pools[0].shape[1:]
    starts = [ints_ref[j] for j in range(count_req)]

    @pl.when(pl.program_id(0) == 0)
    def _():
        position, seg, _ = token_places(starts, tokens, (tokens, tokens), 0)
        other, seg_other, _ = token_places(starts, tokens, (tokens, tokens), 1)
        scores = lax.dot_general(
            c_ref[...], b_ref[...], (((1,), (1,)), ((), ())), preferred_element_type=F32
        )
        scores_ref[...] = jnp.where((seg == seg_other) & (position >= other), scores, 0.0)
        _, seg, _ = token_places(starts, tokens, (tokens, state), 0)
        b_maps = b_ref[...].astype(F32)
        c_maps = c_ref[...].astype(F32)
        for j in range(count_req):
            place = slice(j * state, (j + 1) * state)
            b_part_ref[:, place] = jnp.where(seg == j, b_maps, 0.0).astype(BF16)
            c_part_ref[:, place] = jnp.where(seg == j, c_maps, 0.0).astype(BF16)

    total = own_ref[...].astype(F32)
    for ref in got:
        total = total + ref[...].astype(F32)
    total = total.astype(BF16).astype(F32)
    position, seg, first = token_places(starts, tokens, (tokens, channels), 0)
    cache = cached_rows(
        ints_ref, row_refs, count_req, count_req, places, per_place, pl.program_id(0), channels
    )
    values = conv_silu(total, cache, const_ref, seg, position - first)
    inputs = values.astype(BF16)
    values = inputs.astype(F32)

    lane_head = lax.broadcasted_iota(jnp.int32, (tokens, channels), 1) // width
    scores = scores_ref[...]
    small = small_ref[0]
    tall = small.T
    cum_t, step_t = small[:heads], small[heads : 2 * heads]
    cum, coef = tall[:, :heads], tall[:, 2 * heads :]
    grown = jnp.exp(cum)
    grown_wide = jnp.zeros((tokens, channels), F32)
    coef_wide = jnp.zeros((tokens, channels), F32)
    result = jnp.zeros((tokens, channels), F32)
    for h in range(heads):
        gap = jnp.minimum(cum[:, h : h + 1] - cum_t[h : h + 1, :], 0.0)
        weights = (jnp.exp(gap) * scores * step_t[h : h + 1, :]).astype(BF16)
        mine = lane_head == h
        result = result + jnp.dot(
            weights, jnp.where(mine, values, 0.0).astype(BF16), preferred_element_type=F32
        )
        grown_wide = jnp.where(mine, grown[:, h : h + 1], grown_wide)
        coef_wide = jnp.where(mine, coef[:, h : h + 1], coef_wide)

    from_state = jnp.zeros((tokens, channels), F32)
    carried = (coef_wide * values).astype(BF16)
    fresh = lax.dot_general(
        carried, b_part_ref[...], (((0,), (0,)), ((), ())), preferred_element_type=F32
    )
    for j in range(count_req):
        place = slice(j * state, (j + 1) * state)
        start = pools[j][0].reshape(channels, state) * flag(j, 0)
        for step in range(got_total):
            start = start + states[step][j].astype(F32) * flag(j, step + 1)
        from_state = from_state + lax.dot_general(
            c_part_ref[:, place],
            start.astype(BF16),
            (((1,), (1,)), ((), ())),
            preferred_element_type=F32,
        )
        first_head = pl.program_id(0) * heads
        for h in range(heads):
            rows = slice(h * width, (h + 1) * width)
            state_ref[j, h] = decay_ref[j, first_head + h] * start[rows] + fresh[rows, place]
    out_ref[...] = result + grown_wide * from_state + skip * values


def mixer(
    ints, own, got, row_arrays, row_total, const, b_maps, c_maps, small, decay, pool, states,
    per_place, places
):
    tokens, channels = own.shape
    _, heads, width, state = pool.shape
    count_req = row_arrays[0].shape[0]
    first_slot = ints.shape[0] - count_req
    part = min(HEADS_STEP, heads)
    steps = heads // part
    wide = part * width
    columns = lambda i, *_: (0, i)
    whole = lambda i, *_: (0, 0)

    in_specs = (
        [pl.BlockSpec((tokens, wide), columns)] * (1 + len(got))
        + [rows_spec(array, row_total) for array in row_arrays]
        + [
            pl.BlockSpec((const.shape[0], wide), columns),
            pl.BlockSpec((tokens, state), whole),
            pl.BlockSpec((tokens, state), whole),
            pl.BlockSpec((1,) + small.shape[1:], lambda i, *_: (i, 0, 0)),
            pl.BlockSpec(memory_space=pltpu.SMEM),
        ]
        + [
            pl.BlockSpec(
                (1, part, width, state),
                functools.partial(lambda at, i, ints: (ints[at], i, 0, 0), first_slot + j),
            )
            for j in range(count_req)
        ]
        + [pl.BlockSpec((count_req, wide, state), lambda i, *_: (0, i, 0))] * len(states)
    )
    return pl.pallas_call(
        functools.partial(mixer_kernel, count_req, len(got), per_place, places),
        out_shape=[
            jax.ShapeDtypeStruct((tokens, channels), F32),
            jax.ShapeDtypeStruct((count_req, heads, width, state), F32),
        ],
        grid_spec=pltpu.PrefetchScalarGridSpec(
            num_scalar_prefetch=1,
            grid=(steps,),
            in_specs=in_specs,
            out_specs=[
                pl.BlockSpec((tokens, wide), columns),
                pl.BlockSpec((count_req, part, width, state), lambda i, *_: (0, i, 0, 0)),
            ],
            scratch_shapes=[
                pltpu.VMEM((tokens, tokens), F32),
                pltpu.VMEM((tokens, count_req * state), BF16),
                pltpu.VMEM((tokens, count_req * state), BF16),
            ],
        ),
        compiler_params=params(3 * VMEM_BYTES),
        cost_estimate=cost(1e6, 1e4),
    )(
        ints, own, *got, *row_arrays, const, b_maps, c_maps, small, decay,
        *([pool] * count_req), *states
    )


def on_device(
    x_in,
    w_xz,
    w_dt,
    w_bc,
    dt_bias,
    a_log,
    d_skip,
    conv_x_w,
    conv_x_b,
    conv_bc_w,
    conv_bc_b,
    norm_gain,
    stretch_start,
    prefix_len,
    state_slot,
    ssm_pool,
    conv_x_pool,
    conv_bc_pool,
):
    local_width = w_xz.shape[2]
    state_part = w_bc.shape[1]
    me = lax.axis_index("req")
    req_count = lax.axis_size("req")
    slot_count, heads, head_width, state = ssm_pool.shape
    group_reqs = prefix_len.shape[0]
    lags = conv_x_pool.shape[1]

    direct = req_count == 2 and lax.axis_size("wide") == 16
    if direct:
        block = first_block(x_in)

    def slots_of(index):
        asked = lax.dynamic_slice_in_dim(state_slot, index * group_reqs, group_reqs)
        return jnp.clip(asked - me * slot_count, 0, slot_count - 1)

    per_place = -(-local_width // state) - (-state_part // state)
    row_total = -(-lags * per_place // 16) * 16
    conv_pools = (conv_x_pool, conv_bc_pool)
    got_states = []
    for step in range(1, req_count):
        slots = slots_of((me + step) % req_count)
        packed = pack(ssm_pool, conv_pools, row_total, slots)
        got_states.append(shift_req(packed, step))

    w_step = w_dt
    if direct:
        own_block = first_own_block(after(x_in, packed))
        block = after(block, packed)
        along_z = partner_2(block, "wide", 2)
        along_x = partner_2(block, "wide", 1)
        (
            w_step, state_slot, prefix_len, stretch_start, conv_x_w,
            conv_x_b, conv_bc_w, conv_bc_b, d_skip, norm_gain, dt_bias, a_log
        ) = lax.optimization_barrier((
            (
                w_dt, state_slot, prefix_len, stretch_start, conv_x_w,
                conv_x_b, conv_bc_w, conv_bc_b, d_skip, norm_gain, dt_bias, a_log
            ),
            block,
        ))[0]
        w_step = pinned(w_step)
    own_slots = slots_of(me)
    asked = lax.dynamic_slice_in_dim(state_slot, me * group_reqs, group_reqs)
    came_from = (me - asked // slot_count) % req_count
    live = prefix_len > 0
    flags = (live[:, None] & (came_from[:, None] == jnp.arange(req_count)[None, :])).astype(
        jnp.int32
    )

    kernel_len = conv_x_w.shape[0]
    skip = jnp.repeat(d_skip, head_width)
    const_x = jnp.stack(
        [conv_x_w[k] for k in range(kernel_len)]
        + [conv_x_b, skip, norm_gain, jnp.zeros_like(skip)]
    )
    wide_heads = lambda array: jnp.pad(array, (0, state_part - heads))
    const_bc = jnp.stack(
        [conv_bc_w[k] for k in range(kernel_len)]
        + [conv_bc_b, wide_heads(dt_bias), wide_heads(a_log), jnp.zeros_like(conv_bc_b)]
    )
    ints = jnp.concatenate([stretch_start[0], flags.reshape(-1), own_slots])
    own_rows = own_rows_of(conv_pools, row_total, ints, group_reqs, state)
    if direct:
        both = partner_2(along_z, "wide", 1)
        own_block = after(own_block, along_z)
        own_z = partner_2(own_block, "wide", 2)
        near_three = jnp.stack([block, along_z, along_x])
        core_three = partner_2(near_three, "wide", 0)
        both = after(both[None], own_z, w_step, const_x, const_bc, ints, own_rows)
        core_both = partner_2(both, "wide", 0)
        own_pair = after(jnp.stack([own_block, own_z]), both)
        own_got = partner_2(own_pair, "wide", 1)
        core_both = after(core_both, *got_states)
        theirs = quad_arrange(
            [near_three, both, core_three, core_both], [0, 4, 2, 6, 1, 5, 3, 7]
        )
        features = [own_got, theirs]
    else:
        features = features_in_general(x_in)
    w_map = jnp.concatenate([w_bc, w_step], 1)

    def project(block, kind):
        low = jnp.dot(block, w_map, preferred_element_type=F32).astype(BF16)
        low, block = lax.optimization_barrier((low, block))
        high = jnp.einsum("td,dkc->ktc", block, w_xz, preferred_element_type=F32)
        return {"map": low, "xr": high[1].astype(kind), "z": high[0].astype(kind)}

    came = {"map": [], "xr": [], "z": []}
    parts = []
    for step in range(1, req_count):
        part = lax.optimization_barrier(project(features[step], BF16))
        for name in came:
            came[name].append(shift_req(part[name], step))
        parts.append(part)
    block = features[0]
    if direct:
        own_four = jnp.concatenate([own_pair, after(block, *parts)], 0)
        own_core = partner_2(own_four, "wide", 0)
        block = quad_arrange([own_four, own_core], [0, 4, 2, 6, 1, 5, 3, 7])
    else:
        block = after(block, *parts)
    own = lax.optimization_barrier(project(block, F32))

    row_arrays = [own_rows] + got_states
    bc_conv, small, decay = prep(
        ints, own["map"], came["map"], row_arrays, row_total, const_bc, heads, per_place, lags
    )
    wide_index = lax.axis_index("wide")
    group_span = lax.axis_size("wide") // GROUPS
    bit_total = group_span.bit_length() - 1
    joined = bc_conv
    for bit_index in range(bit_total):
        partner = partner_2(joined, "wide", bit_index)
        upper_half = wide_index // (1 << bit_index) % 2 == 1
        joined = jnp.where(
            upper_half, jnp.concatenate([partner, joined], 1), jnp.concatenate([joined, partner], 1)
        )
    state_width = joined.shape[1] // 2
    came_xr = [after(got, own["xr"], bc_conv) for got in came["xr"]]
    result, final_state = mixer(
        ints, own["xr"], came_xr, row_arrays, row_total, const_x, joined[:, :state_width],
        joined[:, state_width:], small, decay, ssm_pool, got_states,
        per_place, lags
    )
    gate = own["z"].astype(F32)
    for got in came["z"]:
        gate = gate + got.astype(F32)
    gated = result * jax.nn.silu(gate.astype(BF16).astype(F32))
    square_sum = jnp.sum(gated * gated, 1)
    for bit_index in range(bit_total):
        square_sum = square_sum + partner_2(square_sum, "wide", bit_index)
    mean_sq = square_sum / (local_width * group_span)
    normed = gated * lax.rsqrt(mean_sq + NORM_EPS)[:, None] * const_x[kernel_len + 2][None, :]
    return (normed.astype(BF16), final_state)


def solution(mesh):
    in_specs = (
        P("req", "wide"),
        P("req", None, "wide"),
        P("req", "wide"),
        P("req", "wide"),
        P("wide"),
        P("wide"),
        P("wide"),
        P(None, "wide"),
        P("wide"),
        P(None, "wide"),
        P("wide"),
        P("wide"),
        P("req", None),
        P("req"),
        P(),
        P("req", "wide", None, None),
        P("req", None, "wide"),
        P("req", None, "wide"),
    )
    out_specs = (P("req", "wide"), P("req", "wide", None, None))
    return jax.shard_map(
        on_device, mesh=mesh, in_specs=in_specs, out_specs=out_specs, check_vma=False
    )
```

```python
import functools

import jax
import jax.numpy as jnp
from jax import lax
from jax.experimental import pallas as pl
from jax.experimental.layout import Layout, with_layout_constraint
from jax.experimental.pallas import tpu as pltpu
from jax.sharding import PartitionSpec as P

GROUPS = 8
NORM_EPS = 1e-05
F32 = jnp.float32
BF16 = jnp.bfloat16
HIGH = lax.Precision.HIGHEST
VMEM_BYTES = 16 * 1024 * 1024
HEADS_STEP = 4


def cost(flops, bytes_accessed):
    return pl.CostEstimate(flops=int(flops), bytes_accessed=int(bytes_accessed), transcendentals=0)


def params(limit=VMEM_BYTES):
    return pltpu.CompilerParams(vmem_limit_bytes=limit)


def partner_2(block, axis, bit):
    count = lax.axis_size(axis)
    route = []
    for low in range(count):
        high = low | 1 << bit
        if high != low and high < count:
            route += [(low, high), (high, low)]
    return lax.ppermute(block, axis, route)


def shift_req(block, step):
    count = lax.axis_size("req")
    return lax.ppermute(block, "req", [(i, (i + step) % count) for i in range(count)])


def spread_routes():
    first, second = [], []
    for z in range(4):
        for rest in range(4):
            for r in range(2):
                place = (z * 4 + rest) * 2 + r
                other = (((z + 2) % 4) * 4 + rest) * 2 + r
                if z // 2 == r:
                    first.append((place, other))
                else:
                    first.append((place, place ^ 1))
                    second.append((place, other ^ 1))
    return first, second


def arrange_kernel(places_ref, *refs):
    out_ref = refs[-1]
    index = 0
    for ref in refs[:-1]:
        for part in range(ref.shape[0]):
            width = ref.shape[2]
            place = pl.multiple_of(places_ref[index] * width, width)
            out_ref[:, pl.ds(place, width)] = ref[part]
            index += 1


def arrange(stacks, places):
    tokens, width = stacks[0].shape[1:]
    total = sum(stack.shape[0] for stack in stacks) * width
    return pl.pallas_call(
        arrange_kernel,
        out_shape=jax.ShapeDtypeStruct((tokens, total), stacks[0].dtype),
        in_specs=[pl.BlockSpec(memory_space=pltpu.SMEM)]
        + [pl.BlockSpec(memory_space=pltpu.VMEM)] * len(stacks),
        out_specs=pl.BlockSpec(memory_space=pltpu.VMEM),
        compiler_params=params(),
        cost_estimate=cost(1e6, 1e4),
    )(places, *stacks)


def after(value, *others):
    return lax.optimization_barrier((value, others))[0]


def near_blocks(x_in):
    axes = ("wide", "req")
    first, second = spread_routes()
    second = lax.ppermute(x_in, axes, second)
    first = lax.ppermute(x_in, axes, first)
    near = lax.axis_index("wide") // 8 == lax.axis_index("req")
    return jnp.where(near, x_in, first), jnp.where(near, first, second)


def quad_arrange(stacks, apart):
    places = (lax.axis_index("wide") % 8) ^ jnp.array(apart, jnp.int32)
    return arrange(stacks, places)


def features_in_general(x_in):
    req_count = lax.axis_size("req")
    me = lax.axis_index("req")
    own = lax.all_gather(x_in, "wide", axis=1, tiled=True)
    parts = own.reshape(own.shape[0], req_count, own.shape[1] // req_count).transpose(1, 0, 2)
    got = lax.all_to_all(parts, "req", split_axis=0, concat_axis=0, tiled=True)
    return [
        lax.dynamic_index_in_dim(got, (me + step) % req_count, 0, False)
        for step in range(req_count)
    ]


def pinned(array):
    return lax.optimization_barrier(
        with_layout_constraint(array, Layout(tuple(range(array.ndim))))
    )


def token_places(starts, count_tok, shape, axis):
    position = lax.broadcasted_iota(jnp.int32, shape, axis)
    seg = jnp.full(shape, -1, jnp.int32)
    first = jnp.zeros(shape, jnp.int32)
    for start in starts:
        seg = seg + (position >= start).astype(jnp.int32)
        first = jnp.where(position >= start, start, first)
    return position, seg, first


def cached_rows(ints_ref, refs, count_req, first_flag, places, per_place, at, channels):
    rows = []
    for request in range(count_req):
        total = None
        for step, ref in enumerate(refs):
            flag = ints_ref[first_flag + request * len(refs) + step].astype(F32)
            term = ref[request].astype(F32) * flag
            total = term if total is None else total + term
        index = lax.broadcasted_iota(jnp.int32, total.shape, 0)
        rows.append([
            jnp.sum(jnp.where(index == place * per_place + at, total, 0.0), 0, keepdims=True)[
                :, :channels
            ]
            for place in range(places)
        ])
    return rows


def conv_silu(values, cache, const_ref, seg, offset):
    kernel_len = len(cache[0]) + 1
    taps = [const_ref[k : k + 1, :] for k in range(kernel_len)]
    bias = const_ref[kernel_len : kernel_len + 1, :]
    total = bias + taps[kernel_len - 1] * values
    for lag in range(1, kernel_len):
        earlier = pltpu.roll(values, lag, 0)
        total = total + taps[kernel_len - 1 - lag] * jnp.where(offset >= lag, earlier, 0.0)
    cached = jnp.zeros_like(values)
    for request in range(len(cache)):
        for place in range(kernel_len - 1):
            history = jnp.zeros_like(bias)
            for lag in range(place + 1, kernel_len):
                at = kernel_len - 1 + place - lag
                history = history + taps[kernel_len - 1 - lag] * cache[request][at]
            cached = jnp.where((seg == request) & (offset == place), history, cached)
    total = total + cached
    return total * jax.nn.sigmoid(total)


def prep_kernel(count_req, got_total, heads, per_place, places, ints_ref, own_ref, *refs):
    got = refs[:got_total]
    row_refs = refs[got_total : 2 * got_total + 1]
    const_ref, bc_ref, small_ref, decay_ref = refs[2 * got_total + 1 :]
    tokens = own_ref.shape[0]
    channels = const_ref.shape[1]
    dt_bias = const_ref[places + 2 : places + 3, :heads]
    a_log = const_ref[places + 3 : places + 4, :heads]
    starts = [ints_ref[j] for j in range(count_req)]
    total = own_ref[...].astype(F32)
    for ref in got:
        total = total + ref[...].astype(F32)
    total = total.astype(BF16).astype(F32)
    position, seg, first = token_places(starts, tokens, (tokens, channels), 0)
    cache = cached_rows(
        ints_ref, row_refs, count_req, count_req, places, per_place, per_place - 1, channels
    )
    bc = conv_silu(total[:, :channels], cache, const_ref, seg, position - first)
    bc_ref[...] = bc.astype(BF16)
    raw = total[:, channels : channels + heads] + dt_bias
    step = jnp.maximum(raw, 0.0) + jnp.log1p(jnp.exp(-jnp.abs(raw)))
    rate = step * (-jnp.exp(a_log))
    position, seg, first = token_places(starts, tokens, (tokens, tokens), 0)
    other, seg_other, first_other = token_places(starts, tokens, (tokens, tokens), 1)
    same = seg == seg_other
    mask = jnp.where(same & (position >= other), 1.0, 0.0)
    after = jnp.where(same & (position < other), 1.0, 0.0)
    left = jnp.dot(after, rate, precision=HIGH, preferred_element_type=F32)
    cum_t = lax.dot_general(
        rate, mask, (((0,), (1,)), ((), ())), precision=HIGH, preferred_element_type=F32
    )
    step_t = step.T
    coef_t = (jnp.exp(left) * step).T
    steps = small_ref.shape[0]
    part = heads // steps
    for i in range(steps):
        place = slice(i * part, (i + 1) * part)
        for row, array in enumerate((cum_t, step_t, coef_t)):
            small_ref[i, row * part : (row + 1) * part, :] = array[place, :]
    at, seg_at, _ = token_places(starts, tokens, (8, tokens), 1)
    row = lax.broadcasted_iota(jnp.int32, (8, tokens), 0)
    ends = jnp.dot(
        jnp.where(seg_at == row, 1.0, 0.0), rate, precision=HIGH, preferred_element_type=F32
    )
    decay_ref[...] = jnp.exp(ends)


def prep(ints, own, got, row_arrays, row_total, const, heads, per_place, places):
    tokens = own.shape[0]
    channels = const.shape[1]
    part = min(HEADS_STEP, heads)
    count_req = row_arrays[0].shape[0]
    whole = lambda *shape: pl.BlockSpec(shape, lambda i: (0,) * len(shape))
    shapes = [(tokens, channels), (heads // part, 3 * part, tokens), (8, heads)]
    return pl.pallas_call(
        functools.partial(prep_kernel, count_req, len(got), heads, per_place, places),
        out_shape=[
            jax.ShapeDtypeStruct(shape, kind) for shape, kind in zip(shapes, (BF16, F32, F32))
        ],
        grid=(1,),
        in_specs=[pl.BlockSpec(memory_space=pltpu.SMEM)]
        + [whole(*own.shape)] * (1 + len(got))
        + [rows_spec(array, row_total) for array in row_arrays]
        + [whole(*const.shape)],
        out_specs=[whole(*shape) for shape in shapes],
        compiler_params=params(),
        cost_estimate=cost(1e6, 1e4),
    )(ints, own, *got, *row_arrays, const)


def rows_spec(array, row_total):
    last = array.shape[1] // row_total - 1
    block = (array.shape[0], row_total, array.shape[2])
    return pl.BlockSpec(block, lambda i, *_: (0, last, 0))


def conv_rows(slot, pool_refs, row_total, lanes):
    rows = []
    for place in range(pool_refs[0].shape[0]):
        for ref in pool_refs:
            values = ref[place].astype(F32)
            index = lax.broadcasted_iota(jnp.int32, values.shape, 0)
            line = jnp.sum(jnp.where(index == slot, values, 0.0), 0, keepdims=True)
            for first in range(0, line.shape[1], lanes):
                row = line[:, first : first + lanes]
                if row.shape[1] < lanes:
                    row = jnp.concatenate(
                        [row, jnp.zeros((1, lanes - row.shape[1]), F32)], 1
                    )
                rows.append(row)
    rows += [jnp.zeros((1, lanes), F32)] * (row_total - len(rows))
    return jnp.concatenate(rows, 0)


def pack_kernel(row_total, slots_ref, pool_ref, x_ref, bc_ref, out_ref):
    rows, lanes = pool_ref.shape[1] * pool_ref.shape[2], pool_ref.shape[3]
    slot = slots_ref[pl.program_id(0)]
    conv = conv_rows(slot, (x_ref, bc_ref), row_total, lanes)
    out_ref[0, :rows, :] = pool_ref[0].reshape(rows, lanes).astype(out_ref.dtype)
    out_ref[0, rows:, :] = conv.astype(out_ref.dtype)


def pack(pool, conv_pools, row_total, slots):
    count_req = slots.shape[0]
    _, heads, width, state = pool.shape
    conv_pools = [jnp.transpose(array, (1, 0, 2)) for array in conv_pools]
    out_block = (1, heads * width + row_total, state)
    return pl.pallas_call(
        functools.partial(pack_kernel, row_total),
        out_shape=jax.ShapeDtypeStruct((count_req,) + out_block[1:], BF16),
        grid_spec=pltpu.PrefetchScalarGridSpec(
            num_scalar_prefetch=1,
            grid=(count_req,),
            in_specs=[
                pl.BlockSpec((1, heads, width, state), lambda j, slots: (slots[j], 0, 0, 0))
            ]
            + [pl.BlockSpec(array.shape, lambda j, slots: (0, 0, 0)) for array in conv_pools],
            out_specs=pl.BlockSpec(out_block, lambda j, slots: (j, 0, 0)),
        ),
        compiler_params=params(3 * VMEM_BYTES),
        cost_estimate=cost(0, 6 * pool[0].size * count_req),
    )(slots, pool, *conv_pools)


def own_rows_kernel(row_total, first_slot, ints_ref, x_ref, bc_ref, out_ref):
    for request in range(out_ref.shape[0]):
        slot = ints_ref[first_slot + request]
        out_ref[request] = conv_rows(slot, (x_ref, bc_ref), row_total, out_ref.shape[2])


def own_rows_of(conv_pools, row_total, ints, count_req, lanes):
    vmem = pl.BlockSpec(memory_space=pltpu.VMEM)
    first_slot = ints.shape[0] - count_req
    return pl.pallas_call(
        functools.partial(own_rows_kernel, row_total, first_slot),
        out_shape=jax.ShapeDtypeStruct((count_req, row_total, lanes), F32),
        in_specs=[pl.BlockSpec(memory_space=pltpu.SMEM), vmem, vmem],
        out_specs=vmem,
        compiler_params=params(),
        cost_estimate=cost(1e6, 1e4),
    )(ints, *[jnp.transpose(array, (1, 0, 2)) for array in conv_pools])


def mixer_kernel(count_req, got_total, per_place, places, ints_ref, *refs):
    own_ref = refs[0]
    got = refs[1 : 1 + got_total]
    rest = refs[1 + got_total :]
    row_refs = rest[: got_total + 1]
    const_ref, b_ref, c_ref, small_ref, decay_ref = rest[got_total + 1 : got_total + 6]
    rest = rest[got_total + 6 :]
    pools, states = rest[:count_req], rest[count_req : count_req + got_total]
    out_ref, state_ref, scores_ref, c_part_ref, b_part_ref = rest[count_req + got_total :]
    skip = const_ref[places + 2 : places + 3, :]

    def flag(request, step):
        place = count_req + request * (got_total + 1) + step
        return ints_ref[place].astype(F32)

    tokens, channels = own_ref.shape
    heads, width, state = pools[0].shape[1:]
    starts = [ints_ref[j] for j in range(count_req)]

    @pl.when(pl.program_id(0) == 0)
    def _():
        position, seg, _ = token_places(starts, tokens, (tokens, tokens), 0)
        other, seg_other, _ = token_places(starts, tokens, (tokens, tokens), 1)
        scores = lax.dot_general(
            c_ref[...], b_ref[...], (((1,), (1,)), ((), ())), preferred_element_type=F32
        )
        scores_ref[...] = jnp.where((seg == seg_other) & (position >= other), scores, 0.0)
        _, seg, _ = token_places(starts, tokens, (tokens, state), 0)
        b_maps = b_ref[...].astype(F32)
        c_maps = c_ref[...].astype(F32)
        for j in range(count_req):
            place = slice(j * state, (j + 1) * state)
            b_part_ref[:, place] = jnp.where(seg == j, b_maps, 0.0).astype(BF16)
            c_part_ref[:, place] = jnp.where(seg == j, c_maps, 0.0).astype(BF16)

    total = own_ref[...].astype(F32)
    for ref in got:
        total = total + ref[...].astype(F32)
    total = total.astype(BF16).astype(F32)
    position, seg, first = token_places(starts, tokens, (tokens, channels), 0)
    cache = cached_rows(
        ints_ref, row_refs, count_req, count_req, places, per_place, pl.program_id(0), channels
    )
    values = conv_silu(total, cache, const_ref, seg, position - first)
    inputs = values.astype(BF16)
    values = inputs.astype(F32)

    lane_head = lax.broadcasted_iota(jnp.int32, (tokens, channels), 1) // width
    scores = scores_ref[...]
    small = small_ref[0]
    tall = small.T
    cum_t, step_t = small[:heads], small[heads : 2 * heads]
    cum, coef = tall[:, :heads], tall[:, 2 * heads :]
    grown = jnp.exp(cum)
    grown_wide = jnp.zeros((tokens, channels), F32)
    coef_wide = jnp.zeros((tokens, channels), F32)
    result = jnp.zeros((tokens, channels), F32)
    for h in range(heads):
        gap = jnp.minimum(cum[:, h : h + 1] - cum_t[h : h + 1, :], 0.0)
        weights = (jnp.exp(gap) * scores * step_t[h : h + 1, :]).astype(BF16)
        mine = lane_head == h
        result = result + jnp.dot(
            weights, jnp.where(mine, values, 0.0).astype(BF16), preferred_element_type=F32
        )
        grown_wide = jnp.where(mine, grown[:, h : h + 1], grown_wide)
        coef_wide = jnp.where(mine, coef[:, h : h + 1], coef_wide)

    from_state = jnp.zeros((tokens, channels), F32)
    carried = (coef_wide * values).astype(BF16)
    fresh = lax.dot_general(
        carried, b_part_ref[...], (((0,), (0,)), ((), ())), preferred_element_type=F32
    )
    for j in range(count_req):
        place = slice(j * state, (j + 1) * state)
        start = pools[j][0].reshape(channels, state) * flag(j, 0)
        for step in range(got_total):
            start = start + states[step][j].astype(F32) * flag(j, step + 1)
        from_state = from_state + lax.dot_general(
            c_part_ref[:, place],
            start.astype(BF16),
            (((1,), (1,)), ((), ())),
            preferred_element_type=F32,
        )
        first_head = pl.program_id(0) * heads
        for h in range(heads):
            rows = slice(h * width, (h + 1) * width)
            state_ref[j, h] = decay_ref[j, first_head + h] * start[rows] + fresh[rows, place]
    out_ref[...] = result + grown_wide * from_state + skip * values


def mixer(
    ints, own, got, row_arrays, row_total, const, b_maps, c_maps, small, decay, pool, states,
    per_place, places
):
    tokens, channels = own.shape
    _, heads, width, state = pool.shape
    count_req = row_arrays[0].shape[0]
    first_slot = ints.shape[0] - count_req
    part = min(HEADS_STEP, heads)
    steps = heads // part
    wide = part * width
    columns = lambda i, *_: (0, i)
    whole = lambda i, *_: (0, 0)

    in_specs = (
        [pl.BlockSpec((tokens, wide), columns)] * (1 + len(got))
        + [rows_spec(array, row_total) for array in row_arrays]
        + [
            pl.BlockSpec((const.shape[0], wide), columns),
            pl.BlockSpec((tokens, state), whole),
            pl.BlockSpec((tokens, state), whole),
            pl.BlockSpec((1,) + small.shape[1:], lambda i, *_: (i, 0, 0)),
            pl.BlockSpec(memory_space=pltpu.SMEM),
        ]
        + [
            pl.BlockSpec(
                (1, part, width, state),
                functools.partial(lambda at, i, ints: (ints[at], i, 0, 0), first_slot + j),
            )
            for j in range(count_req)
        ]
        + [pl.BlockSpec((count_req, wide, state), lambda i, *_: (0, i, 0))] * len(states)
    )
    return pl.pallas_call(
        functools.partial(mixer_kernel, count_req, len(got), per_place, places),
        out_shape=[
            jax.ShapeDtypeStruct((tokens, channels), F32),
            jax.ShapeDtypeStruct((count_req, heads, width, state), F32),
        ],
        grid_spec=pltpu.PrefetchScalarGridSpec(
            num_scalar_prefetch=1,
            grid=(steps,),
            in_specs=in_specs,
            out_specs=[
                pl.BlockSpec((tokens, wide), columns),
                pl.BlockSpec((count_req, part, width, state), lambda i, *_: (0, i, 0, 0)),
            ],
            scratch_shapes=[
                pltpu.VMEM((tokens, tokens), F32),
                pltpu.VMEM((tokens, count_req * state), BF16),
                pltpu.VMEM((tokens, count_req * state), BF16),
            ],
        ),
        compiler_params=params(3 * VMEM_BYTES),
        cost_estimate=cost(1e6, 1e4),
    )(
        ints, own, *got, *row_arrays, const, b_maps, c_maps, small, decay,
        *([pool] * count_req), *states
    )


def on_device(
    x_in,
    w_xz,
    w_dt,
    w_bc,
    dt_bias,
    a_log,
    d_skip,
    conv_x_w,
    conv_x_b,
    conv_bc_w,
    conv_bc_b,
    norm_gain,
    stretch_start,
    prefix_len,
    state_slot,
    ssm_pool,
    conv_x_pool,
    conv_bc_pool,
):
    local_width = w_xz.shape[2]
    state_part = w_bc.shape[1]
    me = lax.axis_index("req")
    req_count = lax.axis_size("req")
    slot_count, heads, head_width, state = ssm_pool.shape
    group_reqs = prefix_len.shape[0]
    lags = conv_x_pool.shape[1]

    direct = req_count == 2 and lax.axis_size("wide") == 16
    if direct:
        own_block, block = near_blocks(x_in)

    def slots_of(index):
        asked = lax.dynamic_slice_in_dim(state_slot, index * group_reqs, group_reqs)
        return jnp.clip(asked - me * slot_count, 0, slot_count - 1)

    per_place = -(-local_width // state) - (-state_part // state)
    row_total = -(-lags * per_place // 16) * 16
    conv_pools = (conv_x_pool, conv_bc_pool)
    got_states = []
    for step in range(1, req_count):
        slots = slots_of((me + step) % req_count)
        packed = pack(ssm_pool, conv_pools, row_total, slots)
        got_states.append(shift_req(packed, step))

    w_step = w_dt
    if direct:
        block = after(block, packed)
        along_z = partner_2(block, "wide", 2)
        along_x = partner_2(block, "wide", 1)
        (
            w_step, state_slot, prefix_len, stretch_start, conv_x_w,
            conv_x_b, conv_bc_w, conv_bc_b, d_skip, norm_gain, dt_bias, a_log
        ) = lax.optimization_barrier((
            (
                w_dt, state_slot, prefix_len, stretch_start, conv_x_w,
                conv_x_b, conv_bc_w, conv_bc_b, d_skip, norm_gain, dt_bias, a_log
            ),
            block,
        ))[0]
        w_step = pinned(w_step)
    own_slots = slots_of(me)
    asked = lax.dynamic_slice_in_dim(state_slot, me * group_reqs, group_reqs)
    came_from = (me - asked // slot_count) % req_count
    live = prefix_len > 0
    flags = (live[:, None] & (came_from[:, None] == jnp.arange(req_count)[None, :])).astype(
        jnp.int32
    )

    kernel_len = conv_x_w.shape[0]
    skip = jnp.repeat(d_skip, head_width)
    const_x = jnp.stack(
        [conv_x_w[k] for k in range(kernel_len)]
        + [conv_x_b, skip, norm_gain, jnp.zeros_like(skip)]
    )
    wide_heads = lambda array: jnp.pad(array, (0, state_part - heads))
    const_bc = jnp.stack(
        [conv_bc_w[k] for k in range(kernel_len)]
        + [conv_bc_b, wide_heads(dt_bias), wide_heads(a_log), jnp.zeros_like(conv_bc_b)]
    )
    ints = jnp.concatenate([stretch_start[0], flags.reshape(-1), own_slots])
    own_rows = own_rows_of(conv_pools, row_total, ints, group_reqs, state)
    if direct:
        both = partner_2(along_z, "wide", 1)
        own_block = after(own_block, along_z)
        own_z = partner_2(own_block, "wide", 2)
        near_three = jnp.stack([block, along_z, along_x])
        core_three = partner_2(near_three, "wide", 0)
        both = after(both[None], w_step, const_x, const_bc, ints, own_rows)
        core_both = partner_2(both, "wide", 0)
        core_both = after(core_both, *got_states)
        theirs = quad_arrange(
            [near_three, both, core_three, core_both], [0, 4, 2, 6, 1, 5, 3, 7]
        )
        own_pair = after(jnp.stack([own_block, own_z]), theirs)
        own_got = partner_2(own_pair, "wide", 1)
        features = [own_got, theirs]
    else:
        features = features_in_general(x_in)
    w_map = jnp.concatenate([w_bc, w_step], 1)

    def project(block, kind):
        low = jnp.dot(block, w_map, preferred_element_type=F32).astype(BF16)
        low, block = lax.optimization_barrier((low, block))
        high = jnp.einsum("td,dkc->ktc", block, w_xz, preferred_element_type=F32)
        return {"map": low, "xr": high[1].astype(kind), "z": high[0].astype(kind)}

    came = {"map": [], "xr": [], "z": []}
    parts = []
    for step in range(1, req_count):
        part = lax.optimization_barrier(project(features[step], BF16))
        for name in came:
            came[name].append(shift_req(part[name], step))
        parts.append(part)
    block = features[0]
    if direct:
        own_four = jnp.concatenate([own_pair, after(block, *parts)], 0)
        own_core = partner_2(own_four, "wide", 0)
        block = quad_arrange([own_four, own_core], [0, 4, 2, 6, 1, 5, 3, 7])
    else:
        block = after(block, *parts)
    own = lax.optimization_barrier(project(block, F32))

    row_arrays = [own_rows] + got_states
    bc_conv, small, decay = prep(
        ints, own["map"], came["map"], row_arrays, row_total, const_bc, heads, per_place, lags
    )
    wide_index = lax.axis_index("wide")
    group_span = lax.axis_size("wide") // GROUPS
    bit_total = group_span.bit_length() - 1
    joined = bc_conv
    for bit_index in range(bit_total):
        partner = partner_2(joined, "wide", bit_index)
        upper_half = wide_index // (1 << bit_index) % 2 == 1
        joined = jnp.where(
            upper_half, jnp.concatenate([partner, joined], 1), jnp.concatenate([joined, partner], 1)
        )
    state_width = joined.shape[1] // 2
    came_xr = [after(got, own["xr"], bc_conv) for got in came["xr"]]
    result, final_state = mixer(
        ints, own["xr"], came_xr, row_arrays, row_total, const_x, joined[:, :state_width],
        joined[:, state_width:], small, decay, ssm_pool, got_states,
        per_place, lags
    )
    gate = own["z"].astype(F32)
    for got in came["z"]:
        gate = gate + got.astype(F32)
    gated = result * jax.nn.silu(gate.astype(BF16).astype(F32))
    square_sum = jnp.sum(gated * gated, 1)
    for bit_index in range(bit_total):
        square_sum = square_sum + partner_2(square_sum, "wide", bit_index)
    mean_sq = square_sum / (local_width * group_span)
    normed = gated * lax.rsqrt(mean_sq + NORM_EPS)[:, None] * const_x[kernel_len + 2][None, :]
    return (normed.astype(BF16), final_state)


def solution(mesh):
    in_specs = (
        P("req", "wide"),
        P("req", None, "wide"),
        P("req", "wide"),
        P("req", "wide"),
        P("wide"),
        P("wide"),
        P("wide"),
        P(None, "wide"),
        P("wide"),
        P(None, "wide"),
        P("wide"),
        P("wide"),
        P("req", None),
        P("req"),
        P(),
        P("req", "wide", None, None),
        P("req", None, "wide"),
        P("req", None, "wide"),
    )
    out_specs = (P("req", "wide"), P("req", "wide", None, None))
    return jax.shard_map(
        on_device, mesh=mesh, in_specs=in_specs, out_specs=out_specs, check_vma=False
    )
```

```python
import functools

import jax
import jax.numpy as jnp
from jax import lax
from jax.experimental import pallas as pl
from jax.experimental.layout import Layout, with_layout_constraint
from jax.experimental.pallas import tpu as pltpu
from jax.sharding import PartitionSpec as P

GROUPS = 8
NORM_EPS = 1e-05
F32 = jnp.float32
BF16 = jnp.bfloat16
HIGH = lax.Precision.HIGHEST
VMEM_BYTES = 16 * 1024 * 1024
HEADS_STEP = 4


def cost(flops, bytes_accessed):
    return pl.CostEstimate(flops=int(flops), bytes_accessed=int(bytes_accessed), transcendentals=0)


def params(limit=VMEM_BYTES):
    return pltpu.CompilerParams(vmem_limit_bytes=limit)


def partner_2(block, axis, bit):
    count = lax.axis_size(axis)
    route = []
    for low in range(count):
        high = low | 1 << bit
        if high != low and high < count:
            route += [(low, high), (high, low)]
    return lax.ppermute(block, axis, route)


def shift_req(block, step):
    count = lax.axis_size("req")
    return lax.ppermute(block, "req", [(i, (i + step) % count) for i in range(count)])


def spread_routes():
    first, second = [], []
    for z in range(4):
        for rest in range(4):
            for r in range(2):
                place = (z * 4 + rest) * 2 + r
                other = (((z + 2) % 4) * 4 + rest) * 2 + r
                if z // 2 == r:
                    first.append((place, other))
                else:
                    first.append((place, place ^ 1))
                    second.append((place, other ^ 1))
    return first, second


def arrange_kernel(places_ref, *refs):
    out_ref = refs[-1]
    index = 0
    for ref in refs[:-1]:
        for part in range(ref.shape[0]):
            width = ref.shape[2]
            place = pl.multiple_of(places_ref[index] * width, width)
            out_ref[:, pl.ds(place, width)] = ref[part]
            index += 1


def arrange(stacks, places):
    tokens, width = stacks[0].shape[1:]
    total = sum(stack.shape[0] for stack in stacks) * width
    return pl.pallas_call(
        arrange_kernel,
        out_shape=jax.ShapeDtypeStruct((tokens, total), stacks[0].dtype),
        in_specs=[pl.BlockSpec(memory_space=pltpu.SMEM)]
        + [pl.BlockSpec(memory_space=pltpu.VMEM)] * len(stacks),
        out_specs=pl.BlockSpec(memory_space=pltpu.VMEM),
        compiler_params=params(),
        cost_estimate=cost(1e6, 1e4),
    )(places, *stacks)


def after(value, *others):
    return lax.optimization_barrier((value, others))[0]


def near_blocks(x_in):
    axes = ("wide", "req")
    first, second = spread_routes()
    second = lax.ppermute(x_in, axes, second)
    first = lax.ppermute(x_in, axes, first)
    near = lax.axis_index("wide") // 8 == lax.axis_index("req")
    return jnp.where(near, x_in, first), jnp.where(near, first, second)


def quad_arrange(stacks, apart):
    places = (lax.axis_index("wide") % 8) ^ jnp.array(apart, jnp.int32)
    return arrange(stacks, places)


def features_in_general(x_in):
    req_count = lax.axis_size("req")
    me = lax.axis_index("req")
    own = lax.all_gather(x_in, "wide", axis=1, tiled=True)
    parts = own.reshape(own.shape[0], req_count, own.shape[1] // req_count).transpose(1, 0, 2)
    got = lax.all_to_all(parts, "req", split_axis=0, concat_axis=0, tiled=True)
    return [
        lax.dynamic_index_in_dim(got, (me + step) % req_count, 0, False)
        for step in range(req_count)
    ]


def pinned(array):
    return lax.optimization_barrier(
        with_layout_constraint(array, Layout(tuple(range(array.ndim))))
    )


def token_places(starts, count_tok, shape, axis):
    position = lax.broadcasted_iota(jnp.int32, shape, axis)
    seg = jnp.full(shape, -1, jnp.int32)
    first = jnp.zeros(shape, jnp.int32)
    for start in starts:
        seg = seg + (position >= start).astype(jnp.int32)
        first = jnp.where(position >= start, start, first)
    return position, seg, first


def cached_rows(ints_ref, refs, count_req, first_flag, places, per_place, at, channels):
    rows = []
    for request in range(count_req):
        total = None
        for step, ref in enumerate(refs):
            flag = ints_ref[first_flag + request * len(refs) + step].astype(F32)
            term = ref[request].astype(F32) * flag
            total = term if total is None else total + term
        index = lax.broadcasted_iota(jnp.int32, total.shape, 0)
        rows.append([
            jnp.sum(jnp.where(index == place * per_place + at, total, 0.0), 0, keepdims=True)[
                :, :channels
            ]
            for place in range(places)
        ])
    return rows


def conv_silu(values, cache, const_ref, seg, offset):
    kernel_len = len(cache[0]) + 1
    taps = [const_ref[k : k + 1, :] for k in range(kernel_len)]
    bias = const_ref[kernel_len : kernel_len + 1, :]
    total = bias + taps[kernel_len - 1] * values
    for lag in range(1, kernel_len):
        earlier = pltpu.roll(values, lag, 0)
        total = total + taps[kernel_len - 1 - lag] * jnp.where(offset >= lag, earlier, 0.0)
    cached = jnp.zeros_like(values)
    for request in range(len(cache)):
        for place in range(kernel_len - 1):
            history = jnp.zeros_like(bias)
            for lag in range(place + 1, kernel_len):
                at = kernel_len - 1 + place - lag
                history = history + taps[kernel_len - 1 - lag] * cache[request][at]
            cached = jnp.where((seg == request) & (offset == place), history, cached)
    total = total + cached
    return total * jax.nn.sigmoid(total)


def prep_kernel(count_req, got_total, heads, per_place, places, ints_ref, own_ref, *refs):
    got = refs[:got_total]
    row_refs = refs[got_total : 2 * got_total + 1]
    const_ref, bc_ref, small_ref, decay_ref = refs[2 * got_total + 1 :]
    tokens = own_ref.shape[0]
    channels = const_ref.shape[1]
    dt_bias = const_ref[places + 2 : places + 3, :heads]
    a_log = const_ref[places + 3 : places + 4, :heads]
    starts = [ints_ref[j] for j in range(count_req)]
    total = own_ref[...].astype(F32)
    for ref in got:
        total = total + ref[...].astype(F32)
    total = total.astype(BF16).astype(F32)
    position, seg, first = token_places(starts, tokens, (tokens, channels), 0)
    cache = cached_rows(
        ints_ref, row_refs, count_req, count_req, places, per_place, per_place - 1, channels
    )
    bc = conv_silu(total[:, :channels], cache, const_ref, seg, position - first)
    bc_ref[...] = bc.astype(BF16)
    raw = total[:, channels : channels + heads] + dt_bias
    step = jnp.maximum(raw, 0.0) + jnp.log1p(jnp.exp(-jnp.abs(raw)))
    rate = step * (-jnp.exp(a_log))
    position, seg, first = token_places(starts, tokens, (tokens, tokens), 0)
    other, seg_other, first_other = token_places(starts, tokens, (tokens, tokens), 1)
    same = seg == seg_other
    mask = jnp.where(same & (position >= other), 1.0, 0.0)
    after = jnp.where(same & (position < other), 1.0, 0.0)
    left = jnp.dot(after, rate, precision=HIGH, preferred_element_type=F32)
    cum_t = lax.dot_general(
        rate, mask, (((0,), (1,)), ((), ())), precision=HIGH, preferred_element_type=F32
    )
    step_t = step.T
    coef_t = (jnp.exp(left) * step).T
    steps = small_ref.shape[0]
    part = heads // steps
    for i in range(steps):
        place = slice(i * part, (i + 1) * part)
        for row, array in enumerate((cum_t, step_t, coef_t)):
            small_ref[i, row * part : (row + 1) * part, :] = array[place, :]
    at, seg_at, _ = token_places(starts, tokens, (8, tokens), 1)
    row = lax.broadcasted_iota(jnp.int32, (8, tokens), 0)
    ends = jnp.dot(
        jnp.where(seg_at == row, 1.0, 0.0), rate, precision=HIGH, preferred_element_type=F32
    )
    decay_ref[...] = jnp.exp(ends)


def prep(ints, own, got, row_arrays, row_total, const, heads, per_place, places):
    tokens = own.shape[0]
    channels = const.shape[1]
    part = min(HEADS_STEP, heads)
    count_req = row_arrays[0].shape[0]
    whole = lambda *shape: pl.BlockSpec(shape, lambda i: (0,) * len(shape))
    shapes = [(tokens, channels), (heads // part, 3 * part, tokens), (8, heads)]
    return pl.pallas_call(
        functools.partial(prep_kernel, count_req, len(got), heads, per_place, places),
        out_shape=[
            jax.ShapeDtypeStruct(shape, kind) for shape, kind in zip(shapes, (BF16, F32, F32))
        ],
        grid=(1,),
        in_specs=[pl.BlockSpec(memory_space=pltpu.SMEM)]
        + [whole(*own.shape)] * (1 + len(got))
        + [rows_spec(array, row_total) for array in row_arrays]
        + [whole(*const.shape)],
        out_specs=[whole(*shape) for shape in shapes],
        compiler_params=params(),
        cost_estimate=cost(1e6, 1e4),
    )(ints, own, *got, *row_arrays, const)


def rows_spec(array, row_total):
    last = array.shape[1] // row_total - 1
    block = (array.shape[0], row_total, array.shape[2])
    return pl.BlockSpec(block, lambda i, *_: (0, last, 0))


def conv_rows(slot, pool_refs, row_total, lanes):
    rows = []
    for place in range(pool_refs[0].shape[0]):
        for ref in pool_refs:
            values = ref[place].astype(F32)
            index = lax.broadcasted_iota(jnp.int32, values.shape, 0)
            line = jnp.sum(jnp.where(index == slot, values, 0.0), 0, keepdims=True)
            for first in range(0, line.shape[1], lanes):
                row = line[:, first : first + lanes]
                if row.shape[1] < lanes:
                    row = jnp.concatenate(
                        [row, jnp.zeros((1, lanes - row.shape[1]), F32)], 1
                    )
                rows.append(row)
    rows += [jnp.zeros((1, lanes), F32)] * (row_total - len(rows))
    return jnp.concatenate(rows, 0)


def pack_kernel(row_total, slots_ref, pool_ref, x_ref, bc_ref, out_ref):
    rows, lanes = pool_ref.shape[1] * pool_ref.shape[2], pool_ref.shape[3]
    slot = slots_ref[pl.program_id(0)]
    conv = conv_rows(slot, (x_ref, bc_ref), row_total, lanes)
    out_ref[0, :rows, :] = pool_ref[0].reshape(rows, lanes).astype(out_ref.dtype)
    out_ref[0, rows:, :] = conv.astype(out_ref.dtype)


def pack(pool, conv_pools, row_total, slots):
    count_req = slots.shape[0]
    _, heads, width, state = pool.shape
    conv_pools = [jnp.transpose(array, (1, 0, 2)) for array in conv_pools]
    out_block = (1, heads * width + row_total, state)
    return pl.pallas_call(
        functools.partial(pack_kernel, row_total),
        out_shape=jax.ShapeDtypeStruct((count_req,) + out_block[1:], BF16),
        grid_spec=pltpu.PrefetchScalarGridSpec(
            num_scalar_prefetch=1,
            grid=(count_req,),
            in_specs=[
                pl.BlockSpec((1, heads, width, state), lambda j, slots: (slots[j], 0, 0, 0))
            ]
            + [pl.BlockSpec(array.shape, lambda j, slots: (0, 0, 0)) for array in conv_pools],
            out_specs=pl.BlockSpec(out_block, lambda j, slots: (j, 0, 0)),
        ),
        compiler_params=params(3 * VMEM_BYTES),
        cost_estimate=cost(0, 6 * pool[0].size * count_req),
    )(slots, pool, *conv_pools)


def own_rows_kernel(row_total, first_slot, ints_ref, x_ref, bc_ref, out_ref):
    for request in range(out_ref.shape[0]):
        slot = ints_ref[first_slot + request]
        out_ref[request] = conv_rows(slot, (x_ref, bc_ref), row_total, out_ref.shape[2])


def own_rows_of(conv_pools, row_total, ints, count_req, lanes):
    vmem = pl.BlockSpec(memory_space=pltpu.VMEM)
    first_slot = ints.shape[0] - count_req
    return pl.pallas_call(
        functools.partial(own_rows_kernel, row_total, first_slot),
        out_shape=jax.ShapeDtypeStruct((count_req, row_total, lanes), F32),
        in_specs=[pl.BlockSpec(memory_space=pltpu.SMEM), vmem, vmem],
        out_specs=vmem,
        compiler_params=params(),
        cost_estimate=cost(1e6, 1e4),
    )(ints, *[jnp.transpose(array, (1, 0, 2)) for array in conv_pools])


def mixer_kernel(count_req, got_total, per_place, places, ints_ref, *refs):
    own_ref = refs[0]
    got = refs[1 : 1 + got_total]
    rest = refs[1 + got_total :]
    row_refs = rest[: got_total + 1]
    const_ref, b_ref, c_ref, small_ref, decay_ref = rest[got_total + 1 : got_total + 6]
    rest = rest[got_total + 6 :]
    pools, states = rest[:count_req], rest[count_req : count_req + got_total]
    out_ref, state_ref, scores_ref, c_part_ref, b_part_ref = rest[count_req + got_total :]
    skip = const_ref[places + 2 : places + 3, :]

    def flag(request, step):
        place = count_req + request * (got_total + 1) + step
        return ints_ref[place].astype(F32)

    tokens, channels = own_ref.shape
    heads, width, state = pools[0].shape[1:]
    starts = [ints_ref[j] for j in range(count_req)]

    @pl.when(pl.program_id(0) == 0)
    def _():
        position, seg, _ = token_places(starts, tokens, (tokens, tokens), 0)
        other, seg_other, _ = token_places(starts, tokens, (tokens, tokens), 1)
        scores = lax.dot_general(
            c_ref[...], b_ref[...], (((1,), (1,)), ((), ())), preferred_element_type=F32
        )
        scores_ref[...] = jnp.where((seg == seg_other) & (position >= other), scores, 0.0)
        _, seg, _ = token_places(starts, tokens, (tokens, state), 0)
        b_maps = b_ref[...].astype(F32)
        c_maps = c_ref[...].astype(F32)
        for j in range(count_req):
            place = slice(j * state, (j + 1) * state)
            b_part_ref[:, place] = jnp.where(seg == j, b_maps, 0.0).astype(BF16)
            c_part_ref[:, place] = jnp.where(seg == j, c_maps, 0.0).astype(BF16)

    total = own_ref[...].astype(F32)
    for ref in got:
        total = total + ref[...].astype(F32)
    total = total.astype(BF16).astype(F32)
    position, seg, first = token_places(starts, tokens, (tokens, channels), 0)
    cache = cached_rows(
        ints_ref, row_refs, count_req, count_req, places, per_place, pl.program_id(0), channels
    )
    values = conv_silu(total, cache, const_ref, seg, position - first)
    inputs = values.astype(BF16)
    values = inputs.astype(F32)

    lane_head = lax.broadcasted_iota(jnp.int32, (tokens, channels), 1) // width
    scores = scores_ref[...]
    small = small_ref[0]
    tall = small.T
    cum_t, step_t = small[:heads], small[heads : 2 * heads]
    cum, coef = tall[:, :heads], tall[:, 2 * heads :]
    grown = jnp.exp(cum)
    grown_wide = jnp.zeros((tokens, channels), F32)
    coef_wide = jnp.zeros((tokens, channels), F32)
    result = jnp.zeros((tokens, channels), F32)
    for h in range(heads):
        gap = jnp.minimum(cum[:, h : h + 1] - cum_t[h : h + 1, :], 0.0)
        weights = (jnp.exp(gap) * scores * step_t[h : h + 1, :]).astype(BF16)
        mine = lane_head == h
        result = result + jnp.dot(
            weights, jnp.where(mine, values, 0.0).astype(BF16), preferred_element_type=F32
        )
        grown_wide = jnp.where(mine, grown[:, h : h + 1], grown_wide)
        coef_wide = jnp.where(mine, coef[:, h : h + 1], coef_wide)

    from_state = jnp.zeros((tokens, channels), F32)
    carried = (coef_wide * values).astype(BF16)
    fresh = lax.dot_general(
        carried, b_part_ref[...], (((0,), (0,)), ((), ())), preferred_element_type=F32
    )
    for j in range(count_req):
        place = slice(j * state, (j + 1) * state)
        start = pools[j][0].reshape(channels, state) * flag(j, 0)
        for step in range(got_total):
            start = start + states[step][j].astype(F32) * flag(j, step + 1)
        from_state = from_state + lax.dot_general(
            c_part_ref[:, place],
            start.astype(BF16),
            (((1,), (1,)), ((), ())),
            preferred_element_type=F32,
        )
        first_head = pl.program_id(0) * heads
        for h in range(heads):
            rows = slice(h * width, (h + 1) * width)
            state_ref[j, h] = decay_ref[j, first_head + h] * start[rows] + fresh[rows, place]
    out_ref[...] = result + grown_wide * from_state + skip * values


def mixer(
    ints, own, got, row_arrays, row_total, const, b_maps, c_maps, small, decay, pool, states,
    per_place, places
):
    tokens, channels = own.shape
    _, heads, width, state = pool.shape
    count_req = row_arrays[0].shape[0]
    first_slot = ints.shape[0] - count_req
    part = min(HEADS_STEP, heads)
    steps = heads // part
    wide = part * width
    columns = lambda i, *_: (0, i)
    whole = lambda i, *_: (0, 0)

    in_specs = (
        [pl.BlockSpec((tokens, wide), columns)] * (1 + len(got))
        + [rows_spec(array, row_total) for array in row_arrays]
        + [
            pl.BlockSpec((const.shape[0], wide), columns),
            pl.BlockSpec((tokens, state), whole),
            pl.BlockSpec((tokens, state), whole),
            pl.BlockSpec((1,) + small.shape[1:], lambda i, *_: (i, 0, 0)),
            pl.BlockSpec(memory_space=pltpu.SMEM),
        ]
        + [
            pl.BlockSpec(
                (1, part, width, state),
                functools.partial(lambda at, i, ints: (ints[at], i, 0, 0), first_slot + j),
            )
            for j in range(count_req)
        ]
        + [pl.BlockSpec((count_req, wide, state), lambda i, *_: (0, i, 0))] * len(states)
    )
    return pl.pallas_call(
        functools.partial(mixer_kernel, count_req, len(got), per_place, places),
        out_shape=[
            jax.ShapeDtypeStruct((tokens, channels), F32),
            jax.ShapeDtypeStruct((count_req, heads, width, state), F32),
        ],
        grid_spec=pltpu.PrefetchScalarGridSpec(
            num_scalar_prefetch=1,
            grid=(steps,),
            in_specs=in_specs,
            out_specs=[
                pl.BlockSpec((tokens, wide), columns),
                pl.BlockSpec((count_req, part, width, state), lambda i, *_: (0, i, 0, 0)),
            ],
            scratch_shapes=[
                pltpu.VMEM((tokens, tokens), F32),
                pltpu.VMEM((tokens, count_req * state), BF16),
                pltpu.VMEM((tokens, count_req * state), BF16),
            ],
        ),
        compiler_params=params(3 * VMEM_BYTES),
        cost_estimate=cost(1e6, 1e4),
    )(
        ints, own, *got, *row_arrays, const, b_maps, c_maps, small, decay,
        *([pool] * count_req), *states
    )


def on_device(
    x_in,
    w_xz,
    w_dt,
    w_bc,
    dt_bias,
    a_log,
    d_skip,
    conv_x_w,
    conv_x_b,
    conv_bc_w,
    conv_bc_b,
    norm_gain,
    stretch_start,
    prefix_len,
    state_slot,
    ssm_pool,
    conv_x_pool,
    conv_bc_pool,
):
    local_width = w_xz.shape[2]
    state_part = w_bc.shape[1]
    me = lax.axis_index("req")
    req_count = lax.axis_size("req")
    slot_count, heads, head_width, state = ssm_pool.shape
    group_reqs = prefix_len.shape[0]
    lags = conv_x_pool.shape[1]

    direct = req_count == 2 and lax.axis_size("wide") == 16
    if direct:
        own_block, block = near_blocks(x_in)

    def slots_of(index):
        asked = lax.dynamic_slice_in_dim(state_slot, index * group_reqs, group_reqs)
        return jnp.clip(asked - me * slot_count, 0, slot_count - 1)

    per_place = -(-local_width // state) - (-state_part // state)
    row_total = -(-lags * per_place // 16) * 16
    conv_pools = (conv_x_pool, conv_bc_pool)
    got_states = []
    for step in range(1, req_count):
        slots = slots_of((me + step) % req_count)
        packed = pack(ssm_pool, conv_pools, row_total, slots)
        got_states.append(shift_req(packed, step))

    w_step = w_dt
    if direct:
        block = after(block, packed)
        along_z = partner_2(block, "wide", 2)
        along_x = partner_2(block, "wide", 1)
        (
            w_step, state_slot, prefix_len, stretch_start, conv_x_w,
            conv_x_b, conv_bc_w, conv_bc_b, d_skip, norm_gain, dt_bias, a_log
        ) = lax.optimization_barrier((
            (
                w_dt, state_slot, prefix_len, stretch_start, conv_x_w,
                conv_x_b, conv_bc_w, conv_bc_b, d_skip, norm_gain, dt_bias, a_log
            ),
            block,
        ))[0]
        w_step = pinned(w_step)
    own_slots = slots_of(me)
    asked = lax.dynamic_slice_in_dim(state_slot, me * group_reqs, group_reqs)
    came_from = (me - asked // slot_count) % req_count
    live = prefix_len > 0
    flags = (live[:, None] & (came_from[:, None] == jnp.arange(req_count)[None, :])).astype(
        jnp.int32
    )

    kernel_len = conv_x_w.shape[0]
    skip = jnp.repeat(d_skip, head_width)
    const_x = jnp.stack(
        [conv_x_w[k] for k in range(kernel_len)]
        + [conv_x_b, skip, norm_gain, jnp.zeros_like(skip)]
    )
    wide_heads = lambda array: jnp.pad(array, (0, state_part - heads))
    const_bc = jnp.stack(
        [conv_bc_w[k] for k in range(kernel_len)]
        + [conv_bc_b, wide_heads(dt_bias), wide_heads(a_log), jnp.zeros_like(conv_bc_b)]
    )
    ints = jnp.concatenate([stretch_start[0], flags.reshape(-1), own_slots])
    own_rows = own_rows_of(conv_pools, row_total, ints, group_reqs, state)
    if direct:
        both = partner_2(along_z, "wide", 1)
        own_block = after(own_block, along_z)
        own_z = partner_2(own_block, "wide", 2)
        near_three = jnp.stack([block, along_z, along_x])
        core_three = partner_2(near_three, "wide", 0)
        both = after(both[None], w_step, const_x, const_bc, ints, own_rows)
        core_both = partner_2(both, "wide", 0)
        theirs = quad_arrange(
            [near_three, both, core_three, core_both], [0, 4, 2, 6, 1, 5, 3, 7]
        )
        own_pair = after(jnp.stack([own_block, own_z]), theirs)
        own_got = partner_2(own_pair, "wide", 1)
        features = [own_got, theirs]
    else:
        features = features_in_general(x_in)
    w_map = jnp.concatenate([w_bc, w_step], 1)

    def project(block, kind):
        low = jnp.dot(block, w_map, preferred_element_type=F32).astype(BF16)
        low, block = lax.optimization_barrier((low, block))
        high = jnp.einsum("td,dkc->ktc", block, w_xz, preferred_element_type=F32)
        return {"map": low, "xr": high[1].astype(kind), "z": high[0].astype(kind)}

    came = {"map": [], "xr": [], "z": []}
    parts = []
    for step in range(1, req_count):
        part = project(features[step], BF16)
        part = after(part, *got_states) if direct else lax.optimization_barrier(part)
        for name in came:
            came[name].append(shift_req(part[name], step))
        parts.append(part)
    block = features[0]
    if direct:
        own_four = jnp.concatenate([own_pair, after(block, *parts)], 0)
        own_core = partner_2(own_four, "wide", 0)
        block = quad_arrange([own_four, own_core], [0, 4, 2, 6, 1, 5, 3, 7])
    else:
        block = after(block, *parts)
    own = lax.optimization_barrier(project(block, F32))

    row_arrays = [own_rows] + got_states
    bc_conv, small, decay = prep(
        ints, own["map"], came["map"], row_arrays, row_total, const_bc, heads, per_place, lags
    )
    wide_index = lax.axis_index("wide")
    group_span = lax.axis_size("wide") // GROUPS
    bit_total = group_span.bit_length() - 1
    joined = bc_conv
    for bit_index in range(bit_total):
        partner = partner_2(joined, "wide", bit_index)
        upper_half = wide_index // (1 << bit_index) % 2 == 1
        joined = jnp.where(
            upper_half, jnp.concatenate([partner, joined], 1), jnp.concatenate([joined, partner], 1)
        )
    state_width = joined.shape[1] // 2
    came_xr = [after(got, own["xr"], bc_conv) for got in came["xr"]]
    result, final_state = mixer(
        ints, own["xr"], came_xr, row_arrays, row_total, const_x, joined[:, :state_width],
        joined[:, state_width:], small, decay, ssm_pool, got_states,
        per_place, lags
    )
    gate = own["z"].astype(F32)
    for got in came["z"]:
        gate = gate + got.astype(F32)
    gated = result * jax.nn.silu(gate.astype(BF16).astype(F32))
    square_sum = jnp.sum(gated * gated, 1)
    for bit_index in range(bit_total):
        square_sum = square_sum + partner_2(square_sum, "wide", bit_index)
    mean_sq = square_sum / (local_width * group_span)
    normed = gated * lax.rsqrt(mean_sq + NORM_EPS)[:, None] * const_x[kernel_len + 2][None, :]
    return (normed.astype(BF16), final_state)


def solution(mesh):
    in_specs = (
        P("req", "wide"),
        P("req", None, "wide"),
        P("req", "wide"),
        P("req", "wide"),
        P("wide"),
        P("wide"),
        P("wide"),
        P(None, "wide"),
        P("wide"),
        P(None, "wide"),
        P("wide"),
        P("wide"),
        P("req", None),
        P("req"),
        P(),
        P("req", "wide", None, None),
        P("req", None, "wide"),
        P("req", None, "wide"),
    )
    out_specs = (P("req", "wide"), P("req", "wide", None, None))
    return jax.shard_map(
        on_device, mesh=mesh, in_specs=in_specs, out_specs=out_specs, check_vma=False
    )
```

```python
import functools

import jax
import jax.numpy as jnp
from jax import lax
from jax.experimental import pallas as pl
from jax.experimental.layout import Layout, with_layout_constraint
from jax.experimental.pallas import tpu as pltpu
from jax.sharding import PartitionSpec as P

GROUPS = 8
NORM_EPS = 1e-05
F32 = jnp.float32
BF16 = jnp.bfloat16
HIGH = lax.Precision.HIGHEST
VMEM_BYTES = 16 * 1024 * 1024
HEADS_STEP = 4


def cost(flops, bytes_accessed):
    return pl.CostEstimate(flops=int(flops), bytes_accessed=int(bytes_accessed), transcendentals=0)


def params(limit=VMEM_BYTES):
    return pltpu.CompilerParams(vmem_limit_bytes=limit)


def partner_2(block, axis, bit):
    count = lax.axis_size(axis)
    route = []
    for low in range(count):
        high = low | 1 << bit
        if high != low and high < count:
            route += [(low, high), (high, low)]
    return lax.ppermute(block, axis, route)


def shift_req(block, step):
    count = lax.axis_size("req")
    return lax.ppermute(block, "req", [(i, (i + step) % count) for i in range(count)])


def spread_routes():
    first, second = [], []
    for z in range(4):
        for rest in range(4):
            for r in range(2):
                place = (z * 4 + rest) * 2 + r
                other = (((z + 2) % 4) * 4 + rest) * 2 + r
                if z // 2 == r:
                    first.append((place, other))
                else:
                    first.append((place, place ^ 1))
                    second.append((place, other ^ 1))
    return first, second


def arrange_kernel(places_ref, *refs):
    out_ref = refs[-1]
    index = 0
    for ref in refs[:-1]:
        for part in range(ref.shape[0]):
            width = ref.shape[2]
            place = pl.multiple_of(places_ref[index] * width, width)
            out_ref[:, pl.ds(place, width)] = ref[part]
            index += 1


def arrange(stacks, places):
    tokens, width = stacks[0].shape[1:]
    total = sum(stack.shape[0] for stack in stacks) * width
    return pl.pallas_call(
        arrange_kernel,
        out_shape=jax.ShapeDtypeStruct((tokens, total), stacks[0].dtype),
        in_specs=[pl.BlockSpec(memory_space=pltpu.SMEM)]
        + [pl.BlockSpec(memory_space=pltpu.VMEM)] * len(stacks),
        out_specs=pl.BlockSpec(memory_space=pltpu.VMEM),
        compiler_params=params(),
        cost_estimate=cost(1e6, 1e4),
    )(places, *stacks)


def after(value, *others):
    return lax.optimization_barrier((value, others))[0]


def near_blocks(x_in):
    axes = ("wide", "req")
    first, second = spread_routes()
    second = lax.ppermute(x_in, axes, second)
    first = lax.ppermute(x_in, axes, first)
    near = lax.axis_index("wide") // 8 == lax.axis_index("req")
    return jnp.where(near, x_in, first), jnp.where(near, first, second)


def quad_arrange(stacks, apart):
    places = (lax.axis_index("wide") % 8) ^ jnp.array(apart, jnp.int32)
    return arrange(stacks, places)


def features_in_general(x_in):
    req_count = lax.axis_size("req")
    me = lax.axis_index("req")
    own = lax.all_gather(x_in, "wide", axis=1, tiled=True)
    parts = own.reshape(own.shape[0], req_count, own.shape[1] // req_count).transpose(1, 0, 2)
    got = lax.all_to_all(parts, "req", split_axis=0, concat_axis=0, tiled=True)
    return [
        lax.dynamic_index_in_dim(got, (me + step) % req_count, 0, False)
        for step in range(req_count)
    ]


def pinned(array):
    return lax.optimization_barrier(
        with_layout_constraint(array, Layout(tuple(range(array.ndim))))
    )


def token_places(starts, count_tok, shape, axis):
    position = lax.broadcasted_iota(jnp.int32, shape, axis)
    seg = jnp.full(shape, -1, jnp.int32)
    first = jnp.zeros(shape, jnp.int32)
    for start in starts:
        seg = seg + (position >= start).astype(jnp.int32)
        first = jnp.where(position >= start, start, first)
    return position, seg, first


def cached_rows(ints_ref, refs, count_req, first_flag, places, per_place, at, channels):
    rows = []
    for request in range(count_req):
        total = None
        for step, ref in enumerate(refs):
            flag = ints_ref[first_flag + request * len(refs) + step].astype(F32)
            term = ref[request].astype(F32) * flag
            total = term if total is None else total + term
        index = lax.broadcasted_iota(jnp.int32, total.shape, 0)
        rows.append([
            jnp.sum(jnp.where(index == place * per_place + at, total, 0.0), 0, keepdims=True)[
                :, :channels
            ]
            for place in range(places)
        ])
    return rows


def conv_silu(values, cache, const_ref, seg, offset):
    kernel_len = len(cache[0]) + 1
    taps = [const_ref[k : k + 1, :] for k in range(kernel_len)]
    bias = const_ref[kernel_len : kernel_len + 1, :]
    total = bias + taps[kernel_len - 1] * values
    for lag in range(1, kernel_len):
        earlier = pltpu.roll(values, lag, 0)
        total = total + taps[kernel_len - 1 - lag] * jnp.where(offset >= lag, earlier, 0.0)
    cached = jnp.zeros_like(values)
    for request in range(len(cache)):
        for place in range(kernel_len - 1):
            history = jnp.zeros_like(bias)
            for lag in range(place + 1, kernel_len):
                at = kernel_len - 1 + place - lag
                history = history + taps[kernel_len - 1 - lag] * cache[request][at]
            cached = jnp.where((seg == request) & (offset == place), history, cached)
    total = total + cached
    return total * jax.nn.sigmoid(total)


def prep_kernel(count_req, got_total, heads, per_place, places, ints_ref, own_ref, *refs):
    got = refs[:got_total]
    row_refs = refs[got_total : 2 * got_total + 1]
    const_ref, bc_ref, small_ref, decay_ref = refs[2 * got_total + 1 :]
    tokens = own_ref.shape[0]
    channels = const_ref.shape[1]
    dt_bias = const_ref[places + 2 : places + 3, :heads]
    a_log = const_ref[places + 3 : places + 4, :heads]
    starts = [ints_ref[j] for j in range(count_req)]
    total = own_ref[...].astype(F32)
    for ref in got:
        total = total + ref[...].astype(F32)
    total = total.astype(BF16).astype(F32)
    position, seg, first = token_places(starts, tokens, (tokens, channels), 0)
    cache = cached_rows(
        ints_ref, row_refs, count_req, count_req, places, per_place, per_place - 1, channels
    )
    bc = conv_silu(total[:, :channels], cache, const_ref, seg, position - first)
    bc_ref[...] = bc.astype(BF16)
    raw = total[:, channels : channels + heads] + dt_bias
    step = jnp.maximum(raw, 0.0) + jnp.log1p(jnp.exp(-jnp.abs(raw)))
    rate = step * (-jnp.exp(a_log))
    position, seg, first = token_places(starts, tokens, (tokens, tokens), 0)
    other, seg_other, first_other = token_places(starts, tokens, (tokens, tokens), 1)
    same = seg == seg_other
    mask = jnp.where(same & (position >= other), 1.0, 0.0)
    after = jnp.where(same & (position < other), 1.0, 0.0)
    left = jnp.dot(after, rate, precision=HIGH, preferred_element_type=F32)
    cum_t = lax.dot_general(
        rate, mask, (((0,), (1,)), ((), ())), precision=HIGH, preferred_element_type=F32
    )
    step_t = step.T
    coef_t = (jnp.exp(left) * step).T
    steps = small_ref.shape[0]
    part = heads // steps
    for i in range(steps):
        place = slice(i * part, (i + 1) * part)
        for row, array in enumerate((cum_t, step_t, coef_t)):
            small_ref[i, row * part : (row + 1) * part, :] = array[place, :]
    at, seg_at, _ = token_places(starts, tokens, (8, tokens), 1)
    row = lax.broadcasted_iota(jnp.int32, (8, tokens), 0)
    ends = jnp.dot(
        jnp.where(seg_at == row, 1.0, 0.0), rate, precision=HIGH, preferred_element_type=F32
    )
    decay_ref[...] = jnp.exp(ends)


def prep(ints, own, got, row_arrays, row_total, const, heads, per_place, places):
    tokens = own.shape[0]
    channels = const.shape[1]
    part = min(HEADS_STEP, heads)
    count_req = row_arrays[0].shape[0]
    whole = lambda *shape: pl.BlockSpec(shape, lambda i: (0,) * len(shape))
    shapes = [(tokens, channels), (heads // part, 3 * part, tokens), (8, heads)]
    return pl.pallas_call(
        functools.partial(prep_kernel, count_req, len(got), heads, per_place, places),
        out_shape=[
            jax.ShapeDtypeStruct(shape, kind) for shape, kind in zip(shapes, (BF16, F32, F32))
        ],
        grid=(1,),
        in_specs=[pl.BlockSpec(memory_space=pltpu.SMEM)]
        + [whole(*own.shape)] * (1 + len(got))
        + [rows_spec(array, row_total) for array in row_arrays]
        + [whole(*const.shape)],
        out_specs=[whole(*shape) for shape in shapes],
        compiler_params=params(),
        cost_estimate=cost(1e6, 1e4),
    )(ints, own, *got, *row_arrays, const)


def rows_spec(array, row_total):
    last = array.shape[1] // row_total - 1
    block = (array.shape[0], row_total, array.shape[2])
    return pl.BlockSpec(block, lambda i, *_: (0, last, 0))


def conv_rows(slot, pool_refs, row_total, lanes):
    rows = []
    for place in range(pool_refs[0].shape[0]):
        for ref in pool_refs:
            values = ref[place].astype(F32)
            index = lax.broadcasted_iota(jnp.int32, values.shape, 0)
            line = jnp.sum(jnp.where(index == slot, values, 0.0), 0, keepdims=True)
            for first in range(0, line.shape[1], lanes):
                row = line[:, first : first + lanes]
                if row.shape[1] < lanes:
                    row = jnp.concatenate(
                        [row, jnp.zeros((1, lanes - row.shape[1]), F32)], 1
                    )
                rows.append(row)
    rows += [jnp.zeros((1, lanes), F32)] * (row_total - len(rows))
    return jnp.concatenate(rows, 0)


def pack_kernel(row_total, slots_ref, pool_ref, x_ref, bc_ref, out_ref):
    rows, lanes = pool_ref.shape[1] * pool_ref.shape[2], pool_ref.shape[3]
    slot = slots_ref[pl.program_id(0)]
    conv = conv_rows(slot, (x_ref, bc_ref), row_total, lanes)
    out_ref[0, :rows, :] = pool_ref[0].reshape(rows, lanes).astype(out_ref.dtype)
    out_ref[0, rows:, :] = conv.astype(out_ref.dtype)


def pack(pool, conv_pools, row_total, slots):
    count_req = slots.shape[0]
    _, heads, width, state = pool.shape
    conv_pools = [jnp.transpose(array, (1, 0, 2)) for array in conv_pools]
    out_block = (1, heads * width + row_total, state)
    return pl.pallas_call(
        functools.partial(pack_kernel, row_total),
        out_shape=jax.ShapeDtypeStruct((count_req,) + out_block[1:], BF16),
        grid_spec=pltpu.PrefetchScalarGridSpec(
            num_scalar_prefetch=1,
            grid=(count_req,),
            in_specs=[
                pl.BlockSpec((1, heads, width, state), lambda j, slots: (slots[j], 0, 0, 0))
            ]
            + [pl.BlockSpec(array.shape, lambda j, slots: (0, 0, 0)) for array in conv_pools],
            out_specs=pl.BlockSpec(out_block, lambda j, slots: (j, 0, 0)),
        ),
        compiler_params=params(3 * VMEM_BYTES),
        cost_estimate=cost(0, 6 * pool[0].size * count_req),
    )(slots, pool, *conv_pools)


def own_rows_kernel(row_total, first_slot, ints_ref, x_ref, bc_ref, out_ref):
    for request in range(out_ref.shape[0]):
        slot = ints_ref[first_slot + request]
        out_ref[request] = conv_rows(slot, (x_ref, bc_ref), row_total, out_ref.shape[2])


def own_rows_of(conv_pools, row_total, ints, count_req, lanes):
    vmem = pl.BlockSpec(memory_space=pltpu.VMEM)
    first_slot = ints.shape[0] - count_req
    return pl.pallas_call(
        functools.partial(own_rows_kernel, row_total, first_slot),
        out_shape=jax.ShapeDtypeStruct((count_req, row_total, lanes), F32),
        in_specs=[pl.BlockSpec(memory_space=pltpu.SMEM), vmem, vmem],
        out_specs=vmem,
        compiler_params=params(),
        cost_estimate=cost(1e6, 1e4),
    )(ints, *[jnp.transpose(array, (1, 0, 2)) for array in conv_pools])


def mixer_kernel(count_req, got_total, per_place, places, ints_ref, *refs):
    own_ref = refs[0]
    got = refs[1 : 1 + got_total]
    rest = refs[1 + got_total :]
    row_refs = rest[: got_total + 1]
    const_ref, b_ref, c_ref, small_ref, decay_ref = rest[got_total + 1 : got_total + 6]
    rest = rest[got_total + 6 :]
    pools, states = rest[:count_req], rest[count_req : count_req + got_total]
    out_ref, state_ref, scores_ref, c_part_ref, b_part_ref = rest[count_req + got_total :]
    skip = const_ref[places + 2 : places + 3, :]

    def flag(request, step):
        place = count_req + request * (got_total + 1) + step
        return ints_ref[place].astype(F32)

    tokens, channels = own_ref.shape
    heads, width, state = pools[0].shape[1:]
    starts = [ints_ref[j] for j in range(count_req)]

    @pl.when(pl.program_id(0) == 0)
    def _():
        position, seg, _ = token_places(starts, tokens, (tokens, tokens), 0)
        other, seg_other, _ = token_places(starts, tokens, (tokens, tokens), 1)
        scores = lax.dot_general(
            c_ref[...], b_ref[...], (((1,), (1,)), ((), ())), preferred_element_type=F32
        )
        scores_ref[...] = jnp.where((seg == seg_other) & (position >= other), scores, 0.0)
        _, seg, _ = token_places(starts, tokens, (tokens, state), 0)
        b_maps = b_ref[...].astype(F32)
        c_maps = c_ref[...].astype(F32)
        for j in range(count_req):
            place = slice(j * state, (j + 1) * state)
            b_part_ref[:, place] = jnp.where(seg == j, b_maps, 0.0).astype(BF16)
            c_part_ref[:, place] = jnp.where(seg == j, c_maps, 0.0).astype(BF16)

    total = own_ref[...].astype(F32)
    for ref in got:
        total = total + ref[...].astype(F32)
    total = total.astype(BF16).astype(F32)
    position, seg, first = token_places(starts, tokens, (tokens, channels), 0)
    cache = cached_rows(
        ints_ref, row_refs, count_req, count_req, places, per_place, pl.program_id(0), channels
    )
    values = conv_silu(total, cache, const_ref, seg, position - first)
    inputs = values.astype(BF16)
    values = inputs.astype(F32)

    lane_head = lax.broadcasted_iota(jnp.int32, (tokens, channels), 1) // width
    scores = scores_ref[...]
    small = small_ref[0]
    tall = small.T
    cum_t, step_t = small[:heads], small[heads : 2 * heads]
    cum, coef = tall[:, :heads], tall[:, 2 * heads :]
    grown = jnp.exp(cum)
    grown_wide = jnp.zeros((tokens, channels), F32)
    coef_wide = jnp.zeros((tokens, channels), F32)
    result = jnp.zeros((tokens, channels), F32)
    for h in range(heads):
        gap = jnp.minimum(cum[:, h : h + 1] - cum_t[h : h + 1, :], 0.0)
        weights = (jnp.exp(gap) * scores * step_t[h : h + 1, :]).astype(BF16)
        mine = lane_head == h
        result = result + jnp.dot(
            weights, jnp.where(mine, values, 0.0).astype(BF16), preferred_element_type=F32
        )
        grown_wide = jnp.where(mine, grown[:, h : h + 1], grown_wide)
        coef_wide = jnp.where(mine, coef[:, h : h + 1], coef_wide)

    from_state = jnp.zeros((tokens, channels), F32)
    carried = (coef_wide * values).astype(BF16)
    fresh = lax.dot_general(
        carried, b_part_ref[...], (((0,), (0,)), ((), ())), preferred_element_type=F32
    )
    for j in range(count_req):
        place = slice(j * state, (j + 1) * state)
        start = pools[j][0].reshape(channels, state) * flag(j, 0)
        for step in range(got_total):
            start = start + states[step][j].astype(F32) * flag(j, step + 1)
        from_state = from_state + lax.dot_general(
            c_part_ref[:, place],
            start.astype(BF16),
            (((1,), (1,)), ((), ())),
            preferred_element_type=F32,
        )
        first_head = pl.program_id(0) * heads
        for h in range(heads):
            rows = slice(h * width, (h + 1) * width)
            state_ref[j, h] = decay_ref[j, first_head + h] * start[rows] + fresh[rows, place]
    out_ref[...] = result + grown_wide * from_state + skip * values


def mixer(
    ints, own, got, row_arrays, row_total, const, b_maps, c_maps, small, decay, pool, states,
    per_place, places
):
    tokens, channels = own.shape
    _, heads, width, state = pool.shape
    count_req = row_arrays[0].shape[0]
    first_slot = ints.shape[0] - count_req
    part = min(HEADS_STEP, heads)
    steps = heads // part
    wide = part * width
    columns = lambda i, *_: (0, i)
    whole = lambda i, *_: (0, 0)

    in_specs = (
        [pl.BlockSpec((tokens, wide), columns)] * (1 + len(got))
        + [rows_spec(array, row_total) for array in row_arrays]
        + [
            pl.BlockSpec((const.shape[0], wide), columns),
            pl.BlockSpec((tokens, state), whole),
            pl.BlockSpec((tokens, state), whole),
            pl.BlockSpec((1,) + small.shape[1:], lambda i, *_: (i, 0, 0)),
            pl.BlockSpec(memory_space=pltpu.SMEM),
        ]
        + [
            pl.BlockSpec(
                (1, part, width, state),
                functools.partial(lambda at, i, ints: (ints[at], i, 0, 0), first_slot + j),
            )
            for j in range(count_req)
        ]
        + [pl.BlockSpec((count_req, wide, state), lambda i, *_: (0, i, 0))] * len(states)
    )
    return pl.pallas_call(
        functools.partial(mixer_kernel, count_req, len(got), per_place, places),
        out_shape=[
            jax.ShapeDtypeStruct((tokens, channels), F32),
            jax.ShapeDtypeStruct((count_req, heads, width, state), F32),
        ],
        grid_spec=pltpu.PrefetchScalarGridSpec(
            num_scalar_prefetch=1,
            grid=(steps,),
            in_specs=in_specs,
            out_specs=[
                pl.BlockSpec((tokens, wide), columns),
                pl.BlockSpec((count_req, part, width, state), lambda i, *_: (0, i, 0, 0)),
            ],
            scratch_shapes=[
                pltpu.VMEM((tokens, tokens), F32),
                pltpu.VMEM((tokens, count_req * state), BF16),
                pltpu.VMEM((tokens, count_req * state), BF16),
            ],
        ),
        compiler_params=params(3 * VMEM_BYTES),
        cost_estimate=cost(1e6, 1e4),
    )(
        ints, own, *got, *row_arrays, const, b_maps, c_maps, small, decay,
        *([pool] * count_req), *states
    )


def on_device(
    x_in,
    w_xz,
    w_dt,
    w_bc,
    dt_bias,
    a_log,
    d_skip,
    conv_x_w,
    conv_x_b,
    conv_bc_w,
    conv_bc_b,
    norm_gain,
    stretch_start,
    prefix_len,
    state_slot,
    ssm_pool,
    conv_x_pool,
    conv_bc_pool,
):
    local_width = w_xz.shape[2]
    state_part = w_bc.shape[1]
    me = lax.axis_index("req")
    req_count = lax.axis_size("req")
    slot_count, heads, head_width, state = ssm_pool.shape
    group_reqs = prefix_len.shape[0]
    lags = conv_x_pool.shape[1]

    direct = req_count == 2 and lax.axis_size("wide") == 16
    if direct:
        own_block, block = near_blocks(x_in)

    def slots_of(index):
        asked = lax.dynamic_slice_in_dim(state_slot, index * group_reqs, group_reqs)
        return jnp.clip(asked - me * slot_count, 0, slot_count - 1)

    per_place = -(-local_width // state) - (-state_part // state)
    row_total = -(-lags * per_place // 16) * 16
    conv_pools = (conv_x_pool, conv_bc_pool)
    got_states = []
    for step in range(1, req_count):
        slots = slots_of((me + step) % req_count)
        packed = pack(ssm_pool, conv_pools, row_total, slots)
        got_states.append(shift_req(packed, step))

    w_step = w_dt
    if direct:
        block = after(block, packed)
        along_z = partner_2(block, "wide", 2)
        along_x = partner_2(block, "wide", 1)
        (
            w_step, state_slot, prefix_len, stretch_start, conv_x_w,
            conv_x_b, conv_bc_w, conv_bc_b, d_skip, norm_gain, dt_bias, a_log
        ) = lax.optimization_barrier((
            (
                w_dt, state_slot, prefix_len, stretch_start, conv_x_w,
                conv_x_b, conv_bc_w, conv_bc_b, d_skip, norm_gain, dt_bias, a_log
            ),
            block,
        ))[0]
        w_step = pinned(w_step)
    own_slots = slots_of(me)
    asked = lax.dynamic_slice_in_dim(state_slot, me * group_reqs, group_reqs)
    came_from = (me - asked // slot_count) % req_count
    live = prefix_len > 0
    flags = (live[:, None] & (came_from[:, None] == jnp.arange(req_count)[None, :])).astype(
        jnp.int32
    )

    kernel_len = conv_x_w.shape[0]
    skip = jnp.repeat(d_skip, head_width)
    const_x = jnp.stack(
        [conv_x_w[k] for k in range(kernel_len)]
        + [conv_x_b, skip, norm_gain, jnp.zeros_like(skip)]
    )
    wide_heads = lambda array: jnp.pad(array, (0, state_part - heads))
    const_bc = jnp.stack(
        [conv_bc_w[k] for k in range(kernel_len)]
        + [conv_bc_b, wide_heads(dt_bias), wide_heads(a_log), jnp.zeros_like(conv_bc_b)]
    )
    ints = jnp.concatenate([stretch_start[0], flags.reshape(-1), own_slots])
    own_rows = own_rows_of(conv_pools, row_total, ints, group_reqs, state)
    if direct:
        both = partner_2(along_z, "wide", 1)
        own_block = after(own_block, along_z)
        own_z = partner_2(own_block, "wide", 2)
        near_three = [array[None] for array in (block, along_z, along_x)]
        core_three = [partner_2(array, "wide", 0) for array in near_three]
        both = after(both[None], w_step, const_x, const_bc, ints, own_rows)
        core_both = after(partner_2(both, "wide", 0), *got_states)
        theirs = quad_arrange(
            near_three + [both] + core_three + [core_both], [0, 4, 2, 6, 1, 5, 3, 7]
        )
        own_pair = after(jnp.stack([own_block, own_z]), theirs)
        own_got = partner_2(own_pair, "wide", 1)
        features = [own_got, theirs]
    else:
        features = features_in_general(x_in)
    w_map = jnp.concatenate([w_bc, w_step], 1)

    def project(block, kind):
        low = jnp.dot(block, w_map, preferred_element_type=F32).astype(BF16)
        low, block = lax.optimization_barrier((low, block))
        high = jnp.einsum("td,dkc->ktc", block, w_xz, preferred_element_type=F32)
        return {"map": low, "xr": high[1].astype(kind), "z": high[0].astype(kind)}

    came = {"map": [], "xr": [], "z": []}
    parts = []
    for step in range(1, req_count):
        part = project(features[step], BF16)
        part = after(part, *got_states) if direct else lax.optimization_barrier(part)
        for name in came:
            came[name].append(shift_req(part[name], step))
        parts.append(part)
    block = features[0]
    if direct:
        own_four = jnp.concatenate([own_pair, after(block, *parts)], 0)
        own_core = partner_2(own_four, "wide", 0)
        block = quad_arrange([own_four, own_core], [0, 4, 2, 6, 1, 5, 3, 7])
    else:
        block = after(block, *parts)
    own = lax.optimization_barrier(project(block, F32))

    row_arrays = [own_rows] + got_states
    bc_conv, small, decay = prep(
        ints, own["map"], came["map"], row_arrays, row_total, const_bc, heads, per_place, lags
    )
    wide_index = lax.axis_index("wide")
    group_span = lax.axis_size("wide") // GROUPS
    bit_total = group_span.bit_length() - 1
    joined = bc_conv
    for bit_index in range(bit_total):
        partner = partner_2(joined, "wide", bit_index)
        upper_half = wide_index // (1 << bit_index) % 2 == 1
        joined = jnp.where(
            upper_half, jnp.concatenate([partner, joined], 1), jnp.concatenate([joined, partner], 1)
        )
    state_width = joined.shape[1] // 2
    came_xr = [after(got, own["xr"], bc_conv) for got in came["xr"]]
    result, final_state = mixer(
        ints, own["xr"], came_xr, row_arrays, row_total, const_x, joined[:, :state_width],
        joined[:, state_width:], small, decay, ssm_pool, got_states,
        per_place, lags
    )
    gate = own["z"].astype(F32)
    for got in came["z"]:
        gate = gate + got.astype(F32)
    gated = result * jax.nn.silu(gate.astype(BF16).astype(F32))
    square_sum = jnp.sum(gated * gated, 1)
    for bit_index in range(bit_total):
        square_sum = square_sum + partner_2(square_sum, "wide", bit_index)
    mean_sq = square_sum / (local_width * group_span)
    normed = gated * lax.rsqrt(mean_sq + NORM_EPS)[:, None] * const_x[kernel_len + 2][None, :]
    return (normed.astype(BF16), final_state)


def solution(mesh):
    in_specs = (
        P("req", "wide"),
        P("req", None, "wide"),
        P("req", "wide"),
        P("req", "wide"),
        P("wide"),
        P("wide"),
        P("wide"),
        P(None, "wide"),
        P("wide"),
        P(None, "wide"),
        P("wide"),
        P("wide"),
        P("req", None),
        P("req"),
        P(),
        P("req", "wide", None, None),
        P("req", None, "wide"),
        P("req", None, "wide"),
    )
    out_specs = (P("req", "wide"), P("req", "wide", None, None))
    return jax.shard_map(
        on_device, mesh=mesh, in_specs=in_specs, out_specs=out_specs, check_vma=False
    )
```
